32 devices in a mesh: dp: 4 (over z), tr: 2 (over x), tc: 4 (over y, core).
Axes of the slice: x: 2, y: 2, z: 4, core: 2. Of those that a mesh axis runs over, the one named last changes fastest.
Arguments:
- tokens: bfloat16 [4096, 2048], P('dp', 'tc'), may hold values from -6 to 6
- cotangent: bfloat16 [4096, 2048], P('dp', 'tc'), may hold values from -6 to 6
- segment_ids: int32 [4096], P('dp'), may hold values from 0 to 4, as said below
- attn_gain: float32 [2048], P('tc'), may hold values from 0.1 to 1.9
- q_gain: float32 [128], replicated, may hold values from 0.1 to 1.9
- k_gain: float32 [128], replicated, may hold values from 0.1 to 1.9
- mlp_gain: float32 [2048], P('tc'), may hold values from 0.1 to 1.9
- w_query: bfloat16 [2048, 2048], P('tc', 'tr'), may hold values from -0.125 to 0.125
- w_key: bfloat16 [2048, 1024], P('tc', 'tr'), may hold values from -0.125 to 0.125
- w_value: bfloat16 [2048, 1024], P('tc', 'tr'), may hold values from -0.125 to 0.125
- w_out: bfloat16 [2048, 2048], P('tr', 'tc'), may hold values from -1.5 to 1.5
- w_gate: bfloat16 [2048, 6144], P('tc', 'tr'), may hold values from -0.125 to 0.125
- w_up: bfloat16 [2048, 6144], P('tc', 'tr'), may hold values from -0.125 to 0.125
- w_down: bfloat16 [6144, 2048], P('tr', 'tc'), may hold values from -0.078125 to 0.078125
Outputs:
- mixed: bfloat16 [4096, 2048], P('dp', 'tc')
- token_grad: bfloat16 [4096, 2048], P('dp', 'tc')
- attn_gain_grad: float32 [2048], P('tc')
- q_gain_grad: float32 [128], replicated
- k_gain_grad: float32 [128], replicated
- mlp_gain_grad: float32 [2048], P('tc')
- w_query_grad: float32 [2048, 2048], P('tc', 'tr')
- w_key_grad: float32 [2048, 1024], P('tc', 'tr')
- w_value_grad: float32 [2048, 1024], P('tc', 'tr')
- w_out_grad: float32 [2048, 2048], P('tr', 'tc')
- w_gate_grad: float32 [2048, 6144], P('tc', 'tr')
- w_up_grad: float32 [2048, 6144], P('tc', 'tr')
- w_down_grad: float32 [6144, 2048], P('tr', 'tc')
The draws below stay inside these ranges and needn't reach their ends.
Inputs may be any that keep to these rules, and one draw needn't show every extreme that they name: `segment_ids`: within each aligned block of 1024 rows the ids start at 0, never fall and rise by one at each new sequence; some block holds a single sequence of 1024 tokens and some block holds five sequences.
All inputs are finite; a program needn't handle non-finite values.
Results may differ from the reference program's by a relative error of at most 0.017.
Values may be sent and summed in bfloat16 or wider, within the bound.
No kernel may reach another device: no remote copies, remote signals or barrier semaphores. Data moves between devices by JAX's collectives and lax.ppermute only.
A program may use at most 192 MiB of HBM per device.

```python
import jax
import jax.numpy as jnp
from jax import lax

D = 2048
HEADS = 16
KV_HEADS = 8
HEAD = 128
FF = 6144
TOK_DEV = 1024
TOKENS = 4096


def draw_segment_ids(key, part):
    key = jax.random.fold_in(key, 7)
    groups = TOKENS // TOK_DEV
    quarter = TOK_DEV // 4
    key_cut, key_keep, key_one, key_full = jax.random.split(key, 4)
    offsets = jax.random.randint(key_cut, (groups, 4), 1, quarter)
    cut_rows = offsets + jnp.arange(4, dtype=jnp.int32)[None, :] * quarter
    kept_cuts = jax.random.randint(key_keep, (groups, 4), 0, 2)
    single = jax.random.randint(key_one, (), 0, groups)
    fuller = (single + 1 + jax.random.randint(key_full, (), 0, groups - 1)) % groups
    group_index = jnp.arange(groups, dtype=jnp.int32)[:, None]
    kept_cuts = jnp.where(group_index == single, 0, jnp.where(group_index == fuller, 1, kept_cuts))
    row_index = jnp.arange(TOK_DEV, dtype=jnp.int32)[None, None, :]
    segment = jnp.sum(kept_cuts[:, :, None] * (row_index >= cut_rows[:, :, None]).astype(jnp.int32), axis=1)
    return segment.reshape(TOKENS).astype(jnp.int32)


def shard_levels(own_key, extent, cuts, low, top_value):
    factor_of, own = 1.0, jax.random.fold_in(own_key, 6)
    for position, parts in cuts:
        heights = jnp.exp(jax.random.uniform(jax.random.fold_in(own, position), (parts,), jnp.float32, low / len(cuts), top_value / len(cuts)))
        factor_of = factor_of * jnp.repeat(heights, extent[position] // parts).reshape([-1 if axis == position else 1 for axis in range(len(extent))])
    return factor_of


def scatter_about(own_key, dims, scale, most, shards=(), kind=jnp.bfloat16):
    array = jax.random.normal(own_key, dims, jnp.float32) * scale
    if len(shards) > 0:
        array = shard_levels(own_key, dims, shards, -0.22, 0.18) * array
    return jnp.clip(array, min=-most, max=most).astype(kind)


def setup_inputs(seed: int = 0) -> dict:
    key_of = jax.random.split(jax.random.key(seed), 15)
    tokens = scatter_about(key_of[0], (TOKENS, D), 1.0, 6.0, ((0, 4), (1, 4)))
    cotangent = scatter_about(key_of[1], (TOKENS, D), 1.0, 6.0, ((0, 4), (1, 4)))
    segment_ids = draw_segment_ids(jax.random.fold_in(key_of[14], 71), 0)
    attn_gain = jnp.clip(1.0 + 0.18 * jax.random.normal(key_of[3], (D,), jnp.float32), 0.1, 1.9)
    q_gain = jnp.clip(1.0 + 0.18 * jax.random.normal(key_of[4], (HEAD,), jnp.float32), 0.1, 1.9)
    k_gain = jnp.clip(1.0 + 0.18 * jax.random.normal(key_of[5], (HEAD,), jnp.float32), 0.1, 1.9)
    mlp_gain = jnp.clip(1.0 + 0.18 * jax.random.normal(key_of[6], (D,), jnp.float32), 0.1, 1.9)
    w_query = scatter_about(key_of[7], (D, HEADS * HEAD), D ** -0.5, 0.125, ((0, 4), (1, 2)))
    w_key = scatter_about(key_of[8], (D, KV_HEADS * HEAD), D ** -0.5, 0.125, ((0, 4), (1, 2)))
    w_value = scatter_about(key_of[9], (D, KV_HEADS * HEAD), D ** -0.5, 0.125, ((0, 4), (1, 2)))
    w_out = scatter_about(key_of[10], (HEADS * HEAD, D), 16 ** -0.5, 1.5, ((0, 2), (1, 4)))
    w_gate = scatter_about(key_of[11], (D, FF), D ** -0.5, 0.125, ((0, 4), (1, 2)))
    w_up = scatter_about(key_of[12], (D, FF), D ** -0.5, 0.125, ((0, 4), (1, 2)))
    w_down = scatter_about(key_of[13], (FF, D), FF ** -0.5, 0.078125, ((0, 2), (1, 4)))
    return dict(tokens=tokens, cotangent=cotangent, segment_ids=segment_ids, attn_gain=attn_gain, q_gain=q_gain, k_gain=k_gain, mlp_gain=mlp_gain, w_query=w_query, w_key=w_key, w_value=w_value, w_out=w_out, w_gate=w_gate, w_up=w_up, w_down=w_down)


norm_eps = 1e-06
rope_base = 1000000.0
neg_big = -1e+30
highest = lax.Precision.HIGHEST

@jax.custom_vjp
def low(v):
    return lax.optimization_barrier(v.astype(jnp.bfloat16)).astype(jnp.float32)

@jax.custom_vjp
def low_back(v):
    return v

def low_keep(v):
    return (low(v), None)

def low_pass(kept, grad):
    return (grad,)

def back_keep(v):
    return (v, None)

def back_low(kept, grad):
    return (low(grad),)
low.defvjp(low_keep, low_pass)
low_back.defvjp(back_keep, back_low)

def positions_of(segment):
    slot_ids = jnp.arange(5, dtype=jnp.int32)
    before = lax.optimization_barrier(jnp.sum((segment[None, :] < slot_ids[:, None]).astype(jnp.int32), axis=1))
    starts = lax.optimization_barrier(jnp.sum(jnp.where(segment[:, None] == slot_ids[None, :], before[None, :], 0), axis=1))
    return jnp.arange(segment.shape[0], dtype=jnp.int32) - starts.astype(jnp.int32)

def rope_tables(positions, head_size):
    half_size = head_size // 2
    frequency = rope_base ** (-jnp.arange(half_size, dtype=jnp.float32) * 2.0 / head_size)
    angles = positions.astype(jnp.float32)[:, None] * frequency[None, :]
    angles = jnp.concatenate([angles, angles], axis=1)
    return (jnp.cos(angles), jnp.sin(angles))

def rotate(vectors, cos_table, sin_table):
    half_size = vectors.shape[-1] // 2
    turned = jnp.concatenate([-vectors[..., half_size:], vectors[..., :half_size]], axis=-1)
    return vectors * cos_table[:, None, :] + turned * sin_table[:, None, :]

def rms_norm(vectors, gain):
    return vectors * lax.rsqrt(lax.optimization_barrier(jnp.mean(vectors * vectors, axis=-1, keepdims=True)) + norm_eps) * gain

def layer(inputs, attn_gain, q_gain, k_gain, mlp_gain, w_query, w_key, w_value, w_out, w_gate, w_up, w_down, segment):
    row_count = inputs.shape[0]
    normed = low(rms_norm(inputs, attn_gain))
    q_raw = low_back(jnp.dot(normed, w_query, precision=highest, preferred_element_type=jnp.float32))
    k_raw = low_back(jnp.dot(normed, w_key, precision=highest, preferred_element_type=jnp.float32))
    v_raw = low_back(jnp.dot(normed, w_value, precision=highest, preferred_element_type=jnp.float32))
    positions = positions_of(segment)
    cos_table, sin_table = rope_tables(positions, HEAD)
    queries = low(rotate(rms_norm(q_raw.reshape(row_count, HEADS, HEAD), q_gain), cos_table, sin_table))
    keys = low(rotate(rms_norm(k_raw.reshape(row_count, KV_HEADS, HEAD), k_gain), cos_table, sin_table))
    values = low(v_raw).reshape(row_count, KV_HEADS, HEAD)
    repeat_count = HEADS // KV_HEADS
    keys_all = jnp.repeat(keys, repeat_count, axis=1)
    values_all = jnp.repeat(values, repeat_count, axis=1)
    block_rows = min(512, row_count)
    block_count = row_count // block_rows
    scale = HEAD ** (-0.5)
    key_index = jnp.arange(row_count, dtype=jnp.int32)

    @jax.checkpoint
    def one_block(start):
        query_block = lax.dynamic_slice_in_dim(queries, start, block_rows, 0)
        segment_block = lax.dynamic_slice_in_dim(segment, start, block_rows, 0)
        query_index = start + jnp.arange(block_rows, dtype=jnp.int32)
        scores = jnp.einsum('qhd,khd->hqk', query_block, keys_all, precision=highest)
        scores = low_back(scores * scale)
        allowed = (segment_block[:, None] == segment[None, :]) & (key_index[None, :] <= query_index[:, None])
        scores = jnp.where(allowed[None, :, :], scores, neg_big)
        top = lax.optimization_barrier(jnp.max(scores, axis=-1, keepdims=True))
        expd = jnp.exp(scores - top)
        probs = expd / lax.optimization_barrier(jnp.sum(expd, axis=-1, keepdims=True))
        return jnp.einsum('hqk,khd->qhd', low(probs), values_all, precision=highest)
    starts = jnp.arange(block_count, dtype=jnp.int32) * block_rows
    attended = lax.map(one_block, starts).reshape(row_count, HEADS * HEAD)
    attn_out = low_back(jnp.dot(low(attended), w_out, precision=highest, preferred_element_type=jnp.float32))
    residual = inputs + attn_out
    mlp_in = low(rms_norm(residual, mlp_gain))
    gate = low_back(jnp.dot(mlp_in, w_gate, precision=highest, preferred_element_type=jnp.float32))
    up_proj = low_back(jnp.dot(mlp_in, w_up, precision=highest, preferred_element_type=jnp.float32))
    hidden = low(gate * jax.nn.sigmoid(gate) * up_proj)
    mlp_out = jnp.dot(hidden, w_down, precision=highest, preferred_element_type=jnp.float32)
    return residual + mlp_out

def reference(tokens, cotangent, segment_ids, attn_gain, q_gain, k_gain, mlp_gain, w_query, w_key, w_value, w_out, w_gate, w_up, w_down):
    params = tuple((param.astype(jnp.float32) for param in (attn_gain, q_gain, k_gain, mlp_gain, w_query, w_key, w_value, w_out, w_gate, w_up, w_down)))
    groups = TOKENS // TOK_DEV
    token_groups = tokens.reshape(groups, TOK_DEV, D)
    grad_groups = cotangent.reshape(groups, TOK_DEV, D)
    segment_groups = segment_ids.reshape(groups, TOK_DEV)

    def step(carry, group):
        group_tokens, group_grad, group_segment = group

        def forward(inputs, *weights):
            return layer(inputs, *weights, group_segment)
        result, pull = jax.vjp(forward, group_tokens.astype(jnp.float32), *params)
        grads = pull(group_grad.astype(jnp.float32))
        carry = tuple((total + grad for total, grad in zip(carry, grads[1:])))
        return (carry, (result.astype(jnp.bfloat16), grads[0].astype(jnp.bfloat16)))
    init = tuple((jnp.zeros(param.shape, jnp.float32) for param in params))
    totals, (mixed, token_grad) = lax.scan(step, init, (token_groups, grad_groups, segment_groups))
    return (mixed.reshape(TOKENS, D), token_grad.reshape(TOKENS, D), totals[0], totals[1], totals[2], totals[3], totals[4], totals[5], totals[6], totals[7], totals[8], totals[9], totals[10])
```

```python
import jax
import jax.numpy as jnp
from jax import lax
from jax.sharding import PartitionSpec as P

norm_eps = 1e-06
rope_base = 1000000.0
neg_big = -1e30
f32 = jnp.float32
bf16 = jnp.bfloat16


def dot(left_side, right_side):
    return jnp.dot(left_side, right_side, preferred_element_type=f32)


def contract_rows(left_side, right_side):
    return lax.dot_general(
        left_side, right_side, (((0,), (0,)), ((), ())), preferred_element_type=f32
    )


def contract_cols(left_side, right_side):
    return lax.dot_general(
        left_side, right_side, (((1,), (1,)), ((), ())), preferred_element_type=f32
    )


def swap_core(block):
    return lax.ppermute(block, "tc", [(i, i ^ 1) for i in range(4)])


def swap_y(block):
    return lax.ppermute(block, "tc", [(i, i ^ 2) for i in range(4)])


def swap_diag(block):
    return lax.ppermute(block, "tc", [(i, i ^ 3) for i in range(4)])


def swap_x(block):
    return lax.ppermute(block, "tr", [(0, 1), (1, 0)])


def width_total(rows):
    rows = rows + swap_core(rows)
    return rows + swap_y(rows)


def line_total(piece):
    size = lax.axis_size("dp")
    place = lax.axis_index("dp")
    half = size // 2
    for step in range(half - 1):
        got = lax.ppermute(piece, "dp", [(step, step + 1), (size - 1 - step, size - 2 - step)])
        piece = (piece.astype(f32) + got.astype(f32)).astype(piece.dtype)
    got = lax.ppermute(piece, "dp", [(half - 1, half), (half, half - 1)])
    piece = (piece.astype(f32) + got.astype(f32)).astype(piece.dtype)
    for step in reversed(range(half - 1)):
        got = lax.ppermute(piece, "dp", [(step + 1, step), (size - 2 - step, size - 1 - step)])
        piece = jnp.where((place == step) | (place == size - 1 - step), got, piece)
    return piece


def scatter_width(near, far):
    total = near.astype(f32) + swap_core(far).astype(f32)
    cols = total.shape[1] // 2
    sent = swap_y(total[:, cols:].astype(bf16))
    return total[:, :cols] + sent.astype(f32)


def positions_of(segment):
    slot_ids = jnp.arange(5, dtype=jnp.int32)
    before = jnp.sum((segment[None, :] < slot_ids[:, None]).astype(jnp.int32), axis=1)
    starts = jnp.sum(jnp.where(segment[:, None] == slot_ids[None, :], before[None, :], 0), axis=1)
    return jnp.arange(segment.shape[0], dtype=jnp.int32) - starts


def rope_tables(positions, head_size):
    half_size = head_size // 2
    frequency = rope_base ** (-jnp.arange(half_size, dtype=f32) * 2.0 / head_size)
    angles = positions.astype(f32)[:, None] * frequency[None, :]
    angles = jnp.concatenate([angles, angles], axis=1)
    return (jnp.cos(angles), jnp.sin(angles))


def rotate(vectors, cos_table, sin_table):
    half_size = vectors.shape[-1] // 2
    turned = jnp.concatenate([-vectors[..., half_size:], vectors[..., :half_size]], axis=-1)
    return vectors * cos_table[:, None, :] + turned * sin_table[:, None, :]


def head_norm(vectors, gain):
    return (
        vectors * lax.rsqrt(jnp.mean(vectors * vectors, axis=-1, keepdims=True) + norm_eps) * gain
    )


def block_mask(segment, start, block_rows):
    segment_block = lax.dynamic_slice_in_dim(segment, start, block_rows, 0)
    query_index = start + jnp.arange(block_rows, dtype=jnp.int32)
    key_index = jnp.arange(segment.shape[0], dtype=jnp.int32)
    return (segment_block[:, None] == segment[None, :]) & (
        key_index[None, :] <= query_index[:, None]
    )


def attend_forward(queries, keys, values, segment):
    row_count = queries.shape[0]
    block_rows = min(512, row_count)
    block_count = row_count // block_rows
    scale = queries.shape[-1] ** (-0.5)

    def one_block(index):
        start = index * block_rows
        query_block = lax.dynamic_slice_in_dim(queries, start, block_rows, 0)
        scores = (
            jnp.einsum("qgrd,kgd->grqk", query_block, keys, preferred_element_type=f32) * scale
        )
        allowed = block_mask(segment, start, block_rows)
        scores = jnp.where(allowed[None, None, :, :], scores, neg_big)
        top = jnp.max(scores, axis=-1, keepdims=True)
        expd = jnp.exp(scores - top)
        total = jnp.sum(expd, axis=-1, keepdims=True)
        weights = (expd / total).astype(bf16)
        outputs = jnp.einsum("grqk,kgd->qgrd", weights, values, preferred_element_type=f32)
        return (outputs, (top + jnp.log(total))[..., 0])

    outputs, log_totals = lax.map(one_block, jnp.arange(block_count, dtype=jnp.int32))
    return (outputs.reshape(queries.shape), log_totals)


def attend_backward(queries, keys, values, segment, log_totals, out_grad):
    row_count = queries.shape[0]
    block_rows = min(512, row_count)
    block_count = row_count // block_rows
    scale = queries.shape[-1] ** (-0.5)

    def one_block(carry, index):
        key_acc, value_acc = carry
        start = index * block_rows
        query_block = lax.dynamic_slice_in_dim(queries, start, block_rows, 0)
        grad_block = lax.dynamic_slice_in_dim(out_grad, start, block_rows, 0)
        lse_block = lax.dynamic_index_in_dim(log_totals, index, 0, keepdims=False)
        scores = (
            jnp.einsum("qgrd,kgd->grqk", query_block, keys, preferred_element_type=f32) * scale
        )
        allowed = block_mask(segment, start, block_rows)
        scores = jnp.where(allowed[None, None, :, :], scores, neg_big)
        probs = jnp.exp(scores - lse_block[..., None])
        prob_low = probs.astype(bf16)
        prob_grad = jnp.einsum("qgrd,kgd->grqk", grad_block, values, preferred_element_type=f32)
        delta = jnp.sum(probs * prob_grad, axis=-1, keepdims=True)
        score_grad = (probs * (prob_grad - delta)).astype(bf16)
        query_grad = (
            jnp.einsum("grqk,kgd->qgrd", score_grad, keys, preferred_element_type=f32) * scale
        )
        key_acc = (
            key_acc
            + jnp.einsum("grqk,qgrd->kgd", score_grad, query_block, preferred_element_type=f32)
            * scale
        )
        value_acc = value_acc + jnp.einsum(
            "grqk,qgrd->kgd", prob_low, grad_block, preferred_element_type=f32
        )
        return ((key_acc, value_acc), query_grad)

    empty = jnp.zeros(keys.shape, f32)
    (key_grad, value_grad), query_grads = lax.scan(
        one_block, (empty, empty), jnp.arange(block_count, dtype=jnp.int32)
    )
    return (query_grads.reshape(queries.shape), key_grad, value_grad)


def on_device(
    tokens,
    cotangent,
    segment_ids,
    attn_gain,
    q_gain,
    k_gain,
    mlp_gain,
    w_query,
    w_key,
    w_value,
    w_out,
    w_gate,
    w_up,
    w_down,
):
    assert lax.axis_size("tc") == 4 and lax.axis_size("tr") == 2
    col = lax.axis_index("tc")
    side = lax.axis_index("tr")
    rows, width = tokens.shape
    half = rows // 2
    full_width = width * 4
    head_size = q_gain.shape[0]
    q_width = w_query.shape[1] // 4
    k_width = w_key.shape[1] // 4
    units = w_gate.shape[1] // 4
    around = [col, col ^ 1, col ^ 2, col ^ 3]

    def cols_of(array, which, size):
        return lax.dynamic_slice_in_dim(array, around[which] * size, size, 1)

    def rows_of(array, which, size):
        return lax.dynamic_slice_in_dim(array, around[which] * size, size, 0)

    def flip(array):
        return jnp.concatenate(
            [
                lax.dynamic_slice_in_dim(array, side * half, half, 0),
                lax.dynamic_slice_in_dim(array, (1 - side) * half, half, 0),
            ],
            axis=0,
        )

    def qkv_block(which):
        return [
            cols_of(w_query, which, q_width),
            cols_of(w_key, which, k_width),
            cols_of(w_value, which, k_width),
        ]

    qkv_near = jnp.concatenate(qkv_block(0) + qkv_block(2), axis=1)
    qkv_far = jnp.concatenate(qkv_block(1) + qkv_block(3), axis=1)
    inputs = tokens.astype(f32)
    scaled_in = (inputs * attn_gain[None, :]).astype(bf16)
    square_sum = width_total(jnp.sum(inputs * inputs, axis=1))
    far = dot(scaled_in, qkv_far).astype(bf16)
    near = dot(scaled_in, qkv_near)
    projected = scatter_width(near, far)
    attn_rstd = lax.rsqrt(square_sum / full_width + norm_eps)
    attn_hat = inputs * attn_rstd[:, None]
    normed = (attn_hat * attn_gain[None, :]).astype(bf16)
    projected = projected * attn_rstd[:, None]

    def ffn_block(which):
        return jnp.concatenate(
            [cols_of(w_gate, which, units), cols_of(w_up, which, units)], axis=1
        )

    ffn_own = ffn_block(0)
    ffn_core = swap_core(ffn_block(1))
    ffn_y = swap_y(ffn_block(2))
    ffn_diag = swap_diag(ffn_block(3))
    ffn_near = jnp.concatenate([ffn_own, ffn_y], axis=0)
    ffn_far = jnp.concatenate([ffn_core, ffn_diag], axis=0)

    cot_rel = flip(cotangent)
    down_near = jnp.concatenate([rows_of(w_down, 0, units), rows_of(w_down, 2, units)], axis=0)
    down_far = jnp.concatenate([rows_of(w_down, 1, units), rows_of(w_down, 3, units)], axis=0)
    hidden_grad = scatter_width(
        contract_cols(cot_rel, down_near), contract_cols(cot_rel, down_far).astype(bf16)
    )

    positions = positions_of(segment_ids)
    cos_table, sin_table = rope_tables(positions, head_size)
    q_raw = projected[:, :q_width].reshape(rows, -1, head_size)
    k_raw = projected[:, q_width : q_width + k_width].reshape(rows, -1, head_size)
    kv_heads = k_raw.shape[1]
    v_low = projected[:, q_width + k_width :].astype(bf16).reshape(rows, kv_heads, head_size)

    def prepare(query_in, key_in, query_gain, key_gain):
        return (
            rotate(head_norm(query_in, query_gain), cos_table, sin_table),
            rotate(head_norm(key_in, key_gain), cos_table, sin_table),
        )

    (q_rot, k_rot), prepare_back = jax.vjp(prepare, q_raw, k_raw, q_gain, k_gain)
    q_low = q_rot.astype(bf16).reshape(rows, kv_heads, -1, head_size)
    k_low = k_rot.astype(bf16)
    attended, log_totals = attend_forward(q_low, k_low, v_low, segment_ids)
    att_rel = flip(attended.reshape(rows, -1).astype(bf16))
    heads_near = jnp.concatenate([att_rel, swap_y(att_rel)], axis=1)
    heads_far = swap_core(heads_near)
    out_near = jnp.concatenate([rows_of(w_out, 0, q_width), rows_of(w_out, 2, q_width)], axis=0)
    out_far = jnp.concatenate([rows_of(w_out, 1, q_width), rows_of(w_out, 3, q_width)], axis=0)
    away = dot(heads_near[half:], out_near) + dot(heads_far[half:], out_far)
    from_x = swap_x(away.astype(bf16))
    home = dot(heads_near[:half], out_near) + dot(heads_far[:half], out_far)
    tokens_half = lax.dynamic_slice_in_dim(tokens, side * half, half, 0).astype(f32)
    residual = tokens_half + home + from_x.astype(f32)

    mlp_square = width_total(jnp.sum(residual * residual, axis=1))
    mlp_own = (residual * mlp_gain[None, :]).astype(bf16)
    mlp_rstd = lax.rsqrt(mlp_square / full_width + norm_eps)
    rstd_rel = jnp.concatenate([mlp_rstd, swap_x(mlp_rstd)])
    quarter = half // 2
    mlp_x = swap_x(mlp_own)
    mlp_y = swap_y(mlp_own)
    mlp_xy = jnp.concatenate([swap_y(mlp_x[:quarter]), swap_x(mlp_y[quarter:])], axis=0)
    near_own = jnp.concatenate([mlp_own, mlp_y], axis=1)
    near_other = jnp.concatenate([mlp_x, mlp_xy], axis=1)
    far_own = swap_core(near_own)
    far_other = swap_core(near_other)

    def unit_half(near_rows, far_rows, rstd, grad):
        both = (dot(near_rows, ffn_near) + dot(far_rows, ffn_far)) * rstd[:, None]
        gate, up = both[:, :units], both[:, units:]
        sig = jax.nn.sigmoid(gate)
        silu = gate * sig
        hidden = (silu * up).astype(bf16)
        gate_grad = (grad * up * sig * (1.0 + gate * (1.0 - sig))).astype(bf16)
        up_grad = (grad * silu).astype(bf16)
        inner = jnp.sum(gate_grad.astype(f32) * gate + up_grad.astype(f32) * up, axis=1)
        return (hidden, jnp.concatenate([gate_grad, up_grad], axis=1), inner)

    hidden_a, pair_a, inner_a = unit_half(near_own, far_own, rstd_rel[:half], hidden_grad[:half])
    hidden_b, pair_b, inner_b = unit_half(near_other, far_other, rstd_rel[half:], hidden_grad[half:])
    hidden = jnp.concatenate([hidden_a, hidden_b], axis=0)
    pair = jnp.concatenate([pair_a, pair_b], axis=0)
    mlp_in = (
        jnp.concatenate([mlp_own, mlp_x], axis=0).astype(f32) * rstd_rel[:, None]
    ).astype(bf16)

    inner_b_in = swap_x(width_total(inner_b))
    inner_total = width_total(inner_a) + inner_b_in
    back_far = contract_cols(pair, ffn_far).astype(bf16)
    back_near = contract_cols(pair, ffn_near)
    back = (back_near + swap_core(back_far).astype(f32)).astype(bf16)
    x_first = swap_x(jnp.concatenate([back[half : half + quarter]], axis=0))
    y_first = swap_y(
        jnp.concatenate([back[quarter:half, width:], back[half + quarter :, width:]], axis=0)
    )
    top_rows = back[:quarter].astype(f32) + x_first.astype(f32)
    low_own = back[quarter:half, :width].astype(f32) + y_first[:quarter].astype(f32)
    low_other = back[half + quarter :, :width].astype(f32) + y_first[quarter:].astype(f32)
    top_y = swap_y(top_rows[:, width:].astype(bf16))
    low_x = swap_x(low_other.astype(bf16))
    mlp_in_grad = jnp.concatenate(
        [top_rows[:, :width] + top_y.astype(f32), low_own + low_x.astype(f32)], axis=0
    )
    mlp_hat = residual * mlp_rstd[:, None]
    mlp_gain_part = jnp.sum(mlp_in_grad * mlp_hat, axis=0)
    residual_grad = cot_rel[:half].astype(f32) + mlp_rstd[:, None] * (
        mlp_in_grad * mlp_gain[None, :] - mlp_hat * (inner_total / full_width)[:, None]
    )
    residual_low = residual_grad.astype(bf16)
    res_rel = jnp.concatenate([residual_low, swap_x(residual_low)], axis=0)
    head_grad = scatter_width(
        contract_cols(res_rel, out_near), contract_cols(res_rel, out_far).astype(bf16)
    )

    hidden_y = swap_y(hidden)
    hidden_core = swap_core(hidden)
    hidden_diag = swap_core(hidden_y)
    pair_y = swap_y(pair)
    pair_core = swap_core(pair)
    pair_diag = swap_core(pair_y)
    hiddens = [hidden, hidden_core, hidden_y, hidden_diag]
    pairs = [pair, pair_core, pair_y, pair_diag]

    down_grads = [line_total(contract_rows(piece, cot_rel).astype(bf16)) for piece in hiddens]
    ffn_grads = []
    for piece in pairs:
        ffn_grads.append(
            (
                line_total(contract_rows(mlp_in, piece[:, :units]).astype(bf16)),
                line_total(contract_rows(mlp_in, piece[:, units:]).astype(bf16)),
            )
        )
    out_grad = jnp.concatenate(
        [contract_rows(heads_near, res_rel), contract_rows(heads_far, res_rel)], axis=0
    )
    out_grad = line_total(out_grad.astype(bf16))

    mlp_parts = [dot(hiddens[k], rows_of(w_down, k, units)) for k in range(4)]
    mlp_out = (mlp_parts[0] + mlp_parts[1]) + (mlp_parts[2] + mlp_parts[3])
    mlp_from_x = swap_x(mlp_out[half:].astype(bf16))
    mixed_half = (residual + mlp_out[:half] + mlp_from_x.astype(f32)).astype(bf16)
    mixed = flip(jnp.concatenate([mixed_half, swap_x(mixed_half)], axis=0))

    query_grad, key_grad, value_grad = attend_backward(
        q_low,
        k_low,
        v_low,
        segment_ids,
        log_totals,
        flip(head_grad).reshape(rows, kv_heads, -1, head_size),
    )
    q_raw_grad, k_raw_grad, q_gain_part, k_gain_part = prepare_back(
        (query_grad.reshape(rows, -1, head_size), key_grad)
    )
    proj_low = jnp.concatenate(
        [
            q_raw_grad.reshape(rows, -1),
            k_raw_grad.reshape(rows, -1),
            value_grad.reshape(rows, -1),
        ],
        axis=1,
    ).astype(bf16)
    inner_attn = width_total(jnp.sum(proj_low.astype(f32) * projected, axis=1))
    inner_attn = inner_attn + swap_x(inner_attn)
    proj_y = swap_y(proj_low)
    proj_core = swap_core(proj_low)
    proj_diag = swap_core(proj_y)
    proj_near = jnp.concatenate([proj_low, proj_y], axis=1)
    proj_far = jnp.concatenate([proj_core, proj_diag], axis=1)
    normed_part = (contract_cols(proj_near, qkv_near) + contract_cols(proj_far, qkv_far)).astype(
        bf16
    )
    normed_grad = normed_part.astype(f32) + swap_x(normed_part).astype(f32)
    qkv_grads = [
        line_total(contract_rows(normed, piece).astype(bf16))
        for piece in (proj_low, proj_core, proj_y, proj_diag)
    ]
    attn_gain_part = jnp.sum(normed_grad * attn_hat, axis=0)
    token_grad = (
        flip(res_rel).astype(f32)
        + attn_rstd[:, None]
        * (
            normed_grad * attn_gain[None, :]
            - attn_hat * (inner_attn / full_width)[:, None]
        )
    ).astype(bf16)

    head_parts = width_total(jnp.concatenate([q_gain_part, k_gain_part]))
    shared = jnp.concatenate([head_parts, mlp_gain_part])
    shared = shared + swap_x(shared)
    gains = line_total(jnp.concatenate([shared, attn_gain_part]))
    q_gain_grad = gains[:head_size]
    k_gain_grad = gains[head_size : 2 * head_size]
    mlp_gain_grad = gains[2 * head_size : 2 * head_size + width]
    attn_gain_grad = gains[2 * head_size + width :]

    def place_cols(shape, pieces):
        whole = jnp.zeros(shape, f32)
        for which, piece in enumerate(pieces):
            whole = lax.dynamic_update_slice_in_dim(
                whole, piece.astype(f32), around[which] * piece.shape[1], 1
            )
        return whole

    def place_rows(shape, pieces):
        whole = jnp.zeros(shape, f32)
        for which, piece in enumerate(pieces):
            whole = lax.dynamic_update_slice_in_dim(
                whole, piece.astype(f32), around[which] * piece.shape[0], 0
            )
        return whole

    w_query_grad = place_cols(w_query.shape, [g[:, :q_width] for g in qkv_grads])
    w_key_grad = place_cols(w_key.shape, [g[:, q_width : q_width + k_width] for g in qkv_grads])
    w_value_grad = place_cols(w_value.shape, [g[:, q_width + k_width :] for g in qkv_grads])
    out_pieces = [out_grad[i * q_width : (i + 1) * q_width] for i in (0, 2, 1, 3)]
    w_out_grad = place_rows(w_out.shape, out_pieces)
    w_gate_grad = place_cols(w_gate.shape, [g[0] for g in ffn_grads])
    w_up_grad = place_cols(w_up.shape, [g[1] for g in ffn_grads])
    w_down_grad = place_rows(w_down.shape, down_grads)
    return (
        mixed,
        token_grad,
        attn_gain_grad,
        q_gain_grad,
        k_gain_grad,
        mlp_gain_grad,
        w_query_grad,
        w_key_grad,
        w_value_grad,
        w_out_grad,
        w_gate_grad,
        w_up_grad,
        w_down_grad,
    )


def solution(mesh):
    in_specs = (
        P("dp", "tc"),
        P("dp", "tc"),
        P("dp"),
        P("tc"),
        P(),
        P(),
        P("tc"),
        P("tc", "tr"),
        P("tc", "tr"),
        P("tc", "tr"),
        P("tr", "tc"),
        P("tc", "tr"),
        P("tc", "tr"),
        P("tr", "tc"),
    )
    out_specs = (
        P("dp", "tc"),
        P("dp", "tc"),
        P("tc"),
        P(),
        P(),
        P("tc"),
        P("tc", "tr"),
        P("tc", "tr"),
        P("tc", "tr"),
        P("tr", "tc"),
        P("tc", "tr"),
        P("tc", "tr"),
        P("tr", "tc"),
    )
    return jax.shard_map(
        on_device, mesh=mesh, in_specs=in_specs, out_specs=out_specs, check_vma=False
    )
```

```python
import jax
import jax.numpy as jnp
from jax import lax
from jax.sharding import PartitionSpec as P

norm_eps = 1e-06
rope_base = 1000000.0
neg_big = -1e30
f32 = jnp.float32
bf16 = jnp.bfloat16


def dot(left_side, right_side):
    return jnp.dot(left_side, right_side, preferred_element_type=f32)


def contract_rows(left_side, right_side):
    return lax.dot_general(
        left_side, right_side, (((0,), (0,)), ((), ())), preferred_element_type=f32
    )


def contract_cols(left_side, right_side):
    return lax.dot_general(
        left_side, right_side, (((1,), (1,)), ((), ())), preferred_element_type=f32
    )


def swap_core(block):
    return lax.ppermute(block, "tc", [(i, i ^ 1) for i in range(4)])


def swap_y(block):
    return lax.ppermute(block, "tc", [(i, i ^ 2) for i in range(4)])


def swap_diag(block):
    return lax.ppermute(block, "tc", [(i, i ^ 3) for i in range(4)])


def swap_x(block):
    return lax.ppermute(block, "tr", [(0, 1), (1, 0)])


def width_total(rows):
    rows = rows + swap_core(rows)
    return rows + swap_y(rows)


def line_total(piece):
    size = lax.axis_size("dp")
    place = lax.axis_index("dp")
    half = size // 2
    for step in range(half - 1):
        got = lax.ppermute(piece, "dp", [(step, step + 1), (size - 1 - step, size - 2 - step)])
        piece = (piece.astype(f32) + got.astype(f32)).astype(piece.dtype)
    got = lax.ppermute(piece, "dp", [(half - 1, half), (half, half - 1)])
    piece = (piece.astype(f32) + got.astype(f32)).astype(piece.dtype)
    for step in reversed(range(half - 1)):
        got = lax.ppermute(piece, "dp", [(step + 1, step), (size - 2 - step, size - 1 - step)])
        piece = jnp.where((place == step) | (place == size - 1 - step), got, piece)
    return piece


def scatter_width(near, far):
    total = near.astype(f32) + swap_core(far).astype(f32)
    cols = total.shape[1] // 2
    sent = swap_y(total[:, cols:].astype(bf16))
    return total[:, :cols] + sent.astype(f32)


def scatter_all(near, far):
    total = (near.astype(f32) + swap_core(far).astype(f32)).astype(bf16)
    half = total.shape[0] // 2
    quarter = half // 2
    width = total.shape[1] // 2
    x_first = swap_x(total[half : half + quarter])
    y_first = swap_y(
        jnp.concatenate([total[quarter:half, width:], total[half + quarter :, width:]], axis=0)
    )
    top = total[:quarter].astype(f32) + x_first.astype(f32)
    low_own = total[quarter:half, :width].astype(f32) + y_first[:quarter].astype(f32)
    low_other = total[half + quarter :, :width].astype(f32) + y_first[quarter:].astype(f32)
    top_y = swap_y(top[:, width:].astype(bf16))
    low_x = swap_x(low_other.astype(bf16))
    return jnp.concatenate(
        [top[:, :width] + top_y.astype(f32), low_own + low_x.astype(f32)], axis=0
    )


def after(value, *others):
    return lax.optimization_barrier((value, others))[0]


def shares_of_sum(blocks):
    return [lax.psum_scatter(b, "dp", scatter_dimension=0, tiled=True) for b in blocks]


def whole_of(shares):
    return [lax.all_gather(b, "dp", axis=0, tiled=True) for b in shares]


def positions_of(segment):
    slot_ids = jnp.arange(5, dtype=jnp.int32)
    before = jnp.sum((segment[None, :] < slot_ids[:, None]).astype(jnp.int32), axis=1)
    starts = jnp.sum(jnp.where(segment[:, None] == slot_ids[None, :], before[None, :], 0), axis=1)
    return jnp.arange(segment.shape[0], dtype=jnp.int32) - starts


def rope_tables(positions, head_size):
    half_size = head_size // 2
    frequency = rope_base ** (-jnp.arange(half_size, dtype=f32) * 2.0 / head_size)
    angles = positions.astype(f32)[:, None] * frequency[None, :]
    angles = jnp.concatenate([angles, angles], axis=1)
    return (jnp.cos(angles), jnp.sin(angles))


def rotate(vectors, cos_table, sin_table):
    half_size = vectors.shape[-1] // 2
    turned = jnp.concatenate([-vectors[..., half_size:], vectors[..., :half_size]], axis=-1)
    return vectors * cos_table[:, None, :] + turned * sin_table[:, None, :]


def head_norm(vectors, gain):
    return (
        vectors * lax.rsqrt(jnp.mean(vectors * vectors, axis=-1, keepdims=True) + norm_eps) * gain
    )


def block_mask(segment, start, block_rows):
    segment_block = lax.dynamic_slice_in_dim(segment, start, block_rows, 0)
    query_index = start + jnp.arange(block_rows, dtype=jnp.int32)
    key_index = jnp.arange(segment.shape[0], dtype=jnp.int32)
    return (segment_block[:, None] == segment[None, :]) & (
        key_index[None, :] <= query_index[:, None]
    )


def attend_forward(queries, keys, values, segment):
    row_count = queries.shape[0]
    block_rows = min(512, row_count)
    block_count = row_count // block_rows
    scale = queries.shape[-1] ** (-0.5)

    def one_block(index):
        start = index * block_rows
        query_block = lax.dynamic_slice_in_dim(queries, start, block_rows, 0)
        scores = (
            jnp.einsum("qgrd,kgd->grqk", query_block, keys, preferred_element_type=f32) * scale
        )
        allowed = block_mask(segment, start, block_rows)
        scores = jnp.where(allowed[None, None, :, :], scores, neg_big)
        top = jnp.max(scores, axis=-1, keepdims=True)
        expd = jnp.exp(scores - top)
        total = jnp.sum(expd, axis=-1, keepdims=True)
        weights = (expd / total).astype(bf16)
        outputs = jnp.einsum("grqk,kgd->qgrd", weights, values, preferred_element_type=f32)
        return (outputs, (top + jnp.log(total))[..., 0])

    outputs, log_totals = lax.map(one_block, jnp.arange(block_count, dtype=jnp.int32))
    return (outputs.reshape(queries.shape), log_totals)


def attend_backward(queries, keys, values, segment, log_totals, out_grad):
    row_count = queries.shape[0]
    block_rows = min(512, row_count)
    block_count = row_count // block_rows
    scale = queries.shape[-1] ** (-0.5)

    def one_block(carry, index):
        key_acc, value_acc = carry
        start = index * block_rows
        query_block = lax.dynamic_slice_in_dim(queries, start, block_rows, 0)
        grad_block = lax.dynamic_slice_in_dim(out_grad, start, block_rows, 0)
        lse_block = lax.dynamic_index_in_dim(log_totals, index, 0, keepdims=False)
        scores = (
            jnp.einsum("qgrd,kgd->grqk", query_block, keys, preferred_element_type=f32) * scale
        )
        allowed = block_mask(segment, start, block_rows)
        scores = jnp.where(allowed[None, None, :, :], scores, neg_big)
        probs = jnp.exp(scores - lse_block[..., None])
        prob_low = probs.astype(bf16)
        prob_grad = jnp.einsum("qgrd,kgd->grqk", grad_block, values, preferred_element_type=f32)
        delta = jnp.sum(probs * prob_grad, axis=-1, keepdims=True)
        score_grad = (probs * (prob_grad - delta)).astype(bf16)
        query_grad = (
            jnp.einsum("grqk,kgd->qgrd", score_grad, keys, preferred_element_type=f32) * scale
        )
        key_acc = (
            key_acc
            + jnp.einsum("grqk,qgrd->kgd", score_grad, query_block, preferred_element_type=f32)
            * scale
        )
        value_acc = value_acc + jnp.einsum(
            "grqk,qgrd->kgd", prob_low, grad_block, preferred_element_type=f32
        )
        return ((key_acc, value_acc), query_grad)

    empty = jnp.zeros(keys.shape, f32)
    (key_grad, value_grad), query_grads = lax.scan(
        one_block, (empty, empty), jnp.arange(block_count, dtype=jnp.int32)
    )
    return (query_grads.reshape(queries.shape), key_grad, value_grad)


def on_device(
    tokens,
    cotangent,
    segment_ids,
    attn_gain,
    q_gain,
    k_gain,
    mlp_gain,
    w_query,
    w_key,
    w_value,
    w_out,
    w_gate,
    w_up,
    w_down,
):
    assert lax.axis_size("tc") == 4 and lax.axis_size("tr") == 2
    col = lax.axis_index("tc")
    side = lax.axis_index("tr")
    rows, width = tokens.shape
    half = rows // 2
    full_width = width * 4
    head_size = q_gain.shape[0]
    q_width = w_query.shape[1] // 4
    k_width = w_key.shape[1] // 4
    units = w_gate.shape[1] // 4
    around = [col, col ^ 1, col ^ 2, col ^ 3]

    def cols_of(array, which, size):
        return lax.dynamic_slice_in_dim(array, around[which] * size, size, 1)

    def rows_of(array, which, size):
        return lax.dynamic_slice_in_dim(array, around[which] * size, size, 0)

    def flip(array):
        return jnp.concatenate(
            [
                lax.dynamic_slice_in_dim(array, side * half, half, 0),
                lax.dynamic_slice_in_dim(array, (1 - side) * half, half, 0),
            ],
            axis=0,
        )

    def qkv_block(which):
        return [
            cols_of(w_query, which, q_width),
            cols_of(w_key, which, k_width),
            cols_of(w_value, which, k_width),
        ]

    qkv_near = jnp.concatenate(qkv_block(0) + qkv_block(2), axis=1)
    qkv_far = jnp.concatenate(qkv_block(1) + qkv_block(3), axis=1)
    inputs = tokens.astype(f32)
    scaled_in = (inputs * attn_gain[None, :]).astype(bf16)
    square_sum = width_total(jnp.sum(inputs * inputs, axis=1))
    far = dot(scaled_in, qkv_far).astype(bf16)
    near = dot(scaled_in, qkv_near)
    projected = scatter_width(near, far)
    attn_rstd = lax.rsqrt(square_sum / full_width + norm_eps)
    attn_hat = inputs * attn_rstd[:, None]
    normed = (attn_hat * attn_gain[None, :]).astype(bf16)
    projected = projected * attn_rstd[:, None]

    shares = lax.axis_size("dp")
    place = lax.axis_index("dp")

    def share_of(block):
        size = block.shape[0] // shares
        return lax.dynamic_slice_in_dim(block, place * size, size, 0)

    def gather_shares(from_y, from_diag):
        return lax.all_gather(jnp.stack([from_y, from_diag]), "dp", axis=1, tiled=True)

    def ffn_block(which):
        return jnp.concatenate(
            [cols_of(w_gate, which, units), cols_of(w_up, which, units)], axis=1
        )

    def ffn_share(which):
        return jnp.concatenate(
            [share_of(cols_of(w_gate, which, units)), share_of(cols_of(w_up, which, units))], axis=1
        )

    ffn_gathered = gather_shares(swap_y(ffn_share(2)), swap_diag(ffn_share(3)))
    ffn_near = jnp.concatenate([ffn_block(0), ffn_gathered[0]], axis=0)
    ffn_far = jnp.concatenate([swap_core(ffn_block(1)), ffn_gathered[1]], axis=0)

    cot_rel = flip(cotangent)
    cot_y_own = swap_y(cot_rel[:half])
    cot_y = jnp.concatenate([cot_y_own, swap_x(cot_y_own)], axis=0)
    cot_near = jnp.concatenate([cot_rel, cot_y], axis=1)
    cot_far = swap_core(cot_near)
    down_gathered = gather_shares(
        swap_y(share_of(rows_of(w_down, 2, units))), swap_diag(share_of(rows_of(w_down, 3, units)))
    )
    down_near = jnp.concatenate([rows_of(w_down, 0, units), down_gathered[0]], axis=1)
    down_far = jnp.concatenate([swap_core(rows_of(w_down, 1, units)), down_gathered[1]], axis=1)
    hidden_grad = contract_cols(cot_near, down_near) + contract_cols(cot_far, down_far)

    positions = positions_of(segment_ids)
    cos_table, sin_table = rope_tables(positions, head_size)
    q_raw = projected[:, :q_width].reshape(rows, -1, head_size)
    k_raw = projected[:, q_width : q_width + k_width].reshape(rows, -1, head_size)
    kv_heads = k_raw.shape[1]
    v_low = projected[:, q_width + k_width :].astype(bf16).reshape(rows, kv_heads, head_size)

    def prepare(query_in, key_in, query_gain, key_gain):
        return (
            rotate(head_norm(query_in, query_gain), cos_table, sin_table),
            rotate(head_norm(key_in, key_gain), cos_table, sin_table),
        )

    (q_rot, k_rot), prepare_back = jax.vjp(prepare, q_raw, k_raw, q_gain, k_gain)
    q_low = q_rot.astype(bf16).reshape(rows, kv_heads, -1, head_size)
    k_low = k_rot.astype(bf16)
    attended, log_totals = attend_forward(q_low, k_low, v_low, segment_ids)
    att_rel = flip(attended.reshape(rows, -1).astype(bf16))
    heads_near = jnp.concatenate([att_rel, swap_y(att_rel)], axis=1)
    heads_far = swap_core(heads_near)
    out_near = jnp.concatenate([rows_of(w_out, 0, q_width), rows_of(w_out, 2, q_width)], axis=0)
    out_far = jnp.concatenate([rows_of(w_out, 1, q_width), rows_of(w_out, 3, q_width)], axis=0)
    away = dot(heads_near[half:], out_near) + dot(heads_far[half:], out_far)
    from_x = swap_x(away.astype(bf16))
    home = dot(heads_near[:half], out_near) + dot(heads_far[:half], out_far)
    tokens_half = lax.dynamic_slice_in_dim(tokens, side * half, half, 0).astype(f32)
    residual = tokens_half + home + from_x.astype(f32)

    mlp_square = width_total(jnp.sum(residual * residual, axis=1))
    mlp_own = (residual * mlp_gain[None, :]).astype(bf16)
    mlp_rstd = lax.rsqrt(mlp_square / full_width + norm_eps)
    rstd_rel = jnp.concatenate([mlp_rstd, swap_x(mlp_rstd)])
    quarter = half // 2
    mlp_x = swap_x(mlp_own)
    mlp_y = swap_y(mlp_own)
    mlp_xy = jnp.concatenate([swap_y(mlp_x[:quarter]), swap_x(mlp_y[quarter:])], axis=0)
    near_own = jnp.concatenate([mlp_own, mlp_y], axis=1)
    near_other = jnp.concatenate([mlp_x, mlp_xy], axis=1)
    far_own = swap_core(near_own)
    far_other = swap_core(near_other)

    def unit_half(near_rows, far_rows, rstd, grad):
        both = (dot(near_rows, ffn_near) + dot(far_rows, ffn_far)) * rstd[:, None]
        gate, up = both[:, :units], both[:, units:]
        sig = jax.nn.sigmoid(gate)
        silu = gate * sig
        hidden = (silu * up).astype(bf16)
        gate_grad = (grad * up * sig * (1.0 + gate * (1.0 - sig))).astype(bf16)
        up_grad = (grad * silu).astype(bf16)
        inner = jnp.sum(gate_grad.astype(f32) * gate + up_grad.astype(f32) * up, axis=1)
        pair = jnp.concatenate([gate_grad, up_grad], axis=1)
        return (hidden, pair, (pair.astype(f32) * rstd[:, None]).astype(bf16), inner)

    hidden_a, pair_a, scaled_a, inner_a = unit_half(near_own, far_own, rstd_rel[:half], hidden_grad[:half])
    hidden_b, pair_b, scaled_b, inner_b = unit_half(near_other, far_other, rstd_rel[half:], hidden_grad[half:])
    hidden = jnp.concatenate([hidden_a, hidden_b], axis=0)
    pair = jnp.concatenate([pair_a, pair_b], axis=0)
    pair_scaled = jnp.concatenate([scaled_a, scaled_b], axis=0)
    mlp_near = jnp.concatenate([near_own, near_other], axis=0)
    mlp_far = jnp.concatenate([far_own, far_other], axis=0)

    inner_b_in = swap_x(width_total(inner_b))
    inner_total = width_total(inner_a) + inner_b_in
    mlp_in_grad = scatter_all(
        contract_cols(pair, ffn_near), contract_cols(pair, ffn_far).astype(bf16)
    )
    mlp_hat = residual * mlp_rstd[:, None]
    mlp_gain_part = jnp.sum(mlp_in_grad * mlp_hat, axis=0)
    residual_grad = cot_rel[:half].astype(f32) + mlp_rstd[:, None] * (
        mlp_in_grad * mlp_gain[None, :] - mlp_hat * (inner_total / full_width)[:, None]
    )
    residual_low = residual_grad.astype(bf16)
    res_rel = jnp.concatenate([residual_low, swap_x(residual_low)], axis=0)
    head_grad = scatter_width(
        contract_cols(res_rel, out_near), contract_cols(res_rel, out_far).astype(bf16)
    )

    exchange = [lambda b: b, swap_core, swap_y, swap_diag]
    down_blocks = [
        contract_rows(hidden, cot).astype(bf16)
        for cot in (
            cot_near[:, :width],
            cot_far[:, :width],
            cot_near[:, width:],
            cot_far[:, width:],
        )
    ]
    down_shares = shares_of_sum(down_blocks)
    ffn_blocks = [
        contract_rows(side_in[:, width:], pair_scaled).astype(bf16) for side_in in (mlp_near, mlp_far)
    ]
    ffn_blocks = after(ffn_blocks, *down_shares)
    ffn_shares = shares_of_sum(ffn_blocks)
    down_grads = whole_of([exchange[k](down_shares[k]) for k in range(4)])
    ffn_shares_in = after([exchange[k](ffn_shares[k - 2]) for k in (2, 3)], *down_grads)
    ffn_far_grads = whole_of(ffn_shares_in)
    ffn_own = contract_rows(mlp_near[:, :width], pair_scaled).astype(bf16)
    ffn_core = swap_core(contract_rows(mlp_far[:, :width], pair_scaled).astype(bf16))
    ffn_grads = [
        (line_total(piece[:, :units]), line_total(piece[:, units:]))
        for piece in (ffn_own, ffn_core)
    ] + [(piece[:, :units], piece[:, units:]) for piece in ffn_far_grads]
    out_blocks = [
        contract_rows(heads_near, res_rel).astype(bf16),
        contract_rows(heads_far, res_rel).astype(bf16),
    ]
    out_shares = shares_of_sum(after(out_blocks, *ffn_shares))
    out_near_grad, out_far_grad = whole_of(after(out_shares, *ffn_far_grads))

    mlp_out = scatter_all(dot(hidden, down_near), dot(hidden, down_far).astype(bf16))
    mixed_half = (residual + mlp_out).astype(bf16)
    mixed = flip(jnp.concatenate([mixed_half, swap_x(mixed_half)], axis=0))

    query_grad, key_grad, value_grad = attend_backward(
        q_low,
        k_low,
        v_low,
        segment_ids,
        log_totals,
        flip(head_grad).reshape(rows, kv_heads, -1, head_size),
    )
    q_raw_grad, k_raw_grad, q_gain_part, k_gain_part = prepare_back(
        (query_grad.reshape(rows, -1, head_size), key_grad)
    )
    proj_low = jnp.concatenate(
        [
            q_raw_grad.reshape(rows, -1),
            k_raw_grad.reshape(rows, -1),
            value_grad.reshape(rows, -1),
        ],
        axis=1,
    ).astype(bf16)
    inner_attn = width_total(jnp.sum(proj_low.astype(f32) * projected, axis=1))
    inner_attn = inner_attn + swap_x(inner_attn)
    proj_y = swap_y(proj_low)
    proj_core = swap_core(proj_low)
    proj_diag = swap_core(proj_y)
    proj_near = jnp.concatenate([proj_low, proj_y], axis=1)
    proj_far = jnp.concatenate([proj_core, proj_diag], axis=1)
    normed_part = (contract_cols(proj_near, qkv_near) + contract_cols(proj_far, qkv_far)).astype(
        bf16
    )
    normed_grad = normed_part.astype(f32) + swap_x(normed_part).astype(f32)
    qkv_grads = [
        line_total(contract_rows(normed, piece).astype(bf16))
        for piece in (proj_low, proj_core, proj_y, proj_diag)
    ]
    attn_gain_part = jnp.sum(normed_grad * attn_hat, axis=0)
    token_grad = (
        flip(res_rel).astype(f32)
        + attn_rstd[:, None]
        * (
            normed_grad * attn_gain[None, :]
            - attn_hat * (inner_attn / full_width)[:, None]
        )
    ).astype(bf16)

    head_parts = width_total(jnp.concatenate([q_gain_part, k_gain_part]))
    shared = jnp.concatenate([head_parts, mlp_gain_part])
    shared = shared + swap_x(shared)
    gains = line_total(jnp.concatenate([shared, attn_gain_part]))
    q_gain_grad = gains[:head_size]
    k_gain_grad = gains[head_size : 2 * head_size]
    mlp_gain_grad = gains[2 * head_size : 2 * head_size + width]
    attn_gain_grad = gains[2 * head_size + width :]

    def place_cols(shape, pieces):
        whole = jnp.zeros(shape, f32)
        for which, piece in enumerate(pieces):
            whole = lax.dynamic_update_slice_in_dim(
                whole, piece.astype(f32), around[which] * piece.shape[1], 1
            )
        return whole

    def place_rows(shape, pieces):
        whole = jnp.zeros(shape, f32)
        for which, piece in enumerate(pieces):
            whole = lax.dynamic_update_slice_in_dim(
                whole, piece.astype(f32), around[which] * piece.shape[0], 0
            )
        return whole

    w_query_grad = place_cols(w_query.shape, [g[:, :q_width] for g in qkv_grads])
    w_key_grad = place_cols(w_key.shape, [g[:, q_width : q_width + k_width] for g in qkv_grads])
    w_value_grad = place_cols(w_value.shape, [g[:, q_width + k_width :] for g in qkv_grads])
    out_pieces = [
        out_near_grad[:q_width],
        out_far_grad[:q_width],
        out_near_grad[q_width:],
        out_far_grad[q_width:],
    ]
    w_out_grad = place_rows(w_out.shape, out_pieces)
    w_gate_grad = place_cols(w_gate.shape, [g[0] for g in ffn_grads])
    w_up_grad = place_cols(w_up.shape, [g[1] for g in ffn_grads])
    w_down_grad = place_rows(w_down.shape, down_grads)
    return (
        mixed,
        token_grad,
        attn_gain_grad,
        q_gain_grad,
        k_gain_grad,
        mlp_gain_grad,
        w_query_grad,
        w_key_grad,
        w_value_grad,
        w_out_grad,
        w_gate_grad,
        w_up_grad,
        w_down_grad,
    )


def solution(mesh):
    in_specs = (
        P("dp", "tc"),
        P("dp", "tc"),
        P("dp"),
        P("tc"),
        P(),
        P(),
        P("tc"),
        P("tc", "tr"),
        P("tc", "tr"),
        P("tc", "tr"),
        P("tr", "tc"),
        P("tc", "tr"),
        P("tc", "tr"),
        P("tr", "tc"),
    )
    out_specs = (
        P("dp", "tc"),
        P("dp", "tc"),
        P("tc"),
        P(),
        P(),
        P("tc"),
        P("tc", "tr"),
        P("tc", "tr"),
        P("tc", "tr"),
        P("tr", "tc"),
        P("tc", "tr"),
        P("tc", "tr"),
        P("tr", "tc"),
    )
    return jax.shard_map(
        on_device, mesh=mesh, in_specs=in_specs, out_specs=out_specs, check_vma=False
    )
```

```python
import jax
import jax.numpy as jnp
from jax import lax
from jax.experimental import pallas as pl
from jax.experimental.pallas import tpu as pltpu
from jax.sharding import PartitionSpec as P

norm_eps = 1e-06
rope_base = 1000000.0
neg_big = -1e30
f32 = jnp.float32
bf16 = jnp.bfloat16


def dot(left_side, right_side):
    return jnp.dot(left_side, right_side, preferred_element_type=f32)


def contract_rows(left_side, right_side):
    return lax.dot_general(
        left_side, right_side, (((0,), (0,)), ((), ())), preferred_element_type=f32
    )


def contract_cols(left_side, right_side):
    return lax.dot_general(
        left_side, right_side, (((1,), (1,)), ((), ())), preferred_element_type=f32
    )


def swap_core(block):
    return lax.ppermute(block, "tc", [(i, i ^ 1) for i in range(4)])


def swap_y(block):
    return lax.ppermute(block, "tc", [(i, i ^ 2) for i in range(4)])


def swap_diag(block):
    return lax.ppermute(block, "tc", [(i, i ^ 3) for i in range(4)])


def swap_x(block):
    return lax.ppermute(block, "tr", [(0, 1), (1, 0)])


def width_total(rows):
    rows = rows + swap_core(rows)
    return rows + swap_y(rows)


def line_total(piece):
    size = lax.axis_size("dp")
    place = lax.axis_index("dp")
    half = size // 2
    for step in range(half - 1):
        got = lax.ppermute(piece, "dp", [(step, step + 1), (size - 1 - step, size - 2 - step)])
        piece = (piece.astype(f32) + got.astype(f32)).astype(piece.dtype)
    got = lax.ppermute(piece, "dp", [(half - 1, half), (half, half - 1)])
    piece = (piece.astype(f32) + got.astype(f32)).astype(piece.dtype)
    for step in reversed(range(half - 1)):
        got = lax.ppermute(piece, "dp", [(step + 1, step), (size - 2 - step, size - 1 - step)])
        piece = jnp.where((place == step) | (place == size - 1 - step), got, piece)
    return piece


def after(value, *others):
    return lax.optimization_barrier((value, others))[0]


def low(array):
    return array.astype(bf16)


def scatter_width(product):
    from_far = swap_core(low(product(3)))
    from_y = swap_y(low(product(2) + from_far.astype(f32)))
    from_core = swap_core(low(product(1)))
    return (product(0) + from_core.astype(f32), from_y)


def scatter_all(product):
    far_y = swap_core(low(product(3)))
    far_own = swap_core(low(product(1)))
    for_y = low(product(2) + far_y.astype(f32))
    own = low(product(0) + far_own.astype(f32))
    half = own.shape[0] // 2
    quarter = half // 2
    width = own.shape[1]
    y_first = swap_y(jnp.concatenate([for_y[quarter:half], for_y[half + quarter :]], axis=0))
    x_first = swap_x(
        jnp.concatenate([own[half : half + quarter], for_y[half : half + quarter]], axis=1)
    )
    top_y = swap_y(low(for_y[:quarter].astype(f32) + x_first[:, width:].astype(f32)))
    low_x = swap_x(low(own[half + quarter :].astype(f32) + y_first[quarter:].astype(f32)))
    top = own[:quarter].astype(f32) + x_first[:, :width].astype(f32) + top_y.astype(f32)
    bottom = own[quarter:half].astype(f32) + y_first[:quarter].astype(f32) + low_x.astype(f32)
    return (jnp.concatenate([top, bottom], axis=0), (own, for_y))


def positions_of(segment):
    slot_ids = jnp.arange(5, dtype=jnp.int32)
    before = jnp.sum((segment[None, :] < slot_ids[:, None]).astype(jnp.int32), axis=1)
    starts = jnp.sum(jnp.where(segment[:, None] == slot_ids[None, :], before[None, :], 0), axis=1)
    return jnp.arange(segment.shape[0], dtype=jnp.int32) - starts


def rope_tables(positions, head_size):
    half_size = head_size // 2
    frequency = rope_base ** (-jnp.arange(half_size, dtype=f32) * 2.0 / head_size)
    angles = positions.astype(f32)[:, None] * frequency[None, :]
    cosine, sine = jnp.cos(angles), jnp.sin(angles)
    return (
        jnp.concatenate([cosine, cosine], axis=1),
        jnp.concatenate([-sine, sine], axis=1),
    )


def turn(vectors):
    return pltpu.roll(vectors, vectors.shape[-1] // 2, axis=1)


def inverse_norm(vectors):
    return lax.rsqrt(jnp.mean(vectors * vectors, axis=-1, keepdims=True) + norm_eps)


def allowed_keys(seg_col, seg_row, start, size, extent):
    row = lax.broadcasted_iota(jnp.int32, (size, extent), 0) + start
    col = lax.broadcasted_iota(jnp.int32, (size, extent), 1)
    return (seg_col[start : start + size, :] == seg_row[:, :extent]) & (col <= row)


def attend_kernel(
    side, own, from_y, rstd, cos, sin, seg_col, seg_row, q_gain, k_gain,
    proj, q_out, k_out, v_out, lse, att,
):
    rows = own.shape[0]
    size = cos.shape[1]
    heads = q_out.shape[1] // size
    block = rows // 4
    scale = size**-0.5
    k_at = heads * size
    v_at = k_at + size

    def ready(i, carry):
        at = pl.ds(pl.multiple_of(i * block, block), block)
        raw = (own[at, :] + from_y[at, :].astype(f32)) * rstd[at, :]
        proj[at, :] = raw

        def rope(part, gain):
            n = part * inverse_norm(part) * gain[...]
            return (n * cos[at, :] + turn(n) * sin[at, :]).astype(bf16)

        for h in range(heads):
            q_out[at, h * size : (h + 1) * size] = rope(raw[:, h * size : (h + 1) * size], q_gain)
        k_out[at, :] = rope(raw[:, k_at:v_at], k_gain)
        v_out[at, :] = raw[:, v_at:].astype(bf16)
        return carry

    lax.fori_loop(0, 4, ready, 0)
    for i in range(4):
        start = i * block
        extent = start + block
        allowed = allowed_keys(seg_col, seg_row, start, block, extent)
        to = pl.ds(pl.multiple_of(lax.rem(start + side[0] * (rows // 2), rows), block), block)
        for h in range(heads):
            of_head = slice(h * size, (h + 1) * size)
            scores = contract_cols(q_out[start:extent, of_head], k_out[:extent, :]) * scale
            scores = jnp.where(allowed, scores, neg_big)
            top = jnp.max(scores, axis=-1, keepdims=True)
            expd = jnp.exp(scores - top)
            total = jnp.sum(expd, axis=-1, keepdims=True)
            weights = (expd * (1.0 / total)).astype(bf16)
            att[to, of_head] = dot(weights, v_out[:extent, :]).astype(bf16)
            lse[start:extent, h : h + 1] = top + jnp.log(total)


def attend_back_kernel(
    side, own, from_y, proj, q_in, k_in, v_in, lse, cos, sin, seg_col, seg_row, q_gain, k_gain,
    grads, q_gain_part, k_gain_part, inner, k_acc, v_acc,
):
    rows = own.shape[0]
    size = cos.shape[1]
    heads = q_in.shape[1] // size
    block = rows // 4
    scale = size**-0.5
    k_at = heads * size
    v_at = k_at + size

    def unrope(grad, part, gain, start):
        rows_at = slice(start, start + block)
        m = grad * cos[rows_at, :] - turn(grad) * sin[rows_at, :]
        r = inverse_norm(part)
        hat = part * r
        mg = m * gain[...]
        back = (r * (mg - hat * jnp.mean(mg * hat, axis=-1, keepdims=True))).astype(bf16)
        gain_part = jnp.sum(m * hat, axis=0, keepdims=True)
        return (back, gain_part, jnp.sum(back.astype(f32) * part, axis=-1, keepdims=True))

    k_acc[...] = jnp.zeros_like(k_acc)
    v_acc[...] = jnp.zeros_like(v_acc)
    q_total = jnp.zeros(q_gain_part.shape, f32)
    for i in range(4):
        start = i * block
        extent = start + block
        allowed = allowed_keys(seg_col, seg_row, start, block, extent)
        at = pl.ds(pl.multiple_of(lax.rem(start + side[0] * (rows // 2), rows), block), block)
        inner_sum = jnp.zeros((block, 1), f32)
        for h in range(heads):
            of_head = slice(h * size, (h + 1) * size)
            query = q_in[start:extent, of_head]
            grad = (own[at, of_head] + from_y[at, of_head].astype(f32)).astype(bf16)
            scores = contract_cols(query, k_in[:extent, :]) * scale
            scores = jnp.where(allowed, scores, neg_big)
            probs = jnp.exp(scores - lse[start:extent, h : h + 1])
            prob_grad = contract_cols(grad, v_in[:extent, :])
            delta = jnp.sum(probs * prob_grad, axis=-1, keepdims=True)
            score_grad = (probs * (prob_grad - delta)).astype(bf16)
            query_grad = dot(score_grad, k_in[:extent, :]) * scale
            k_acc[:extent, :] += contract_rows(score_grad, query) * scale
            v_acc[:extent, :] += contract_rows(probs.astype(bf16), grad)
            back, gain_part, part_inner = unrope(
                query_grad, proj[start:extent, of_head], q_gain, start
            )
            grads[start:extent, of_head] = back
            q_total = q_total + gain_part
            inner_sum = inner_sum + part_inner
        inner[start:extent, :] = inner_sum
    q_gain_part[...] = q_total
    k_total = jnp.zeros(k_gain_part.shape, f32)
    for i in range(4):
        start = i * block
        extent = start + block
        back, gain_part, part_inner = unrope(
            k_acc[start:extent, :], proj[start:extent, k_at:v_at], k_gain, start
        )
        grads[start:extent, k_at:v_at] = back
        k_total = k_total + gain_part
        v_back = v_acc[start:extent, :].astype(bf16)
        grads[start:extent, v_at:] = v_back
        inner[start:extent, :] += part_inner + jnp.sum(
            v_back.astype(f32) * proj[start:extent, v_at:], axis=-1, keepdims=True
        )
    k_gain_part[...] = k_total


vmem = pl.BlockSpec(memory_space=pltpu.VMEM)
smem = pl.BlockSpec(memory_space=pltpu.SMEM)
big_vmem = pltpu.CompilerParams(vmem_limit_bytes=50 * 2**20)


def whole_kernel(body, outs, flops, scratch=()):
    def call(*operands):
        nbytes = sum(o.size * o.dtype.itemsize for o in (*operands, *outs))
        return pl.pallas_call(
            body,
            out_shape=outs,
            in_specs=[smem] + [vmem] * (len(operands) - 1),
            out_specs=[vmem] * len(outs),
            scratch_shapes=scratch,
            compiler_params=big_vmem,
            cost_estimate=pl.CostEstimate(flops=flops, bytes_accessed=nbytes, transcendentals=0),
        )(*operands)

    return call


def units_kernel(*refs):
    ins, weights = refs[:4], refs[4:8]
    rstd_ref, grad_ref = refs[8:10]
    hidden, pair, scaled, inner = refs[-4:]
    both = dot(ins[0][...], weights[0][...])
    for k in range(1, 4):
        both = both + dot(ins[k][...], weights[k][...])
    rstd = rstd_ref[...]
    both = both * rstd
    units = hidden.shape[1]
    gate, up = both[:, :units], both[:, units:]
    grad = grad_ref[...]
    sig = jax.nn.sigmoid(gate)
    silu = gate * sig
    hidden[...] = (silu * up).astype(bf16)
    gate_grad = (grad * up * sig * (1.0 + gate * (1.0 - sig))).astype(bf16).astype(f32)
    up_grad = (grad * silu).astype(bf16).astype(f32)
    pair[:, :units] = gate_grad.astype(bf16)
    pair[:, units:] = up_grad.astype(bf16)
    scaled[:, :units] = (gate_grad * rstd).astype(bf16)
    scaled[:, units:] = (up_grad * rstd).astype(bf16)
    inner[...] = jnp.sum(gate_grad * gate + up_grad * up, axis=-1, keepdims=True)


def units_of_half(ins, weights, rstd, grad, which, earlier):
    half, depth = ins[0].shape
    units = grad.shape[1]
    block = half // 2
    first = which * (half // block)
    outs = [
        jax.ShapeDtypeStruct((2 * half, units), bf16),
        jax.ShapeDtypeStruct((2 * half, 2 * units), bf16),
        jax.ShapeDtypeStruct((2 * half, 2 * units), bf16),
        jax.ShapeDtypeStruct((2 * half, 1), f32),
    ]
    rows_spec = [pl.BlockSpec((block, depth), lambda i: (i, 0))] * 4
    whole_spec = [pl.BlockSpec((depth, 2 * units), lambda i: (0, 0))] * 4
    at = [
        pl.BlockSpec((block, 1), lambda i: (first + i, 0)),
        pl.BlockSpec((block, units), lambda i: (first + i, 0)),
    ]
    earlier = list(earlier or [])
    kept = [pl.BlockSpec(memory_space=pl.ANY)] * len(earlier)
    return pl.pallas_call(
        units_kernel,
        grid=(half // block,),
        out_shape=outs,
        in_specs=rows_spec + whole_spec + at + kept,
        out_specs=[pl.BlockSpec((block, o.shape[1]), lambda i: (first + i, 0)) for o in outs],
        input_output_aliases={10 + k: k for k in range(len(earlier))},
        compiler_params=big_vmem,
        cost_estimate=pl.CostEstimate(
            flops=2 * half * 4 * depth * 2 * units,
            bytes_accessed=2 * (4 * depth * 2 * units + half * (4 * depth + 7 * units)),
            transcendentals=half * units,
        ),
    )(*ins, *weights, rstd, grad, *earlier)


def on_device(
    tokens,
    cotangent,
    segment_ids,
    attn_gain,
    q_gain,
    k_gain,
    mlp_gain,
    w_query,
    w_key,
    w_value,
    w_out,
    w_gate,
    w_up,
    w_down,
):
    assert lax.axis_size("tc") == 4 and lax.axis_size("tr") == 2
    col = lax.axis_index("tc")
    side = lax.axis_index("tr")
    rows, width = tokens.shape
    half = rows // 2
    full_width = width * 4
    head_size = q_gain.shape[0]
    q_width = w_query.shape[1] // 4
    k_width = w_key.shape[1] // 4
    units = w_gate.shape[1] // 4
    around = [col, col ^ 1, col ^ 2, col ^ 3]

    def cols_of(array, which, size):
        return lax.dynamic_slice_in_dim(array, around[which] * size, size, 1)

    def rows_of(array, which, size):
        return lax.dynamic_slice_in_dim(array, around[which] * size, size, 0)

    def flip(array):
        return jnp.concatenate(
            [
                lax.dynamic_slice_in_dim(array, side * half, half, 0),
                lax.dynamic_slice_in_dim(array, (1 - side) * half, half, 0),
            ],
            axis=0,
        )

    shares = lax.axis_size("dp")
    place = lax.axis_index("dp")

    def share_of(block):
        size = block.shape[0] // shares
        return lax.dynamic_slice_in_dim(block, place * size, size, 0)

    def gather_shares(from_y, from_diag):
        return lax.all_gather(jnp.stack([from_y, from_diag]), "dp", axis=1, tiled=True)

    def ffn_block(which):
        return jnp.concatenate(
            [cols_of(w_gate, which, units), cols_of(w_up, which, units)], axis=1
        )

    def ffn_share(which):
        return jnp.concatenate(
            [share_of(cols_of(w_gate, which, units)), share_of(cols_of(w_up, which, units))], axis=1
        )

    share_y, share_diag = ffn_share(2), ffn_share(3)
    ffn_gathered = gather_shares(swap_y(share_y), swap_diag(share_diag))

    qkv_weights = [
        jnp.concatenate(
            [cols_of(w_query, k, q_width), cols_of(w_key, k, k_width), cols_of(w_value, k, k_width)],
            axis=1,
        )
        for k in range(4)
    ]
    inputs = tokens.astype(f32)
    scaled_in = after(low(inputs * attn_gain[None, :]), share_y, share_diag)
    square_sum = width_total(jnp.sum(inputs * inputs, axis=1))
    raw_own, raw_y = scatter_width(lambda k: dot(scaled_in, qkv_weights[k]))
    attn_rstd = lax.rsqrt(square_sum / full_width + norm_eps)
    attn_hat = inputs * attn_rstd[:, None]
    normed = low(attn_hat * attn_gain[None, :])

    cot_rel = flip(after(cotangent, raw_y))
    down_blocks = [rows_of(w_down, k, units) for k in range(4)]
    cot_y_own = swap_y(cot_rel[:half])
    cot_y = jnp.concatenate([cot_y_own, swap_x(cot_y_own)], axis=0)
    cots = [cot_rel, swap_core(cot_rel), cot_y, swap_core(cot_y)]
    down_gathered = gather_shares(
        swap_y(after(share_of(down_blocks[2]), raw_y)),
        swap_diag(after(share_of(down_blocks[3]), raw_y)),
    )
    downs = [down_blocks[0], swap_core(down_blocks[1]), down_gathered[0], down_gathered[1]]
    hidden_grad = (contract_cols(cots[0], downs[0]) + contract_cols(cots[1], downs[1])) + (
        contract_cols(cots[2], downs[2]) + contract_cols(cots[3], downs[3])
    )
    ffns = [ffn_block(0), swap_core(after(ffn_block(1), raw_y)), ffn_gathered[0], ffn_gathered[1]]

    cos_table, sin_table = rope_tables(positions_of(segment_ids), head_size)
    side_word = side.astype(jnp.int32).reshape(1)
    tables = (
        cos_table,
        sin_table,
        segment_ids.reshape(rows, 1),
        segment_ids.reshape(1, rows),
        q_gain.reshape(1, head_size),
        k_gain.reshape(1, head_size),
    )
    heads = q_width // head_size
    pairs_of_rows = rows * rows * heads * head_size
    projected, q_low, k_low, v_low, log_totals, att_rel = whole_kernel(
        attend_kernel,
        [
            jax.ShapeDtypeStruct((rows, q_width + 2 * k_width), f32),
            jax.ShapeDtypeStruct((rows, q_width), bf16),
            jax.ShapeDtypeStruct((rows, k_width), bf16),
            jax.ShapeDtypeStruct((rows, k_width), bf16),
            jax.ShapeDtypeStruct((rows, heads), f32),
            jax.ShapeDtypeStruct((rows, q_width), bf16),
        ],
        flops=4 * pairs_of_rows,
    )(side_word, raw_own, raw_y, attn_rstd.reshape(rows, 1), *tables)
    att_y = swap_y(att_rel)
    atts = [att_rel, swap_core(att_rel), att_y, swap_core(att_y)]
    outs = [rows_of(w_out, k, q_width) for k in range(4)]

    def out_rows(at):
        return (dot(atts[0][at], outs[0]) + dot(atts[1][at], outs[1])) + (
            dot(atts[2][at], outs[2]) + dot(atts[3][at], outs[3])
        )

    from_x = swap_x(low(out_rows(slice(half, rows))))
    tokens_half = lax.dynamic_slice_in_dim(tokens, side * half, half, 0).astype(f32)
    residual = tokens_half + out_rows(slice(0, half)) + from_x.astype(f32)

    mlp_square = width_total(jnp.sum(residual * residual, axis=1))
    mlp_own = low(residual * mlp_gain[None, :])
    mlp_rstd = lax.rsqrt(mlp_square / full_width + norm_eps)
    rstd_rel = jnp.concatenate([mlp_rstd, swap_x(mlp_rstd)]).reshape(rows, 1)
    quarter = half // 2
    mlp_x = swap_x(mlp_own)
    mlp_y = swap_y(mlp_own)
    mlp_xy = jnp.concatenate([swap_y(mlp_x[:quarter]), swap_x(mlp_y[quarter:])], axis=0)
    ins_own = [mlp_own, swap_core(mlp_own), mlp_y, swap_core(mlp_y)]
    ins_other = [mlp_x, swap_core(mlp_x), mlp_xy, swap_core(mlp_xy)]
    first = units_of_half(ins_own, ffns, rstd_rel, hidden_grad, 0, None)
    hidden, pair, pair_scaled, inner = units_of_half(
        ins_other, ffns, rstd_rel, hidden_grad, 1, first
    )

    mlp_in_grad, mlp_sent = scatter_all(lambda k: contract_cols(pair, ffns[k]))
    inner_total = width_total(inner[:half, 0]) + swap_x(width_total(inner[half:, 0]))
    mlp_hat = residual * mlp_rstd[:, None]
    mlp_gain_part = jnp.sum(mlp_in_grad * mlp_hat, axis=0)
    residual_grad = cot_rel[:half].astype(f32) + mlp_rstd[:, None] * (
        mlp_in_grad * mlp_gain[None, :] - mlp_hat * (inner_total / full_width)[:, None]
    )
    residual_low = low(residual_grad)
    res_rel = jnp.concatenate([residual_low, swap_x(residual_low)], axis=0)
    head_own, head_y = scatter_width(lambda k: contract_cols(res_rel, outs[k]))

    exchange = [lambda b: b, swap_core, swap_y, swap_diag]
    mlp_all = [jnp.concatenate([a, b], axis=0) for a, b in zip(ins_own, ins_other)]

    def ffn_grads_of(which, ready):
        down = low(contract_rows(after(hidden, ready), cots[which]))
        gate_up = low(contract_rows(mlp_all[which], after(pair_scaled, ready)))
        return [exchange[which](down), exchange[which](gate_up)]

    near_grads = ffn_grads_of(0, mlp_sent) + ffn_grads_of(1, mlp_sent)

    proj_low, q_gain_part, k_gain_part, inner_attn = whole_kernel(
        attend_back_kernel,
        [
            jax.ShapeDtypeStruct((rows, q_width + 2 * k_width), bf16),
            jax.ShapeDtypeStruct((1, head_size), f32),
            jax.ShapeDtypeStruct((1, head_size), f32),
            jax.ShapeDtypeStruct((rows, 1), f32),
        ],
        flops=10 * pairs_of_rows,
        scratch=[pltpu.VMEM((rows, k_width), f32), pltpu.VMEM((rows, k_width), f32)],
    )(side_word, head_own, head_y, projected, q_low, k_low, v_low, log_totals, *tables)
    inner_attn = width_total(inner_attn[:, 0])
    inner_attn = inner_attn + swap_x(inner_attn)
    proj_y = swap_y(proj_low)
    projs = [proj_low, swap_core(proj_low), proj_y, swap_core(proj_y)]
    normed_part = low(
        (contract_cols(projs[0], qkv_weights[0]) + contract_cols(projs[1], qkv_weights[1]))
        + (contract_cols(projs[2], qkv_weights[2]) + contract_cols(projs[3], qkv_weights[3]))
    )
    normed_grad = normed_part.astype(f32) + swap_x(normed_part).astype(f32)
    attn_gain_part = jnp.sum(normed_grad * attn_hat, axis=0)
    token_grad = low(
        flip(res_rel).astype(f32)
        + attn_rstd[:, None]
        * (normed_grad * attn_gain[None, :] - attn_hat * (inner_attn / full_width)[:, None])
    )

    mlp_out, _ = scatter_all(lambda k: dot(after(hidden, proj_y), downs[k]))
    mixed_half = low(residual + mlp_out)
    mixed = flip(jnp.concatenate([mixed_half, swap_x(mixed_half)], axis=0))

    far_grads = ffn_grads_of(2, proj_y) + ffn_grads_of(3, proj_y)
    out_grads = [low(contract_rows(piece, res_rel)) for piece in atts]
    qkv_grads = [low(contract_rows(normed, piece)) for piece in projs]
    near_sums = lax.psum(near_grads, "dp")
    far_sums, out_grads, qkv_grads = lax.psum(
        after((far_grads, out_grads, qkv_grads), *near_sums), "dp"
    )
    down_grads = [near_sums[0], near_sums[2], far_sums[0], far_sums[2]]
    ffn_grads = [near_sums[1], near_sums[3], far_sums[1], far_sums[3]]

    head_parts = width_total(jnp.concatenate([q_gain_part[0], k_gain_part[0]]))
    shared = jnp.concatenate([head_parts, mlp_gain_part])
    shared = shared + swap_x(shared)
    gains = line_total(jnp.concatenate([shared, attn_gain_part]))
    q_gain_grad = gains[:head_size]
    k_gain_grad = gains[head_size : 2 * head_size]
    mlp_gain_grad = gains[2 * head_size : 2 * head_size + width]
    attn_gain_grad = gains[2 * head_size + width :]

    def place_cols(shape, pieces):
        whole = jnp.zeros(shape, f32)
        for which, piece in enumerate(pieces):
            whole = lax.dynamic_update_slice_in_dim(
                whole, piece.astype(f32), around[which] * piece.shape[1], 1
            )
        return whole

    def place_rows(shape, pieces):
        whole = jnp.zeros(shape, f32)
        for which, piece in enumerate(pieces):
            whole = lax.dynamic_update_slice_in_dim(
                whole, piece.astype(f32), around[which] * piece.shape[0], 0
            )
        return whole

    w_query_grad = place_cols(w_query.shape, [g[:, :q_width] for g in qkv_grads])
    w_key_grad = place_cols(w_key.shape, [g[:, q_width : q_width + k_width] for g in qkv_grads])
    w_value_grad = place_cols(w_value.shape, [g[:, q_width + k_width :] for g in qkv_grads])
    w_out_grad = place_rows(w_out.shape, out_grads)
    w_gate_grad = place_cols(w_gate.shape, [g[:, :units] for g in ffn_grads])
    w_up_grad = place_cols(w_up.shape, [g[:, units:] for g in ffn_grads])
    w_down_grad = place_rows(w_down.shape, down_grads)
    return (
        mixed,
        token_grad,
        attn_gain_grad,
        q_gain_grad,
        k_gain_grad,
        mlp_gain_grad,
        w_query_grad,
        w_key_grad,
        w_value_grad,
        w_out_grad,
        w_gate_grad,
        w_up_grad,
        w_down_grad,
    )


def solution(mesh):
    in_specs = (
        P("dp", "tc"),
        P("dp", "tc"),
        P("dp"),
        P("tc"),
        P(),
        P(),
        P("tc"),
        P("tc", "tr"),
        P("tc", "tr"),
        P("tc", "tr"),
        P("tr", "tc"),
        P("tc", "tr"),
        P("tc", "tr"),
        P("tr", "tc"),
    )
    out_specs = (
        P("dp", "tc"),
        P("dp", "tc"),
        P("tc"),
        P(),
        P(),
        P("tc"),
        P("tc", "tr"),
        P("tc", "tr"),
        P("tc", "tr"),
        P("tr", "tc"),
        P("tc", "tr"),
        P("tc", "tr"),
        P("tr", "tc"),
    )
    return jax.shard_map(
        on_device, mesh=mesh, in_specs=in_specs, out_specs=out_specs, check_vma=False
    )
```

```python
import jax
import jax.numpy as jnp
from jax import lax
from jax.experimental import pallas as pl
from jax.experimental.pallas import tpu as pltpu
from jax.sharding import PartitionSpec as P

norm_eps = 1e-06
rope_base = 1000000.0
neg_big = -1e30
f32 = jnp.float32
bf16 = jnp.bfloat16


def dot(left_side, right_side):
    return jnp.dot(left_side, right_side, preferred_element_type=f32)


def contract_rows(left_side, right_side):
    return lax.dot_general(
        left_side, right_side, (((0,), (0,)), ((), ())), preferred_element_type=f32
    )


def contract_cols(left_side, right_side):
    return lax.dot_general(
        left_side, right_side, (((1,), (1,)), ((), ())), preferred_element_type=f32
    )


def swap_core(block):
    return lax.ppermute(block, "tc", [(i, i ^ 1) for i in range(4)])


def swap_y(block):
    return lax.ppermute(block, "tc", [(i, i ^ 2) for i in range(4)])


def swap_diag(block):
    return lax.ppermute(block, "tc", [(i, i ^ 3) for i in range(4)])


def swap_x(block):
    return lax.ppermute(block, "tr", [(0, 1), (1, 0)])


def width_total(rows):
    rows = rows + swap_core(rows)
    return rows + swap_y(rows)


def line_total(piece):
    size = lax.axis_size("dp")
    place = lax.axis_index("dp")
    half = size // 2
    for step in range(half - 1):
        got = lax.ppermute(piece, "dp", [(step, step + 1), (size - 1 - step, size - 2 - step)])
        piece = (piece.astype(f32) + got.astype(f32)).astype(piece.dtype)
    got = lax.ppermute(piece, "dp", [(half - 1, half), (half, half - 1)])
    piece = (piece.astype(f32) + got.astype(f32)).astype(piece.dtype)
    for step in reversed(range(half - 1)):
        got = lax.ppermute(piece, "dp", [(step + 1, step), (size - 2 - step, size - 1 - step)])
        piece = jnp.where((place == step) | (place == size - 1 - step), got, piece)
    return piece


def after(value, *others):
    return lax.optimization_barrier((value, others))[0]


def low(array):
    return array.astype(bf16)


def scatter_width(product):
    from_far = swap_core(low(product(3)))
    for_y = low(product(2) + from_far.astype(f32))
    from_y = swap_y(for_y)
    from_core = swap_core(low(product(1)))
    return (product(0) + from_core.astype(f32), from_y, for_y)


def scatter_all(product, filler=lambda ready: ()):
    far_y = swap_core(low(product(3)))
    far_own = swap_core(low(product(1)))
    for_y = low(product(2) + far_y.astype(f32))
    own = low(product(0) + far_own.astype(f32))
    half = own.shape[0] // 2
    quarter = half // 2
    width = own.shape[1]
    y_first = swap_y(jnp.concatenate([for_y[quarter:half], for_y[half + quarter :]], axis=0))
    x_first = swap_x(
        jnp.concatenate([own[half : half + quarter], for_y[half : half + quarter]], axis=1)
    )
    fill = filler((own, for_y))
    x_first, y_first = after((x_first, y_first), fill)
    top_y = swap_y(low(for_y[:quarter].astype(f32) + x_first[:, width:].astype(f32)))
    low_x = swap_x(low(own[half + quarter :].astype(f32) + y_first[quarter:].astype(f32)))
    top = own[:quarter].astype(f32) + x_first[:, :width].astype(f32) + top_y.astype(f32)
    bottom = own[quarter:half].astype(f32) + y_first[:quarter].astype(f32) + low_x.astype(f32)
    return (jnp.concatenate([top, bottom], axis=0), fill)


def positions_of(segment):
    slot_ids = jnp.arange(5, dtype=jnp.int32)
    before = jnp.sum((segment[None, :] < slot_ids[:, None]).astype(jnp.int32), axis=1)
    starts = jnp.sum(jnp.where(segment[:, None] == slot_ids[None, :], before[None, :], 0), axis=1)
    return jnp.arange(segment.shape[0], dtype=jnp.int32) - starts


def rope_tables(positions, head_size):
    half_size = head_size // 2
    frequency = rope_base ** (-jnp.arange(half_size, dtype=f32) * 2.0 / head_size)
    angles = positions.astype(f32)[:, None] * frequency[None, :]
    cosine, sine = jnp.cos(angles), jnp.sin(angles)
    return (
        jnp.concatenate([cosine, cosine], axis=1),
        jnp.concatenate([-sine, sine], axis=1),
    )


def turn(vectors):
    return pltpu.roll(vectors, vectors.shape[-1] // 2, axis=1)


def inverse_norm(vectors):
    return lax.rsqrt(jnp.mean(vectors * vectors, axis=-1, keepdims=True) + norm_eps)


def allowed_keys(seg_col, seg_row, start, size, extent):
    row = lax.broadcasted_iota(jnp.int32, (size, extent), 0) + start
    col = lax.broadcasted_iota(jnp.int32, (size, extent), 1)
    return (seg_col[start : start + size, :] == seg_row[:, :extent]) & (col <= row)


def attend_kernel(
    side, own, from_y, rstd, cos, sin, seg_col, seg_row, q_gain, k_gain,
    proj, q_out, k_out, v_out, lse, att,
):
    rows = own.shape[0]
    size = cos.shape[1]
    heads = q_out.shape[1] // size
    block = rows // 4
    scale = size**-0.5
    k_at = heads * size
    v_at = k_at + size

    def ready(i, carry):
        at = pl.ds(pl.multiple_of(i * block, block), block)
        raw = (own[at, :] + from_y[at, :].astype(f32)) * rstd[at, :]
        proj[at, :] = raw

        def rope(part, gain):
            n = part * inverse_norm(part) * gain[...]
            return (n * cos[at, :] + turn(n) * sin[at, :]).astype(bf16)

        for h in range(heads):
            q_out[at, h * size : (h + 1) * size] = rope(raw[:, h * size : (h + 1) * size], q_gain)
        k_out[at, :] = rope(raw[:, k_at:v_at], k_gain)
        v_out[at, :] = raw[:, v_at:].astype(bf16)
        return carry

    lax.fori_loop(0, 4, ready, 0)
    for i in range(4):
        start = i * block
        extent = start + block
        allowed = allowed_keys(seg_col, seg_row, start, block, extent)
        to = pl.ds(pl.multiple_of(lax.rem(start + side[0] * (rows // 2), rows), block), block)
        for h in range(heads):
            of_head = slice(h * size, (h + 1) * size)
            scores = contract_cols(q_out[start:extent, of_head], k_out[:extent, :]) * scale
            scores = jnp.where(allowed, scores, neg_big)
            top = jnp.max(scores, axis=-1, keepdims=True)
            expd = jnp.exp(scores - top)
            total = jnp.sum(expd, axis=-1, keepdims=True)
            weights = (expd * (1.0 / total)).astype(bf16)
            att[to, of_head] = dot(weights, v_out[:extent, :]).astype(bf16)
            lse[start:extent, h : h + 1] = top + jnp.log(total)


def attend_back_kernel(
    side, own, from_y, proj, q_in, k_in, v_in, lse, cos, sin, seg_col, seg_row, q_gain, k_gain,
    grads, q_gain_part, k_gain_part, inner, k_acc, v_acc,
):
    rows = own.shape[0]
    size = cos.shape[1]
    heads = q_in.shape[1] // size
    block = rows // 4
    scale = size**-0.5
    k_at = heads * size
    v_at = k_at + size

    def unrope(grad, part, gain, start):
        rows_at = slice(start, start + block)
        m = grad * cos[rows_at, :] - turn(grad) * sin[rows_at, :]
        r = inverse_norm(part)
        hat = part * r
        mg = m * gain[...]
        back = (r * (mg - hat * jnp.mean(mg * hat, axis=-1, keepdims=True))).astype(bf16)
        gain_part = jnp.sum(m * hat, axis=0, keepdims=True)
        return (back, gain_part, jnp.sum(back.astype(f32) * part, axis=-1, keepdims=True))

    k_acc[...] = jnp.zeros_like(k_acc)
    v_acc[...] = jnp.zeros_like(v_acc)
    q_total = jnp.zeros(q_gain_part.shape, f32)
    for i in range(4):
        start = i * block
        extent = start + block
        allowed = allowed_keys(seg_col, seg_row, start, block, extent)
        at = pl.ds(pl.multiple_of(lax.rem(start + side[0] * (rows // 2), rows), block), block)
        inner_sum = jnp.zeros((block, 1), f32)
        for h in range(heads):
            of_head = slice(h * size, (h + 1) * size)
            query = q_in[start:extent, of_head]
            grad = (own[at, of_head] + from_y[at, of_head].astype(f32)).astype(bf16)
            scores = contract_cols(query, k_in[:extent, :]) * scale
            scores = jnp.where(allowed, scores, neg_big)
            probs = jnp.exp(scores - lse[start:extent, h : h + 1])
            prob_grad = contract_cols(grad, v_in[:extent, :])
            delta = jnp.sum(probs * prob_grad, axis=-1, keepdims=True)
            score_grad = (probs * (prob_grad - delta)).astype(bf16)
            query_grad = dot(score_grad, k_in[:extent, :]) * scale
            k_acc[:extent, :] += contract_rows(score_grad, query) * scale
            v_acc[:extent, :] += contract_rows(probs.astype(bf16), grad)
            back, gain_part, part_inner = unrope(
                query_grad, proj[start:extent, of_head], q_gain, start
            )
            grads[start:extent, of_head] = back
            q_total = q_total + gain_part
            inner_sum = inner_sum + part_inner
        inner[start:extent, :] = inner_sum
    q_gain_part[...] = q_total
    k_total = jnp.zeros(k_gain_part.shape, f32)
    for i in range(4):
        start = i * block
        extent = start + block
        back, gain_part, part_inner = unrope(
            k_acc[start:extent, :], proj[start:extent, k_at:v_at], k_gain, start
        )
        grads[start:extent, k_at:v_at] = back
        k_total = k_total + gain_part
        v_back = v_acc[start:extent, :].astype(bf16)
        grads[start:extent, v_at:] = v_back
        inner[start:extent, :] += part_inner + jnp.sum(
            v_back.astype(f32) * proj[start:extent, v_at:], axis=-1, keepdims=True
        )
    k_gain_part[...] = k_total


vmem = pl.BlockSpec(memory_space=pltpu.VMEM)
smem = pl.BlockSpec(memory_space=pltpu.SMEM)
big_vmem = pltpu.CompilerParams(vmem_limit_bytes=50 * 2**20)


def whole_kernel(body, outs, flops, scratch=()):
    def call(*operands):
        nbytes = sum(o.size * o.dtype.itemsize for o in (*operands, *outs))
        return pl.pallas_call(
            body,
            out_shape=outs,
            in_specs=[smem] + [vmem] * (len(operands) - 1),
            out_specs=[vmem] * len(outs),
            scratch_shapes=scratch,
            compiler_params=big_vmem,
            cost_estimate=pl.CostEstimate(flops=flops, bytes_accessed=nbytes, transcendentals=0),
        )(*operands)

    return call


def units_kernel(*refs):
    ins, weights = refs[:4], refs[4:8]
    rstd_ref, grad_ref = refs[8:10]
    hidden, pair, scaled, inner = refs[-4:]
    both = dot(ins[0][...], weights[0][...])
    for k in range(1, 4):
        both = both + dot(ins[k][...], weights[k][...])
    rstd = rstd_ref[...]
    both = both * rstd
    units = hidden.shape[1]
    gate, up = both[:, :units], both[:, units:]
    grad = grad_ref[...]
    sig = jax.nn.sigmoid(gate)
    silu = gate * sig
    hidden[...] = (silu * up).astype(bf16)
    gate_grad = (grad * up * sig * (1.0 + gate * (1.0 - sig))).astype(bf16).astype(f32)
    up_grad = (grad * silu).astype(bf16).astype(f32)
    pair[:, :units] = gate_grad.astype(bf16)
    pair[:, units:] = up_grad.astype(bf16)
    scaled[:, :units] = (gate_grad * rstd).astype(bf16)
    scaled[:, units:] = (up_grad * rstd).astype(bf16)
    inner[...] = jnp.sum(gate_grad * gate + up_grad * up, axis=-1, keepdims=True)


def units_of_half(ins, weights, rstd, grad, which, earlier):
    half, depth = ins[0].shape
    units = grad.shape[1]
    block = half // 2
    first = which * (half // block)
    outs = [
        jax.ShapeDtypeStruct((2 * half, units), bf16),
        jax.ShapeDtypeStruct((2 * half, 2 * units), bf16),
        jax.ShapeDtypeStruct((2 * half, 2 * units), bf16),
        jax.ShapeDtypeStruct((2 * half, 1), f32),
    ]
    rows_spec = [pl.BlockSpec((block, depth), lambda i: (i, 0))] * 4
    whole_spec = [pl.BlockSpec((depth, 2 * units), lambda i: (0, 0))] * 4
    at = [
        pl.BlockSpec((block, 1), lambda i: (first + i, 0)),
        pl.BlockSpec((block, units), lambda i: (first + i, 0)),
    ]
    earlier = list(earlier or [])
    kept = [pl.BlockSpec(memory_space=pl.ANY)] * len(earlier)
    return pl.pallas_call(
        units_kernel,
        grid=(half // block,),
        out_shape=outs,
        in_specs=rows_spec + whole_spec + at + kept,
        out_specs=[pl.BlockSpec((block, o.shape[1]), lambda i: (first + i, 0)) for o in outs],
        input_output_aliases={10 + k: k for k in range(len(earlier))},
        compiler_params=big_vmem,
        cost_estimate=pl.CostEstimate(
            flops=2 * half * 4 * depth * 2 * units,
            bytes_accessed=2 * (4 * depth * 2 * units + half * (4 * depth + 7 * units)),
            transcendentals=half * units,
        ),
    )(*ins, *weights, rstd, grad, *earlier)


def on_device(
    tokens,
    cotangent,
    segment_ids,
    attn_gain,
    q_gain,
    k_gain,
    mlp_gain,
    w_query,
    w_key,
    w_value,
    w_out,
    w_gate,
    w_up,
    w_down,
):
    assert lax.axis_size("tc") == 4 and lax.axis_size("tr") == 2
    col = lax.axis_index("tc")
    side = lax.axis_index("tr")
    rows, width = tokens.shape
    half = rows // 2
    full_width = width * 4
    head_size = q_gain.shape[0]
    q_width = w_query.shape[1] // 4
    k_width = w_key.shape[1] // 4
    units = w_gate.shape[1] // 4
    around = [col, col ^ 1, col ^ 2, col ^ 3]

    def cols_of(array, which, size):
        return lax.dynamic_slice_in_dim(array, around[which] * size, size, 1)

    def rows_of(array, which, size):
        return lax.dynamic_slice_in_dim(array, around[which] * size, size, 0)

    def flip(array):
        return jnp.concatenate(
            [
                lax.dynamic_slice_in_dim(array, side * half, half, 0),
                lax.dynamic_slice_in_dim(array, (1 - side) * half, half, 0),
            ],
            axis=0,
        )

    shares = lax.axis_size("dp")
    place = lax.axis_index("dp")

    def share_of(block):
        size = block.shape[0] // shares
        return lax.dynamic_slice_in_dim(block, place * size, size, 0)

    def gather_shares(from_y, from_diag):
        return lax.all_gather(jnp.stack([from_y, from_diag]), "dp", axis=1, tiled=True)

    def ffn_block(which):
        return jnp.concatenate(
            [cols_of(w_gate, which, units), cols_of(w_up, which, units)], axis=1
        )

    def ffn_share(which):
        return jnp.concatenate(
            [share_of(cols_of(w_gate, which, units)), share_of(cols_of(w_up, which, units))], axis=1
        )

    down_blocks = [rows_of(w_down, k, units) for k in range(4)]
    down_y, down_diag = share_of(down_blocks[2]), share_of(down_blocks[3])
    down_gathered = gather_shares(swap_y(down_y), swap_diag(down_diag))
    share_y, share_diag = ffn_share(2), ffn_share(3)

    qkv_weights = [
        jnp.concatenate(
            [cols_of(w_query, k, q_width), cols_of(w_key, k, k_width), cols_of(w_value, k, k_width)],
            axis=1,
        )
        for k in range(4)
    ]
    inputs = tokens.astype(f32)
    scaled_in = after(low(inputs * attn_gain[None, :]), down_y, down_diag)
    square_sum = width_total(jnp.sum(inputs * inputs, axis=1))
    raw_own, raw_y, for_y = scatter_width(lambda k: dot(scaled_in, qkv_weights[k]))
    share_y, share_diag = after((share_y, share_diag), for_y)
    share_y, share_diag = swap_y(share_y), swap_diag(share_diag)
    attn_rstd = lax.rsqrt(square_sum / full_width + norm_eps)
    attn_hat = inputs * attn_rstd[:, None]
    normed = low(attn_hat * attn_gain[None, :])

    cos_table, sin_table = rope_tables(positions_of(segment_ids), head_size)
    side_word = side.astype(jnp.int32).reshape(1)
    tables = (
        cos_table,
        sin_table,
        segment_ids.reshape(rows, 1),
        segment_ids.reshape(1, rows),
        q_gain.reshape(1, head_size),
        k_gain.reshape(1, head_size),
    )
    heads = q_width // head_size
    pairs_of_rows = rows * rows * heads * head_size
    projected, q_low, k_low, v_low, log_totals, att_rel = whole_kernel(
        attend_kernel,
        [
            jax.ShapeDtypeStruct((rows, q_width + 2 * k_width), f32),
            jax.ShapeDtypeStruct((rows, q_width), bf16),
            jax.ShapeDtypeStruct((rows, k_width), bf16),
            jax.ShapeDtypeStruct((rows, k_width), bf16),
            jax.ShapeDtypeStruct((rows, heads), f32),
            jax.ShapeDtypeStruct((rows, q_width), bf16),
        ],
        flops=4 * pairs_of_rows,
    )(side_word, raw_own, raw_y, attn_rstd.reshape(rows, 1), *tables)
    ffn_gathered = gather_shares(*after((share_y, share_diag), att_rel))
    att_y = swap_y(att_rel)
    atts = [att_rel, swap_core(att_rel), att_y, swap_core(att_y)]
    outs = [rows_of(w_out, k, q_width) for k in range(4)]

    def out_rows(at):
        return (dot(atts[0][at], outs[0]) + dot(atts[1][at], outs[1])) + (
            dot(atts[2][at], outs[2]) + dot(atts[3][at], outs[3])
        )

    out_away = low(out_rows(slice(half, rows)))
    from_x = swap_x(out_away)

    cot_rel = flip(cotangent)
    cot_y_own = swap_y(after(cot_rel[:half], att_rel))
    cot_y = jnp.concatenate([cot_y_own, swap_x(after(cot_y_own, out_away))], axis=0)
    cots = [cot_rel, swap_core(cot_rel), cot_y, swap_core(cot_y)]
    downs = [down_blocks[0], swap_core(down_blocks[1]), down_gathered[0], down_gathered[1]]
    hidden_grad = (contract_cols(cots[0], downs[0]) + contract_cols(cots[1], downs[1])) + (
        contract_cols(cots[2], downs[2]) + contract_cols(cots[3], downs[3])
    )
    ffns = [ffn_block(0), swap_core(ffn_block(1)), ffn_gathered[0], ffn_gathered[1]]

    tokens_half = lax.dynamic_slice_in_dim(tokens, side * half, half, 0).astype(f32)
    residual = tokens_half + out_rows(slice(0, half)) + from_x.astype(f32)

    mlp_square = width_total(jnp.sum(residual * residual, axis=1))
    mlp_own = low(residual * mlp_gain[None, :])
    mlp_rstd = lax.rsqrt(mlp_square / full_width + norm_eps)
    rstd_rel = jnp.concatenate([mlp_rstd, swap_x(mlp_rstd)]).reshape(rows, 1)
    quarter = half // 2
    mlp_x = swap_x(mlp_own)
    mlp_y = swap_y(mlp_own)
    mlp_xy = jnp.concatenate([swap_y(mlp_x[:quarter]), swap_x(mlp_y[quarter:])], axis=0)
    ins_own = [mlp_own, swap_core(mlp_own), mlp_y, swap_core(mlp_y)]
    ins_other = [mlp_x, swap_core(mlp_x), mlp_xy, swap_core(mlp_xy)]
    first = units_of_half(ins_own, ffns, rstd_rel, hidden_grad, 0, None)
    hidden, pair, pair_scaled, inner = units_of_half(
        ins_other, ffns, rstd_rel, hidden_grad, 1, first
    )

    exchange = [lambda b: b, swap_core, swap_y, swap_diag]
    mlp_all = [jnp.concatenate([a, b], axis=0) for a, b in zip(ins_own, ins_other)]

    def down_grad_of(which, ready):
        return low(contract_rows(after(hidden, ready), cots[which]))

    def ffn_grad_of(which, ready):
        return low(contract_rows(mlp_all[which], after(pair_scaled, ready)))

    def near_products(ready):
        return [f(k, ready) for k in (1, 0) for f in (ffn_grad_of, down_grad_of)]

    mlp_in_grad, near_grads = scatter_all(lambda k: contract_cols(pair, ffns[k]), near_products)
    near_grads = [swap_core(g) for g in near_grads[:2]] + near_grads[2:]
    near_sums = lax.psum(near_grads, "dp")
    inner_total = width_total(inner[:half, 0]) + swap_x(width_total(inner[half:, 0]))
    mlp_hat = residual * mlp_rstd[:, None]
    mlp_gain_part = jnp.sum(mlp_in_grad * mlp_hat, axis=0)
    residual_grad = cot_rel[:half].astype(f32) + mlp_rstd[:, None] * (
        mlp_in_grad * mlp_gain[None, :] - mlp_hat * (inner_total / full_width)[:, None]
    )
    residual_low = low(residual_grad)
    res_rel = jnp.concatenate([residual_low, swap_x(residual_low)], axis=0)
    head_own, head_y, head_for_y = scatter_width(lambda k: contract_cols(res_rel, outs[k]))

    far_down = [line_total(exchange[k](down_grad_of(k, head_for_y))) for k in (2, 3)]

    proj_low, q_gain_part, k_gain_part, inner_attn = whole_kernel(
        attend_back_kernel,
        [
            jax.ShapeDtypeStruct((rows, q_width + 2 * k_width), bf16),
            jax.ShapeDtypeStruct((1, head_size), f32),
            jax.ShapeDtypeStruct((1, head_size), f32),
            jax.ShapeDtypeStruct((rows, 1), f32),
        ],
        flops=10 * pairs_of_rows,
        scratch=[pltpu.VMEM((rows, k_width), f32), pltpu.VMEM((rows, k_width), f32)],
    )(side_word, head_own, head_y, projected, q_low, k_low, v_low, log_totals, *tables)
    inner_attn = width_total(inner_attn[:, 0])
    inner_attn = inner_attn + swap_x(inner_attn)
    proj_y = swap_y(proj_low)
    projs = [proj_low, swap_core(proj_low), proj_y, swap_core(proj_y)]
    far_ffn = []
    for k in (2, 3):
        block = ffn_grad_of(k, proj_low)
        far_ffn.append([line_total(exchange[k](b)) for b in (block[:, :units], block[:, units:])])
    normed_part = low(
        (contract_cols(projs[0], qkv_weights[0]) + contract_cols(projs[1], qkv_weights[1]))
        + (contract_cols(projs[2], qkv_weights[2]) + contract_cols(projs[3], qkv_weights[3]))
    )
    normed_grad = normed_part.astype(f32) + swap_x(normed_part).astype(f32)
    attn_gain_part = jnp.sum(normed_grad * attn_hat, axis=0)
    token_grad = low(
        flip(res_rel).astype(f32)
        + attn_rstd[:, None]
        * (normed_grad * attn_gain[None, :] - attn_hat * (inner_attn / full_width)[:, None])
    )

    mlp_out, _ = scatter_all(lambda k: dot(after(hidden, proj_y), downs[k]))
    mixed_half = low(residual + mlp_out)
    mixed = flip(jnp.concatenate([mixed_half, swap_x(mixed_half)], axis=0))

    out_grads = [low(contract_rows(piece, res_rel)) for piece in atts]
    qkv_grads = [low(contract_rows(normed, piece)) for piece in projs]
    out_grads, qkv_grads = lax.psum(after((out_grads, qkv_grads), *near_sums), "dp")
    down_grads = [near_sums[3], near_sums[1]] + far_down
    gate_grads = [g[:, :units] for g in (near_sums[2], near_sums[0])] + [g[0] for g in far_ffn]
    up_grads = [g[:, units:] for g in (near_sums[2], near_sums[0])] + [g[1] for g in far_ffn]

    head_parts = width_total(jnp.concatenate([q_gain_part[0], k_gain_part[0]]))
    shared = jnp.concatenate([head_parts, mlp_gain_part])
    shared = shared + swap_x(shared)
    gains = line_total(jnp.concatenate([shared, attn_gain_part]))
    q_gain_grad = gains[:head_size]
    k_gain_grad = gains[head_size : 2 * head_size]
    mlp_gain_grad = gains[2 * head_size : 2 * head_size + width]
    attn_gain_grad = gains[2 * head_size + width :]

    def place_cols(shape, pieces):
        whole = jnp.zeros(shape, f32)
        for which, piece in enumerate(pieces):
            whole = lax.dynamic_update_slice_in_dim(
                whole, piece.astype(f32), around[which] * piece.shape[1], 1
            )
        return whole

    def place_rows(shape, pieces):
        whole = jnp.zeros(shape, f32)
        for which, piece in enumerate(pieces):
            whole = lax.dynamic_update_slice_in_dim(
                whole, piece.astype(f32), around[which] * piece.shape[0], 0
            )
        return whole

    w_query_grad = place_cols(w_query.shape, [g[:, :q_width] for g in qkv_grads])
    w_key_grad = place_cols(w_key.shape, [g[:, q_width : q_width + k_width] for g in qkv_grads])
    w_value_grad = place_cols(w_value.shape, [g[:, q_width + k_width :] for g in qkv_grads])
    w_out_grad = place_rows(w_out.shape, out_grads)
    w_gate_grad = place_cols(w_gate.shape, gate_grads)
    w_up_grad = place_cols(w_up.shape, up_grads)
    w_down_grad = place_rows(w_down.shape, down_grads)
    return (
        mixed,
        token_grad,
        attn_gain_grad,
        q_gain_grad,
        k_gain_grad,
        mlp_gain_grad,
        w_query_grad,
        w_key_grad,
        w_value_grad,
        w_out_grad,
        w_gate_grad,
        w_up_grad,
        w_down_grad,
    )


def solution(mesh):
    in_specs = (
        P("dp", "tc"),
        P("dp", "tc"),
        P("dp"),
        P("tc"),
        P(),
        P(),
        P("tc"),
        P("tc", "tr"),
        P("tc", "tr"),
        P("tc", "tr"),
        P("tr", "tc"),
        P("tc", "tr"),
        P("tc", "tr"),
        P("tr", "tc"),
    )
    out_specs = (
        P("dp", "tc"),
        P("dp", "tc"),
        P("tc"),
        P(),
        P(),
        P("tc"),
        P("tc", "tr"),
        P("tc", "tr"),
        P("tc", "tr"),
        P("tr", "tc"),
        P("tc", "tr"),
        P("tc", "tr"),
        P("tr", "tc"),
    )
    return jax.shard_map(
        on_device, mesh=mesh, in_specs=in_specs, out_specs=out_specs, check_vma=False
    )
```

```python
import jax
import jax.numpy as jnp
from jax import lax
from jax.experimental import pallas as pl
from jax.experimental.pallas import tpu as pltpu
from jax.sharding import PartitionSpec as P

norm_eps = 1e-06
rope_base = 1000000.0
neg_big = -1e30
f32 = jnp.float32
bf16 = jnp.bfloat16


def dot(left_side, right_side):
    return jnp.dot(left_side, right_side, preferred_element_type=f32)


def contract_rows(left_side, right_side):
    return lax.dot_general(
        left_side, right_side, (((0,), (0,)), ((), ())), preferred_element_type=f32
    )


def contract_cols(left_side, right_side):
    return lax.dot_general(
        left_side, right_side, (((1,), (1,)), ((), ())), preferred_element_type=f32
    )


def swap_core(block):
    return lax.ppermute(block, "tc", [(i, i ^ 1) for i in range(4)])


def swap_y(block):
    return lax.ppermute(block, "tc", [(i, i ^ 2) for i in range(4)])


def swap_diag(block):
    return lax.ppermute(block, "tc", [(i, i ^ 3) for i in range(4)])


def swap_x(block):
    return lax.ppermute(block, "tr", [(0, 1), (1, 0)])


def width_total(rows):
    rows = rows + swap_core(rows)
    return rows + swap_y(rows)


def line_totals(pieces):
    size = lax.axis_size("dp")
    place = lax.axis_index("dp")
    half = size // 2
    totals, firsts = [], []
    for piece in pieces:
        if len(firsts) > 1:
            piece = after(piece, firsts[-2])
        for step in range(half):
            pairs = [(step, step + 1), (size - 1 - step, size - 2 - step)]
            got = lax.ppermute(piece, "dp", pairs)
            if step == 0:
                firsts.append(got)
            piece = low(piece.astype(f32) + got.astype(f32))
        for step in reversed(range(half - 1)):
            got = lax.ppermute(piece, "dp", [(step + 1, step), (size - 2 - step, size - 1 - step)])
            piece = jnp.where((place == step) | (place == size - 1 - step), got, piece)
        totals.append(piece)
    return totals


def after(value, *others):
    return lax.optimization_barrier((value, others))[0]


def low(array):
    return array.astype(bf16)


def scatter_width(product):
    from_far = swap_core(low(product(3)))
    for_y = low(product(2) + from_far.astype(f32))
    from_y = swap_y(for_y)
    from_core = swap_core(low(product(1)))
    return (product(0) + from_core.astype(f32), from_y, for_y)


def scatter_all(product, filler=lambda ready: ()):
    far_y = swap_core(low(product(3)))
    far_own = swap_core(low(product(1)))
    for_y = low(product(2) + far_y.astype(f32))
    own = low(product(0) + far_own.astype(f32))
    half = own.shape[0] // 2
    quarter = half // 2
    width = own.shape[1]
    y_first = swap_y(jnp.concatenate([for_y[quarter:half], for_y[half + quarter :]], axis=0))
    x_first = swap_x(
        jnp.concatenate([own[half : half + quarter], for_y[half : half + quarter]], axis=1)
    )
    fill = filler((own, for_y))
    x_first, y_first = after((x_first, y_first), fill)
    top_in = low(for_y[:quarter].astype(f32) + x_first[:, width:].astype(f32))
    low_in = low(own[half + quarter :].astype(f32) + y_first[quarter:].astype(f32))
    top_y, low_x = after((swap_y(top_in), swap_x(low_in)), top_in, low_in)
    top = own[:quarter].astype(f32) + x_first[:, :width].astype(f32) + top_y.astype(f32)
    bottom = own[quarter:half].astype(f32) + y_first[:quarter].astype(f32) + low_x.astype(f32)
    return (jnp.concatenate([top, bottom], axis=0), fill, top_in)


def positions_of(segment):
    slot_ids = jnp.arange(5, dtype=jnp.int32)
    before = jnp.sum((segment[None, :] < slot_ids[:, None]).astype(jnp.int32), axis=1)
    starts = jnp.sum(jnp.where(segment[:, None] == slot_ids[None, :], before[None, :], 0), axis=1)
    return jnp.arange(segment.shape[0], dtype=jnp.int32) - starts


def rope_tables(positions, head_size):
    half_size = head_size // 2
    frequency = rope_base ** (-jnp.arange(half_size, dtype=f32) * 2.0 / head_size)
    angles = positions.astype(f32)[:, None] * frequency[None, :]
    cosine, sine = jnp.cos(angles), jnp.sin(angles)
    return (
        jnp.concatenate([cosine, cosine], axis=1),
        jnp.concatenate([-sine, sine], axis=1),
    )


def turn(vectors):
    return pltpu.roll(vectors, vectors.shape[-1] // 2, axis=1)


def inverse_norm(vectors):
    return lax.rsqrt(jnp.mean(vectors * vectors, axis=-1, keepdims=True) + norm_eps)


def allowed_keys(seg_col, seg_row, start, size, extent):
    row = lax.broadcasted_iota(jnp.int32, (size, extent), 0) + start
    col = lax.broadcasted_iota(jnp.int32, (size, extent), 1)
    return (seg_col[start : start + size, :] == seg_row[:, :extent]) & (col <= row)


def attend_kernel(
    side, own, from_y, rstd, cos, sin, seg_col, seg_row, q_gain, k_gain,
    proj, q_out, k_out, v_out, lse, att,
):
    rows = own.shape[0]
    size = cos.shape[1]
    heads = q_out.shape[1] // size
    block = rows // 4
    scale = size**-0.5
    k_at = heads * size
    v_at = k_at + size

    def ready(i, carry):
        at = pl.ds(pl.multiple_of(i * block, block), block)
        raw = (own[at, :] + from_y[at, :].astype(f32)) * rstd[at, :]
        proj[at, :] = raw

        def rope(part, gain):
            n = part * inverse_norm(part) * gain[...]
            return (n * cos[at, :] + turn(n) * sin[at, :]).astype(bf16)

        for h in range(heads):
            q_out[at, h * size : (h + 1) * size] = rope(raw[:, h * size : (h + 1) * size], q_gain)
        k_out[at, :] = rope(raw[:, k_at:v_at], k_gain)
        v_out[at, :] = raw[:, v_at:].astype(bf16)
        return carry

    lax.fori_loop(0, 4, ready, 0)
    for i in range(4):
        start = i * block
        extent = start + block
        allowed = allowed_keys(seg_col, seg_row, start, block, extent)
        to = pl.ds(pl.multiple_of(lax.rem(start + side[0] * (rows // 2), rows), block), block)
        for h in range(heads):
            of_head = slice(h * size, (h + 1) * size)
            scores = contract_cols(q_out[start:extent, of_head], k_out[:extent, :]) * scale
            scores = jnp.where(allowed, scores, neg_big)
            top = jnp.max(scores, axis=-1, keepdims=True)
            expd = jnp.exp(scores - top)
            total = jnp.sum(expd, axis=-1, keepdims=True)
            weights = (expd * (1.0 / total)).astype(bf16)
            att[to, of_head] = dot(weights, v_out[:extent, :]).astype(bf16)
            lse[start:extent, h : h + 1] = top + jnp.log(total)


def attend_back_kernel(
    side, own, from_y, proj, q_in, k_in, v_in, lse, cos, sin, seg_col, seg_row, q_gain, k_gain,
    grads, q_gain_part, k_gain_part, inner, k_acc, v_acc,
):
    rows = own.shape[0]
    size = cos.shape[1]
    heads = q_in.shape[1] // size
    block = rows // 4
    scale = size**-0.5
    k_at = heads * size
    v_at = k_at + size

    def unrope(grad, part, gain, start):
        rows_at = slice(start, start + block)
        m = grad * cos[rows_at, :] - turn(grad) * sin[rows_at, :]
        r = inverse_norm(part)
        hat = part * r
        mg = m * gain[...]
        back = (r * (mg - hat * jnp.mean(mg * hat, axis=-1, keepdims=True))).astype(bf16)
        gain_part = jnp.sum(m * hat, axis=0, keepdims=True)
        return (back, gain_part, jnp.sum(back.astype(f32) * part, axis=-1, keepdims=True))

    k_acc[...] = jnp.zeros_like(k_acc)
    v_acc[...] = jnp.zeros_like(v_acc)
    q_total = jnp.zeros(q_gain_part.shape, f32)
    for i in range(4):
        start = i * block
        extent = start + block
        allowed = allowed_keys(seg_col, seg_row, start, block, extent)
        at = pl.ds(pl.multiple_of(lax.rem(start + side[0] * (rows // 2), rows), block), block)
        inner_sum = jnp.zeros((block, 1), f32)
        for h in range(heads):
            of_head = slice(h * size, (h + 1) * size)
            query = q_in[start:extent, of_head]
            grad = (own[at, of_head] + from_y[at, of_head].astype(f32)).astype(bf16)
            scores = contract_cols(query, k_in[:extent, :]) * scale
            scores = jnp.where(allowed, scores, neg_big)
            probs = jnp.exp(scores - lse[start:extent, h : h + 1])
            prob_grad = contract_cols(grad, v_in[:extent, :])
            delta = jnp.sum(probs * prob_grad, axis=-1, keepdims=True)
            score_grad = (probs * (prob_grad - delta)).astype(bf16)
            query_grad = dot(score_grad, k_in[:extent, :]) * scale
            k_acc[:extent, :] += contract_rows(score_grad, query) * scale
            v_acc[:extent, :] += contract_rows(probs.astype(bf16), grad)
            back, gain_part, part_inner = unrope(
                query_grad, proj[start:extent, of_head], q_gain, start
            )
            grads[start:extent, of_head] = back
            q_total = q_total + gain_part
            inner_sum = inner_sum + part_inner
        inner[start:extent, :] = inner_sum
    q_gain_part[...] = q_total
    k_total = jnp.zeros(k_gain_part.shape, f32)
    for i in range(4):
        start = i * block
        extent = start + block
        back, gain_part, part_inner = unrope(
            k_acc[start:extent, :], proj[start:extent, k_at:v_at], k_gain, start
        )
        grads[start:extent, k_at:v_at] = back
        k_total = k_total + gain_part
        v_back = v_acc[start:extent, :].astype(bf16)
        grads[start:extent, v_at:] = v_back
        inner[start:extent, :] += part_inner + jnp.sum(
            v_back.astype(f32) * proj[start:extent, v_at:], axis=-1, keepdims=True
        )
    k_gain_part[...] = k_total


vmem = pl.BlockSpec(memory_space=pltpu.VMEM)
smem = pl.BlockSpec(memory_space=pltpu.SMEM)
big_vmem = pltpu.CompilerParams(vmem_limit_bytes=50 * 2**20)


def whole_kernel(body, outs, flops, scratch=()):
    def call(*operands):
        nbytes = sum(o.size * o.dtype.itemsize for o in (*operands, *outs))
        return pl.pallas_call(
            body,
            out_shape=outs,
            in_specs=[smem] + [vmem] * (len(operands) - 1),
            out_specs=[vmem] * len(outs),
            scratch_shapes=scratch,
            compiler_params=big_vmem,
            cost_estimate=pl.CostEstimate(flops=flops, bytes_accessed=nbytes, transcendentals=0),
        )(*operands)

    return call


def units_kernel(*refs):
    ins, weights = refs[:4], refs[4:8]
    rstd_ref, grad_ref = refs[8:10]
    hidden, pair, scaled, inner = refs[-4:]
    units = hidden.shape[1]
    chunk = min(256, units)
    rstd = rstd_ref[...]

    def product(at):
        total = dot(ins[0][...], weights[0][:, at])
        for k in range(1, 4):
            total = total + dot(ins[k][...], weights[k][:, at])
        return total * rstd

    inner_sum = jnp.zeros(inner.shape, f32)
    for start in range(0, units, chunk):
        of_gate = slice(start, start + chunk)
        of_up = slice(units + start, units + start + chunk)
        gate, up = product(of_gate), product(of_up)
        grad = grad_ref[:, of_gate]
        sig = jax.nn.sigmoid(gate)
        silu = gate * sig
        hidden[:, of_gate] = low(silu * up)
        gate_grad = low(grad * up * sig * (1.0 + gate * (1.0 - sig)))
        up_grad = low(grad * silu)
        pair[:, of_gate] = gate_grad
        pair[:, of_up] = up_grad
        gate_grad, up_grad = gate_grad.astype(f32), up_grad.astype(f32)
        scaled[:, of_gate] = low(gate_grad * rstd)
        scaled[:, of_up] = low(up_grad * rstd)
        inner_sum = inner_sum + jnp.sum(gate_grad * gate + up_grad * up, axis=-1, keepdims=True)
    inner[...] = inner_sum


def units_of_half(ins, weights, rstd, grad, which, earlier):
    half, depth = ins[0].shape
    units = grad.shape[1]
    block = half // 2
    first = which * (half // block)
    outs = [
        jax.ShapeDtypeStruct((2 * half, units), bf16),
        jax.ShapeDtypeStruct((2 * half, 2 * units), bf16),
        jax.ShapeDtypeStruct((2 * half, 2 * units), bf16),
        jax.ShapeDtypeStruct((2 * half, 1), f32),
    ]
    rows_spec = [pl.BlockSpec((block, depth), lambda i: (i, 0))] * 4
    whole_spec = [pl.BlockSpec((depth, 2 * units), lambda i: (0, 0))] * 4
    at = [
        pl.BlockSpec((block, 1), lambda i: (first + i, 0)),
        pl.BlockSpec((block, units), lambda i: (first + i, 0)),
    ]
    earlier = list(earlier or [])
    kept = [pl.BlockSpec(memory_space=pl.ANY)] * len(earlier)
    return pl.pallas_call(
        units_kernel,
        grid=(half // block,),
        out_shape=outs,
        in_specs=rows_spec + whole_spec + at + kept,
        out_specs=[pl.BlockSpec((block, o.shape[1]), lambda i: (first + i, 0)) for o in outs],
        input_output_aliases={10 + k: k for k in range(len(earlier))},
        compiler_params=big_vmem,
        cost_estimate=pl.CostEstimate(
            flops=2 * half * 4 * depth * 2 * units,
            bytes_accessed=2 * (4 * depth * 2 * units + half * (4 * depth + 7 * units)),
            transcendentals=half * units,
        ),
    )(*ins, *weights, rstd, grad, *earlier)


def on_device(
    tokens,
    cotangent,
    segment_ids,
    attn_gain,
    q_gain,
    k_gain,
    mlp_gain,
    w_query,
    w_key,
    w_value,
    w_out,
    w_gate,
    w_up,
    w_down,
):
    assert lax.axis_size("tc") == 4 and lax.axis_size("tr") == 2
    col = lax.axis_index("tc")
    side = lax.axis_index("tr")
    rows, width = tokens.shape
    half = rows // 2
    full_width = width * 4
    head_size = q_gain.shape[0]
    q_width = w_query.shape[1] // 4
    k_width = w_key.shape[1] // 4
    units = w_gate.shape[1] // 4
    around = [col, col ^ 1, col ^ 2, col ^ 3]

    def cols_of(array, which, size):
        return lax.dynamic_slice_in_dim(array, around[which] * size, size, 1)

    def rows_of(array, which, size):
        return lax.dynamic_slice_in_dim(array, around[which] * size, size, 0)

    def flip(array):
        return jnp.concatenate(
            [
                lax.dynamic_slice_in_dim(array, side * half, half, 0),
                lax.dynamic_slice_in_dim(array, (1 - side) * half, half, 0),
            ],
            axis=0,
        )

    shares = lax.axis_size("dp")
    place = lax.axis_index("dp")

    def share_of(block):
        size = block.shape[0] // shares
        return lax.dynamic_slice_in_dim(block, place * size, size, 0)

    def gather_shares(from_y, from_diag):
        return lax.all_gather(jnp.stack([from_y, from_diag]), "dp", axis=1, tiled=True)

    def ffn_block(which):
        return jnp.concatenate(
            [cols_of(w_gate, which, units), cols_of(w_up, which, units)], axis=1
        )

    def ffn_share(which):
        return jnp.concatenate(
            [share_of(cols_of(w_gate, which, units)), share_of(cols_of(w_up, which, units))], axis=1
        )

    down_y, down_diag = (share_of(rows_of(w_down, k, units)) for k in (2, 3))
    down_gathered = gather_shares(swap_y(down_y), swap_diag(down_diag))
    share_y, share_diag = ffn_share(2), ffn_share(3)

    qkv_weights = [
        jnp.concatenate(
            [cols_of(w_query, k, q_width), cols_of(w_key, k, k_width), cols_of(w_value, k, k_width)],
            axis=1,
        )
        for k in range(4)
    ]
    inputs = tokens.astype(f32)
    scaled_in = after(low(inputs * attn_gain[None, :]), down_y, down_diag)
    square_sum = width_total(jnp.sum(inputs * inputs, axis=1))
    raw_own, raw_y, for_y = scatter_width(lambda k: dot(scaled_in, qkv_weights[k]))
    share_y, share_diag = after((share_y, share_diag), raw_own)
    share_y, share_diag = swap_y(share_y), swap_diag(share_diag)
    w_gate, w_up, w_down, w_out, segment_ids, cotangent = after(
        (w_gate, w_up, w_down, w_out, segment_ids, cotangent), for_y
    )
    attn_rstd = lax.rsqrt(square_sum / full_width + norm_eps)
    attn_hat = inputs * attn_rstd[:, None]
    normed = low(attn_hat * attn_gain[None, :])

    cos_table, sin_table = rope_tables(positions_of(segment_ids), head_size)
    side_word = side.astype(jnp.int32).reshape(1)
    tables = (
        cos_table,
        sin_table,
        segment_ids.reshape(rows, 1),
        segment_ids.reshape(1, rows),
        q_gain.reshape(1, head_size),
        k_gain.reshape(1, head_size),
    )
    heads = q_width // head_size
    pairs_of_rows = rows * rows * heads * head_size
    projected, q_low, k_low, v_low, log_totals, att_rel = whole_kernel(
        attend_kernel,
        [
            jax.ShapeDtypeStruct((rows, q_width + 2 * k_width), f32),
            jax.ShapeDtypeStruct((rows, q_width), bf16),
            jax.ShapeDtypeStruct((rows, k_width), bf16),
            jax.ShapeDtypeStruct((rows, k_width), bf16),
            jax.ShapeDtypeStruct((rows, heads), f32),
            jax.ShapeDtypeStruct((rows, q_width), bf16),
        ],
        flops=4 * pairs_of_rows,
    )(side_word, raw_own, raw_y, attn_rstd.reshape(rows, 1), *tables)
    ffn_gathered = gather_shares(*after((share_y, share_diag), att_rel))
    att_y = swap_y(att_rel)
    atts = [att_rel, swap_core(att_rel), att_y, swap_core(att_y)]
    outs = [rows_of(w_out, k, q_width) for k in range(4)]

    def out_rows(at):
        return (dot(atts[0][at], outs[0]) + dot(atts[1][at], outs[1])) + (
            dot(atts[2][at], outs[2]) + dot(atts[3][at], outs[3])
        )

    out_away = low(out_rows(slice(half, rows)))
    from_x = swap_x(out_away)

    cot_rel = flip(cotangent)
    cot_y_own = swap_y(after(cot_rel[:half], att_rel))
    cot_y = jnp.concatenate([cot_y_own, swap_x(after(cot_y_own, out_away))], axis=0)
    cots = [cot_rel, swap_core(cot_rel), cot_y, swap_core(cot_y)]
    downs = [
        rows_of(w_down, 0, units),
        swap_core(rows_of(w_down, 1, units)),
        down_gathered[0],
        down_gathered[1],
    ]
    hidden_grad = contract_cols(cots[0], downs[0]) + contract_cols(cots[1], downs[1])
    from_x, hidden_grad = after((from_x, hidden_grad), hidden_grad)
    hidden_grad = hidden_grad + (
        contract_cols(cots[2], downs[2]) + contract_cols(cots[3], downs[3])
    )
    ffns = [ffn_block(0), swap_core(ffn_block(1)), ffn_gathered[0], ffn_gathered[1]]

    tokens_half = lax.dynamic_slice_in_dim(tokens, side * half, half, 0).astype(f32)
    residual = tokens_half + out_rows(slice(0, half)) + from_x.astype(f32)

    mlp_square = width_total(jnp.sum(residual * residual, axis=1))
    mlp_own = low(residual * mlp_gain[None, :])
    mlp_rstd = lax.rsqrt(mlp_square / full_width + norm_eps)
    rstd_rel = jnp.concatenate([mlp_rstd, swap_x(mlp_rstd)]).reshape(rows, 1)
    quarter = half // 2
    mlp_x = swap_x(mlp_own)
    mlp_y = swap_y(mlp_own)
    mlp_xy = jnp.concatenate([swap_y(mlp_x[:quarter]), swap_x(mlp_y[quarter:])], axis=0)
    ins_own = [mlp_own, swap_core(mlp_own), mlp_y, swap_core(mlp_y)]
    ins_other = [mlp_x, swap_core(mlp_x), mlp_xy, swap_core(mlp_xy)]
    first = units_of_half(ins_own, ffns, rstd_rel, hidden_grad, 0, None)
    hidden, pair, pair_scaled, inner = units_of_half(
        ins_other, ffns, rstd_rel, hidden_grad, 1, first
    )

    exchange = [lambda b: b, swap_core, swap_y, swap_diag]
    mlp_all = [jnp.concatenate([a, b], axis=0) for a, b in zip(ins_own, ins_other)]

    def down_grad_of(which, ready):
        return low(contract_rows(after(hidden, ready), cots[which]))

    def ffn_grad_of(which, ready):
        return low(contract_rows(mlp_all[which], after(pair_scaled, ready)))

    def near_products(ready):
        inner_total = width_total(inner[:half, 0]) + swap_x(width_total(inner[half:, 0]))
        near = [f(k, ready) for k in (1, 0) for f in (ffn_grad_of, down_grad_of)]
        return (near, inner_total, down_grad_of(2, ready))

    mlp_in_grad, (near_grads, inner_total, down_for_y), sent = scatter_all(
        lambda k: contract_cols(pair, ffns[k]), near_products
    )
    far_pieces = [swap_y(after(down_for_y, sent))]
    near_grads = [swap_core(g) for g in near_grads[:2]] + near_grads[2:]
    near_sums = lax.psum(near_grads, "dp")
    mlp_hat = residual * mlp_rstd[:, None]
    mlp_gain_part = jnp.sum(mlp_in_grad * mlp_hat, axis=0)
    residual_grad = cot_rel[:half].astype(f32) + mlp_rstd[:, None] * (
        mlp_in_grad * mlp_gain[None, :] - mlp_hat * (inner_total / full_width)[:, None]
    )
    residual_low = low(residual_grad)
    res_rel = jnp.concatenate([residual_low, swap_x(residual_low)], axis=0)
    head_own, head_y, head_for_y = scatter_width(lambda k: contract_cols(res_rel, outs[k]))

    far_pieces.append(swap_diag(down_grad_of(3, head_for_y)))

    proj_low, q_gain_part, k_gain_part, inner_attn = whole_kernel(
        attend_back_kernel,
        [
            jax.ShapeDtypeStruct((rows, q_width + 2 * k_width), bf16),
            jax.ShapeDtypeStruct((1, head_size), f32),
            jax.ShapeDtypeStruct((1, head_size), f32),
            jax.ShapeDtypeStruct((rows, 1), f32),
        ],
        flops=10 * pairs_of_rows,
        scratch=[pltpu.VMEM((rows, k_width), f32), pltpu.VMEM((rows, k_width), f32)],
    )(side_word, head_own, head_y, projected, q_low, k_low, v_low, log_totals, *tables)
    inner_attn = width_total(inner_attn[:, 0])
    inner_attn = inner_attn + swap_x(inner_attn)
    proj_y = swap_y(proj_low)
    projs = [proj_low, swap_core(proj_low), proj_y, swap_core(proj_y)]
    for k, swap in ((2, swap_y), (3, swap_diag)):
        block = ffn_grad_of(k, proj_low)
        far_pieces += [swap(block[:, :units]), swap(block[:, units:])]
    normed_part = low(
        (contract_cols(projs[0], qkv_weights[0]) + contract_cols(projs[1], qkv_weights[1]))
        + (contract_cols(projs[2], qkv_weights[2]) + contract_cols(projs[3], qkv_weights[3]))
    )
    normed_grad = normed_part.astype(f32) + swap_x(normed_part).astype(f32)
    attn_gain_part = jnp.sum(normed_grad * attn_hat, axis=0)
    token_grad = low(
        flip(res_rel).astype(f32)
        + attn_rstd[:, None]
        * (normed_grad * attn_gain[None, :] - attn_hat * (inner_attn / full_width)[:, None])
    )

    mlp_out, _, _ = scatter_all(lambda k: dot(after(hidden, normed_part), downs[k]))
    mixed_half = low(residual + mlp_out)
    mixed = flip(jnp.concatenate([mixed_half, swap_x(mixed_half)], axis=0))

    shared = width_total(jnp.concatenate([q_gain_part[0], k_gain_part[0]]))
    shared = jnp.concatenate([shared, mlp_gain_part])
    shared = shared + swap_x(shared)
    gains = low(jnp.concatenate([shared, attn_gain_part]))
    gains = jnp.pad(gains, (0, 16 * width - gains.shape[0])).reshape(16, width)
    out_grads = [low(contract_rows(piece, res_rel)) for piece in atts]
    out_grads[0] = jnp.concatenate([out_grads[0], gains], axis=0)
    qkv_grads = [low(contract_rows(normed, piece)) for piece in projs]
    out_grads, qkv_grads = lax.psum(
        (out_grads, qkv_grads), "dp", axis_index_groups=[list(reversed(range(shares)))]
    )
    far_pieces[0] = after(far_pieces[0], normed_part)
    far_sums = line_totals(far_pieces)
    down_grads = [near_sums[3], near_sums[1]] + far_sums[:2]
    gate_grads = [g[:, :units] for g in (near_sums[2], near_sums[0])] + far_sums[2::2]
    up_grads = [g[:, units:] for g in (near_sums[2], near_sums[0])] + far_sums[3::2]
    gains = out_grads[0][q_width:].astype(f32).reshape(-1)
    out_grads[0] = out_grads[0][:q_width]
    q_gain_grad = gains[:head_size]
    k_gain_grad = gains[head_size : 2 * head_size]
    mlp_gain_grad = gains[2 * head_size : 2 * head_size + width]
    attn_gain_grad = gains[2 * head_size + width : 2 * head_size + 2 * width]

    def place_cols(shape, pieces):
        whole = jnp.zeros(shape, f32)
        for which, piece in enumerate(pieces):
            whole = lax.dynamic_update_slice_in_dim(
                whole, piece.astype(f32), around[which] * piece.shape[1], 1
            )
        return whole

    def place_rows(shape, pieces):
        whole = jnp.zeros(shape, f32)
        for which, piece in enumerate(pieces):
            whole = lax.dynamic_update_slice_in_dim(
                whole, piece.astype(f32), around[which] * piece.shape[0], 0
            )
        return whole

    w_query_grad = place_cols(w_query.shape, [g[:, :q_width] for g in qkv_grads])
    w_key_grad = place_cols(w_key.shape, [g[:, q_width : q_width + k_width] for g in qkv_grads])
    w_value_grad = place_cols(w_value.shape, [g[:, q_width + k_width :] for g in qkv_grads])
    w_out_grad = place_rows(w_out.shape, out_grads)
    w_gate_grad = place_cols(w_gate.shape, gate_grads)
    w_up_grad = place_cols(w_up.shape, up_grads)
    w_down_grad = place_rows(w_down.shape, down_grads)
    return (
        mixed,
        token_grad,
        attn_gain_grad,
        q_gain_grad,
        k_gain_grad,
        mlp_gain_grad,
        w_query_grad,
        w_key_grad,
        w_value_grad,
        w_out_grad,
        w_gate_grad,
        w_up_grad,
        w_down_grad,
    )


def solution(mesh):
    in_specs = (
        P("dp", "tc"),
        P("dp", "tc"),
        P("dp"),
        P("tc"),
        P(),
        P(),
        P("tc"),
        P("tc", "tr"),
        P("tc", "tr"),
        P("tc", "tr"),
        P("tr", "tc"),
        P("tc", "tr"),
        P("tc", "tr"),
        P("tr", "tc"),
    )
    out_specs = (
        P("dp", "tc"),
        P("dp", "tc"),
        P("tc"),
        P(),
        P(),
        P("tc"),
        P("tc", "tr"),
        P("tc", "tr"),
        P("tc", "tr"),
        P("tr", "tc"),
        P("tc", "tr"),
        P("tc", "tr"),
        P("tr", "tc"),
    )
    return jax.shard_map(
        on_device, mesh=mesh, in_specs=in_specs, out_specs=out_specs, check_vma=False
    )
```

```python
import jax
import jax.numpy as jnp
from jax import lax
from jax.experimental import pallas as pl
from jax.experimental.pallas import tpu as pltpu
from jax.sharding import PartitionSpec as P

norm_eps = 1e-06
rope_base = 1000000.0
neg_big = -1e30
f32 = jnp.float32
bf16 = jnp.bfloat16


def dot(left_side, right_side):
    return jnp.dot(left_side, right_side, preferred_element_type=f32)


def contract_rows(left_side, right_side):
    return lax.dot_general(
        left_side, right_side, (((0,), (0,)), ((), ())), preferred_element_type=f32
    )


def contract_cols(left_side, right_side):
    return lax.dot_general(
        left_side, right_side, (((1,), (1,)), ((), ())), preferred_element_type=f32
    )


def swap_core(block):
    return lax.ppermute(block, "tc", [(i, i ^ 1) for i in range(4)])


def swap_y(block):
    return lax.ppermute(block, "tc", [(i, i ^ 2) for i in range(4)])


def swap_diag(block):
    return lax.ppermute(block, "tc", [(i, i ^ 3) for i in range(4)])


def swap_x(block):
    return lax.ppermute(block, "tr", [(0, 1), (1, 0)])


def width_total(rows):
    rows = rows + swap_core(rows)
    return rows + swap_y(rows)


def line_total(piece):
    size = lax.axis_size("dp")
    place = lax.axis_index("dp")
    half = size // 2
    for step in range(half):
        got = lax.ppermute(piece, "dp", [(step, step + 1), (size - 1 - step, size - 2 - step)])
        piece = piece + got
    for step in reversed(range(half - 1)):
        got = lax.ppermute(piece, "dp", [(step + 1, step), (size - 2 - step, size - 1 - step)])
        piece = jnp.where((place == step) | (place == size - 1 - step), got, piece)
    return piece


class LineSums:
    def __init__(self):
        self.short = lax.axis_size("dp") == 4
        place = lax.axis_index("dp")
        self.middle = (place == 1) | (place == 2)
        self.queue, self.names, self.pieces = [], [], []
        self.outer, self.inward, self.total = [], [], []

    def _back(self, which):
        return self.total[which] if 0 <= which < len(self.total) else None

    def _consume(self, which, marker):
        got, piece = after((self.outer[which], self.pieces[which]), marker)
        inward = low(piece.astype(f32) + got.astype(f32))
        across = lax.ppermute(inward, "dp", [(1, 2), (2, 1)])
        self.inward.append(inward)
        self.total.append(low(inward.astype(f32) + across.astype(f32)))
        return inward

    def add(self, name, grad, axis):
        size = min(grad.shape)
        for k in range(0, grad.shape[axis], size):
            self.queue.append((name, lax.slice_in_dim(grad, k, k + size, axis=axis)))

    def waiting(self):
        return [piece for _, piece in self.queue]

    def send(self, marker=()):
        which = len(self.pieces)
        name, piece = self.queue.pop(0)
        self.names.append(name)
        self.pieces.append(piece)
        if not self.short:
            return piece
        if which >= 2:
            marker = self._consume(which - 2, marker)
        back = self._back(which - 3)
        out = after(piece, marker)
        if back is not None:
            out = jnp.where(self.middle, back, out)
        self.outer.append(lax.ppermute(out, "dp", [(0, 1), (1, 0), (2, 3), (3, 2)]))
        return marker

    def finish(self):
        count = len(self.pieces)
        if not self.short:
            sums = [lax.psum(piece, "dp") for piece in self.pieces]
            return lambda name: [s for n, s in zip(self.names, sums) if n == name]
        for which in (count - 2, count - 1):
            self._consume(which, ())
        for which in range(count - 3, count):
            self.outer.append(
                lax.ppermute(self.total[which], "dp", [(0, 1), (1, 0), (2, 3), (3, 2)])
            )
        sums = [jnp.where(self.middle, self.total[k], self.outer[k + 3]) for k in range(count)]
        return lambda name: [s for n, s in zip(self.names, sums) if n == name]


def after(value, *others):
    return lax.optimization_barrier((value, others))[0]


def low(array):
    return array.astype(bf16)


def scatter_width(product, near=lambda ready: ready):
    from_far = swap_core(low(product(3)))
    from_core = swap_core(low(product(1)))
    from_far = after(from_far, near(from_far))
    for_y = low(product(2) + from_far.astype(f32))
    from_y = swap_y(for_y)
    return (product(0) + from_core.astype(f32), from_y, for_y)


def scatter_all(product, started, turned):
    far_y = swap_core(low(product(3)))
    far_own = swap_core(low(product(1)))
    for_y = low(product(2) + far_y.astype(f32))
    own = low(product(0) + far_own.astype(f32))
    half = own.shape[0] // 2
    quarter = half // 2
    width = own.shape[1]
    y_first = swap_y(jnp.concatenate([for_y[quarter:half], for_y[half + quarter :]], axis=0))
    x_first = swap_x(
        jnp.concatenate([own[half : half + quarter], for_y[half : half + quarter]], axis=1)
    )
    x_first, y_first = after((x_first, y_first), started((own, for_y)))
    top_in = low(for_y[:quarter].astype(f32) + x_first[:, width:].astype(f32))
    low_in = low(own[half + quarter :].astype(f32) + y_first[quarter:].astype(f32))
    top_y, low_x = after((swap_y(top_in), swap_x(low_in)), turned((top_in, low_in)))
    top = own[:quarter].astype(f32) + x_first[:, :width].astype(f32) + top_y.astype(f32)
    bottom = own[quarter:half].astype(f32) + y_first[:quarter].astype(f32) + low_x.astype(f32)
    return jnp.concatenate([top, bottom], axis=0)


def positions_of(segment):
    slot_ids = jnp.arange(5, dtype=jnp.int32)
    before = jnp.sum((segment[None, :] < slot_ids[:, None]).astype(jnp.int32), axis=1)
    starts = jnp.sum(jnp.where(segment[:, None] == slot_ids[None, :], before[None, :], 0), axis=1)
    return jnp.arange(segment.shape[0], dtype=jnp.int32) - starts


def rope_tables(positions, head_size):
    half_size = head_size // 2
    frequency = rope_base ** (-jnp.arange(half_size, dtype=f32) * 2.0 / head_size)
    angles = positions.astype(f32)[:, None] * frequency[None, :]
    cosine, sine = jnp.cos(angles), jnp.sin(angles)
    return (
        jnp.concatenate([cosine, cosine], axis=1),
        jnp.concatenate([-sine, sine], axis=1),
    )


def turn(vectors):
    return pltpu.roll(vectors, vectors.shape[-1] // 2, axis=1)


def inverse_norm(vectors):
    return lax.rsqrt(jnp.mean(vectors * vectors, axis=-1, keepdims=True) + norm_eps)


def allowed_keys(seg_col, seg_row, start, size, extent):
    row = lax.broadcasted_iota(jnp.int32, (size, extent), 0) + start
    col = lax.broadcasted_iota(jnp.int32, (size, extent), 1)
    return (seg_col[start : start + size, :] == seg_row[:, :extent]) & (col <= row)


def attend_kernel(
    side, own, from_y, rstd, cos, sin, seg_col, seg_row, q_gain, k_gain,
    proj, q_out, k_out, v_out, lse, att,
):
    rows = own.shape[0]
    size = cos.shape[1]
    heads = q_out.shape[1] // size
    block = rows // 4
    scale = size**-0.5
    k_at = heads * size
    v_at = k_at + size

    def ready(i, carry):
        at = pl.ds(pl.multiple_of(i * block, block), block)
        raw = (own[at, :] + from_y[at, :].astype(f32)) * rstd[at, :]
        proj[at, :] = raw

        def rope(part, gain):
            n = part * inverse_norm(part) * gain[...]
            return (n * cos[at, :] + turn(n) * sin[at, :]).astype(bf16)

        for h in range(heads):
            q_out[at, h * size : (h + 1) * size] = rope(raw[:, h * size : (h + 1) * size], q_gain)
        k_out[at, :] = rope(raw[:, k_at:v_at], k_gain)
        v_out[at, :] = raw[:, v_at:].astype(bf16)
        return carry

    lax.fori_loop(0, 4, ready, 0)
    for i in range(4):
        start = i * block
        extent = start + block
        allowed = allowed_keys(seg_col, seg_row, start, block, extent)
        to = pl.ds(pl.multiple_of(lax.rem(start + side[0] * (rows // 2), rows), block), block)
        for h in range(heads):
            of_head = slice(h * size, (h + 1) * size)
            scores = contract_cols(q_out[start:extent, of_head], k_out[:extent, :]) * scale
            scores = jnp.where(allowed, scores, neg_big)
            top = jnp.max(scores, axis=-1, keepdims=True)
            expd = jnp.exp(scores - top)
            total = jnp.sum(expd, axis=-1, keepdims=True)
            weights = (expd * (1.0 / total)).astype(bf16)
            att[to, of_head] = dot(weights, v_out[:extent, :]).astype(bf16)
            lse[start:extent, h : h + 1] = top + jnp.log(total)


def attend_back_kernel(
    side, own, from_y, proj, q_in, k_in, v_in, lse, cos, sin, seg_col, seg_row, q_gain, k_gain,
    grads, q_gain_part, k_gain_part, inner, k_acc, v_acc,
):
    rows = own.shape[0]
    size = cos.shape[1]
    heads = q_in.shape[1] // size
    block = rows // 4
    scale = size**-0.5
    k_at = heads * size
    v_at = k_at + size

    def unrope(grad, part, gain, start):
        rows_at = slice(start, start + block)
        m = grad * cos[rows_at, :] - turn(grad) * sin[rows_at, :]
        r = inverse_norm(part)
        hat = part * r
        mg = m * gain[...]
        back = (r * (mg - hat * jnp.mean(mg * hat, axis=-1, keepdims=True))).astype(bf16)
        gain_part = jnp.sum(m * hat, axis=0, keepdims=True)
        return (back, gain_part, jnp.sum(back.astype(f32) * part, axis=-1, keepdims=True))

    k_acc[...] = jnp.zeros_like(k_acc)
    v_acc[...] = jnp.zeros_like(v_acc)
    q_total = jnp.zeros(q_gain_part.shape, f32)
    for i in range(4):
        start = i * block
        extent = start + block
        allowed = allowed_keys(seg_col, seg_row, start, block, extent)
        at = pl.ds(pl.multiple_of(lax.rem(start + side[0] * (rows // 2), rows), block), block)
        inner_sum = jnp.zeros((block, 1), f32)
        for h in range(heads):
            of_head = slice(h * size, (h + 1) * size)
            query = q_in[start:extent, of_head]
            grad = (own[at, of_head] + from_y[at, of_head].astype(f32)).astype(bf16)
            scores = contract_cols(query, k_in[:extent, :]) * scale
            scores = jnp.where(allowed, scores, neg_big)
            probs = jnp.exp(scores - lse[start:extent, h : h + 1])
            prob_grad = contract_cols(grad, v_in[:extent, :])
            delta = jnp.sum(probs * prob_grad, axis=-1, keepdims=True)
            score_grad = (probs * (prob_grad - delta)).astype(bf16)
            query_grad = dot(score_grad, k_in[:extent, :]) * scale
            k_acc[:extent, :] += contract_rows(score_grad, query) * scale
            v_acc[:extent, :] += contract_rows(probs.astype(bf16), grad)
            back, gain_part, part_inner = unrope(
                query_grad, proj[start:extent, of_head], q_gain, start
            )
            grads[start:extent, of_head] = back
            q_total = q_total + gain_part
            inner_sum = inner_sum + part_inner
        inner[start:extent, :] = inner_sum
    q_gain_part[...] = q_total
    k_total = jnp.zeros(k_gain_part.shape, f32)
    for i in range(4):
        start = i * block
        extent = start + block
        back, gain_part, part_inner = unrope(
            k_acc[start:extent, :], proj[start:extent, k_at:v_at], k_gain, start
        )
        grads[start:extent, k_at:v_at] = back
        k_total = k_total + gain_part
        v_back = v_acc[start:extent, :].astype(bf16)
        grads[start:extent, v_at:] = v_back
        inner[start:extent, :] += part_inner + jnp.sum(
            v_back.astype(f32) * proj[start:extent, v_at:], axis=-1, keepdims=True
        )
    k_gain_part[...] = k_total


vmem = pl.BlockSpec(memory_space=pltpu.VMEM)
smem = pl.BlockSpec(memory_space=pltpu.SMEM)
big_vmem = pltpu.CompilerParams(vmem_limit_bytes=50 * 2**20)


def whole_kernel(body, outs, flops, scratch=()):
    def call(*operands):
        nbytes = sum(o.size * o.dtype.itemsize for o in (*operands, *outs))
        return pl.pallas_call(
            body,
            out_shape=outs,
            in_specs=[smem] + [vmem] * (len(operands) - 1),
            out_specs=[vmem] * len(outs),
            scratch_shapes=scratch,
            compiler_params=big_vmem,
            cost_estimate=pl.CostEstimate(flops=flops, bytes_accessed=nbytes, transcendentals=0),
        )(*operands)

    return call


def units_kernel(*refs):
    ins, weights, cots, downs = refs[:4], refs[4:8], refs[8:12], refs[12:16]
    rstd_ref = refs[16]
    hidden, pair, scaled, inner = refs[-4:]
    units = hidden.shape[1]
    chunk = min(256, units)
    rstd = rstd_ref[...]

    def product(at):
        total = dot(ins[0][...], weights[0][:, at])
        for k in range(1, 4):
            total = total + dot(ins[k][...], weights[k][:, at])
        return total * rstd

    inner_sum = jnp.zeros(inner.shape, f32)
    for start in range(0, units, chunk):
        of_gate = slice(start, start + chunk)
        of_up = slice(units + start, units + start + chunk)
        gate, up = product(of_gate), product(of_up)
        grad = contract_cols(cots[0][...], downs[0][of_gate, :])
        for k in range(1, 4):
            grad = grad + contract_cols(cots[k][...], downs[k][of_gate, :])
        sig = jax.nn.sigmoid(gate)
        silu = gate * sig
        hidden[:, of_gate] = low(silu * up)
        gate_grad = low(grad * up * sig * (1.0 + gate * (1.0 - sig)))
        up_grad = low(grad * silu)
        pair[:, of_gate] = gate_grad
        pair[:, of_up] = up_grad
        gate_grad, up_grad = gate_grad.astype(f32), up_grad.astype(f32)
        scaled[:, of_gate] = low(gate_grad * rstd)
        scaled[:, of_up] = low(up_grad * rstd)
        inner_sum = inner_sum + jnp.sum(gate_grad * gate + up_grad * up, axis=-1, keepdims=True)
    inner[...] = inner_sum


def units_of_half(ins, weights, cots, downs, rstd, which, earlier):
    half, depth = ins[0].shape
    units = downs[0].shape[0]
    block = half // 2
    first = which * (half // block)
    outs = [
        jax.ShapeDtypeStruct((half, units), bf16),
        jax.ShapeDtypeStruct((2 * half, 2 * units), bf16),
        jax.ShapeDtypeStruct((2 * half, 2 * units), bf16),
        jax.ShapeDtypeStruct((2 * half, 1), f32),
    ]

    def whole(array):
        return pl.BlockSpec(array.shape, lambda i: (0, 0))

    def of_two(array, k):
        return pl.BlockSpec((None, *array.shape[1:]), lambda i: (k, 0, 0))

    def four(blocks):
        near_by, core, both = blocks
        return (
            [near_by, core, both, both],
            [whole(near_by), whole(core), of_two(both, 0), of_two(both, 1)],
        )

    rows_spec = [pl.BlockSpec((block, depth), lambda i: (i, 0))] * 4
    weights, weight_specs = four(weights)
    downs, down_specs = four(downs)
    earlier = list(earlier or [])
    kept = [pl.BlockSpec(memory_space=pl.ANY)] * len(earlier)
    at = lambda i: (first + i, 0)
    return pl.pallas_call(
        units_kernel,
        grid=(half // block,),
        out_shape=outs,
        in_specs=rows_spec
        + weight_specs
        + rows_spec
        + down_specs
        + [pl.BlockSpec((block, 1), at)]
        + kept,
        out_specs=[pl.BlockSpec((block, units), lambda i: (i, 0))]
        + [pl.BlockSpec((block, o.shape[1]), at) for o in outs[1:]],
        input_output_aliases={17 + k: 1 + k for k in range(len(earlier))},
        compiler_params=big_vmem,
        cost_estimate=pl.CostEstimate(
            flops=2 * half * 4 * depth * 3 * units,
            bytes_accessed=2 * (4 * depth * 3 * units + half * (8 * depth + 5 * units)),
            transcendentals=half * units,
        ),
    )(*ins, *weights, *cots, *downs, rstd, *earlier)


def on_device(
    tokens,
    cotangent,
    segment_ids,
    attn_gain,
    q_gain,
    k_gain,
    mlp_gain,
    w_query,
    w_key,
    w_value,
    w_out,
    w_gate,
    w_up,
    w_down,
):
    assert lax.axis_size("tc") == 4 and lax.axis_size("tr") == 2
    col = lax.axis_index("tc")
    side = lax.axis_index("tr")
    rows, width = tokens.shape
    half = rows // 2
    full_width = width * 4
    head_size = q_gain.shape[0]
    q_width = w_query.shape[1] // 4
    k_width = w_key.shape[1] // 4
    units = w_gate.shape[1] // 4
    around = [col, col ^ 1, col ^ 2, col ^ 3]

    def cols_of(array, which, size):
        return lax.dynamic_slice_in_dim(array, around[which] * size, size, 1)

    def rows_of(array, which, size):
        return lax.dynamic_slice_in_dim(array, around[which] * size, size, 0)

    def flip(array):
        return jnp.concatenate(
            [
                lax.dynamic_slice_in_dim(array, side * half, half, 0),
                lax.dynamic_slice_in_dim(array, (1 - side) * half, half, 0),
            ],
            axis=0,
        )

    shares = lax.axis_size("dp")
    place = lax.axis_index("dp")

    def share_of(block):
        size = block.shape[0] // shares
        return lax.dynamic_slice_in_dim(block, place * size, size, 0)

    def gather_shares(from_y, from_diag):
        return lax.all_gather(jnp.stack([from_y, from_diag]), "dp", axis=1, tiled=True)

    def ffn_block(which):
        return jnp.concatenate(
            [cols_of(w_gate, which, units), cols_of(w_up, which, units)], axis=1
        )

    def ffn_share(which):
        return jnp.concatenate(
            [share_of(cols_of(w_gate, which, units)), share_of(cols_of(w_up, which, units))], axis=1
        )

    down_y, down_diag = (share_of(rows_of(w_down, k, units)) for k in (2, 3))
    down_y, down_diag = swap_y(down_y), swap_diag(down_diag)

    qkv_weights = [
        jnp.concatenate(
            [cols_of(w_query, k, q_width), cols_of(w_key, k, k_width), cols_of(w_value, k, k_width)],
            axis=1,
        )
        for k in range(4)
    ]
    inputs = tokens.astype(f32)
    scaled_in = low(inputs * attn_gain[None, :])
    raw_own, raw_y, for_y = scatter_width(lambda k: dot(scaled_in, qkv_weights[k]))
    down_gathered = gather_shares(*after((down_y, down_diag), for_y))
    w_gate, w_up, w_down, w_out, segment_ids, cotangent, inputs = after(
        (w_gate, w_up, w_down, w_out, segment_ids, cotangent, inputs), for_y
    )
    share_y, share_diag = swap_y(ffn_share(2)), swap_diag(ffn_share(3))
    square_sum = width_total(jnp.sum(inputs * inputs, axis=1))
    attn_rstd = lax.rsqrt(square_sum / full_width + norm_eps)
    attn_hat = inputs * attn_rstd[:, None]
    normed = low(attn_hat * attn_gain[None, :])

    cos_table, sin_table = rope_tables(positions_of(segment_ids), head_size)
    side_word = side.astype(jnp.int32).reshape(1)
    tables = (
        cos_table,
        sin_table,
        segment_ids.reshape(rows, 1),
        segment_ids.reshape(1, rows),
        q_gain.reshape(1, head_size),
        k_gain.reshape(1, head_size),
    )
    heads = q_width // head_size
    pairs_of_rows = rows * rows * heads * head_size
    projected, q_low, k_low, v_low, log_totals, att_rel = whole_kernel(
        attend_kernel,
        [
            jax.ShapeDtypeStruct((rows, q_width + 2 * k_width), f32),
            jax.ShapeDtypeStruct((rows, q_width), bf16),
            jax.ShapeDtypeStruct((rows, k_width), bf16),
            jax.ShapeDtypeStruct((rows, k_width), bf16),
            jax.ShapeDtypeStruct((rows, heads), f32),
            jax.ShapeDtypeStruct((rows, q_width), bf16),
        ],
        flops=4 * pairs_of_rows,
    )(side_word, raw_own, raw_y, attn_rstd.reshape(rows, 1), *tables)
    ffn_gathered = gather_shares(*after((share_y, share_diag), att_rel))
    att_y = swap_y(att_rel)
    atts = [att_rel, swap_core(att_rel), att_y, swap_core(att_y)]
    outs = [rows_of(w_out, k, q_width) for k in range(4)]

    def out_rows(at):
        return (dot(atts[0][at], outs[0]) + dot(atts[1][at], outs[1])) + (
            dot(atts[2][at], outs[2]) + dot(atts[3][at], outs[3])
        )

    from_x = swap_x(low(out_rows(slice(half, rows))))
    tokens_half = lax.dynamic_slice_in_dim(tokens, side * half, half, 0).astype(f32)
    residual = tokens_half + out_rows(slice(0, half)) + from_x.astype(f32)

    mlp_square = width_total(jnp.sum(residual * residual, axis=1))
    mlp_own = low(residual * mlp_gain[None, :])
    mlp_rstd = lax.rsqrt(mlp_square / full_width + norm_eps)
    rstd_rel = jnp.concatenate([mlp_rstd, swap_x(mlp_rstd)]).reshape(rows, 1)
    quarter = half // 2
    mlp_x = swap_x(mlp_own)
    mlp_y = swap_y(mlp_own)
    mlp_xy = jnp.concatenate([swap_y(mlp_x[:quarter]), swap_x(mlp_y[quarter:])], axis=0)
    ins_own = [mlp_own, swap_core(mlp_own), mlp_y, swap_core(mlp_y)]
    ins_other = [mlp_x, swap_core(mlp_x), mlp_xy, swap_core(mlp_xy)]
    cot_rel = flip(cotangent)
    cot_own, cot_other = cot_rel[:half], cot_rel[half:]
    cot_y = swap_y(after(cot_own, att_rel))
    cot_x = swap_x(after(cot_y, mlp_own))
    cots_own = [cot_own, swap_core(cot_own), cot_y, swap_core(cot_y)]
    cots_other = [cot_other, swap_core(cot_other), cot_x, swap_core(cot_x)]
    ffns = (ffn_block(0), swap_core(ffn_block(1)), ffn_gathered)
    downs = (rows_of(w_down, 0, units), swap_core(rows_of(w_down, 1, units)), down_gathered)
    hidden_own, *first = units_of_half(ins_own, ffns, cots_own, downs, rstd_rel, 0, None)
    hidden_other, pair, pair_scaled, inner = units_of_half(
        ins_other, ffns, cots_other, downs, rstd_rel, 1, first
    )
    hiddens = [lax.all_gather(h, "tc", axis=1, tiled=True) for h in (hidden_own, hidden_other)]
    pairs = lax.all_gather(after(pair_scaled, hidden_other), "tc")

    line = LineSums()
    mlp_in = jnp.concatenate([mlp_own, mlp_x], axis=0)

    def add_ffn(which, marker):
        block = after(
            pair_scaled
            if which == 0
            else lax.dynamic_index_in_dim(pairs, around[which], 0, keepdims=False),
            marker,
        )
        line.add(("ffn", which), low(contract_rows(mlp_in, block)), 1)

    add_ffn(0, ())
    line.send()
    pair = after(pair, line.send(), line.waiting())

    def inner_sums(marker):
        own_sum, other_sum = after((inner[:half, 0], inner[half:, 0]), marker)
        return width_total(own_sum) + swap_x(width_total(other_sum))

    kept = {}

    def started(marker):
        kept["inner"] = inner_sums(marker)
        marker = line.send(marker)
        down_grad = low(
            contract_rows(after(hiddens[0], marker), cot_own)
            + contract_rows(after(hiddens[1], marker), cot_other)
        )
        line.add("down", down_grad, 0)
        return (marker, kept["inner"])

    def turned(marker):
        return line.send(marker)

    ffn_blocks = [ffns[0], ffns[1], ffns[2][0], ffns[2][1]]
    mlp_in_grad = scatter_all(lambda k: contract_cols(pair, ffn_blocks[k]), started, turned)
    inner_total = kept["inner"]
    mlp_hat = residual * mlp_rstd[:, None]
    mlp_gain_part = jnp.sum(mlp_in_grad * mlp_hat, axis=0)
    residual_grad = cot_rel[:half].astype(f32) + mlp_rstd[:, None] * (
        mlp_in_grad * mlp_gain[None, :] - mlp_hat * (inner_total / full_width)[:, None]
    )
    residual_low = low(residual_grad)
    res_x = after(swap_x(residual_low), line.send(residual_low))
    res_rel = jnp.concatenate([residual_low, res_x], axis=0)
    head_own, head_y, head_sent = scatter_width(
        lambda k: contract_cols(res_rel, outs[k]), line.send
    )
    out_grads = [low(contract_rows(after(part, head_sent), res_rel)) for part in atts]
    line.add("out", jnp.concatenate(out_grads, axis=0), 0)
    head_own, head_y = after((head_own, head_y), line.send(out_grads), line.waiting())

    proj_low, q_gain_part, k_gain_part, inner_attn = whole_kernel(
        attend_back_kernel,
        [
            jax.ShapeDtypeStruct((rows, q_width + 2 * k_width), bf16),
            jax.ShapeDtypeStruct((1, head_size), f32),
            jax.ShapeDtypeStruct((1, head_size), f32),
            jax.ShapeDtypeStruct((rows, 1), f32),
        ],
        flops=10 * pairs_of_rows,
        scratch=[pltpu.VMEM((rows, k_width), f32), pltpu.VMEM((rows, k_width), f32)],
    )(side_word, head_own, head_y, projected, q_low, k_low, v_low, log_totals, *tables)
    proj_y = swap_y(proj_low)
    proj_core = swap_core(proj_low)
    marker = line.send(proj_low)
    inner_attn = width_total(after(inner_attn, marker)[:, 0])
    inner_attn = inner_attn + swap_x(inner_attn)
    marker = line.send(inner_attn)
    proj_y, proj_core = after((proj_y, proj_core), marker)
    projs = [proj_low, proj_core, proj_y, swap_core(proj_y)]
    normed_part = low(
        (contract_cols(projs[0], qkv_weights[0]) + contract_cols(projs[1], qkv_weights[1]))
        + (contract_cols(projs[2], qkv_weights[2]) + contract_cols(projs[3], qkv_weights[3]))
    )
    normed_x = after(swap_x(normed_part), line.send(normed_part))
    normed_grad = normed_part.astype(f32) + normed_x.astype(f32)
    attn_gain_part = jnp.sum(normed_grad * attn_hat, axis=0)
    token_grad = low(
        flip(res_rel).astype(f32)
        + attn_rstd[:, None]
        * (normed_grad * attn_gain[None, :] - attn_hat * (inner_attn / full_width)[:, None])
    )

    add_ffn(1, normed_part)
    mlp_away = low(dot(after(hiddens[1], normed_grad), w_down))
    mlp_x_out = after(swap_x(mlp_away), line.send(mlp_away))
    mixed_half = low(residual + dot(hiddens[0], w_down) + mlp_x_out.astype(f32))
    mixed_x = swap_x(mixed_half)
    marker = line.send(mixed_half)
    mixed = flip(jnp.concatenate([mixed_half, mixed_x], axis=0))

    for k in (2, 3):
        add_ffn(k, marker)
        while line.queue:
            marker = line.send()
    for k, part in enumerate(projs):
        line.add(("qkv", k), low(contract_rows(after(normed, marker), part)), 1)
    while line.queue:
        line.send()
    sums_of = line.finish()
    qkv_grads = [jnp.concatenate(sums_of(("qkv", k)), axis=1) for k in range(4)]

    shared = width_total(jnp.concatenate([q_gain_part[0], k_gain_part[0]]))
    shared = jnp.concatenate([shared, mlp_gain_part])
    shared = shared + swap_x(shared)
    gains = line_total(jnp.concatenate([shared, attn_gain_part]))
    q_gain_grad = gains[:head_size]
    k_gain_grad = gains[head_size : 2 * head_size]
    mlp_gain_grad = gains[2 * head_size : 2 * head_size + width]
    attn_gain_grad = gains[2 * head_size + width :]

    def place_cols(shape, pieces):
        whole = jnp.zeros(shape, f32)
        for which, piece in enumerate(pieces):
            whole = lax.dynamic_update_slice_in_dim(
                whole, piece.astype(f32), around[which] * piece.shape[1], 1
            )
        return whole

    def place_rows(shape, pieces):
        whole = jnp.zeros(shape, f32)
        for which, piece in enumerate(pieces):
            whole = lax.dynamic_update_slice_in_dim(
                whole, piece.astype(f32), around[which] * piece.shape[0], 0
            )
        return whole

    w_query_grad = place_cols(w_query.shape, [g[:, :q_width] for g in qkv_grads])
    w_key_grad = place_cols(w_key.shape, [g[:, q_width : q_width + k_width] for g in qkv_grads])
    w_value_grad = place_cols(w_value.shape, [g[:, q_width + k_width :] for g in qkv_grads])
    out_sum = jnp.concatenate(sums_of("out"), axis=0)
    w_out_grad = place_rows(
        w_out.shape, [out_sum[k * q_width : (k + 1) * q_width] for k in range(4)]
    )
    w_gate_grad = jnp.zeros(w_gate.shape, f32)
    w_up_grad = jnp.zeros(w_up.shape, f32)
    step = width // 2
    for which in range(4):
        for at, part in enumerate(sums_of(("ffn", which))):
            for start in (0, step):
                column = at * width + start
                block = part[:, start : start + step].astype(f32)
                to = (0, around[which] * units + column % units)
                if column < units:
                    w_gate_grad = lax.dynamic_update_slice(w_gate_grad, block, to)
                else:
                    w_up_grad = lax.dynamic_update_slice(w_up_grad, block, to)
    w_down_grad = jnp.concatenate(sums_of("down"), axis=0).astype(f32)
    return (
        mixed,
        token_grad,
        attn_gain_grad,
        q_gain_grad,
        k_gain_grad,
        mlp_gain_grad,
        w_query_grad,
        w_key_grad,
        w_value_grad,
        w_out_grad,
        w_gate_grad,
        w_up_grad,
        w_down_grad,
    )


def solution(mesh):
    in_specs = (
        P("dp", "tc"),
        P("dp", "tc"),
        P("dp"),
        P("tc"),
        P(),
        P(),
        P("tc"),
        P("tc", "tr"),
        P("tc", "tr"),
        P("tc", "tr"),
        P("tr", "tc"),
        P("tc", "tr"),
        P("tc", "tr"),
        P("tr", "tc"),
    )
    out_specs = (
        P("dp", "tc"),
        P("dp", "tc"),
        P("tc"),
        P(),
        P(),
        P("tc"),
        P("tc", "tr"),
        P("tc", "tr"),
        P("tc", "tr"),
        P("tr", "tc"),
        P("tc", "tr"),
        P("tc", "tr"),
        P("tr", "tc"),
    )
    return jax.shard_map(
        on_device, mesh=mesh, in_specs=in_specs, out_specs=out_specs, check_vma=False
    )
```

```python
import jax
import jax.numpy as jnp
from jax import lax
from jax.experimental import pallas as pl
from jax.experimental.pallas import tpu as pltpu
from jax.sharding import PartitionSpec as P

norm_eps = 1e-06
rope_base = 1000000.0
neg_big = -1e30
f32 = jnp.float32
bf16 = jnp.bfloat16


def dot(left_side, right_side):
    return jnp.dot(left_side, right_side, preferred_element_type=f32)


def contract_rows(left_side, right_side):
    return lax.dot_general(
        left_side, right_side, (((0,), (0,)), ((), ())), preferred_element_type=f32
    )


def contract_cols(left_side, right_side):
    return lax.dot_general(
        left_side, right_side, (((1,), (1,)), ((), ())), preferred_element_type=f32
    )


def swap_core(block):
    return lax.ppermute(block, "tc", [(i, i ^ 1) for i in range(4)])


def swap_y(block):
    return lax.ppermute(block, "tc", [(i, i ^ 2) for i in range(4)])


def swap_diag(block):
    return lax.ppermute(block, "tc", [(i, i ^ 3) for i in range(4)])


def swap_x(block):
    return lax.ppermute(block, "tr", [(0, 1), (1, 0)])


def width_total(rows):
    rows = rows + swap_core(rows)
    return rows + swap_y(rows)


def line_total(piece):
    size = lax.axis_size("dp")
    place = lax.axis_index("dp")
    half = size // 2
    for step in range(half):
        got = lax.ppermute(piece, "dp", [(step, step + 1), (size - 1 - step, size - 2 - step)])
        piece = piece + got
    for step in reversed(range(half - 1)):
        got = lax.ppermute(piece, "dp", [(step + 1, step), (size - 2 - step, size - 1 - step)])
        piece = jnp.where((place == step) | (place == size - 1 - step), got, piece)
    return piece


class LineSums:
    def __init__(self):
        self.short = lax.axis_size("dp") == 4
        place = lax.axis_index("dp")
        self.middle = (place == 1) | (place == 2)
        self.queue, self.names, self.pieces = [], [], []
        self.outer, self.inward, self.total = [], [], []

    def _back(self, which):
        return self.total[which] if 0 <= which < len(self.total) else None

    def _consume(self, which, marker):
        got, piece = after((self.outer[which], self.pieces[which]), marker)
        inward = low(piece.astype(f32) + got.astype(f32))
        across = lax.ppermute(inward, "dp", [(1, 2), (2, 1)])
        self.inward.append(inward)
        self.total.append(low(inward.astype(f32) + across.astype(f32)))
        return inward

    def add(self, name, grad, axis):
        size = min(grad.shape)
        for k in range(0, grad.shape[axis], size):
            self.queue.append((name, lax.slice_in_dim(grad, k, k + size, axis=axis)))

    def waiting(self):
        return [piece for _, piece in self.queue]

    def send(self, marker=()):
        which = len(self.pieces)
        name, piece = self.queue.pop(0)
        self.names.append(name)
        self.pieces.append(piece)
        if not self.short:
            return piece
        if which >= 2:
            marker = self._consume(which - 2, marker)
        back = self._back(which - 3)
        out = after(piece, marker)
        if back is not None:
            out = jnp.where(self.middle, back, out)
        self.outer.append(lax.ppermute(out, "dp", [(0, 1), (1, 0), (2, 3), (3, 2)]))
        return marker

    def finish(self):
        count = len(self.pieces)
        if not self.short:
            sums = [lax.psum(piece, "dp") for piece in self.pieces]
            return lambda name: [s for n, s in zip(self.names, sums) if n == name]
        for which in (count - 2, count - 1):
            self._consume(which, ())
        for which in range(count - 3, count):
            self.outer.append(
                lax.ppermute(self.total[which], "dp", [(0, 1), (1, 0), (2, 3), (3, 2)])
            )
        sums = [jnp.where(self.middle, self.total[k], self.outer[k + 3]) for k in range(count)]
        return lambda name: [s for n, s in zip(self.names, sums) if n == name]


def after(value, *others):
    return lax.optimization_barrier((value, others))[0]


def low(array):
    return array.astype(bf16)


def scatter_width(product, near=lambda ready: ready):
    from_far = swap_core(low(product(3)))
    from_core = swap_core(low(product(1)))
    from_far = after(from_far, near(from_far))
    for_y = low(product(2) + from_far.astype(f32))
    from_y = swap_y(for_y)
    return (product(0) + from_core.astype(f32), from_y, for_y)


def scatter_all(product, first_sent, ready, started, turned):
    far_y = swap_core(low(product(3)))
    far_own = low(product(1))
    far_y, far_own = after((far_y, swap_core(far_own)), first_sent(far_own))
    for_y = low(product(2) + far_y.astype(f32))
    own = low(product(0) + far_own.astype(f32))
    for_y, own = after((for_y, own), ready)
    half = own.shape[0] // 2
    quarter = half // 2
    width = own.shape[1]
    y_first = swap_y(jnp.concatenate([for_y[quarter:half], for_y[half + quarter :]], axis=0))
    x_first = swap_x(
        jnp.concatenate([own[half : half + quarter], for_y[half : half + quarter]], axis=1)
    )
    x_first, y_first = after((x_first, y_first), started((own, for_y)))
    top_in = low(for_y[:quarter].astype(f32) + x_first[:, width:].astype(f32))
    low_in = low(own[half + quarter :].astype(f32) + y_first[quarter:].astype(f32))
    top_y, low_x = after((swap_y(top_in), swap_x(low_in)), turned((top_in, low_in)))
    top = own[:quarter].astype(f32) + x_first[:, :width].astype(f32) + top_y.astype(f32)
    bottom = own[quarter:half].astype(f32) + y_first[:quarter].astype(f32) + low_x.astype(f32)
    return jnp.concatenate([top, bottom], axis=0)


def positions_of(segment):
    slot_ids = jnp.arange(5, dtype=jnp.int32)
    before = jnp.sum((segment[None, :] < slot_ids[:, None]).astype(jnp.int32), axis=1)
    starts = jnp.sum(jnp.where(segment[:, None] == slot_ids[None, :], before[None, :], 0), axis=1)
    return jnp.arange(segment.shape[0], dtype=jnp.int32) - starts


def rope_tables(positions, head_size):
    half_size = head_size // 2
    frequency = rope_base ** (-jnp.arange(half_size, dtype=f32) * 2.0 / head_size)
    angles = positions.astype(f32)[:, None] * frequency[None, :]
    cosine, sine = jnp.cos(angles), jnp.sin(angles)
    return (
        jnp.concatenate([cosine, cosine], axis=1),
        jnp.concatenate([-sine, sine], axis=1),
    )


def turn(vectors):
    return pltpu.roll(vectors, vectors.shape[-1] // 2, axis=1)


def inverse_norm(vectors):
    return lax.rsqrt(jnp.mean(vectors * vectors, axis=-1, keepdims=True) + norm_eps)


def allowed_keys(seg_col, seg_row, start, size, extent):
    row = lax.broadcasted_iota(jnp.int32, (size, extent), 0) + start
    col = lax.broadcasted_iota(jnp.int32, (size, extent), 1)
    return (seg_col[start : start + size, :] == seg_row[:, :extent]) & (col <= row)


def attend_kernel(
    side, own, from_y, rstd, cos, sin, seg_col, seg_row, q_gain, k_gain,
    proj, q_out, k_out, v_out, lse, att,
):
    rows = own.shape[0]
    size = cos.shape[1]
    heads = q_out.shape[1] // size
    block = rows // 4
    scale = size**-0.5
    k_at = heads * size
    v_at = k_at + size

    def ready(i, carry):
        at = pl.ds(pl.multiple_of(i * block, block), block)
        raw = (own[at, :] + from_y[at, :].astype(f32)) * rstd[at, :]
        proj[at, :] = raw

        def rope(part, gain):
            n = part * inverse_norm(part) * gain[...]
            return (n * cos[at, :] + turn(n) * sin[at, :]).astype(bf16)

        for h in range(heads):
            q_out[at, h * size : (h + 1) * size] = rope(raw[:, h * size : (h + 1) * size], q_gain)
        k_out[at, :] = rope(raw[:, k_at:v_at], k_gain)
        v_out[at, :] = raw[:, v_at:].astype(bf16)
        return carry

    lax.fori_loop(0, 4, ready, 0)
    for i in range(4):
        start = i * block
        extent = start + block
        allowed = allowed_keys(seg_col, seg_row, start, block, extent)
        to = pl.ds(pl.multiple_of(lax.rem(start + side[0] * (rows // 2), rows), block), block)
        for h in range(heads):
            of_head = slice(h * size, (h + 1) * size)
            scores = contract_cols(q_out[start:extent, of_head], k_out[:extent, :]) * scale
            scores = jnp.where(allowed, scores, neg_big)
            top = jnp.max(scores, axis=-1, keepdims=True)
            expd = jnp.exp(scores - top)
            total = jnp.sum(expd, axis=-1, keepdims=True)
            weights = (expd * (1.0 / total)).astype(bf16)
            att[to, of_head] = dot(weights, v_out[:extent, :]).astype(bf16)
            lse[start:extent, h : h + 1] = top + jnp.log(total)


def attend_back_kernel(
    side, own, from_y, proj, q_in, k_in, v_in, lse, cos, sin, seg_col, seg_row, q_gain, k_gain,
    grads, q_gain_part, k_gain_part, inner, k_acc, v_acc,
):
    rows = own.shape[0]
    size = cos.shape[1]
    heads = q_in.shape[1] // size
    block = rows // 4
    scale = size**-0.5
    k_at = heads * size
    v_at = k_at + size

    def unrope(grad, part, gain, start):
        rows_at = slice(start, start + block)
        m = grad * cos[rows_at, :] - turn(grad) * sin[rows_at, :]
        r = inverse_norm(part)
        hat = part * r
        mg = m * gain[...]
        back = (r * (mg - hat * jnp.mean(mg * hat, axis=-1, keepdims=True))).astype(bf16)
        gain_part = jnp.sum(m * hat, axis=0, keepdims=True)
        return (back, gain_part, jnp.sum(back.astype(f32) * part, axis=-1, keepdims=True))

    k_acc[...] = jnp.zeros_like(k_acc)
    v_acc[...] = jnp.zeros_like(v_acc)
    q_total = jnp.zeros(q_gain_part.shape, f32)
    for i in range(4):
        start = i * block
        extent = start + block
        allowed = allowed_keys(seg_col, seg_row, start, block, extent)
        at = pl.ds(pl.multiple_of(lax.rem(start + side[0] * (rows // 2), rows), block), block)
        inner_sum = jnp.zeros((block, 1), f32)
        for h in range(heads):
            of_head = slice(h * size, (h + 1) * size)
            query = q_in[start:extent, of_head]
            grad = (own[at, of_head] + from_y[at, of_head].astype(f32)).astype(bf16)
            scores = contract_cols(query, k_in[:extent, :]) * scale
            scores = jnp.where(allowed, scores, neg_big)
            probs = jnp.exp(scores - lse[start:extent, h : h + 1])
            prob_grad = contract_cols(grad, v_in[:extent, :])
            delta = jnp.sum(probs * prob_grad, axis=-1, keepdims=True)
            score_grad = (probs * (prob_grad - delta)).astype(bf16)
            query_grad = dot(score_grad, k_in[:extent, :]) * scale
            k_acc[:extent, :] += contract_rows(score_grad, query) * scale
            v_acc[:extent, :] += contract_rows(probs.astype(bf16), grad)
            back, gain_part, part_inner = unrope(
                query_grad, proj[start:extent, of_head], q_gain, start
            )
            grads[start:extent, of_head] = back
            q_total = q_total + gain_part
            inner_sum = inner_sum + part_inner
        inner[start:extent, :] = inner_sum
    q_gain_part[...] = q_total
    k_total = jnp.zeros(k_gain_part.shape, f32)
    for i in range(4):
        start = i * block
        extent = start + block
        back, gain_part, part_inner = unrope(
            k_acc[start:extent, :], proj[start:extent, k_at:v_at], k_gain, start
        )
        grads[start:extent, k_at:v_at] = back
        k_total = k_total + gain_part
        v_back = v_acc[start:extent, :].astype(bf16)
        grads[start:extent, v_at:] = v_back
        inner[start:extent, :] += part_inner + jnp.sum(
            v_back.astype(f32) * proj[start:extent, v_at:], axis=-1, keepdims=True
        )
    k_gain_part[...] = k_total


vmem = pl.BlockSpec(memory_space=pltpu.VMEM)
smem = pl.BlockSpec(memory_space=pltpu.SMEM)
big_vmem = pltpu.CompilerParams(vmem_limit_bytes=50 * 2**20)


def whole_kernel(body, outs, flops, scratch=()):
    def call(*operands):
        nbytes = sum(o.size * o.dtype.itemsize for o in (*operands, *outs))
        return pl.pallas_call(
            body,
            out_shape=outs,
            in_specs=[smem] + [vmem] * (len(operands) - 1),
            out_specs=[vmem] * len(outs),
            scratch_shapes=scratch,
            compiler_params=big_vmem,
            cost_estimate=pl.CostEstimate(flops=flops, bytes_accessed=nbytes, transcendentals=0),
        )(*operands)

    return call


def units_kernel(*refs):
    ins, weights, cots, downs = refs[:4], refs[4:8], refs[8:12], refs[12:16]
    rstd_ref = refs[16]
    hidden, pair, scaled, inner = refs[-4:]
    size = hidden.shape[1]
    rstd = rstd_ref[...]
    both = dot(ins[0][...], weights[0][...])
    grad = contract_cols(cots[0][...], downs[0][...])
    for k in range(1, 4):
        both = both + dot(ins[k][...], weights[k][...])
        grad = grad + contract_cols(cots[k][...], downs[k][...])
    both = both * rstd
    gate, up = both[:, :size], both[:, size:]
    sig = jax.nn.sigmoid(gate)
    silu = gate * sig
    hidden[...] = low(silu * up)
    gate_grad = low(grad * up * sig * (1.0 + gate * (1.0 - sig)))
    up_grad = low(grad * silu)
    pair[:, :size] = gate_grad
    pair[:, size:] = up_grad
    gate_grad, up_grad = gate_grad.astype(f32), up_grad.astype(f32)
    scaled[:, :size] = low(gate_grad * rstd)
    scaled[:, size:] = low(up_grad * rstd)
    part = jnp.sum(gate_grad * gate + up_grad * up, axis=-1, keepdims=True)

    @pl.when(pl.program_id(0) == 0)
    def _():
        inner[...] = part

    @pl.when(pl.program_id(0) > 0)
    def _():
        inner[...] += part


def units_of_half(ins, weights, cots, downs, rstd, which, earlier):
    half, depth = ins[0].shape
    units = downs[0].shape[0]
    block = min(256, units)
    outs = [
        jax.ShapeDtypeStruct((2 * half, units), bf16),
        jax.ShapeDtypeStruct((2 * half, 2 * units), bf16),
        jax.ShapeDtypeStruct((2 * half, 2 * units), bf16),
        jax.ShapeDtypeStruct((2 * half, 1), f32),
    ]
    earlier = list(earlier or [])
    here = pl.BlockSpec((half, depth), lambda j: (0, 0))
    of_all = pl.BlockSpec((half, depth), lambda j: (which, 0))
    by_cols = [pl.BlockSpec((depth, 2 * block), lambda j: (0, j))] * 2 + [
        pl.BlockSpec((None, depth, 2 * block), lambda j, k=k: (k, 0, j)) for k in (0, 1)
    ]
    by_rows = [pl.BlockSpec((block, depth), lambda j: (j, 0))] * 2 + [
        pl.BlockSpec((None, block, depth), lambda j, k=k: (k, j, 0)) for k in (0, 1)
    ]
    column = pl.BlockSpec((half, 1), lambda j: (which, 0))
    return pl.pallas_call(
        units_kernel,
        grid=(units // block,),
        out_shape=outs,
        in_specs=[here] * 4
        + by_cols
        + [of_all, of_all, here, here]
        + by_rows
        + [column]
        + [pl.BlockSpec(memory_space=pl.ANY)] * len(earlier),
        out_specs=[
            pl.BlockSpec((half, block), lambda j: (which, j)),
            pl.BlockSpec((half, 2 * block), lambda j: (which, j)),
            pl.BlockSpec((half, 2 * block), lambda j: (which, j)),
            column,
        ],
        input_output_aliases={17 + k: k for k in range(len(earlier))},
        compiler_params=big_vmem,
        cost_estimate=pl.CostEstimate(
            flops=2 * half * 4 * depth * 3 * units,
            bytes_accessed=2 * (4 * depth * 3 * units + half * (8 * depth + 5 * units)),
            transcendentals=half * units,
        ),
    )(*ins, weights[0], weights[1], weights[2], weights[2], *cots,
      downs[0], downs[1], downs[2], downs[2], rstd, *earlier)


def on_device(
    tokens,
    cotangent,
    segment_ids,
    attn_gain,
    q_gain,
    k_gain,
    mlp_gain,
    w_query,
    w_key,
    w_value,
    w_out,
    w_gate,
    w_up,
    w_down,
):
    assert lax.axis_size("tc") == 4 and lax.axis_size("tr") == 2
    col = lax.axis_index("tc")
    side = lax.axis_index("tr")
    rows, width = tokens.shape
    half = rows // 2
    full_width = width * 4
    head_size = q_gain.shape[0]
    q_width = w_query.shape[1] // 4
    k_width = w_key.shape[1] // 4
    units = w_gate.shape[1] // 4
    around = [col, col ^ 1, col ^ 2, col ^ 3]

    def cols_of(array, which, size):
        return lax.dynamic_slice_in_dim(array, around[which] * size, size, 1)

    def rows_of(array, which, size):
        return lax.dynamic_slice_in_dim(array, around[which] * size, size, 0)

    def flip(array):
        return jnp.concatenate(
            [
                lax.dynamic_slice_in_dim(array, side * half, half, 0),
                lax.dynamic_slice_in_dim(array, (1 - side) * half, half, 0),
            ],
            axis=0,
        )

    shares = lax.axis_size("dp")
    place = lax.axis_index("dp")

    def share_of(block):
        size = block.shape[0] // shares
        return lax.dynamic_slice_in_dim(block, place * size, size, 0)

    def gather_shares(from_y, from_diag):
        return lax.all_gather(jnp.stack([from_y, from_diag]), "dp", axis=1, tiled=True)

    ffn_step = min(256, units)

    def ffn_columns(which, rows_at):
        gate, up = (rows_at(cols_of(w, which, units)) for w in (w_gate, w_up))
        blocks = [w[:, k : k + ffn_step] for k in range(0, units, ffn_step) for w in (gate, up)]
        return jnp.concatenate(blocks, axis=1)

    down_y, down_diag = (share_of(rows_of(w_down, k, units)) for k in (2, 3))
    down_y, down_diag = swap_y(down_y), swap_diag(down_diag)

    qkv_weights = [
        jnp.concatenate(
            [cols_of(w_query, k, q_width), cols_of(w_key, k, k_width), cols_of(w_value, k, k_width)],
            axis=1,
        )
        for k in range(4)
    ]
    inputs = tokens.astype(f32)
    scaled_in = low(inputs * attn_gain[None, :])
    raw_own, raw_y, for_y = scatter_width(lambda k: dot(scaled_in, qkv_weights[k]))
    down_gathered = gather_shares(*after((down_y, down_diag), for_y))
    w_gate, w_up, w_down, w_out, segment_ids, cotangent, inputs = after(
        (w_gate, w_up, w_down, w_out, segment_ids, cotangent, inputs), for_y
    )
    share_y, share_diag = after((ffn_columns(2, share_of), ffn_columns(3, share_of)), raw_own)
    share_y, share_diag = swap_y(share_y), swap_diag(share_diag)
    square_sum = width_total(jnp.sum(inputs * inputs, axis=1))
    attn_rstd = lax.rsqrt(square_sum / full_width + norm_eps)
    attn_hat = inputs * attn_rstd[:, None]
    normed = low(attn_hat * attn_gain[None, :])

    cos_table, sin_table = rope_tables(positions_of(segment_ids), head_size)
    side_word = side.astype(jnp.int32).reshape(1)
    tables = (
        cos_table,
        sin_table,
        segment_ids.reshape(rows, 1),
        segment_ids.reshape(1, rows),
        q_gain.reshape(1, head_size),
        k_gain.reshape(1, head_size),
    )
    heads = q_width // head_size
    pairs_of_rows = rows * rows * heads * head_size
    projected, q_low, k_low, v_low, log_totals, att_rel = whole_kernel(
        attend_kernel,
        [
            jax.ShapeDtypeStruct((rows, q_width + 2 * k_width), f32),
            jax.ShapeDtypeStruct((rows, q_width), bf16),
            jax.ShapeDtypeStruct((rows, k_width), bf16),
            jax.ShapeDtypeStruct((rows, k_width), bf16),
            jax.ShapeDtypeStruct((rows, heads), f32),
            jax.ShapeDtypeStruct((rows, q_width), bf16),
        ],
        flops=4 * pairs_of_rows,
    )(side_word, raw_own, raw_y, attn_rstd.reshape(rows, 1), *tables)
    ffn_gathered = gather_shares(*after((share_y, share_diag), att_rel))
    att_y = swap_y(att_rel)
    atts = [att_rel, swap_core(att_rel), att_y, swap_core(att_y)]
    outs = [rows_of(w_out, k, q_width) for k in range(4)]

    def out_rows(at):
        return (dot(atts[0][at], outs[0]) + dot(atts[1][at], outs[1])) + (
            dot(atts[2][at], outs[2]) + dot(atts[3][at], outs[3])
        )

    from_x = swap_x(low(out_rows(slice(half, rows))))
    tokens_half = lax.dynamic_slice_in_dim(tokens, side * half, half, 0).astype(f32)
    residual = tokens_half + out_rows(slice(0, half)) + from_x.astype(f32)

    mlp_square = width_total(jnp.sum(residual * residual, axis=1))
    mlp_own = low(residual * mlp_gain[None, :])
    mlp_rstd = lax.rsqrt(mlp_square / full_width + norm_eps)
    rstd_rel = jnp.concatenate([mlp_rstd, swap_x(mlp_rstd)]).reshape(rows, 1)
    quarter = half // 2
    mlp_x = swap_x(mlp_own)
    mlp_y = swap_y(mlp_own)
    mlp_xy = jnp.concatenate([swap_y(mlp_x[:quarter]), swap_x(mlp_y[quarter:])], axis=0)
    ins_own = [mlp_own, swap_core(mlp_own), mlp_y, swap_core(mlp_y)]
    ins_other = [mlp_x, swap_core(mlp_x), mlp_xy, swap_core(mlp_xy)]
    cot_rel = flip(cotangent)
    cot_core = swap_core(cot_rel)
    cot_y = swap_y(after(cot_rel[:half], att_rel))
    cot_x = swap_x(after(cot_y, mlp_xy))
    cots_own = [cot_rel, cot_core, cot_y, swap_core(cot_y)]
    cots_other = [cot_rel, cot_core, cot_x, swap_core(cot_x)]
    whole = lambda block: block
    ffns = (ffn_columns(0, whole), swap_core(ffn_columns(1, whole)), ffn_gathered)
    downs = (rows_of(w_down, 0, units), swap_core(rows_of(w_down, 1, units)), down_gathered)
    first = units_of_half(ins_own, ffns, cots_own, downs, rstd_rel, 0, None)
    hidden, pair, pair_scaled, inner = units_of_half(
        ins_other, ffns, cots_other, downs, rstd_rel, 1, first
    )

    line = LineSums()
    mlp_in, mlp_core = (jnp.concatenate([ins_own[k], ins_other[k]], axis=0) for k in (0, 1))
    line.add(("ffn", 0), low(contract_rows(mlp_in, pair_scaled)), 1)
    line.send()
    pair = after(pair, line.send(), line.waiting())
    inner_total = width_total(inner[:half, 0]) + swap_x(width_total(inner[half:, 0]))

    kept = {}

    def first_sent(marker):
        block = low(contract_rows(mlp_core, after(pair_scaled, marker)))
        line.add(("ffn", 1), swap_core(block), 1)
        return block

    def started(marker):
        marker = line.send(marker)
        down_core = low(contract_rows(after(hidden, marker), cot_core))
        down_own = low(contract_rows(after(hidden, marker), cot_rel))
        line.add("near", jnp.concatenate([down_own, swap_core(down_core)], axis=0), 0)
        return (marker, down_own)

    def turned(marker):
        kept["hidden"] = lax.all_gather(after(hidden, marker), "tc", axis=1, tiled=True)
        return line.send(marker)

    ffn_blocks = [ffns[0], ffns[1], ffns[2][0], ffns[2][1]]
    mlp_in_grad = scatter_all(
        lambda k: contract_cols(pair, ffn_blocks[k]), first_sent, inner_total, started, turned
    )
    hiddens = kept["hidden"]
    pairs = lax.all_gather(after(pair_scaled, mlp_in_grad), "tc")
    mlp_hat = residual * mlp_rstd[:, None]
    mlp_gain_part = jnp.sum(mlp_in_grad * mlp_hat, axis=0)
    residual_grad = cot_rel[:half].astype(f32) + mlp_rstd[:, None] * (
        mlp_in_grad * mlp_gain[None, :] - mlp_hat * (inner_total / full_width)[:, None]
    )
    residual_low = low(residual_grad)
    res_x = after(swap_x(residual_low), line.send(residual_low))
    res_rel = jnp.concatenate([residual_low, res_x], axis=0)
    head_own, head_y, head_sent = scatter_width(
        lambda k: contract_cols(res_rel, outs[k]), line.send
    )
    marker = line.send(head_sent)
    out_grads = [low(contract_rows(after(part, marker), res_rel)) for part in atts]
    line.add("out", jnp.concatenate(out_grads, axis=0), 0)
    head_own, head_y = after((head_own, head_y), line.send(out_grads), line.waiting())

    proj_low, q_gain_part, k_gain_part, inner_attn = whole_kernel(
        attend_back_kernel,
        [
            jax.ShapeDtypeStruct((rows, q_width + 2 * k_width), bf16),
            jax.ShapeDtypeStruct((1, head_size), f32),
            jax.ShapeDtypeStruct((1, head_size), f32),
            jax.ShapeDtypeStruct((rows, 1), f32),
        ],
        flops=10 * pairs_of_rows,
        scratch=[pltpu.VMEM((rows, k_width), f32), pltpu.VMEM((rows, k_width), f32)],
    )(side_word, head_own, head_y, projected, q_low, k_low, v_low, log_totals, *tables)
    proj_y = swap_y(proj_low)
    proj_core = swap_core(proj_low)
    marker = line.send(proj_low)
    inner_attn = width_total(after(inner_attn, marker)[:, 0])
    inner_attn = inner_attn + swap_x(inner_attn)
    marker = line.send(inner_attn)
    proj_y, proj_core = after((proj_y, proj_core), marker)
    projs = [proj_low, proj_core, proj_y, swap_core(proj_y)]
    normed_part = low(
        (contract_cols(projs[0], qkv_weights[0]) + contract_cols(projs[1], qkv_weights[1]))
        + (contract_cols(projs[2], qkv_weights[2]) + contract_cols(projs[3], qkv_weights[3]))
    )
    normed_x = after(swap_x(normed_part), line.send(normed_part))
    normed_grad = normed_part.astype(f32) + normed_x.astype(f32)
    attn_gain_part = jnp.sum(normed_grad * attn_hat, axis=0)
    token_grad = low(
        flip(res_rel).astype(f32)
        + attn_rstd[:, None]
        * (normed_grad * attn_gain[None, :] - attn_hat * (inner_attn / full_width)[:, None])
    )

    far_down = [
        low(contract_rows(after(cols_of(hiddens, k, units), normed_part), cot_rel)) for k in (2, 3)
    ]
    line.add("far", jnp.concatenate(far_down, axis=0), 0)
    mlp_away = low(dot(after(hiddens[half:], normed_grad), w_down))
    mlp_x_out = after(swap_x(mlp_away), line.send(mlp_away))
    mixed_half = low(residual + dot(hiddens[:half], w_down) + mlp_x_out.astype(f32))
    mixed_x = swap_x(mixed_half)
    marker = line.send(mixed_half)
    mixed = flip(jnp.concatenate([mixed_half, mixed_x], axis=0))

    for k, part in enumerate(projs):
        line.add(("qkv", k), low(contract_rows(after(normed, marker), part)), 1)
    while line.queue:
        marker = line.send()
    for k in (2, 3):
        block = after(lax.dynamic_index_in_dim(pairs, around[k], 0, keepdims=False), marker)
        line.add(("ffn", k), low(contract_rows(mlp_in, block)), 1)
        while line.queue:
            marker = line.send()
    sums_of = line.finish()
    qkv_grads = [jnp.concatenate(sums_of(("qkv", k)), axis=1) for k in range(4)]
    down_grads = jnp.concatenate(sums_of("near") + sums_of("far"), axis=0)

    shared = width_total(jnp.concatenate([q_gain_part[0], k_gain_part[0]]))
    shared = jnp.concatenate([shared, mlp_gain_part])
    shared = shared + swap_x(shared)
    gains = line_total(jnp.concatenate([shared, attn_gain_part]))
    q_gain_grad = gains[:head_size]
    k_gain_grad = gains[head_size : 2 * head_size]
    mlp_gain_grad = gains[2 * head_size : 2 * head_size + width]
    attn_gain_grad = gains[2 * head_size + width :]

    def place_cols(shape, pieces):
        whole = jnp.zeros(shape, f32)
        for which, piece in enumerate(pieces):
            whole = lax.dynamic_update_slice_in_dim(
                whole, piece.astype(f32), around[which] * piece.shape[1], 1
            )
        return whole

    def place_rows(shape, pieces):
        whole = jnp.zeros(shape, f32)
        for which, piece in enumerate(pieces):
            whole = lax.dynamic_update_slice_in_dim(
                whole, piece.astype(f32), around[which] * piece.shape[0], 0
            )
        return whole

    w_query_grad = place_cols(w_query.shape, [g[:, :q_width] for g in qkv_grads])
    w_key_grad = place_cols(w_key.shape, [g[:, q_width : q_width + k_width] for g in qkv_grads])
    w_value_grad = place_cols(w_value.shape, [g[:, q_width + k_width :] for g in qkv_grads])
    out_sum = jnp.concatenate(sums_of("out"), axis=0)
    w_out_grad = place_rows(
        w_out.shape, [out_sum[k * q_width : (k + 1) * q_width] for k in range(4)]
    )
    w_gate_grad = jnp.zeros(w_gate.shape, f32)
    w_up_grad = jnp.zeros(w_up.shape, f32)
    for which in range(4):
        parts = jnp.concatenate(sums_of(("ffn", which)), axis=1)
        for start in range(0, units, ffn_step):
            to = (0, around[which] * units + start)
            gate = parts[:, 2 * start : 2 * start + ffn_step].astype(f32)
            up = parts[:, 2 * start + ffn_step : 2 * start + 2 * ffn_step].astype(f32)
            w_gate_grad = lax.dynamic_update_slice(w_gate_grad, gate, to)
            w_up_grad = lax.dynamic_update_slice(w_up_grad, up, to)
    w_down_grad = place_rows(
        w_down.shape, [down_grads[k * units : (k + 1) * units] for k in range(4)]
    )
    return (
        mixed,
        token_grad,
        attn_gain_grad,
        q_gain_grad,
        k_gain_grad,
        mlp_gain_grad,
        w_query_grad,
        w_key_grad,
        w_value_grad,
        w_out_grad,
        w_gate_grad,
        w_up_grad,
        w_down_grad,
    )


def solution(mesh):
    in_specs = (
        P("dp", "tc"),
        P("dp", "tc"),
        P("dp"),
        P("tc"),
        P(),
        P(),
        P("tc"),
        P("tc", "tr"),
        P("tc", "tr"),
        P("tc", "tr"),
        P("tr", "tc"),
        P("tc", "tr"),
        P("tc", "tr"),
        P("tr", "tc"),
    )
    out_specs = (
        P("dp", "tc"),
        P("dp", "tc"),
        P("tc"),
        P(),
        P(),
        P("tc"),
        P("tc", "tr"),
        P("tc", "tr"),
        P("tc", "tr"),
        P("tr", "tc"),
        P("tc", "tr"),
        P("tc", "tr"),
        P("tr", "tc"),
    )
    return jax.shard_map(
        on_device, mesh=mesh, in_specs=in_specs, out_specs=out_specs, check_vma=False
    )
```

```python
import jax
import jax.numpy as jnp
from jax import lax
from jax.experimental import pallas as pl
from jax.experimental.pallas import tpu as pltpu
from jax.sharding import PartitionSpec as P

norm_eps = 1e-06
rope_base = 1000000.0
neg_big = -1e30
f32 = jnp.float32
bf16 = jnp.bfloat16


def dot(left_side, right_side):
    return jnp.dot(left_side, right_side, preferred_element_type=f32)


def contract_rows(left_side, right_side):
    return lax.dot_general(
        left_side, right_side, (((0,), (0,)), ((), ())), preferred_element_type=f32
    )


def contract_cols(left_side, right_side):
    return lax.dot_general(
        left_side, right_side, (((1,), (1,)), ((), ())), preferred_element_type=f32
    )


def swap_core(block):
    return lax.ppermute(block, "tc", [(i, i ^ 1) for i in range(4)])


def swap_y(block):
    return lax.ppermute(block, "tc", [(i, i ^ 2) for i in range(4)])


def swap_diag(block):
    return lax.ppermute(block, "tc", [(i, i ^ 3) for i in range(4)])


def swap_x(block):
    return lax.ppermute(block, "tr", [(0, 1), (1, 0)])


def width_total(rows):
    rows = rows + swap_core(rows)
    return rows + swap_y(rows)


def line_total(piece):
    size = lax.axis_size("dp")
    place = lax.axis_index("dp")
    half = size // 2
    for step in range(half):
        got = lax.ppermute(piece, "dp", [(step, step + 1), (size - 1 - step, size - 2 - step)])
        piece = piece + got
    for step in reversed(range(half - 1)):
        got = lax.ppermute(piece, "dp", [(step + 1, step), (size - 2 - step, size - 1 - step)])
        piece = jnp.where((place == step) | (place == size - 1 - step), got, piece)
    return piece


class LineSums:
    def __init__(self, size):
        self.size = size
        self.short = lax.axis_size("dp") == 4
        place = lax.axis_index("dp")
        self.middle = (place == 1) | (place == 2)
        self.stream, self.parts, self.pieces = [], [], []
        self.outer, self.total = [], []

    def add(self, name, columns):
        self.stream.append((name, columns))

    def waiting(self):
        return [columns for _, columns in self.stream]

    def _next(self):
        wanted, parts, blocks = self.size, [], []
        while wanted and self.stream:
            name, columns = self.stream.pop(0)
            taken = min(wanted, columns.shape[1])
            parts.append((name, taken))
            blocks.append(columns[:, :taken])
            if taken < columns.shape[1]:
                self.stream.insert(0, (name, columns[:, taken:]))
            wanted -= taken
        assert wanted == 0
        self.parts.append(parts)
        self.pieces.append(blocks[0] if len(blocks) == 1 else jnp.concatenate(blocks, axis=1))

    def _consume(self, which, marker):
        got, piece = after((self.outer[which], self.pieces[which]), marker)
        inward = low(piece.astype(f32) + got.astype(f32))
        across = lax.ppermute(inward, "dp", [(1, 2), (2, 1)])
        self.total.append(low(inward.astype(f32) + across.astype(f32)))
        return inward

    def _swap_outer(self, piece):
        self.outer.append(lax.ppermute(piece, "dp", [(0, 1), (1, 0), (2, 3), (3, 2)]))

    def send(self, marker=()):
        which = len(self.pieces)
        self._next()
        if not self.short:
            return self.pieces[which]
        if which >= 2:
            marker = self._consume(which - 2, marker)
        out = after(self.pieces[which], marker)
        if which >= 3:
            out = jnp.where(self.middle, self.total[which - 3], out)
        self._swap_outer(out)
        return marker

    def finish(self):
        count = len(self.pieces)
        if self.short:
            for which in (count - 2, count - 1):
                self._consume(which, ())
            for which in range(count - 3, count):
                self._swap_outer(self.total[which])
            sums = [jnp.where(self.middle, self.total[k], self.outer[k + 3]) for k in range(count)]
        else:
            sums = [lax.psum(piece, "dp") for piece in self.pieces]
        named = {}
        for parts, piece in zip(self.parts, sums):
            start = 0
            for name, taken in parts:
                named.setdefault(name, []).append(piece[:, start : start + taken])
                start += taken
        return lambda name: jnp.concatenate(named[name], axis=1)


def after(value, *others):
    return lax.optimization_barrier((value, others))[0]


def low(array):
    return array.astype(bf16)


def scatter_width(product, near=lambda ready: ready):
    from_far = swap_core(low(product(3)))
    from_core = swap_core(low(product(1)))
    from_far = after(from_far, near(from_far))
    for_y = low(product(2) + from_far.astype(f32))
    from_y = swap_y(for_y)
    return (product(0) + from_core.astype(f32), from_y, for_y)


def scatter_all(product, first_sent, ready, started, turned):
    far_y = swap_core(low(product(3)))
    far_own = low(product(1))
    far_y, far_own = after((far_y, swap_core(far_own)), first_sent(far_own))
    for_y = low(product(2) + far_y.astype(f32))
    own = low(product(0) + far_own.astype(f32))
    for_y, own = after((for_y, own), ready)
    half = own.shape[0] // 2
    quarter = half // 2
    width = own.shape[1]
    y_first = swap_y(jnp.concatenate([for_y[quarter:half], for_y[half + quarter :]], axis=0))
    x_first = swap_x(
        jnp.concatenate([own[half : half + quarter], for_y[half : half + quarter]], axis=1)
    )
    x_first, y_first = after((x_first, y_first), started((own, for_y)))
    top_in = low(for_y[:quarter].astype(f32) + x_first[:, width:].astype(f32))
    low_in = low(own[half + quarter :].astype(f32) + y_first[quarter:].astype(f32))
    top_y, low_x = after((swap_y(top_in), swap_x(low_in)), turned((top_in, low_in)))
    top = own[:quarter].astype(f32) + x_first[:, :width].astype(f32) + top_y.astype(f32)
    bottom = own[quarter:half].astype(f32) + y_first[:quarter].astype(f32) + low_x.astype(f32)
    return jnp.concatenate([top, bottom], axis=0)


def positions_of(segment):
    slot_ids = jnp.arange(5, dtype=jnp.int32)
    before = jnp.sum((segment[None, :] < slot_ids[:, None]).astype(jnp.int32), axis=1)
    starts = jnp.sum(jnp.where(segment[:, None] == slot_ids[None, :], before[None, :], 0), axis=1)
    return jnp.arange(segment.shape[0], dtype=jnp.int32) - starts


def rope_tables(positions, head_size):
    half_size = head_size // 2
    frequency = rope_base ** (-jnp.arange(half_size, dtype=f32) * 2.0 / head_size)
    angles = positions.astype(f32)[:, None] * frequency[None, :]
    cosine, sine = jnp.cos(angles), jnp.sin(angles)
    return (
        jnp.concatenate([cosine, cosine], axis=1),
        jnp.concatenate([-sine, sine], axis=1),
    )


def turn(vectors):
    return pltpu.roll(vectors, vectors.shape[-1] // 2, axis=1)


def inverse_norm(vectors):
    return lax.rsqrt(jnp.mean(vectors * vectors, axis=-1, keepdims=True) + norm_eps)


def allowed_keys(seg_col, seg_row, start, size, extent):
    row = lax.broadcasted_iota(jnp.int32, (size, extent), 0) + start
    col = lax.broadcasted_iota(jnp.int32, (size, extent), 1)
    return (seg_col[start : start + size, :] == seg_row[:, :extent]) & (col <= row)


def attend_kernel(
    side, own, from_y, rstd, cos, sin, seg_col, seg_row, q_gain, k_gain,
    proj, q_out, k_out, v_out, lse, att,
):
    rows = own.shape[0]
    size = cos.shape[1]
    heads = q_out.shape[1] // size
    block = rows // 4
    scale = size**-0.5
    k_at = heads * size
    v_at = k_at + size

    def ready(i, carry):
        at = pl.ds(pl.multiple_of(i * block, block), block)
        raw = (own[at, :] + from_y[at, :].astype(f32)) * rstd[at, :]
        proj[at, :] = raw

        def rope(part, gain):
            n = part * inverse_norm(part) * gain[...]
            return (n * cos[at, :] + turn(n) * sin[at, :]).astype(bf16)

        for h in range(heads):
            q_out[at, h * size : (h + 1) * size] = rope(raw[:, h * size : (h + 1) * size], q_gain)
        k_out[at, :] = rope(raw[:, k_at:v_at], k_gain)
        v_out[at, :] = raw[:, v_at:].astype(bf16)
        return carry

    lax.fori_loop(0, 4, ready, 0)
    for i in range(4):
        start = i * block
        extent = start + block
        allowed = allowed_keys(seg_col, seg_row, start, block, extent)
        to = pl.ds(pl.multiple_of(lax.rem(start + side[0] * (rows // 2), rows), block), block)
        for h in range(heads):
            of_head = slice(h * size, (h + 1) * size)
            scores = contract_cols(q_out[start:extent, of_head], k_out[:extent, :]) * scale
            scores = jnp.where(allowed, scores, neg_big)
            top = jnp.max(scores, axis=-1, keepdims=True)
            expd = jnp.exp(scores - top)
            total = jnp.sum(expd, axis=-1, keepdims=True)
            weights = (expd * (1.0 / total)).astype(bf16)
            att[to, of_head] = dot(weights, v_out[:extent, :]).astype(bf16)
            lse[start:extent, h : h + 1] = top + jnp.log(total)


def attend_back_kernel(
    side, own, from_y, proj, q_in, k_in, v_in, lse, cos, sin, seg_col, seg_row, q_gain, k_gain,
    grads, q_gain_part, k_gain_part, inner, k_acc, v_acc,
):
    rows = own.shape[0]
    size = cos.shape[1]
    heads = q_in.shape[1] // size
    block = rows // 4
    scale = size**-0.5
    k_at = heads * size
    v_at = k_at + size

    def unrope(grad, part, gain, start):
        rows_at = slice(start, start + block)
        m = grad * cos[rows_at, :] - turn(grad) * sin[rows_at, :]
        r = inverse_norm(part)
        hat = part * r
        mg = m * gain[...]
        back = (r * (mg - hat * jnp.mean(mg * hat, axis=-1, keepdims=True))).astype(bf16)
        gain_part = jnp.sum(m * hat, axis=0, keepdims=True)
        return (back, gain_part, jnp.sum(back.astype(f32) * part, axis=-1, keepdims=True))

    k_acc[...] = jnp.zeros_like(k_acc)
    v_acc[...] = jnp.zeros_like(v_acc)
    q_total = jnp.zeros(q_gain_part.shape, f32)
    for i in range(4):
        start = i * block
        extent = start + block
        allowed = allowed_keys(seg_col, seg_row, start, block, extent)
        at = pl.ds(pl.multiple_of(lax.rem(start + side[0] * (rows // 2), rows), block), block)
        inner_sum = jnp.zeros((block, 1), f32)
        for h in range(heads):
            of_head = slice(h * size, (h + 1) * size)
            query = q_in[start:extent, of_head]
            grad = (own[at, of_head] + from_y[at, of_head].astype(f32)).astype(bf16)
            scores = contract_cols(query, k_in[:extent, :]) * scale
            scores = jnp.where(allowed, scores, neg_big)
            probs = jnp.exp(scores - lse[start:extent, h : h + 1])
            prob_grad = contract_cols(grad, v_in[:extent, :])
            delta = jnp.sum(probs * prob_grad, axis=-1, keepdims=True)
            score_grad = (probs * (prob_grad - delta)).astype(bf16)
            query_grad = dot(score_grad, k_in[:extent, :]) * scale
            k_acc[:extent, :] += contract_rows(score_grad, query) * scale
            v_acc[:extent, :] += contract_rows(probs.astype(bf16), grad)
            back, gain_part, part_inner = unrope(
                query_grad, proj[start:extent, of_head], q_gain, start
            )
            grads[start:extent, of_head] = back
            q_total = q_total + gain_part
            inner_sum = inner_sum + part_inner
        inner[start:extent, :] = inner_sum
    q_gain_part[...] = q_total
    k_total = jnp.zeros(k_gain_part.shape, f32)
    for i in range(4):
        start = i * block
        extent = start + block
        back, gain_part, part_inner = unrope(
            k_acc[start:extent, :], proj[start:extent, k_at:v_at], k_gain, start
        )
        grads[start:extent, k_at:v_at] = back
        k_total = k_total + gain_part
        v_back = v_acc[start:extent, :].astype(bf16)
        grads[start:extent, v_at:] = v_back
        inner[start:extent, :] += part_inner + jnp.sum(
            v_back.astype(f32) * proj[start:extent, v_at:], axis=-1, keepdims=True
        )
    k_gain_part[...] = k_total


vmem = pl.BlockSpec(memory_space=pltpu.VMEM)
smem = pl.BlockSpec(memory_space=pltpu.SMEM)
big_vmem = pltpu.CompilerParams(vmem_limit_bytes=50 * 2**20)


def whole_kernel(body, outs, flops, scratch=()):
    def call(*operands):
        nbytes = sum(o.size * o.dtype.itemsize for o in (*operands, *outs))
        return pl.pallas_call(
            body,
            out_shape=outs,
            in_specs=[smem] + [vmem] * (len(operands) - 1),
            out_specs=[vmem] * len(outs),
            scratch_shapes=scratch,
            compiler_params=big_vmem,
            cost_estimate=pl.CostEstimate(flops=flops, bytes_accessed=nbytes, transcendentals=0),
        )(*operands)

    return call


def units_kernel(*refs):
    ins, weights, cots, downs = refs[:4], refs[4:8], refs[8:12], refs[12:16]
    rstd_ref = refs[16]
    hidden, pair, scaled, inner = refs[-4:]
    size = hidden.shape[1]
    rstd = rstd_ref[...]
    both = dot(ins[0][...], weights[0][...])
    grad = contract_cols(cots[0][...], downs[0][...])
    for k in range(1, 4):
        both = both + dot(ins[k][...], weights[k][...])
        grad = grad + contract_cols(cots[k][...], downs[k][...])
    both = both * rstd
    gate, up = both[:, :size], both[:, size:]
    sig = jax.nn.sigmoid(gate)
    silu = gate * sig
    hidden[...] = low(silu * up)
    gate_grad = low(grad * up * sig * (1.0 + gate * (1.0 - sig)))
    up_grad = low(grad * silu)
    pair[:, :size] = gate_grad
    pair[:, size:] = up_grad
    gate_grad, up_grad = gate_grad.astype(f32), up_grad.astype(f32)
    scaled[:, :size] = low(gate_grad * rstd)
    scaled[:, size:] = low(up_grad * rstd)
    part = jnp.sum(gate_grad * gate + up_grad * up, axis=-1, keepdims=True)

    @pl.when(pl.program_id(0) == 0)
    def _():
        inner[...] = part

    @pl.when(pl.program_id(0) > 0)
    def _():
        inner[...] += part


def units_of_half(ins, weights, cots, downs, rstd, which, earlier):
    half, depth = ins[0].shape
    units = downs[0].shape[0]
    block = min(256, units)
    outs = [
        jax.ShapeDtypeStruct((2 * half, units), bf16),
        jax.ShapeDtypeStruct((2 * half, 2 * units), bf16),
        jax.ShapeDtypeStruct((2 * half, 2 * units), bf16),
        jax.ShapeDtypeStruct((2 * half, 1), f32),
    ]
    earlier = list(earlier or [])
    here = pl.BlockSpec((half, depth), lambda j: (0, 0))
    of_all = pl.BlockSpec((half, depth), lambda j: (which, 0))
    by_cols = [pl.BlockSpec((depth, 2 * block), lambda j: (0, j))] * 2 + [
        pl.BlockSpec((None, depth, 2 * block), lambda j, k=k: (k, 0, j)) for k in (0, 1)
    ]
    by_rows = [pl.BlockSpec((block, depth), lambda j: (j, 0))] * 2 + [
        pl.BlockSpec((None, block, depth), lambda j, k=k: (k, j, 0)) for k in (0, 1)
    ]
    column = pl.BlockSpec((half, 1), lambda j: (which, 0))
    return pl.pallas_call(
        units_kernel,
        grid=(units // block,),
        out_shape=outs,
        in_specs=[here] * 4
        + by_cols
        + [of_all, of_all, here, here]
        + by_rows
        + [pl.BlockSpec((half, 1), lambda j: (0, 0))]
        + [pl.BlockSpec(memory_space=pl.ANY)] * len(earlier),
        out_specs=[
            pl.BlockSpec((half, block), lambda j: (which, j)),
            pl.BlockSpec((half, 2 * block), lambda j: (which, j)),
            pl.BlockSpec((half, 2 * block), lambda j: (which, j)),
            column,
        ],
        input_output_aliases={17 + k: k for k in range(len(earlier))},
        compiler_params=big_vmem,
        cost_estimate=pl.CostEstimate(
            flops=2 * half * 4 * depth * 3 * units,
            bytes_accessed=2 * (4 * depth * 3 * units + half * (8 * depth + 5 * units)),
            transcendentals=half * units,
        ),
    )(*ins, weights[0], weights[1], weights[2], weights[2], *cots,
      downs[0], downs[1], downs[2], downs[2], rstd, *earlier)


def on_device(
    tokens,
    cotangent,
    segment_ids,
    attn_gain,
    q_gain,
    k_gain,
    mlp_gain,
    w_query,
    w_key,
    w_value,
    w_out,
    w_gate,
    w_up,
    w_down,
):
    assert lax.axis_size("tc") == 4 and lax.axis_size("tr") == 2
    col = lax.axis_index("tc")
    side = lax.axis_index("tr")
    rows, width = tokens.shape
    half = rows // 2
    full_width = width * 4
    head_size = q_gain.shape[0]
    q_width = w_query.shape[1] // 4
    k_width = w_key.shape[1] // 4
    units = w_gate.shape[1] // 4
    around = [col, col ^ 1, col ^ 2, col ^ 3]

    def cols_of(array, which, size):
        return lax.dynamic_slice_in_dim(array, around[which] * size, size, 1)

    def rows_of(array, which, size):
        return lax.dynamic_slice_in_dim(array, around[which] * size, size, 0)

    def flip(array):
        return jnp.concatenate(
            [
                lax.dynamic_slice_in_dim(array, side * half, half, 0),
                lax.dynamic_slice_in_dim(array, (1 - side) * half, half, 0),
            ],
            axis=0,
        )

    shares = lax.axis_size("dp")
    place = lax.axis_index("dp")

    def share_of(block):
        size = block.shape[0] // shares
        return lax.dynamic_slice_in_dim(block, place * size, size, 0)

    def gather_shares(from_y, from_diag):
        return lax.all_gather(jnp.stack([from_y, from_diag]), "dp", axis=1, tiled=True)

    ffn_step = min(256, units)

    def ffn_columns(which, rows_at):
        gate, up = (rows_at(cols_of(w, which, units)) for w in (w_gate, w_up))
        blocks = [w[:, k : k + ffn_step] for k in range(0, units, ffn_step) for w in (gate, up)]
        return jnp.concatenate(blocks, axis=1)

    down_y, down_diag = (share_of(rows_of(w_down, k, units)) for k in (2, 3))
    down_y, down_diag = swap_y(down_y), swap_diag(down_diag)

    qkv_weights = [
        jnp.concatenate(
            [cols_of(w_query, k, q_width), cols_of(w_key, k, k_width), cols_of(w_value, k, k_width)],
            axis=1,
        )
        for k in range(4)
    ]
    inputs = tokens.astype(f32)
    square_sum = width_total(jnp.sum(inputs * inputs, axis=1))
    scaled_in = low(inputs * attn_gain[None, :])
    raw_own, raw_y, for_y = scatter_width(lambda k: dot(scaled_in, qkv_weights[k]))
    down_gathered = gather_shares(*after((down_y, down_diag), for_y))
    w_gate, w_up, w_down, w_out, segment_ids, cotangent, inputs = after(
        (w_gate, w_up, w_down, w_out, segment_ids, cotangent, inputs), for_y
    )
    share_y, share_diag = after(
        (ffn_columns(2, share_of), ffn_columns(3, share_of)), raw_own, square_sum
    )
    share_y, share_diag = swap_y(share_y), swap_diag(share_diag)
    attn_rstd = lax.rsqrt(square_sum / full_width + norm_eps)
    attn_hat = inputs * attn_rstd[:, None]
    normed = low(attn_hat * attn_gain[None, :])

    cos_table, sin_table = rope_tables(positions_of(segment_ids), head_size)
    side_word = side.astype(jnp.int32).reshape(1)
    tables = (
        cos_table,
        sin_table,
        segment_ids.reshape(rows, 1),
        segment_ids.reshape(1, rows),
        q_gain.reshape(1, head_size),
        k_gain.reshape(1, head_size),
    )
    heads = q_width // head_size
    pairs_of_rows = rows * rows * heads * head_size
    projected, q_low, k_low, v_low, log_totals, att_rel = whole_kernel(
        attend_kernel,
        [
            jax.ShapeDtypeStruct((rows, q_width + 2 * k_width), f32),
            jax.ShapeDtypeStruct((rows, q_width), bf16),
            jax.ShapeDtypeStruct((rows, k_width), bf16),
            jax.ShapeDtypeStruct((rows, k_width), bf16),
            jax.ShapeDtypeStruct((rows, heads), f32),
            jax.ShapeDtypeStruct((rows, q_width), bf16),
        ],
        flops=4 * pairs_of_rows,
    )(side_word, raw_own, raw_y, attn_rstd.reshape(rows, 1), *tables)
    ffn_gathered = gather_shares(*after((share_y, share_diag), att_rel))
    att_y = swap_y(att_rel)
    atts = [att_rel, swap_core(att_rel), att_y, swap_core(att_y)]
    outs = [rows_of(w_out, k, q_width) for k in range(4)]

    def out_rows(at):
        return (dot(atts[0][at], outs[0]) + dot(atts[1][at], outs[1])) + (
            dot(atts[2][at], outs[2]) + dot(atts[3][at], outs[3])
        )

    from_x = swap_x(low(out_rows(slice(half, rows))))
    tokens_half = lax.dynamic_slice_in_dim(tokens, side * half, half, 0).astype(f32)
    residual = tokens_half + out_rows(slice(0, half)) + from_x.astype(f32)

    mlp_square = width_total(jnp.sum(residual * residual, axis=1))
    mlp_own = low(residual * mlp_gain[None, :])
    mlp_rstd = lax.rsqrt(mlp_square / full_width + norm_eps)
    quarter = half // 2
    mlp_x, mlp_y = after((swap_x(mlp_own), swap_y(mlp_own)), mlp_rstd)
    mlp_xy = jnp.concatenate([swap_y(mlp_x[:quarter]), swap_x(mlp_y[quarter:])], axis=0)
    rstd_x = swap_x(mlp_rstd)
    rstds = [r.reshape(half, 1) for r in (mlp_rstd, rstd_x)]
    ins_own = [mlp_own, swap_core(mlp_own), mlp_y, swap_core(mlp_y)]
    ins_other = [mlp_x, swap_core(mlp_x), mlp_xy, swap_core(mlp_xy)]
    cot_rel = flip(cotangent)
    cot_core = swap_core(cot_rel)
    cot_y = after(swap_y(after(cot_rel[:half], att_rel)), mlp_xy)
    cot_x = swap_x(cot_y)
    cots_own = [cot_rel, cot_core, cot_y, swap_core(cot_y)]
    cots_other = [cot_rel, cot_core, cot_x, swap_core(cot_x)]
    whole = lambda block: block
    ffns = (ffn_columns(0, whole), swap_core(ffn_columns(1, whole)), ffn_gathered)
    downs = (rows_of(w_down, 0, units), swap_core(rows_of(w_down, 1, units)), down_gathered)
    first = units_of_half(ins_own, ffns, cots_own, downs, rstds[0], 0, None)
    hidden, pair, pair_scaled, inner = units_of_half(
        ins_other, ffns, cots_other, downs, rstds[1], 1, first
    )

    line = LineSums(2 * width)
    mlp_in, mlp_core = (jnp.concatenate([ins_own[k], ins_other[k]], axis=0) for k in (0, 1))
    line.add(("ffn", 0), low(contract_rows(mlp_in, pair_scaled)))
    line.send()
    pair = after(pair, line.pieces, line.waiting())
    inner_total = width_total(inner[:half, 0]) + swap_x(width_total(inner[half:, 0]))

    kept = {}

    def first_sent(marker):
        block = low(contract_rows(mlp_core, after(pair_scaled, marker)))
        line.add(("ffn", 1), swap_core(block))
        return block

    def started(marker):
        marker = line.send(marker)
        down_core = low(contract_rows(cot_core, after(hidden, marker)))
        down_own = low(contract_rows(cot_rel, after(hidden, marker)))
        line.add(("down", 0), down_own)
        line.add(("down", 1), swap_core(down_core))
        return (marker, down_own)

    def turned(marker):
        kept["hidden"] = lax.all_gather(after(hidden, marker), "tc", axis=1, tiled=True)
        return line.send(marker)

    ffn_blocks = [ffns[0], ffns[1], ffns[2][0], ffns[2][1]]
    mlp_in_grad = scatter_all(
        lambda k: contract_cols(pair, ffn_blocks[k]), first_sent, inner_total, started, turned
    )
    hiddens = kept["hidden"]
    mlp_hat = residual * mlp_rstd[:, None]
    mlp_gain_part = jnp.sum(mlp_in_grad * mlp_hat, axis=0)
    residual_grad = cot_rel[:half].astype(f32) + mlp_rstd[:, None] * (
        mlp_in_grad * mlp_gain[None, :] - mlp_hat * (inner_total / full_width)[:, None]
    )
    residual_low = low(residual_grad)
    res_x = after(swap_x(residual_low), line.send(residual_low))
    res_rel = jnp.concatenate([residual_low, res_x], axis=0)
    head_own, head_y, head_sent = scatter_width(lambda k: contract_cols(res_rel, outs[k]))
    for k, part in enumerate(atts):
        line.add(("out", k), low(contract_rows(res_rel, after(part, head_sent))))
    marker = line.send(line.waiting())
    head_own, head_y = after((head_own, head_y), marker)
    pairs = lax.all_gather(after(pair_scaled, head_y), "tc")

    proj_low, q_gain_part, k_gain_part, inner_attn = whole_kernel(
        attend_back_kernel,
        [
            jax.ShapeDtypeStruct((rows, q_width + 2 * k_width), bf16),
            jax.ShapeDtypeStruct((1, head_size), f32),
            jax.ShapeDtypeStruct((1, head_size), f32),
            jax.ShapeDtypeStruct((rows, 1), f32),
        ],
        flops=10 * pairs_of_rows,
        scratch=[pltpu.VMEM((rows, k_width), f32), pltpu.VMEM((rows, k_width), f32)],
    )(side_word, head_own, head_y, projected, q_low, k_low, v_low, log_totals, *tables)
    inner_attn = inner_attn[:, 0]
    inner_attn = inner_attn + swap_y(inner_attn)
    proj_y, proj_core = swap_y(after(proj_low, inner_attn)), swap_core(proj_low)
    inner_attn = inner_attn + swap_core(inner_attn)
    inner_attn = inner_attn + swap_x(inner_attn)
    for k in (2, 3):
        far = after(cols_of(hiddens, k, units), proj_low, inner_attn)
        line.add(("down", k), low(contract_rows(cot_rel, far)))
    proj_y, proj_core = after((proj_y, proj_core), line.send(line.waiting()))
    projs = [proj_low, proj_core, proj_y, swap_core(proj_y)]
    normed_part = low(
        (contract_cols(projs[0], qkv_weights[0]) + contract_cols(projs[1], qkv_weights[1]))
        + (contract_cols(projs[2], qkv_weights[2]) + contract_cols(projs[3], qkv_weights[3]))
    )
    normed_x = after(swap_x(normed_part), line.send(normed_part))
    normed_grad = normed_part.astype(f32) + normed_x.astype(f32)
    attn_gain_part = jnp.sum(normed_grad * attn_hat, axis=0)
    token_grad = low(
        flip(res_rel).astype(f32)
        + attn_rstd[:, None]
        * (normed_grad * attn_gain[None, :] - attn_hat * (inner_attn / full_width)[:, None])
    )

    for k, part in enumerate(projs):
        line.add(("qkv", k), low(contract_rows(after(normed, normed_part), part)))
    marker = line.send((normed_grad, line.waiting()))
    mlp_away = low(dot(after(hiddens[half:], marker), w_down))
    mlp_x_out = after(swap_x(mlp_away), line.send(mlp_away))
    mixed_half = low(residual + dot(hiddens[:half], w_down) + mlp_x_out.astype(f32))
    mixed_x = swap_x(mixed_half)
    mixed = flip(jnp.concatenate([mixed_half, mixed_x], axis=0))

    for k in (2, 3):
        block = after(lax.dynamic_index_in_dim(pairs, around[k], 0, keepdims=False), mixed_half)
        line.add(("ffn", k), low(contract_rows(mlp_in, block)))
    marker = mixed_half
    while line.stream:
        marker = line.send(marker)
    sums_of = line.finish()

    shared = after(jnp.concatenate([q_gain_part[0], k_gain_part[0]]), marker)
    shared = width_total(shared)
    shared = jnp.concatenate([shared, mlp_gain_part])
    shared = shared + swap_x(shared)
    gains = line_total(jnp.concatenate([shared, attn_gain_part]))
    q_gain_grad = gains[:head_size]
    k_gain_grad = gains[head_size : 2 * head_size]
    mlp_gain_grad = gains[2 * head_size : 2 * head_size + width]
    attn_gain_grad = gains[2 * head_size + width :]

    def place_cols(shape, pieces):
        whole = jnp.zeros(shape, f32)
        for which, piece in enumerate(pieces):
            whole = lax.dynamic_update_slice_in_dim(
                whole, piece.astype(f32), around[which] * piece.shape[1], 1
            )
        return whole

    def place_rows(shape, pieces):
        whole = jnp.zeros(shape, f32)
        for which, piece in enumerate(pieces):
            whole = lax.dynamic_update_slice_in_dim(
                whole, piece.astype(f32), around[which] * piece.shape[0], 0
            )
        return whole

    qkv_grads = [sums_of(("qkv", k)) for k in range(4)]
    w_query_grad = place_cols(w_query.shape, [g[:, :q_width] for g in qkv_grads])
    w_key_grad = place_cols(w_key.shape, [g[:, q_width : q_width + k_width] for g in qkv_grads])
    w_value_grad = place_cols(w_value.shape, [g[:, q_width + k_width :] for g in qkv_grads])
    w_out_grad = place_rows(w_out.shape, [sums_of(("out", k)).T for k in range(4)])
    w_down_grad = place_rows(w_down.shape, [sums_of(("down", k)).T for k in range(4)])
    w_gate_grad = jnp.zeros(w_gate.shape, f32)
    w_up_grad = jnp.zeros(w_up.shape, f32)
    for which in range(4):
        parts = sums_of(("ffn", which))
        for start in range(0, units, ffn_step):
            to = (0, around[which] * units + start)
            gate = parts[:, 2 * start : 2 * start + ffn_step].astype(f32)
            up = parts[:, 2 * start + ffn_step : 2 * start + 2 * ffn_step].astype(f32)
            w_gate_grad = lax.dynamic_update_slice(w_gate_grad, gate, to)
            w_up_grad = lax.dynamic_update_slice(w_up_grad, up, to)
    return (
        mixed,
        token_grad,
        attn_gain_grad,
        q_gain_grad,
        k_gain_grad,
        mlp_gain_grad,
        w_query_grad,
        w_key_grad,
        w_value_grad,
        w_out_grad,
        w_gate_grad,
        w_up_grad,
        w_down_grad,
    )


def solution(mesh):
    in_specs = (
        P("dp", "tc"),
        P("dp", "tc"),
        P("dp"),
        P("tc"),
        P(),
        P(),
        P("tc"),
        P("tc", "tr"),
        P("tc", "tr"),
        P("tc", "tr"),
        P("tr", "tc"),
        P("tc", "tr"),
        P("tc", "tr"),
        P("tr", "tc"),
    )
    out_specs = (
        P("dp", "tc"),
        P("dp", "tc"),
        P("tc"),
        P(),
        P(),
        P("tc"),
        P("tc", "tr"),
        P("tc", "tr"),
        P("tc", "tr"),
        P("tr", "tc"),
        P("tc", "tr"),
        P("tc", "tr"),
        P("tr", "tc"),
    )
    return jax.shard_map(
        on_device, mesh=mesh, in_specs=in_specs, out_specs=out_specs, check_vma=False
    )
```

```python
import jax
import jax.numpy as jnp
from jax import lax
from jax.experimental import pallas as pl
from jax.experimental.pallas import tpu as pltpu
from jax.sharding import PartitionSpec as P

norm_eps = 1e-06
rope_base = 1000000.0
neg_big = -1e30
f32 = jnp.float32
bf16 = jnp.bfloat16


def dot(left_side, right_side):
    return jnp.dot(left_side, right_side, preferred_element_type=f32)


def contract_rows(left_side, right_side):
    return lax.dot_general(
        left_side, right_side, (((0,), (0,)), ((), ())), preferred_element_type=f32
    )


def contract_cols(left_side, right_side):
    return lax.dot_general(
        left_side, right_side, (((1,), (1,)), ((), ())), preferred_element_type=f32
    )


def swap_core(block):
    return lax.ppermute(block, "tc", [(i, i ^ 1) for i in range(4)])


def swap_y(block):
    return lax.ppermute(block, "tc", [(i, i ^ 2) for i in range(4)])


def swap_diag(block):
    return lax.ppermute(block, "tc", [(i, i ^ 3) for i in range(4)])


def swap_x(block):
    return lax.ppermute(block, "tr", [(0, 1), (1, 0)])


def width_total(rows):
    rows = rows + swap_core(rows)
    return rows + swap_y(rows)


def line_total(piece):
    size = lax.axis_size("dp")
    place = lax.axis_index("dp")
    half = size // 2
    for step in range(half):
        got = lax.ppermute(piece, "dp", [(step, step + 1), (size - 1 - step, size - 2 - step)])
        piece = piece + got
    for step in reversed(range(half - 1)):
        got = lax.ppermute(piece, "dp", [(step + 1, step), (size - 2 - step, size - 1 - step)])
        piece = jnp.where((place == step) | (place == size - 1 - step), got, piece)
    return piece


class LineSums:
    def __init__(self, size):
        self.size = size
        self.short = lax.axis_size("dp") == 4
        place = lax.axis_index("dp")
        self.middle = (place == 1) | (place == 2)
        self.stream, self.parts, self.pieces = [], [], []
        self.outer, self.total = [], []

    def add(self, name, columns):
        self.stream.append((name, columns))

    def waiting(self):
        return [columns for _, columns in self.stream]

    def _next(self):
        wanted, parts, blocks = self.size, [], []
        while wanted and self.stream:
            name, columns = self.stream.pop(0)
            taken = min(wanted, columns.shape[1])
            parts.append((name, taken))
            blocks.append(columns[:, :taken])
            if taken < columns.shape[1]:
                self.stream.insert(0, (name, columns[:, taken:]))
            wanted -= taken
        assert wanted == 0
        self.parts.append(parts)
        self.pieces.append(blocks[0] if len(blocks) == 1 else jnp.concatenate(blocks, axis=1))

    def _consume(self, which, marker):
        got, piece = after((self.outer[which], self.pieces[which]), marker)
        inward = low(piece.astype(f32) + got.astype(f32))
        across = lax.ppermute(inward, "dp", [(1, 2), (2, 1)])
        self.total.append(low(inward.astype(f32) + across.astype(f32)))
        return inward

    def _swap_outer(self, piece):
        self.outer.append(lax.ppermute(piece, "dp", [(0, 1), (1, 0), (2, 3), (3, 2)]))

    def send(self, marker=()):
        which = len(self.pieces)
        self._next()
        if not self.short:
            return self.pieces[which]
        if which >= 2:
            marker = self._consume(which - 2, marker)
        out = after(self.pieces[which], marker)
        if which >= 3:
            out = jnp.where(self.middle, self.total[which - 3], out)
        self._swap_outer(out)
        return marker

    def finish(self):
        count = len(self.pieces)
        if self.short:
            for which in (count - 2, count - 1):
                self._consume(which, ())
            for which in range(count - 3, count):
                self._swap_outer(self.total[which])
            sums = [jnp.where(self.middle, self.total[k], self.outer[k + 3]) for k in range(count)]
        else:
            sums = [lax.psum(piece, "dp") for piece in self.pieces]
        named = {}
        for parts, piece in zip(self.parts, sums):
            start = 0
            for name, taken in parts:
                named.setdefault(name, []).append(piece[:, start : start + taken])
                start += taken
        return lambda name: jnp.concatenate(named[name], axis=1)


def after(value, *others):
    return lax.optimization_barrier((value, others))[0]


def low(array):
    return array.astype(bf16)


def scatter_width(product, near=lambda ready: ready):
    from_far = swap_core(low(product(3)))
    from_core = swap_core(low(product(1)))
    from_far = after(from_far, near(from_far))
    for_y = low(product(2) + from_far.astype(f32))
    from_y = swap_y(for_y)
    return (product(0) + from_core.astype(f32), from_y, for_y)


def scatter_all(product, first_sent, ready, started, turned):
    far_y = swap_core(low(product(3)))
    far_own = low(product(1))
    far_y, far_own = after((far_y, swap_core(far_own)), first_sent(far_own))
    for_y = low(product(2) + far_y.astype(f32))
    own = low(product(0) + far_own.astype(f32))
    for_y, own = after((for_y, own), ready)
    half = own.shape[0] // 2
    quarter = half // 2
    width = own.shape[1]
    y_first = swap_y(jnp.concatenate([for_y[quarter:half], for_y[half + quarter :]], axis=0))
    x_first = swap_x(
        jnp.concatenate([own[half : half + quarter], for_y[half : half + quarter]], axis=1)
    )
    x_first, y_first = after((x_first, y_first), started((own, for_y)))
    top_in = low(for_y[:quarter].astype(f32) + x_first[:, width:].astype(f32))
    low_in = low(own[half + quarter :].astype(f32) + y_first[quarter:].astype(f32))
    top_y, low_x = after((swap_y(top_in), swap_x(low_in)), turned((top_in, low_in)))
    top = own[:quarter].astype(f32) + x_first[:, :width].astype(f32) + top_y.astype(f32)
    bottom = own[quarter:half].astype(f32) + y_first[:quarter].astype(f32) + low_x.astype(f32)
    return jnp.concatenate([top, bottom], axis=0)


def positions_of(segment):
    slot_ids = jnp.arange(5, dtype=jnp.int32)
    before = jnp.sum((segment[None, :] < slot_ids[:, None]).astype(jnp.int32), axis=1)
    starts = jnp.sum(jnp.where(segment[:, None] == slot_ids[None, :], before[None, :], 0), axis=1)
    return jnp.arange(segment.shape[0], dtype=jnp.int32) - starts


def rope_tables(positions, head_size):
    half_size = head_size // 2
    frequency = rope_base ** (-jnp.arange(half_size, dtype=f32) * 2.0 / head_size)
    angles = positions.astype(f32)[:, None] * frequency[None, :]
    cosine, sine = jnp.cos(angles), jnp.sin(angles)
    return (
        jnp.concatenate([cosine, cosine], axis=1),
        jnp.concatenate([-sine, sine], axis=1),
    )


def turn(vectors):
    return pltpu.roll(vectors, vectors.shape[-1] // 2, axis=1)


def inverse_norm(vectors):
    return lax.rsqrt(jnp.mean(vectors * vectors, axis=-1, keepdims=True) + norm_eps)


def allowed_keys(seg_col, seg_row, start, size, extent):
    row = lax.broadcasted_iota(jnp.int32, (size, extent), 0) + start
    col = lax.broadcasted_iota(jnp.int32, (size, extent), 1)
    return (seg_col[start : start + size, :] == seg_row[:, :extent]) & (col <= row)


def attend_kernel(
    side, own, from_y, rstd, cos, sin, seg_col, seg_row, q_gain, k_gain,
    proj, q_out, k_out, v_out, lse, att,
):
    rows = own.shape[0]
    size = cos.shape[1]
    heads = q_out.shape[1] // size
    block = rows // 4
    scale = size**-0.5
    k_at = heads * size
    v_at = k_at + size

    def ready(i, carry):
        at = pl.ds(pl.multiple_of(i * block, block), block)
        raw = (own[at, :] + from_y[at, :].astype(f32)) * rstd[at, :]
        proj[at, :] = raw

        def rope(part, gain):
            n = part * inverse_norm(part) * gain[...]
            return (n * cos[at, :] + turn(n) * sin[at, :]).astype(bf16)

        for h in range(heads):
            q_out[at, h * size : (h + 1) * size] = rope(raw[:, h * size : (h + 1) * size], q_gain)
        k_out[at, :] = rope(raw[:, k_at:v_at], k_gain)
        v_out[at, :] = raw[:, v_at:].astype(bf16)
        return carry

    lax.fori_loop(0, 4, ready, 0)
    for i in range(4):
        start = i * block
        extent = start + block
        allowed = allowed_keys(seg_col, seg_row, start, block, extent)
        to = pl.ds(pl.multiple_of(lax.rem(start + side[0] * (rows // 2), rows), block), block)
        for h in range(heads):
            of_head = slice(h * size, (h + 1) * size)
            scores = contract_cols(q_out[start:extent, of_head], k_out[:extent, :]) * scale
            scores = jnp.where(allowed, scores, neg_big)
            top = jnp.max(scores, axis=-1, keepdims=True)
            expd = jnp.exp(scores - top)
            total = jnp.sum(expd, axis=-1, keepdims=True)
            weights = (expd * (1.0 / total)).astype(bf16)
            att[to, of_head] = dot(weights, v_out[:extent, :]).astype(bf16)
            lse[start:extent, h : h + 1] = top + jnp.log(total)


def attend_back_kernel(
    side, own, from_y, proj, q_in, k_in, v_in, lse, cos, sin, seg_col, seg_row, q_gain, k_gain,
    grads, q_gain_part, k_gain_part, inner, k_acc, v_acc,
):
    rows = own.shape[0]
    size = cos.shape[1]
    heads = q_in.shape[1] // size
    block = rows // 4
    scale = size**-0.5
    k_at = heads * size
    v_at = k_at + size

    def unrope(grad, part, gain, start):
        rows_at = slice(start, start + block)
        m = grad * cos[rows_at, :] - turn(grad) * sin[rows_at, :]
        r = inverse_norm(part)
        hat = part * r
        mg = m * gain[...]
        back = (r * (mg - hat * jnp.mean(mg * hat, axis=-1, keepdims=True))).astype(bf16)
        gain_part = jnp.sum(m * hat, axis=0, keepdims=True)
        return (back, gain_part, jnp.sum(back.astype(f32) * part, axis=-1, keepdims=True))

    k_acc[...] = jnp.zeros_like(k_acc)
    v_acc[...] = jnp.zeros_like(v_acc)
    q_total = jnp.zeros(q_gain_part.shape, f32)
    for i in range(4):
        start = i * block
        extent = start + block
        allowed = allowed_keys(seg_col, seg_row, start, block, extent)
        at = pl.ds(pl.multiple_of(lax.rem(start + side[0] * (rows // 2), rows), block), block)
        inner_sum = jnp.zeros((block, 1), f32)
        for h in range(heads):
            of_head = slice(h * size, (h + 1) * size)
            query = q_in[start:extent, of_head]
            grad = (own[at, of_head] + from_y[at, of_head].astype(f32)).astype(bf16)
            scores = contract_cols(query, k_in[:extent, :]) * scale
            scores = jnp.where(allowed, scores, neg_big)
            probs = jnp.exp(scores - lse[start:extent, h : h + 1])
            prob_grad = contract_cols(grad, v_in[:extent, :])
            delta = jnp.sum(probs * prob_grad, axis=-1, keepdims=True)
            score_grad = (probs * (prob_grad - delta)).astype(bf16)
            query_grad = dot(score_grad, k_in[:extent, :]) * scale
            k_acc[:extent, :] += contract_rows(score_grad, query) * scale
            v_acc[:extent, :] += contract_rows(probs.astype(bf16), grad)
            back, gain_part, part_inner = unrope(
                query_grad, proj[start:extent, of_head], q_gain, start
            )
            grads[start:extent, of_head] = back
            q_total = q_total + gain_part
            inner_sum = inner_sum + part_inner
        inner[start:extent, :] = inner_sum
    q_gain_part[...] = q_total
    k_total = jnp.zeros(k_gain_part.shape, f32)
    for i in range(4):
        start = i * block
        extent = start + block
        back, gain_part, part_inner = unrope(
            k_acc[start:extent, :], proj[start:extent, k_at:v_at], k_gain, start
        )
        grads[start:extent, k_at:v_at] = back
        k_total = k_total + gain_part
        v_back = v_acc[start:extent, :].astype(bf16)
        grads[start:extent, v_at:] = v_back
        inner[start:extent, :] += part_inner + jnp.sum(
            v_back.astype(f32) * proj[start:extent, v_at:], axis=-1, keepdims=True
        )
    k_gain_part[...] = k_total


vmem = pl.BlockSpec(memory_space=pltpu.VMEM)
smem = pl.BlockSpec(memory_space=pltpu.SMEM)
big_vmem = pltpu.CompilerParams(vmem_limit_bytes=50 * 2**20)


def whole_kernel(body, outs, scratch=()):
    def call(*operands):
        return pl.pallas_call(
            body,
            out_shape=outs,
            in_specs=[smem] + [vmem] * (len(operands) - 1),
            out_specs=[vmem] * len(outs),
            scratch_shapes=scratch,
            compiler_params=big_vmem,
            cost_estimate=pl.CostEstimate(flops=0, bytes_accessed=2**10, transcendentals=0),
        )(*operands)

    return call


def units_kernel(*refs):
    ins, weights, cots, downs = refs[:4], refs[4:8], refs[8:12], refs[12:16]
    rstd_ref = refs[16]
    hidden, pair, scaled, inner = refs[-4:]
    units = hidden.shape[1]
    chunk = min(256, units)
    rstd = rstd_ref[...]

    def product(at):
        total = dot(ins[0][...], weights[0][:, at])
        for k in range(1, 4):
            total = total + dot(ins[k][...], weights[k][:, at])
        return total * rstd

    inner_sum = jnp.zeros(inner.shape, f32)
    for start in range(0, units, chunk):
        of_gate = slice(start, start + chunk)
        of_up = slice(units + start, units + start + chunk)
        gate, up = product(of_gate), product(of_up)
        grad = contract_cols(cots[0][...], downs[0][of_gate, :])
        for k in range(1, 4):
            grad = grad + contract_cols(cots[k][...], downs[k][of_gate, :])
        sig = jax.nn.sigmoid(gate)
        silu = gate * sig
        hidden[:, of_gate] = low(silu * up)
        gate_grad = low(grad * up * sig * (1.0 + gate * (1.0 - sig)))
        up_grad = low(grad * silu)
        pair[:, of_gate] = gate_grad
        pair[:, of_up] = up_grad
        gate_grad, up_grad = gate_grad.astype(f32), up_grad.astype(f32)
        scaled[:, of_gate] = low(gate_grad * rstd)
        scaled[:, of_up] = low(up_grad * rstd)
        inner_sum = inner_sum + jnp.sum(gate_grad * gate + up_grad * up, axis=-1, keepdims=True)
    inner[...] = inner_sum


def units_of_half(ins, weights, cots, downs, rstd, which, earlier):
    half, depth = ins[0].shape
    units = downs[0].shape[0]
    block = half // 2
    first = which * (half // block)
    outs = [
        jax.ShapeDtypeStruct((2 * half, units), bf16),
        jax.ShapeDtypeStruct((2 * half, 2 * units), bf16),
        jax.ShapeDtypeStruct((2 * half, 2 * units), bf16),
        jax.ShapeDtypeStruct((2 * half, 1), f32),
    ]

    def whole(array):
        return pl.BlockSpec(array.shape, lambda i: (0, 0))

    def of_two(array, k):
        return pl.BlockSpec((None, *array.shape[1:]), lambda i: (k, 0, 0))

    near_by, core, both = downs
    downs = [near_by, core, both, both]
    down_specs = [whole(near_by), whole(core), of_two(both, 0), of_two(both, 1)]
    here = pl.BlockSpec((block, depth), lambda i: (i, 0))
    at = lambda i: (first + i, 0)
    of_all = pl.BlockSpec((block, depth), at)
    earlier = list(earlier or [])
    return pl.pallas_call(
        units_kernel,
        grid=(half // block,),
        out_shape=outs,
        in_specs=[here] * 4
        + [whole(w) for w in weights]
        + [of_all, of_all, here, here]
        + down_specs
        + [pl.BlockSpec((block, 1), at)]
        + [pl.BlockSpec(memory_space=pl.ANY)] * len(earlier),
        out_specs=[pl.BlockSpec((block, o.shape[1]), at) for o in outs],
        input_output_aliases={17 + k: k for k in range(len(earlier))},
        compiler_params=big_vmem,
        cost_estimate=pl.CostEstimate(flops=0, bytes_accessed=2**10, transcendentals=0),
    )(*ins, *weights, *cots, *downs, rstd, *earlier)


def on_device(
    tokens,
    cotangent,
    segment_ids,
    attn_gain,
    q_gain,
    k_gain,
    mlp_gain,
    w_query,
    w_key,
    w_value,
    w_out,
    w_gate,
    w_up,
    w_down,
):
    assert lax.axis_size("tc") == 4 and lax.axis_size("tr") == 2
    col = lax.axis_index("tc")
    side = lax.axis_index("tr")
    rows, width = tokens.shape
    half = rows // 2
    full_width = width * 4
    head_size = q_gain.shape[0]
    q_width = w_query.shape[1] // 4
    k_width = w_key.shape[1] // 4
    units = w_gate.shape[1] // 4
    around = [col, col ^ 1, col ^ 2, col ^ 3]

    def cols_of(array, which, size):
        return lax.dynamic_slice_in_dim(array, around[which] * size, size, 1)

    def rows_of(array, which, size):
        return lax.dynamic_slice_in_dim(array, around[which] * size, size, 0)

    def flip(array):
        return jnp.concatenate(
            [
                lax.dynamic_slice_in_dim(array, side * half, half, 0),
                lax.dynamic_slice_in_dim(array, (1 - side) * half, half, 0),
            ],
            axis=0,
        )

    shares = lax.axis_size("dp")
    place = lax.axis_index("dp")

    def share_of(block):
        size = block.shape[0] // shares
        return lax.dynamic_slice_in_dim(block, place * size, size, 0)

    def gather_shares(from_y, from_diag):
        return lax.all_gather(jnp.stack([from_y, from_diag]), "dp", axis=1, tiled=True)

    def ffn_columns(which, rows_at):
        return jnp.concatenate(
            [rows_at(cols_of(w, which, units)) for w in (w_gate, w_up)], axis=1
        )

    down_y, down_diag = (share_of(rows_of(w_down, k, units)) for k in (2, 3))
    share_y, share_diag = ffn_columns(2, share_of), ffn_columns(3, share_of)

    qkv_weights = [
        jnp.concatenate(
            [cols_of(w_query, k, q_width), cols_of(w_key, k, k_width), cols_of(w_value, k, k_width)],
            axis=1,
        )
        for k in range(4)
    ]
    inputs = tokens.astype(f32)
    scaled_in = after(
        low(inputs * attn_gain[None, :]), down_y, down_diag, share_y, share_diag
    )
    raw_own, raw_y, for_y = scatter_width(lambda k: dot(scaled_in, qkv_weights[k]))
    down_y, down_diag = swap_y(down_y), swap_diag(down_diag)
    down_gathered = gather_shares(down_y, down_diag)
    share_y, share_diag = after((share_y, share_diag), down_y, down_diag)
    w_gate, w_up, w_down, w_out, segment_ids, cotangent, inputs = after(
        (w_gate, w_up, w_down, w_out, segment_ids, cotangent, inputs), for_y
    )
    square_sum = width_total(jnp.sum(inputs * inputs, axis=1))
    cos_table, sin_table = rope_tables(positions_of(segment_ids), head_size)
    side_word = side.astype(jnp.int32).reshape(1)
    tables = (
        cos_table,
        sin_table,
        segment_ids.reshape(rows, 1),
        segment_ids.reshape(1, rows),
        q_gain.reshape(1, head_size),
        k_gain.reshape(1, head_size),
    )
    whole = lambda block: block
    blocks_core = (ffn_columns(1, whole), rows_of(w_down, 1, units))
    raw_y, share_y, share_diag, square_sum = after(
        (raw_y, swap_y(share_y), swap_diag(share_diag), square_sum), raw_own, tables, blocks_core
    )
    ffn_y, ffn_diag = (lax.all_gather(w, "dp", axis=0, tiled=True) for w in (share_y, share_diag))
    attn_rstd = lax.rsqrt(square_sum / full_width + norm_eps)
    attn_hat = inputs * attn_rstd[:, None]
    normed = low(attn_hat * attn_gain[None, :])

    heads = q_width // head_size
    projected, q_low, k_low, v_low, log_totals, att_rel = whole_kernel(
        attend_kernel,
        [
            jax.ShapeDtypeStruct((rows, q_width + 2 * k_width), f32),
            jax.ShapeDtypeStruct((rows, q_width), bf16),
            jax.ShapeDtypeStruct((rows, k_width), bf16),
            jax.ShapeDtypeStruct((rows, k_width), bf16),
            jax.ShapeDtypeStruct((rows, heads), f32),
            jax.ShapeDtypeStruct((rows, q_width), bf16),
        ],
    )(side_word, raw_own, raw_y, attn_rstd.reshape(rows, 1), *tables)
    cot_rel = flip(cotangent)
    cot_y = swap_y(after(cot_rel[:half], raw_y))
    att_y, cot_x, down_gathered = after((swap_y(att_rel), swap_x(cot_y), down_gathered), att_rel)
    atts = [att_rel, swap_core(att_rel), att_y, swap_core(att_y)]
    outs = [rows_of(w_out, k, q_width) for k in range(4)]

    def out_rows(at):
        return (dot(atts[0][at], outs[0]) + dot(atts[1][at], outs[1])) + (
            dot(atts[2][at], outs[2]) + dot(atts[3][at], outs[3])
        )

    from_x = swap_x(low(out_rows(slice(half, rows))))
    home = out_rows(slice(0, half))

    prefetched = (
        swap_core(cot_rel),
        *map(swap_core, blocks_core),
    )
    from_x, (cot_core, ffn_core, down_core), ffn_y = after((from_x, prefetched, ffn_y), home)
    cot_y_core, cot_x_core = swap_core(cot_y), swap_core(cot_x)
    downs = (rows_of(w_down, 0, units), down_core, down_gathered)
    tokens_half = lax.dynamic_slice_in_dim(tokens, side * half, half, 0).astype(f32)
    residual = tokens_half + home + from_x.astype(f32)

    mlp_square = jnp.sum(residual * residual, axis=1)
    mlp_square = width_total(jnp.concatenate([mlp_square, swap_x(mlp_square)]))
    mlp_own = low(residual * mlp_gain[None, :])
    mlp_rstd = lax.rsqrt(mlp_square / full_width + norm_eps)
    quarter = half // 2
    mlp_x, mlp_y, mlp_rstd, ffn_diag = after(
        (swap_x(mlp_own), swap_y(mlp_own), mlp_rstd, ffn_diag), cot_y_core, cot_x_core
    )
    mlp_xy = jnp.concatenate([swap_y(mlp_x[:quarter]), swap_x(mlp_y[quarter:])], axis=0)
    ins_own = [mlp_own, swap_core(mlp_own), mlp_y, swap_core(mlp_y)]
    ins_other = [mlp_x, swap_core(mlp_x), mlp_xy, swap_core(mlp_xy)]
    cots_own = [cot_rel, cot_core, cot_y, cot_y_core]
    cots_other = [cot_rel, cot_core, cot_x, cot_x_core]
    ffns = [ffn_columns(0, whole), ffn_core, ffn_y, ffn_diag]
    rstd_rel = mlp_rstd.reshape(rows, 1)
    first = units_of_half(ins_own, ffns, cots_own, downs, rstd_rel, 0, None)
    hidden, pair, pair_scaled, inner = units_of_half(
        ins_other, ffns, cots_other, downs, rstd_rel, 1, first
    )

    mlp_in, mlp_core = (jnp.concatenate([ins_own[k], ins_other[k]], axis=0) for k in (0, 1))
    inner_total = width_total(inner[:half, 0]) + swap_x(width_total(inner[half:, 0]))
    kept = {}

    def first_sent(marker):
        block = low(contract_rows(mlp_core, after(pair_scaled, marker)))
        kept["ffn"] = [swap_core(block)]
        return block

    def started(marker):
        block = low(contract_rows(mlp_in, after(pair_scaled, marker)))
        kept["ffn"].insert(0, block)
        down_core = low(contract_rows(cot_core, after(hidden, block)))
        down_own = low(contract_rows(cot_rel, after(hidden, block)))
        kept["down"] = [down_own, swap_core(down_core)]
        return down_own

    def turned(marker):
        return marker

    mlp_in_grad = scatter_all(
        lambda k: contract_cols(pair, ffns[k]), first_sent, inner_total, started, turned
    )
    near_ffn = lax.psum(kept["ffn"], "dp")
    pairs = lax.all_gather(after(pair_scaled, mlp_in_grad), "tc")
    mlp_hat = residual * mlp_rstd[:half, None]
    mlp_gain_part = jnp.sum(mlp_in_grad * mlp_hat, axis=0)
    residual_grad = cot_rel[:half].astype(f32) + mlp_rstd[:half, None] * (
        mlp_in_grad * mlp_gain[None, :] - mlp_hat * (inner_total / full_width)[:, None]
    )
    residual_low = low(residual_grad)
    res_x = swap_x(residual_low)
    res_rel = jnp.concatenate([residual_low, res_x], axis=0)
    head_own, head_y, head_sent = scatter_width(lambda k: contract_cols(res_rel, outs[k]))
    out_grads = [low(contract_rows(res_rel, after(part, head_sent))) for part in atts]
    head_own, head_y = after((head_own, head_y), out_grads)

    proj_low, q_gain_part, k_gain_part, inner_attn = whole_kernel(
        attend_back_kernel,
        [
            jax.ShapeDtypeStruct((rows, q_width + 2 * k_width), bf16),
            jax.ShapeDtypeStruct((1, head_size), f32),
            jax.ShapeDtypeStruct((1, head_size), f32),
            jax.ShapeDtypeStruct((rows, 1), f32),
        ],
        scratch=[pltpu.VMEM((rows, k_width), f32), pltpu.VMEM((rows, k_width), f32)],
    )(side_word, head_own, head_y, projected, q_low, k_low, v_low, log_totals, *tables)
    inner_attn = inner_attn[:, 0]
    inner_attn = inner_attn + swap_y(inner_attn)
    proj_y, proj_core = swap_y(after(proj_low, inner_attn)), swap_core(proj_low)
    inner_attn = inner_attn + swap_core(inner_attn)
    inner_attn = inner_attn + swap_x(inner_attn)
    line = LineSums(width)
    for k in (0, 1):
        line.add(("down", k), kept["down"][k])
    for k in range(4):
        line.add(("out", k), out_grads[k])
    hiddens = lax.all_gather(after(hidden, proj_low), "tc", axis=1, tiled=True)
    marker = (proj_low, inner_attn)
    for _ in range(3):
        marker = line.send(marker)
    proj_y, proj_core = after((proj_y, proj_core), marker)
    projs = [proj_low, proj_core, proj_y, swap_core(proj_y)]
    normed_part = low(
        (contract_cols(projs[0], qkv_weights[0]) + contract_cols(projs[1], qkv_weights[1]))
        + (contract_cols(projs[2], qkv_weights[2]) + contract_cols(projs[3], qkv_weights[3]))
    )
    normed_x = after(swap_x(normed_part), line.send(normed_part))
    normed_grad = normed_part.astype(f32) + normed_x.astype(f32)
    attn_gain_part = jnp.sum(normed_grad * attn_hat, axis=0)
    token_grad = low(
        flip(res_rel).astype(f32)
        + attn_rstd[:, None]
        * (normed_grad * attn_gain[None, :] - attn_hat * (inner_attn / full_width)[:, None])
    )

    for k, part in enumerate(projs):
        line.add(("qkv", k), low(contract_rows(after(normed, normed_part), part)))
    marker = line.send((normed_grad, line.waiting()))
    for _ in range(4):
        marker = line.send(marker)
    pairs, near_ffn = after((pairs, near_ffn), marker)
    for k in (2, 3):
        block = lax.dynamic_index_in_dim(pairs, around[k], 0, keepdims=False)
        line.add(("ffn", k), low(contract_rows(mlp_in, block)))
    for _ in range(5):
        marker = line.send(marker)

    hiddens = after(hiddens, marker)
    for k in (2, 3):
        line.add(("down", k), low(contract_rows(cot_rel, cols_of(hiddens, k, units))))
    mlp_away = low(dot(hiddens[half:], w_down))
    mlp_x_out = after(swap_x(mlp_away), line.send(mlp_away))
    mixed_half = low(residual + dot(hiddens[:half], w_down) + mlp_x_out.astype(f32))
    mixed_x = after(swap_x(mixed_half), line.send(mixed_half))
    mixed = flip(jnp.concatenate([mixed_half, mixed_x], axis=0))
    marker = mixed_x
    while line.stream:
        marker = line.send(marker)
    sums_of = line.finish()

    shared = after(jnp.concatenate([q_gain_part[0], k_gain_part[0]]), marker)
    shared = width_total(shared)
    shared = jnp.concatenate([shared, mlp_gain_part])
    shared = shared + swap_x(shared)
    gains = line_total(jnp.concatenate([shared, attn_gain_part]))
    q_gain_grad = gains[:head_size]
    k_gain_grad = gains[head_size : 2 * head_size]
    mlp_gain_grad = gains[2 * head_size : 2 * head_size + width]
    attn_gain_grad = gains[2 * head_size + width :]

    def place_cols(shape, pieces):
        whole = jnp.zeros(shape, f32)
        for which, piece in enumerate(pieces):
            whole = lax.dynamic_update_slice_in_dim(
                whole, piece.astype(f32), around[which] * piece.shape[1], 1
            )
        return whole

    def place_rows(shape, pieces):
        whole = jnp.zeros(shape, f32)
        for which, piece in enumerate(pieces):
            whole = lax.dynamic_update_slice_in_dim(
                whole, piece.astype(f32), around[which] * piece.shape[0], 0
            )
        return whole

    qkv_grads = [sums_of(("qkv", k)) for k in range(4)]
    w_query_grad = place_cols(w_query.shape, [g[:, :q_width] for g in qkv_grads])
    w_key_grad = place_cols(w_key.shape, [g[:, q_width : q_width + k_width] for g in qkv_grads])
    w_value_grad = place_cols(w_value.shape, [g[:, q_width + k_width :] for g in qkv_grads])
    w_out_grad = place_rows(w_out.shape, [sums_of(("out", k)).T for k in range(4)])
    w_down_grad = place_rows(w_down.shape, [sums_of(("down", k)).T for k in range(4)])
    ffn_grads = near_ffn + [sums_of(("ffn", k)) for k in (2, 3)]
    w_gate_grad = place_cols(w_gate.shape, [g[:, :units] for g in ffn_grads])
    w_up_grad = place_cols(w_up.shape, [g[:, units:] for g in ffn_grads])
    return (
        mixed,
        token_grad,
        attn_gain_grad,
        q_gain_grad,
        k_gain_grad,
        mlp_gain_grad,
        w_query_grad,
        w_key_grad,
        w_value_grad,
        w_out_grad,
        w_gate_grad,
        w_up_grad,
        w_down_grad,
    )


def solution(mesh):
    in_specs = (
        P("dp", "tc"),
        P("dp", "tc"),
        P("dp"),
        P("tc"),
        P(),
        P(),
        P("tc"),
        P("tc", "tr"),
        P("tc", "tr"),
        P("tc", "tr"),
        P("tr", "tc"),
        P("tc", "tr"),
        P("tc", "tr"),
        P("tr", "tc"),
    )
    out_specs = (
        P("dp", "tc"),
        P("dp", "tc"),
        P("tc"),
        P(),
        P(),
        P("tc"),
        P("tc", "tr"),
        P("tc", "tr"),
        P("tc", "tr"),
        P("tr", "tc"),
        P("tc", "tr"),
        P("tc", "tr"),
        P("tr", "tc"),
    )
    return jax.shard_map(
        on_device, mesh=mesh, in_specs=in_specs, out_specs=out_specs, check_vma=False
    )
```

```python
import jax
import jax.numpy as jnp
from jax import lax
from jax.experimental import pallas as pl
from jax.experimental.pallas import tpu as pltpu
from jax.sharding import PartitionSpec as P

norm_eps = 1e-06
rope_base = 1000000.0
neg_big = -1e30
f32 = jnp.float32
bf16 = jnp.bfloat16


def dot(left_side, right_side):
    return jnp.dot(left_side, right_side, preferred_element_type=f32)


def contract_rows(left_side, right_side):
    return lax.dot_general(
        left_side, right_side, (((0,), (0,)), ((), ())), preferred_element_type=f32
    )


def contract_cols(left_side, right_side):
    return lax.dot_general(
        left_side, right_side, (((1,), (1,)), ((), ())), preferred_element_type=f32
    )


def swap_core(block):
    return lax.ppermute(block, "tc", [(i, i ^ 1) for i in range(4)])


def swap_y(block):
    return lax.ppermute(block, "tc", [(i, i ^ 2) for i in range(4)])


def swap_diag(block):
    return lax.ppermute(block, "tc", [(i, i ^ 3) for i in range(4)])


def swap_x(block):
    return lax.ppermute(block, "tr", [(0, 1), (1, 0)])


def width_total(rows):
    rows = rows + swap_core(rows)
    return rows + swap_y(rows)


class LineSums:
    def __init__(self, size):
        self.size = size
        self.short = lax.axis_size("dp") == 4
        place = lax.axis_index("dp")
        self.middle = (place == 1) | (place == 2)
        self.stream, self.parts, self.pieces = [], [], []
        self.outer, self.total = [], []

    def add(self, name, columns):
        self.stream.append((name, columns))

    def waiting(self):
        return [columns for _, columns in self.stream]

    def _next(self):
        wanted, parts, blocks = self.size, [], []
        while wanted and self.stream:
            name, columns = self.stream.pop(0)
            taken = min(wanted, columns.shape[1])
            parts.append((name, taken))
            blocks.append(columns[:, :taken])
            if taken < columns.shape[1]:
                self.stream.insert(0, (name, columns[:, taken:]))
            wanted -= taken
        assert wanted == 0
        self.parts.append(parts)
        self.pieces.append(blocks[0] if len(blocks) == 1 else jnp.concatenate(blocks, axis=1))

    def _consume(self, which, marker):
        got, piece = after((self.outer[which], self.pieces[which]), marker)
        inward = low(piece.astype(f32) + got.astype(f32))
        across = lax.ppermute(inward, "dp", [(1, 2), (2, 1)])
        self.total.append(low(inward.astype(f32) + across.astype(f32)))
        return inward

    def _swap_outer(self, piece):
        self.outer.append(lax.ppermute(piece, "dp", [(0, 1), (1, 0), (2, 3), (3, 2)]))

    def send(self, marker=()):
        which = len(self.pieces)
        self._next()
        if not self.short:
            return self.pieces[which]
        if which >= 2:
            marker = self._consume(which - 2, marker)
        out = after(self.pieces[which], marker)
        if which >= 3:
            out = jnp.where(self.middle, self.total[which - 3], out)
        self._swap_outer(out)
        return marker

    def finish(self):
        count = len(self.pieces)
        if self.short:
            for which in (count - 2, count - 1):
                self._consume(which, ())
            for which in range(count - 3, count):
                self._swap_outer(self.total[which])
            sums = [jnp.where(self.middle, self.total[k], self.outer[k + 3]) for k in range(count)]
        else:
            sums = [lax.psum(piece, "dp") for piece in self.pieces]
        named = {}
        for parts, piece in zip(self.parts, sums):
            start = 0
            for name, taken in parts:
                named.setdefault(name, []).append(piece[:, start : start + taken])
                start += taken
        return lambda name: jnp.concatenate(named[name], axis=1)


def after(value, *others):
    return lax.optimization_barrier((value, others))[0]


def low(array):
    return array.astype(bf16)


def scatter_width(product, near=lambda ready: ready):
    from_far = swap_core(low(product(3)))
    from_core = swap_core(low(product(1)))
    from_far = after(from_far, near(from_far))
    for_y = low(product(2) + from_far.astype(f32))
    from_y = swap_y(for_y)
    return (product(0) + from_core.astype(f32), from_y, for_y)


def scatter_all(product, between=lambda k, marker: marker, started=lambda marker: marker):
    far_y = low(product(3, ()))
    marker = between(0, far_y)
    far_y = swap_core(far_y)
    far_own = low(product(1, marker))
    marker = between(1, far_own)
    far_own = swap_core(far_own)
    for_y = low(product(2, marker) + far_y.astype(f32))
    marker = between(2, for_y)
    own = low(product(0, marker) + far_own.astype(f32))
    half = own.shape[0] // 2
    quarter = half // 2
    width = own.shape[1]
    y_first = swap_y(jnp.concatenate([for_y[quarter:half], for_y[half + quarter :]], axis=0))
    x_first = swap_x(
        jnp.concatenate([own[half : half + quarter], for_y[half : half + quarter]], axis=1)
    )
    x_first, y_first = after((x_first, y_first), started((own, for_y)))
    top_in = low(for_y[:quarter].astype(f32) + x_first[:, width:].astype(f32))
    low_in = low(own[half + quarter :].astype(f32) + y_first[quarter:].astype(f32))
    top_y, low_x = after((swap_y(top_in), swap_x(low_in)), (top_in, low_in))
    top = own[:quarter].astype(f32) + x_first[:, :width].astype(f32) + top_y.astype(f32)
    bottom = own[quarter:half].astype(f32) + y_first[:quarter].astype(f32) + low_x.astype(f32)
    return jnp.concatenate([top, bottom], axis=0)


def positions_of(segment):
    slot_ids = jnp.arange(5, dtype=jnp.int32)
    before = jnp.sum((segment[None, :] < slot_ids[:, None]).astype(jnp.int32), axis=1)
    starts = jnp.sum(jnp.where(segment[:, None] == slot_ids[None, :], before[None, :], 0), axis=1)
    return jnp.arange(segment.shape[0], dtype=jnp.int32) - starts


def rope_tables(positions, head_size):
    half_size = head_size // 2
    frequency = rope_base ** (-jnp.arange(half_size, dtype=f32) * 2.0 / head_size)
    angles = positions.astype(f32)[:, None] * frequency[None, :]
    cosine, sine = jnp.cos(angles), jnp.sin(angles)
    return (
        jnp.concatenate([cosine, cosine], axis=1),
        jnp.concatenate([-sine, sine], axis=1),
    )


def turn(vectors):
    return pltpu.roll(vectors, vectors.shape[-1] // 2, axis=1)


def inverse_norm(vectors):
    return lax.rsqrt(jnp.mean(vectors * vectors, axis=-1, keepdims=True) + norm_eps)


def allowed_keys(seg_col, seg_row, start, size, extent):
    row = lax.broadcasted_iota(jnp.int32, (size, extent), 0) + start
    col = lax.broadcasted_iota(jnp.int32, (size, extent), 1)
    return (seg_col[start : start + size, :] == seg_row[:, :extent]) & (col <= row)


def attend_kernel(
    side, own, from_y, rstd, cos, sin, seg_col, seg_row, q_gain, k_gain,
    proj, q_out, k_out, v_out, lse, att,
):
    rows = own.shape[0]
    size = cos.shape[1]
    heads = q_out.shape[1] // size
    block = rows // 4
    scale = size**-0.5
    k_at = heads * size
    v_at = k_at + size

    def ready(i, carry):
        at = pl.ds(pl.multiple_of(i * block, block), block)
        raw = (own[at, :] + from_y[at, :].astype(f32)) * rstd[at, :]
        proj[at, :] = raw

        def rope(part, gain):
            n = part * inverse_norm(part) * gain[...]
            return (n * cos[at, :] + turn(n) * sin[at, :]).astype(bf16)

        for h in range(heads):
            q_out[at, h * size : (h + 1) * size] = rope(raw[:, h * size : (h + 1) * size], q_gain)
        k_out[at, :] = rope(raw[:, k_at:v_at], k_gain)
        v_out[at, :] = raw[:, v_at:].astype(bf16)
        return carry

    lax.fori_loop(0, 4, ready, 0)
    for i in range(4):
        start = i * block
        extent = start + block
        allowed = allowed_keys(seg_col, seg_row, start, block, extent)
        to = pl.ds(pl.multiple_of(lax.rem(start + side[0] * (rows // 2), rows), block), block)
        for h in range(heads):
            of_head = slice(h * size, (h + 1) * size)
            scores = contract_cols(q_out[start:extent, of_head], k_out[:extent, :]) * scale
            scores = jnp.where(allowed, scores, neg_big)
            top = jnp.max(scores, axis=-1, keepdims=True)
            expd = jnp.exp(scores - top)
            total = jnp.sum(expd, axis=-1, keepdims=True)
            weights = (expd * (1.0 / total)).astype(bf16)
            att[to, of_head] = dot(weights, v_out[:extent, :]).astype(bf16)
            lse[start:extent, h : h + 1] = top + jnp.log(total)


def attend_back_kernel(
    side, own, from_y, proj, q_in, k_in, v_in, lse, cos, sin, seg_col, seg_row, q_gain, k_gain,
    grads, q_gain_part, k_gain_part, inner, k_acc, v_acc,
):
    rows = own.shape[0]
    size = cos.shape[1]
    heads = q_in.shape[1] // size
    block = rows // 4
    scale = size**-0.5
    k_at = heads * size
    v_at = k_at + size

    def unrope(grad, part, gain, start):
        rows_at = slice(start, start + block)
        m = grad * cos[rows_at, :] - turn(grad) * sin[rows_at, :]
        r = inverse_norm(part)
        hat = part * r
        mg = m * gain[...]
        back = (r * (mg - hat * jnp.mean(mg * hat, axis=-1, keepdims=True))).astype(bf16)
        gain_part = jnp.sum(m * hat, axis=0, keepdims=True)
        return (back, gain_part, jnp.sum(back.astype(f32) * part, axis=-1, keepdims=True))

    k_acc[...] = jnp.zeros_like(k_acc)
    v_acc[...] = jnp.zeros_like(v_acc)
    q_total = jnp.zeros(q_gain_part.shape, f32)
    for i in range(4):
        start = i * block
        extent = start + block
        allowed = allowed_keys(seg_col, seg_row, start, block, extent)
        at = pl.ds(pl.multiple_of(lax.rem(start + side[0] * (rows // 2), rows), block), block)
        inner_sum = jnp.zeros((block, 1), f32)
        for h in range(heads):
            of_head = slice(h * size, (h + 1) * size)
            query = q_in[start:extent, of_head]
            grad = (own[at, of_head] + from_y[at, of_head].astype(f32)).astype(bf16)
            scores = contract_cols(query, k_in[:extent, :]) * scale
            scores = jnp.where(allowed, scores, neg_big)
            probs = jnp.exp(scores - lse[start:extent, h : h + 1])
            prob_grad = contract_cols(grad, v_in[:extent, :])
            delta = jnp.sum(probs * prob_grad, axis=-1, keepdims=True)
            score_grad = (probs * (prob_grad - delta)).astype(bf16)
            query_grad = dot(score_grad, k_in[:extent, :]) * scale
            k_acc[:extent, :] += contract_rows(score_grad, query) * scale
            v_acc[:extent, :] += contract_rows(probs.astype(bf16), grad)
            back, gain_part, part_inner = unrope(
                query_grad, proj[start:extent, of_head], q_gain, start
            )
            grads[start:extent, of_head] = back
            q_total = q_total + gain_part
            inner_sum = inner_sum + part_inner
        inner[start:extent, :] = inner_sum
    q_gain_part[...] = q_total
    k_total = jnp.zeros(k_gain_part.shape, f32)
    for i in range(4):
        start = i * block
        extent = start + block
        back, gain_part, part_inner = unrope(
            k_acc[start:extent, :], proj[start:extent, k_at:v_at], k_gain, start
        )
        grads[start:extent, k_at:v_at] = back
        k_total = k_total + gain_part
        v_back = v_acc[start:extent, :].astype(bf16)
        grads[start:extent, v_at:] = v_back
        inner[start:extent, :] += part_inner + jnp.sum(
            v_back.astype(f32) * proj[start:extent, v_at:], axis=-1, keepdims=True
        )
    k_gain_part[...] = k_total


vmem = pl.BlockSpec(memory_space=pltpu.VMEM)
smem = pl.BlockSpec(memory_space=pltpu.SMEM)
def whole_kernel(body, outs, scratch=(), grant=24):
    def call(*operands):
        return pl.pallas_call(
            body,
            out_shape=outs,
            in_specs=[smem if o.ndim == 1 else vmem for o in operands],
            out_specs=[vmem] * len(outs),
            scratch_shapes=scratch,
            compiler_params=pltpu.CompilerParams(vmem_limit_bytes=grant * 2**20),
            cost_estimate=pl.CostEstimate(flops=0, bytes_accessed=2**10, transcendentals=0),
        )(*operands)

    return call


def units_kernel(*refs):
    halves, weights, cots, downs = (refs[:4], refs[4:8]), refs[8:12], refs[12:18], refs[18:21]
    rstd_ref = refs[21]
    hidden, pair, scaled, inner = refs[22:]
    half = halves[0][0].shape[0]
    units = hidden.shape[1]
    block = min(256, half)
    chunk = min(256, units)
    for which, ins in enumerate(halves):

        def rows(i, carry, which=which, ins=ins):
            here = pl.ds(pl.multiple_of(i * block, block), block)
            at = pl.ds(pl.multiple_of(which * half + i * block, block), block)
            sides = [cots[0][at, :], cots[1][at, :]]
            sides += [c[here, :] for c in cots[2 + 2 * which : 4 + 2 * which]]
            rstd = rstd_ref[at, :]
            inner_sum = jnp.zeros((block, 1), f32)
            for start in range(0, units, chunk):
                of_gate = slice(start, start + chunk)
                of_up = slice(units + start, units + start + chunk)
                gate = dot(ins[0][here, :], weights[0][:, of_gate])
                up = dot(ins[0][here, :], weights[0][:, of_up])
                for k in range(1, 4):
                    gate = gate + dot(ins[k][here, :], weights[k][:, of_gate])
                    up = up + dot(ins[k][here, :], weights[k][:, of_up])
                gate, up = gate * rstd, up * rstd
                grad = contract_cols(sides[0], downs[0][of_gate, :])
                grad = grad + contract_cols(sides[1], downs[1][of_gate, :])
                for k in (0, 1):
                    grad = grad + contract_cols(sides[2 + k], downs[2][k, of_gate, :])
                sig = jax.nn.sigmoid(gate)
                silu = gate * sig
                hidden[at, of_gate] = low(silu * up)
                gate_grad = low(grad * up * sig * (1.0 + gate * (1.0 - sig)))
                up_grad = low(grad * silu)
                pair[at, of_gate] = gate_grad
                pair[at, of_up] = up_grad
                gate_grad, up_grad = gate_grad.astype(f32), up_grad.astype(f32)
                scaled[at, of_gate] = low(gate_grad * rstd)
                scaled[at, of_up] = low(up_grad * rstd)
                inner_sum = inner_sum + jnp.sum(
                    gate_grad * gate + up_grad * up, axis=-1, keepdims=True
                )
            inner[at, :] = inner_sum
            return carry

        lax.fori_loop(0, half // block, rows, 0)


def on_device(
    tokens,
    cotangent,
    segment_ids,
    attn_gain,
    q_gain,
    k_gain,
    mlp_gain,
    w_query,
    w_key,
    w_value,
    w_out,
    w_gate,
    w_up,
    w_down,
):
    assert lax.axis_size("tc") == 4 and lax.axis_size("tr") == 2
    col = lax.axis_index("tc")
    side = lax.axis_index("tr")
    rows, width = tokens.shape
    half = rows // 2
    full_width = width * 4
    head_size = q_gain.shape[0]
    q_width = w_query.shape[1] // 4
    k_width = w_key.shape[1] // 4
    units = w_gate.shape[1] // 4
    around = [col, col ^ 1, col ^ 2, col ^ 3]

    def cols_of(array, which, size):
        return lax.dynamic_slice_in_dim(array, around[which] * size, size, 1)

    def rows_of(array, which, size):
        return lax.dynamic_slice_in_dim(array, around[which] * size, size, 0)

    def flip(array):
        return jnp.concatenate(
            [
                lax.dynamic_slice_in_dim(array, side * half, half, 0),
                lax.dynamic_slice_in_dim(array, (1 - side) * half, half, 0),
            ],
            axis=0,
        )

    shares = lax.axis_size("dp")
    place = lax.axis_index("dp")

    def share_of(block):
        size = block.shape[0] // shares
        return lax.dynamic_slice_in_dim(block, place * size, size, 0)

    def gather_shares(from_y, from_diag):
        return lax.all_gather(jnp.stack([from_y, from_diag]), "dp", axis=1, tiled=True)

    def ffn_columns(which, rows_at):
        return jnp.concatenate(
            [rows_at(cols_of(w, which, units)) for w in (w_gate, w_up)], axis=1
        )

    down_y, down_diag = (share_of(rows_of(w_down, k, units)) for k in (2, 3))
    share_y, share_diag = ffn_columns(2, share_of), ffn_columns(3, share_of)

    qkv_weights = [
        jnp.concatenate(
            [cols_of(w_query, k, q_width), cols_of(w_key, k, k_width), cols_of(w_value, k, k_width)],
            axis=1,
        )
        for k in range(4)
    ]
    inputs = tokens.astype(f32)
    down_y, down_diag = swap_y(down_y), swap_diag(down_diag)
    share_y, share_diag, inputs = after((share_y, share_diag, inputs), down_y, down_diag)
    scaled_in = low(inputs * attn_gain[None, :])
    raw_own, raw_y, for_y = scatter_width(lambda k: dot(scaled_in, qkv_weights[k]))
    down_gathered = gather_shares(down_y, down_diag)
    w_gate, w_up, w_down, w_out, segment_ids, cotangent, inputs = after(
        (w_gate, w_up, w_down, w_out, segment_ids, cotangent, inputs), for_y
    )
    square_sum = width_total(jnp.sum(inputs * inputs, axis=1))
    cos_table, sin_table = rope_tables(positions_of(segment_ids), head_size)
    side_word = side.astype(jnp.int32).reshape(1)
    tables = (
        cos_table,
        sin_table,
        segment_ids.reshape(rows, 1),
        segment_ids.reshape(1, rows),
        q_gain.reshape(1, head_size),
        k_gain.reshape(1, head_size),
    )
    whole = lambda block: block
    blocks_core = (ffn_columns(1, whole), rows_of(w_down, 1, units))
    raw_y, share_y, share_diag, square_sum = after(
        (raw_y, swap_y(share_y), swap_diag(share_diag), square_sum), raw_own, tables, blocks_core
    )
    ffn_y, ffn_diag = (lax.all_gather(w, "dp", axis=0, tiled=True) for w in (share_y, share_diag))
    attn_rstd = lax.rsqrt(square_sum / full_width + norm_eps)
    attn_hat = inputs * attn_rstd[:, None]
    normed = low(attn_hat * attn_gain[None, :])

    heads = q_width // head_size
    projected, q_low, k_low, v_low, log_totals, att_rel = whole_kernel(
        attend_kernel,
        [
            jax.ShapeDtypeStruct((rows, q_width + 2 * k_width), f32),
            jax.ShapeDtypeStruct((rows, q_width), bf16),
            jax.ShapeDtypeStruct((rows, k_width), bf16),
            jax.ShapeDtypeStruct((rows, k_width), bf16),
            jax.ShapeDtypeStruct((rows, heads), f32),
            jax.ShapeDtypeStruct((rows, q_width), bf16),
        ],
    )(side_word, raw_own, raw_y, attn_rstd.reshape(rows, 1), *tables)
    cot_rel = flip(cotangent)
    cot_y = swap_y(after(cot_rel[:half], raw_y))
    att_y, cot_x, down_gathered = after((swap_y(att_rel), swap_x(cot_y), down_gathered), att_rel)
    atts = [att_rel, swap_core(att_rel), att_y, swap_core(att_y)]
    outs = [rows_of(w_out, k, q_width) for k in range(4)]

    def out_rows(at):
        return (dot(atts[0][at], outs[0]) + dot(atts[1][at], outs[1])) + (
            dot(atts[2][at], outs[2]) + dot(atts[3][at], outs[3])
        )

    from_x = swap_x(low(out_rows(slice(half, rows))))
    home = out_rows(slice(0, half))

    prefetched = (
        swap_core(cot_rel),
        *map(swap_core, blocks_core),
    )
    from_x, (cot_core, ffn_core, down_core), ffn_y = after((from_x, prefetched, ffn_y), home)
    cot_y_core, cot_x_core = swap_core(cot_y), swap_core(cot_x)
    downs = (rows_of(w_down, 0, units), down_core, down_gathered)
    tokens_half = lax.dynamic_slice_in_dim(tokens, side * half, half, 0).astype(f32)
    residual = tokens_half + home + from_x.astype(f32)

    mlp_square = jnp.sum(residual * residual, axis=1)
    mlp_square = width_total(jnp.concatenate([mlp_square, swap_x(mlp_square)]))
    mlp_own = low(residual * mlp_gain[None, :])
    mlp_rstd = lax.rsqrt(mlp_square / full_width + norm_eps)
    quarter = half // 2
    mlp_x, mlp_y, mlp_rstd = after(
        (swap_x(mlp_own), swap_y(mlp_own), mlp_rstd), cot_y_core, cot_x_core
    )
    mlp_xy, ffn_diag = after(((swap_y(mlp_x[:quarter]), swap_x(mlp_y[quarter:])), ffn_diag), ())
    mlp_xy = jnp.concatenate(mlp_xy, axis=0)
    ins_own = [mlp_own, swap_core(mlp_own), mlp_y, swap_core(mlp_y)]
    ins_other = [mlp_x, swap_core(mlp_x), mlp_xy, swap_core(mlp_xy)]
    ffns = [ffn_columns(0, whole), ffn_core, ffn_y, ffn_diag]
    downs = [rows_of(w_down, 0, units), down_core, down_gathered]
    hidden, pair, pair_scaled, inner = whole_kernel(
        units_kernel,
        [
            jax.ShapeDtypeStruct((rows, units), bf16),
            jax.ShapeDtypeStruct((rows, 2 * units), bf16),
            jax.ShapeDtypeStruct((rows, 2 * units), bf16),
            jax.ShapeDtypeStruct((rows, 1), f32),
        ],
        grant=32,
    )(
        *ins_own,
        *ins_other,
        *ffns,
        cot_rel,
        cot_core,
        cot_y,
        cot_y_core,
        cot_x,
        cot_x_core,
        *downs,
        mlp_rstd.reshape(rows, 1),
    )

    mlp_in, mlp_core = (jnp.concatenate([ins_own[k], ins_other[k]], axis=0) for k in (0, 1))
    kept = {"inner": inner[:, 0]}

    def between(k, marker):
        sums = after(kept["inner"], marker)
        if k < 2:
            kept["inner"] = sums + (swap_core, swap_y)[k](sums)
        else:
            kept["inner"] = sums[:half] + swap_x(sums[half:])
        return kept["inner"] if k > 0 else marker

    def started(marker):
        block = low(contract_rows(mlp_core, after(pair_scaled, marker)))
        kept["core"] = swap_core(block)
        kept["own"] = low(contract_rows(mlp_in, after(pair_scaled, block)))
        down_core = low(contract_rows(cot_core, after(hidden, kept["own"])))
        down_own = low(contract_rows(cot_rel, after(hidden, kept["own"])))
        kept["down"] = [down_own, swap_core(down_core)]
        return down_own

    mlp_in_grad = scatter_all(
        lambda k, marker: contract_cols(after(pair, marker), ffns[k]), between, started
    )
    inner_total = kept["inner"]
    early_width = width + width // 4
    early = [kept["own"], kept["core"][:, :early_width]]
    early = lax.psum(early, "dp")
    pairs = lax.all_gather(after(pair_scaled, mlp_in_grad), "tc")
    mlp_hat = residual * mlp_rstd[:half, None]
    mlp_gain_part = jnp.sum(mlp_in_grad * mlp_hat, axis=0)
    residual_grad = cot_rel[:half].astype(f32) + mlp_rstd[:half, None] * (
        mlp_in_grad * mlp_gain[None, :] - mlp_hat * (inner_total / full_width)[:, None]
    )
    residual_low = low(residual_grad)
    res_x = swap_x(residual_low)
    res_rel = jnp.concatenate([residual_low, res_x], axis=0)
    head_own, head_y, head_sent = scatter_width(lambda k: contract_cols(res_rel, outs[k]))
    out_grads = [low(contract_rows(res_rel, after(part, head_sent))) for part in atts]
    head_own, head_y = after((head_own, head_y), out_grads)

    proj_low, q_gain_part, k_gain_part, inner_attn = whole_kernel(
        attend_back_kernel,
        [
            jax.ShapeDtypeStruct((rows, q_width + 2 * k_width), bf16),
            jax.ShapeDtypeStruct((1, head_size), f32),
            jax.ShapeDtypeStruct((1, head_size), f32),
            jax.ShapeDtypeStruct((rows, 1), f32),
        ],
        scratch=[pltpu.VMEM((rows, k_width), f32), pltpu.VMEM((rows, k_width), f32)],
    )(side_word, head_own, head_y, projected, q_low, k_low, v_low, log_totals, *tables)
    proj_y, proj_core = swap_y(proj_low), swap_core(proj_low)

    line = LineSums(width)
    for k in (0, 1):
        line.add(("down", k), kept["down"][k])
    for k in range(4):
        line.add(("out", k), out_grads[k])
    line.add(("ffn", 1), kept["core"][:, early_width:])
    hiddens = lax.all_gather(after(hidden, proj_low), "tc", axis=1, tiled=True)
    marker = proj_low
    for _ in range(4):
        marker = line.send(marker)
    proj_y, proj_core = after((proj_y, proj_core), marker)
    projs = [proj_low, proj_core, proj_y, swap_core(proj_y)]
    normed_part = low(
        (contract_cols(projs[0], qkv_weights[0]) + contract_cols(projs[1], qkv_weights[1]))
        + (contract_cols(projs[2], qkv_weights[2]) + contract_cols(projs[3], qkv_weights[3]))
    )
    small = jnp.concatenate([inner_attn[:, 0], q_gain_part[0], k_gain_part[0]])
    small = width_total(after(small, normed_part))
    small = jnp.concatenate([small, mlp_gain_part])
    normed_x, small_x = after((swap_x(normed_part), swap_x(small)), line.send(small))
    small = small + small_x
    inner_attn, gains = small[:rows], small[rows:]
    normed_grad = normed_part.astype(f32) + normed_x.astype(f32)
    token_grad = low(
        flip(res_rel).astype(f32)
        + attn_rstd[:, None]
        * (normed_grad * attn_gain[None, :] - attn_hat * (inner_attn / full_width)[:, None])
    )

    for k, part in enumerate(projs):
        line.add(("qkv", k), low(contract_rows(after(normed, normed_part), part)))
    spare = jnp.pad(low(gains), (0, width * width // 4 - gains.shape[0]))
    line.add("gains", spare.reshape(width, width // 4))
    marker = line.send((token_grad, line.waiting()))
    for _ in range(5):
        marker = line.send(marker)
    pairs, early = after((pairs, early), marker)
    for k in (2, 3):
        block = lax.dynamic_index_in_dim(pairs, around[k], 0, keepdims=False)
        line.add(("ffn", k), low(contract_rows(mlp_in, block)))
    for _ in range(5):
        marker = line.send(marker)

    hiddens = after(hiddens, marker)
    for k in (2, 3):
        line.add(("down", k), low(contract_rows(cot_rel, cols_of(hiddens, k, units))))
    mlp_away = low(dot(hiddens[half:], w_down))
    mlp_x_out = after(swap_x(mlp_away), line.send(mlp_away))
    mixed_half = low(residual + dot(hiddens[:half], w_down) + mlp_x_out.astype(f32))
    mixed_x = after(swap_x(mixed_half), line.send(mixed_half))
    mixed = flip(jnp.concatenate([mixed_half, mixed_x], axis=0))
    marker = mixed_x
    while line.stream:
        marker = line.send(marker)
    sums_of = line.finish()

    gains = sums_of("gains").reshape(-1)[: gains.shape[0]].astype(f32)
    q_gain_grad = gains[:head_size]
    k_gain_grad = gains[head_size : 2 * head_size]
    mlp_gain_grad = gains[2 * head_size :]

    def place_cols(shape, pieces):
        whole = jnp.zeros(shape, f32)
        for which, piece in enumerate(pieces):
            whole = lax.dynamic_update_slice_in_dim(
                whole, piece.astype(f32), around[which] * piece.shape[1], 1
            )
        return whole

    def place_rows(shape, pieces):
        whole = jnp.zeros(shape, f32)
        for which, piece in enumerate(pieces):
            whole = lax.dynamic_update_slice_in_dim(
                whole, piece.astype(f32), around[which] * piece.shape[0], 0
            )
        return whole

    qkv_grads = [sums_of(("qkv", k)) for k in range(4)]
    attn_gain_part = sum(
        jnp.sum(w.astype(f32) * g.astype(f32), axis=1) for w, g in zip(qkv_weights, qkv_grads)
    )
    attn_gain_grad = (attn_gain_part + swap_x(attn_gain_part)) / attn_gain
    w_query_grad = place_cols(w_query.shape, [g[:, :q_width] for g in qkv_grads])
    w_key_grad = place_cols(w_key.shape, [g[:, q_width : q_width + k_width] for g in qkv_grads])
    w_value_grad = place_cols(w_value.shape, [g[:, q_width + k_width :] for g in qkv_grads])
    w_out_grad = place_rows(w_out.shape, [sums_of(("out", k)).T for k in range(4)])
    w_down_grad = place_rows(w_down.shape, [sums_of(("down", k)).T for k in range(4)])
    core_grad = jnp.concatenate([early[1], sums_of(("ffn", 1))], axis=1)
    ffn_grads = [early[0], core_grad] + [sums_of(("ffn", k)) for k in (2, 3)]
    w_gate_grad = place_cols(w_gate.shape, [g[:, :units] for g in ffn_grads])
    w_up_grad = place_cols(w_up.shape, [g[:, units:] for g in ffn_grads])
    return (
        mixed,
        token_grad,
        attn_gain_grad,
        q_gain_grad,
        k_gain_grad,
        mlp_gain_grad,
        w_query_grad,
        w_key_grad,
        w_value_grad,
        w_out_grad,
        w_gate_grad,
        w_up_grad,
        w_down_grad,
    )


def solution(mesh):
    in_specs = (
        P("dp", "tc"),
        P("dp", "tc"),
        P("dp"),
        P("tc"),
        P(),
        P(),
        P("tc"),
        P("tc", "tr"),
        P("tc", "tr"),
        P("tc", "tr"),
        P("tr", "tc"),
        P("tc", "tr"),
        P("tc", "tr"),
        P("tr", "tc"),
    )
    out_specs = (
        P("dp", "tc"),
        P("dp", "tc"),
        P("tc"),
        P(),
        P(),
        P("tc"),
        P("tc", "tr"),
        P("tc", "tr"),
        P("tc", "tr"),
        P("tr", "tc"),
        P("tc", "tr"),
        P("tc", "tr"),
        P("tr", "tc"),
    )
    return jax.shard_map(
        on_device, mesh=mesh, in_specs=in_specs, out_specs=out_specs, check_vma=False
    )
```

```python
import jax
import jax.numpy as jnp
from jax import lax
from jax.experimental import pallas as pl
from jax.experimental.pallas import tpu as pltpu
from jax.sharding import PartitionSpec as P

norm_eps = 1e-06
rope_base = 1000000.0
neg_big = -1e30
f32 = jnp.float32
bf16 = jnp.bfloat16


def dot(left_side, right_side):
    return jnp.dot(left_side, right_side, preferred_element_type=f32)


def contract_rows(left_side, right_side):
    return lax.dot_general(
        left_side, right_side, (((0,), (0,)), ((), ())), preferred_element_type=f32
    )


def contract_cols(left_side, right_side):
    return lax.dot_general(
        left_side, right_side, (((1,), (1,)), ((), ())), preferred_element_type=f32
    )


def swap_core(block):
    return lax.ppermute(block, "tc", [(i, i ^ 1) for i in range(4)])


def swap_y(block):
    return lax.ppermute(block, "tc", [(i, i ^ 2) for i in range(4)])


def swap_diag(block):
    return lax.ppermute(block, "tc", [(i, i ^ 3) for i in range(4)])


def swap_x(block):
    return lax.ppermute(block, "tr", [(0, 1), (1, 0)])


def width_total(rows):
    rows = rows + swap_core(rows)
    return rows + swap_y(rows)


class LineSums:
    def __init__(self):
        self.short = lax.axis_size("dp") == 4
        place = lax.axis_index("dp")
        self.middle = (place == 1) | (place == 2)
        self.queue, self.names, self.pieces = [], [], []
        self.outer, self.total = [], []

    def add(self, name, grad, axis):
        size = min(grad.shape)
        for k in range(0, grad.shape[axis], size):
            self.queue.append((name, lax.slice_in_dim(grad, k, k + size, axis=axis)))

    def waiting(self):
        return [piece for _, piece in self.queue]

    def _consume(self, which, marker):
        got, piece = after((self.outer[which], self.pieces[which]), marker)
        inward = low(piece.astype(f32) + got.astype(f32))
        across = lax.ppermute(inward, "dp", [(1, 2), (2, 1)])
        self.total.append(low(inward.astype(f32) + across.astype(f32)))
        return inward

    def _swap_outer(self, piece):
        self.outer.append(lax.ppermute(piece, "dp", [(0, 1), (1, 0), (2, 3), (3, 2)]))

    def send(self, marker=()):
        which = len(self.pieces)
        name, piece = self.queue.pop(0)
        self.names.append(name)
        self.pieces.append(piece)
        if not self.short:
            return piece
        if which >= 2:
            marker = self._consume(which - 2, marker)
        out = after(piece, marker)
        if which >= 3:
            out = jnp.where(self.middle, self.total[which - 3], out)
        self._swap_outer(out)
        return marker

    def finish(self):
        count = len(self.pieces)
        if self.short:
            for which in (count - 2, count - 1):
                self._consume(which, ())
            for which in range(count - 3, count):
                self._swap_outer(self.total[which])
            sums = [(self.total[k], self.outer[k + 3]) for k in range(count)]
        else:
            sums = [(lax.psum(piece, "dp"),) for piece in self.pieces]
        return lambda name: [s for n, s in zip(self.names, sums) if n == name]


def after(value, *others):
    return lax.optimization_barrier((value, others))[0]


def low(array):
    return array.astype(bf16)


def scatter_width(product, near=lambda ready: ready):
    from_far = swap_core(low(product(3)))
    from_core = swap_core(low(product(1)))
    from_far = after(from_far, near(from_far))
    for_y = low(product(2) + from_far.astype(f32))
    from_y = swap_y(for_y)
    return (product(0) + from_core.astype(f32), from_y, for_y)


def scatter_all(product, started, turned):
    far_y, far_own = swap_core(low(product(3))), swap_core(low(product(1)))
    for_y = low(product(2) + far_y.astype(f32))
    own = low(product(0) + far_own.astype(f32))
    half = own.shape[0] // 2
    quarter = half // 2
    width = own.shape[1]
    y_first = swap_y(jnp.concatenate([for_y[quarter:half], for_y[half + quarter :]], axis=0))
    x_first = swap_x(
        jnp.concatenate([own[half : half + quarter], for_y[half : half + quarter]], axis=1)
    )
    x_first, y_first = after((x_first, y_first), started((own, for_y)))
    top_in = low(for_y[:quarter].astype(f32) + x_first[:, width:].astype(f32))
    low_in = low(own[half + quarter :].astype(f32) + y_first[quarter:].astype(f32))
    top_y, low_x = after((swap_y(top_in), swap_x(low_in)), turned((top_in, low_in)))
    top = own[:quarter].astype(f32) + x_first[:, :width].astype(f32) + top_y.astype(f32)
    bottom = own[quarter:half].astype(f32) + y_first[:quarter].astype(f32) + low_x.astype(f32)
    return jnp.concatenate([top, bottom], axis=0)


def positions_of(segment):
    slot_ids = jnp.arange(5, dtype=jnp.int32)
    before = jnp.sum((segment[None, :] < slot_ids[:, None]).astype(jnp.int32), axis=1)
    starts = jnp.sum(jnp.where(segment[:, None] == slot_ids[None, :], before[None, :], 0), axis=1)
    return jnp.arange(segment.shape[0], dtype=jnp.int32) - starts


def rope_tables(positions, head_size):
    half_size = head_size // 2
    frequency = rope_base ** (-jnp.arange(half_size, dtype=f32) * 2.0 / head_size)
    angles = positions.astype(f32)[:, None] * frequency[None, :]
    cosine, sine = jnp.cos(angles), jnp.sin(angles)
    return (
        jnp.concatenate([cosine, cosine], axis=1),
        jnp.concatenate([-sine, sine], axis=1),
    )


def turn(vectors):
    return pltpu.roll(vectors, vectors.shape[-1] // 2, axis=1)


def inverse_norm(vectors):
    return lax.rsqrt(jnp.mean(vectors * vectors, axis=-1, keepdims=True) + norm_eps)


def allowed_keys(seg_col, seg_row, start, size, extent):
    row = lax.broadcasted_iota(jnp.int32, (size, extent), 0) + start
    col = lax.broadcasted_iota(jnp.int32, (size, extent), 1)
    return (seg_col[start : start + size, :] == seg_row[:, :extent]) & (col <= row)


def attend_kernel(
    side, own, from_y, rstd, cos, sin, seg_col, seg_row, q_gain, k_gain,
    proj, q_out, k_out, v_out, lse, att,
):
    rows = own.shape[0]
    size = cos.shape[1]
    heads = q_out.shape[1] // size
    block = rows // 4
    scale = size**-0.5
    k_at = heads * size
    v_at = k_at + size

    def ready(i, carry):
        at = pl.ds(pl.multiple_of(i * block, block), block)
        raw = (own[at, :] + from_y[at, :].astype(f32)) * rstd[at, :]
        proj[at, :] = raw

        def rope(part, gain):
            n = part * inverse_norm(part) * gain[...]
            return (n * cos[at, :] + turn(n) * sin[at, :]).astype(bf16)

        for h in range(heads):
            q_out[at, h * size : (h + 1) * size] = rope(raw[:, h * size : (h + 1) * size], q_gain)
        k_out[at, :] = rope(raw[:, k_at:v_at], k_gain)
        v_out[at, :] = raw[:, v_at:].astype(bf16)
        return carry

    lax.fori_loop(0, 4, ready, 0)
    for i in range(4):
        start = i * block
        extent = start + block
        allowed = allowed_keys(seg_col, seg_row, start, block, extent)
        to = pl.ds(pl.multiple_of(lax.rem(start + side[0] * (rows // 2), rows), block), block)
        for h in range(heads):
            of_head = slice(h * size, (h + 1) * size)
            scores = contract_cols(q_out[start:extent, of_head], k_out[:extent, :]) * scale
            scores = jnp.where(allowed, scores, neg_big)
            top = jnp.max(scores, axis=-1, keepdims=True)
            expd = jnp.exp(scores - top)
            total = jnp.sum(expd, axis=-1, keepdims=True)
            weights = (expd * (1.0 / total)).astype(bf16)
            att[to, of_head] = dot(weights, v_out[:extent, :]).astype(bf16)
            lse[start:extent, h : h + 1] = top + jnp.log(total)


def attend_back_kernel(
    side, own, from_y, proj, q_in, k_in, v_in, lse, cos, sin, seg_col, seg_row, q_gain, k_gain,
    grads, q_gain_part, k_gain_part, inner, k_acc, v_acc,
):
    rows = own.shape[0]
    size = cos.shape[1]
    heads = q_in.shape[1] // size
    block = rows // 4
    scale = size**-0.5
    k_at = heads * size
    v_at = k_at + size

    def unrope(grad, part, gain, start):
        rows_at = slice(start, start + block)
        m = grad * cos[rows_at, :] - turn(grad) * sin[rows_at, :]
        r = inverse_norm(part)
        hat = part * r
        mg = m * gain[...]
        back = (r * (mg - hat * jnp.mean(mg * hat, axis=-1, keepdims=True))).astype(bf16)
        gain_part = jnp.sum(m * hat, axis=0, keepdims=True)
        return (back, gain_part, jnp.sum(back.astype(f32) * part, axis=-1, keepdims=True))

    k_acc[...] = jnp.zeros_like(k_acc)
    v_acc[...] = jnp.zeros_like(v_acc)
    q_total = jnp.zeros(q_gain_part.shape, f32)
    for i in range(4):
        start = i * block
        extent = start + block
        allowed = allowed_keys(seg_col, seg_row, start, block, extent)
        at = pl.ds(pl.multiple_of(lax.rem(start + side[0] * (rows // 2), rows), block), block)
        inner_sum = jnp.zeros((block, 1), f32)
        for h in range(heads):
            of_head = slice(h * size, (h + 1) * size)
            query = q_in[start:extent, of_head]
            grad = (own[at, of_head] + from_y[at, of_head].astype(f32)).astype(bf16)
            scores = contract_cols(query, k_in[:extent, :]) * scale
            scores = jnp.where(allowed, scores, neg_big)
            probs = jnp.exp(scores - lse[start:extent, h : h + 1])
            prob_grad = contract_cols(grad, v_in[:extent, :])
            delta = jnp.sum(probs * prob_grad, axis=-1, keepdims=True)
            score_grad = (probs * (prob_grad - delta)).astype(bf16)
            query_grad = dot(score_grad, k_in[:extent, :]) * scale
            k_acc[:extent, :] += contract_rows(score_grad, query) * scale
            v_acc[:extent, :] += contract_rows(probs.astype(bf16), grad)
            back, gain_part, part_inner = unrope(
                query_grad, proj[start:extent, of_head], q_gain, start
            )
            grads[start:extent, of_head] = back
            q_total = q_total + gain_part
            inner_sum = inner_sum + part_inner
        inner[start:extent, :] = inner_sum
    q_gain_part[...] = q_total
    k_total = jnp.zeros(k_gain_part.shape, f32)
    for i in range(4):
        start = i * block
        extent = start + block
        back, gain_part, part_inner = unrope(
            k_acc[start:extent, :], proj[start:extent, k_at:v_at], k_gain, start
        )
        grads[start:extent, k_at:v_at] = back
        k_total = k_total + gain_part
        v_back = v_acc[start:extent, :].astype(bf16)
        grads[start:extent, v_at:] = v_back
        inner[start:extent, :] += part_inner + jnp.sum(
            v_back.astype(f32) * proj[start:extent, v_at:], axis=-1, keepdims=True
        )
    k_gain_part[...] = k_total


vmem = pl.BlockSpec(memory_space=pltpu.VMEM)
smem = pl.BlockSpec(memory_space=pltpu.SMEM)
def whole_kernel(body, outs, scratch=(), grant=50):
    def call(*operands):
        return pl.pallas_call(
            body,
            out_shape=outs,
            in_specs=[smem if o.ndim == 1 else vmem for o in operands],
            out_specs=[vmem] * len(outs),
            scratch_shapes=scratch,
            compiler_params=pltpu.CompilerParams(vmem_limit_bytes=grant * 2**20),
            cost_estimate=pl.CostEstimate(flops=0, bytes_accessed=2**10, transcendentals=0),
        )(*operands)

    return call


def units_kernel(*refs):
    ins, weights, cots, downs = refs[:4], refs[4:8], refs[8:12], refs[12:16]
    rstd_ref = refs[16]
    hidden, pair, scaled, inner = refs[-4:]
    units = hidden.shape[1]
    chunk = min(256, units)
    rstd = rstd_ref[...]

    def product(at):
        total = dot(ins[0][...], weights[0][:, at])
        for k in range(1, 4):
            total = total + dot(ins[k][...], weights[k][:, at])
        return total * rstd

    inner_sum = jnp.zeros(inner.shape, f32)
    for start in range(0, units, chunk):
        of_gate = slice(start, start + chunk)
        of_up = slice(units + start, units + start + chunk)
        gate, up = product(of_gate), product(of_up)
        grad = contract_cols(cots[0][...], downs[0][of_gate, :])
        for k in range(1, 4):
            grad = grad + contract_cols(cots[k][...], downs[k][of_gate, :])
        sig = jax.nn.sigmoid(gate)
        silu = gate * sig
        hidden[:, of_gate] = low(silu * up)
        gate_grad = low(grad * up * sig * (1.0 + gate * (1.0 - sig)))
        up_grad = low(grad * silu)
        pair[:, of_gate] = gate_grad
        pair[:, of_up] = up_grad
        gate_grad, up_grad = gate_grad.astype(f32), up_grad.astype(f32)
        scaled[:, of_gate] = low(gate_grad * rstd)
        scaled[:, of_up] = low(up_grad * rstd)
        inner_sum = inner_sum + jnp.sum(gate_grad * gate + up_grad * up, axis=-1, keepdims=True)
    inner[...] = inner_sum


def units_of_half(ins, weights, cots, downs, rstd, which, earlier):
    half, depth = ins[0].shape
    units = downs[0].shape[0]
    block = half // 2
    first = which * (half // block)
    outs = [
        jax.ShapeDtypeStruct((2 * half, units), bf16),
        jax.ShapeDtypeStruct((2 * half, 2 * units), bf16),
        jax.ShapeDtypeStruct((2 * half, 2 * units), bf16),
        jax.ShapeDtypeStruct((2 * half, 1), f32),
    ]

    def whole(array):
        return pl.BlockSpec(array.shape, lambda i: (0, 0))

    def of_two(array, k):
        return pl.BlockSpec((None, *array.shape[1:]), lambda i: (k, 0, 0))

    near_by, core, both = downs
    downs = [near_by, core, both, both]
    down_specs = [whole(near_by), whole(core), of_two(both, 0), of_two(both, 1)]
    here = pl.BlockSpec((block, depth), lambda i: (i, 0))
    at = lambda i: (first + i, 0)
    of_all = pl.BlockSpec((block, depth), at)
    earlier = list(earlier or [])
    return pl.pallas_call(
        units_kernel,
        grid=(half // block,),
        out_shape=outs,
        in_specs=[here] * 4
        + [whole(w) for w in weights]
        + [of_all, of_all, here, here]
        + down_specs
        + [pl.BlockSpec((block, 1), at)]
        + [pl.BlockSpec(memory_space=pl.ANY)] * len(earlier),
        out_specs=[pl.BlockSpec((block, o.shape[1]), at) for o in outs],
        input_output_aliases={17 + k: k for k in range(len(earlier))},
        compiler_params=pltpu.CompilerParams(vmem_limit_bytes=50 * 2**20),
        cost_estimate=pl.CostEstimate(flops=0, bytes_accessed=2**10, transcendentals=0),
    )(*ins, *weights, *cots, *downs, rstd, *earlier)


def place_sums(scalars, pieces, outs, plan):
    flat = [a for piece in pieces for a in piece]

    def kernel(words, *refs):
        ins, results = list(refs[: len(flat)]), refs[len(flat) :]
        groups = [[ins.pop(0) for _ in piece] for piece in pieces]
        for k in range(4):

            @pl.when(pl.program_id(0) == k)
            def _(k=k):
                for piece, at, out, to in plan[k]:
                    value = groups[piece][0][at]
                    if len(groups[piece]) == 2:
                        value = jnp.where(words[4] == 1, value, groups[piece][1][at])
                    results[out][to] = value.astype(f32)

    def quarter(shape, axis):
        block = tuple(n // 4 if i == axis else n for i, n in enumerate(shape))
        if axis == 0:
            return pl.BlockSpec(block, lambda k, words: (words[k], 0))
        return pl.BlockSpec(block, lambda k, words: (0, words[k]))

    return pl.pallas_call(
        kernel,
        grid_spec=pltpu.PrefetchScalarGridSpec(
            num_scalar_prefetch=1,
            grid=(4,),
            in_specs=[pl.BlockSpec(a.shape, lambda k, words: (0, 0)) for a in flat],
            out_specs=[quarter(*out) for out in outs],
        ),
        out_shape=[jax.ShapeDtypeStruct(shape, f32) for shape, _ in outs],
        compiler_params=pltpu.CompilerParams(vmem_limit_bytes=50 * 2**20),
        cost_estimate=pl.CostEstimate(flops=0, bytes_accessed=2**10, transcendentals=0),
    )(scalars, *flat)


def on_device(
    tokens,
    cotangent,
    segment_ids,
    attn_gain,
    q_gain,
    k_gain,
    mlp_gain,
    w_query,
    w_key,
    w_value,
    w_out,
    w_gate,
    w_up,
    w_down,
):
    assert lax.axis_size("tc") == 4 and lax.axis_size("tr") == 2
    col = lax.axis_index("tc")
    side = lax.axis_index("tr")
    rows, width = tokens.shape
    half = rows // 2
    full_width = width * 4
    head_size = q_gain.shape[0]
    q_width = w_query.shape[1] // 4
    k_width = w_key.shape[1] // 4
    units = w_gate.shape[1] // 4
    around = [col, col ^ 1, col ^ 2, col ^ 3]

    def cols_of(array, which, size):
        return lax.dynamic_slice_in_dim(array, around[which] * size, size, 1)

    def rows_of(array, which, size):
        return lax.dynamic_slice_in_dim(array, around[which] * size, size, 0)

    def flip(array):
        return jnp.concatenate(
            [
                lax.dynamic_slice_in_dim(array, side * half, half, 0),
                lax.dynamic_slice_in_dim(array, (1 - side) * half, half, 0),
            ],
            axis=0,
        )

    shares = lax.axis_size("dp")
    place = lax.axis_index("dp")

    def share_of(block):
        size = block.shape[0] // shares
        return lax.dynamic_slice_in_dim(block, place * size, size, 0)

    def gather_shares(from_y, from_diag):
        return lax.all_gather(jnp.stack([from_y, from_diag]), "dp", axis=1, tiled=True)

    def ffn_columns(which, rows_at):
        return jnp.concatenate(
            [rows_at(cols_of(w, which, units)) for w in (w_gate, w_up)], axis=1
        )

    down_y, down_diag = (share_of(rows_of(w_down, k, units)) for k in (2, 3))
    share_y, share_diag = ffn_columns(2, share_of), ffn_columns(3, share_of)

    qkv_weights = [
        jnp.concatenate(
            [cols_of(w_query, k, q_width), cols_of(w_key, k, k_width), cols_of(w_value, k, k_width)],
            axis=1,
        )
        for k in range(4)
    ]
    inputs = tokens.astype(f32)
    down_y, down_diag = swap_y(down_y), swap_diag(down_diag)
    share_y, share_diag, inputs = after((share_y, share_diag, inputs), down_y, down_diag)
    scaled_in = low(inputs * attn_gain[None, :])
    raw_own, raw_y, for_y = scatter_width(lambda k: dot(scaled_in, qkv_weights[k]))
    down_gathered = gather_shares(down_y, down_diag)
    w_gate, w_up, w_down, w_out, segment_ids, cotangent, inputs = after(
        (w_gate, w_up, w_down, w_out, segment_ids, cotangent, inputs), for_y
    )
    square_sum = width_total(jnp.sum(inputs * inputs, axis=1))
    cos_table, sin_table = rope_tables(positions_of(segment_ids), head_size)
    side_word = side.astype(jnp.int32).reshape(1)
    tables = (
        cos_table,
        sin_table,
        segment_ids.reshape(rows, 1),
        segment_ids.reshape(1, rows),
        q_gain.reshape(1, head_size),
        k_gain.reshape(1, head_size),
    )
    whole = lambda block: block
    blocks_core = (ffn_columns(1, whole), rows_of(w_down, 1, units))
    raw_y, share_y, share_diag, square_sum = after(
        (raw_y, swap_y(share_y), swap_diag(share_diag), square_sum), raw_own, tables, blocks_core
    )
    ffn_y, ffn_diag = (lax.all_gather(w, "dp", axis=0, tiled=True) for w in (share_y, share_diag))
    attn_rstd = lax.rsqrt(square_sum / full_width + norm_eps)
    attn_hat = inputs * attn_rstd[:, None]
    normed = low(attn_hat * attn_gain[None, :])

    heads = q_width // head_size
    projected, q_low, k_low, v_low, log_totals, att_rel = whole_kernel(
        attend_kernel,
        [
            jax.ShapeDtypeStruct((rows, q_width + 2 * k_width), f32),
            jax.ShapeDtypeStruct((rows, q_width), bf16),
            jax.ShapeDtypeStruct((rows, k_width), bf16),
            jax.ShapeDtypeStruct((rows, k_width), bf16),
            jax.ShapeDtypeStruct((rows, heads), f32),
            jax.ShapeDtypeStruct((rows, q_width), bf16),
        ],
    )(side_word, raw_own, raw_y, attn_rstd.reshape(rows, 1), *tables)
    cot_rel = flip(cotangent)
    cot_y = swap_y(after(cot_rel[:half], raw_y))
    att_y, cot_x, down_gathered = after((swap_y(att_rel), swap_x(cot_y), down_gathered), att_rel)
    atts = [att_rel, swap_core(att_rel), att_y, swap_core(att_y)]
    outs = [rows_of(w_out, k, q_width) for k in range(4)]

    def out_rows(at):
        return (dot(atts[0][at], outs[0]) + dot(atts[1][at], outs[1])) + (
            dot(atts[2][at], outs[2]) + dot(atts[3][at], outs[3])
        )

    from_x = swap_x(low(out_rows(slice(half, rows))))
    home = out_rows(slice(0, half))

    prefetched = (
        swap_core(cot_rel),
        *map(swap_core, blocks_core),
    )
    from_x, (cot_core, ffn_core, down_core), ffn_y = after((from_x, prefetched, ffn_y), home)
    cot_y_core, cot_x_core = swap_core(cot_y), swap_core(cot_x)
    downs = (rows_of(w_down, 0, units), down_core, down_gathered)
    tokens_half = lax.dynamic_slice_in_dim(tokens, side * half, half, 0).astype(f32)
    residual = tokens_half + home + from_x.astype(f32)

    mlp_square = jnp.sum(residual * residual, axis=1)
    mlp_square = width_total(jnp.concatenate([mlp_square, swap_x(mlp_square)]))
    mlp_own = low(residual * mlp_gain[None, :])
    mlp_rstd = lax.rsqrt(mlp_square / full_width + norm_eps)
    quarter = half // 2
    mlp_x, mlp_y, mlp_rstd = after(
        (swap_x(mlp_own), swap_y(mlp_own), mlp_rstd), cot_y_core, cot_x_core
    )
    mlp_xy = (swap_y(mlp_x[:quarter]), swap_x(mlp_y[quarter:]))
    mlp_x_core = swap_core(mlp_x)
    ffns = [ffn_columns(0, whole), ffn_core, ffn_y, ffn_diag]
    downs = [rows_of(w_down, 0, units), down_core, down_gathered]
    ins_own = [mlp_own, swap_core(mlp_own), mlp_y, swap_core(mlp_y)]
    cots_own = [cot_rel, cot_core, cot_y, cot_y_core]
    cots_other = [cot_rel, cot_core, cot_x, cot_x_core]
    rstd_rel = mlp_rstd.reshape(rows, 1)
    first = units_of_half(ins_own, ffns, cots_own, downs, rstd_rel, 0, None)
    mlp_xy, mlp_x_core = after((mlp_xy, mlp_x_core), first)
    mlp_xy = jnp.concatenate(mlp_xy, axis=0)
    ins_other = [mlp_x, mlp_x_core, mlp_xy, swap_core(mlp_xy)]
    hidden, pair, pair_scaled, inner = units_of_half(
        ins_other, ffns, cots_other, downs, rstd_rel, 1, first
    )

    mlp_in, mlp_core = (jnp.concatenate([ins_own[k], ins_other[k]], axis=0) for k in (0, 1))
    own_ffn = low(contract_rows(mlp_in, pair_scaled))
    pair = after(pair, own_ffn)
    own_ffn = lax.psum(own_ffn, "dp")

    kept = {}

    def started(marker):
        sums = width_total(after(inner[:, 0], marker))
        kept["inner"] = sums
        block = low(contract_rows(mlp_core, after(pair_scaled, marker)))
        kept["core"] = swap_core(block)
        down_core = low(contract_rows(after(hidden, block), cot_core))
        down_own = low(contract_rows(after(hidden, block), cot_rel))
        kept["down"] = [down_own, swap_core(down_core)]
        return (down_own, sums)

    def turned(marker):
        sums = after(kept["inner"], marker)
        kept["inner"] = sums[:half] + swap_x(sums[half:])
        return kept["inner"]

    mlp_in_grad = scatter_all(lambda k: contract_cols(pair, ffns[k]), started, turned)
    inner_total = kept["inner"]
    pairs = lax.all_gather(after(pair_scaled, mlp_in_grad), "tc")
    mlp_hat = residual * mlp_rstd[:half, None]
    mlp_gain_part = jnp.sum(mlp_in_grad * mlp_hat, axis=0)
    residual_grad = cot_rel[:half].astype(f32) + mlp_rstd[:half, None] * (
        mlp_in_grad * mlp_gain[None, :] - mlp_hat * (inner_total / full_width)[:, None]
    )
    residual_low = low(residual_grad)
    res_x = swap_x(residual_low)
    res_rel = jnp.concatenate([residual_low, res_x], axis=0)
    head_own, head_y, head_sent = scatter_width(lambda k: contract_cols(res_rel, outs[k]))

    line = LineSums()
    line.add("down", jnp.concatenate(kept["down"], axis=0), 0)
    line.add("ffn", kept["core"], 1)
    marker = line.send(line.send((head_sent, line.waiting())))
    out_grads = [low(contract_rows(after(part, marker), res_rel)) for part in atts]
    line.add("out", jnp.concatenate(out_grads, axis=0), 0)
    head_own, head_y = after((head_own, head_y), line.waiting())

    proj_low, q_gain_part, k_gain_part, inner_attn = whole_kernel(
        attend_back_kernel,
        [
            jax.ShapeDtypeStruct((rows, q_width + 2 * k_width), bf16),
            jax.ShapeDtypeStruct((1, head_size), f32),
            jax.ShapeDtypeStruct((1, head_size), f32),
            jax.ShapeDtypeStruct((rows, 1), f32),
        ],
        scratch=[pltpu.VMEM((rows, k_width), f32), pltpu.VMEM((rows, k_width), f32)],
    )(side_word, head_own, head_y, projected, q_low, k_low, v_low, log_totals, *tables)
    proj_y, proj_core = swap_y(proj_low), swap_core(proj_low)

    hiddens = lax.all_gather(after(hidden, proj_low), "tc", axis=1, tiled=True)
    marker = proj_low
    for _ in range(4):
        marker = line.send(marker)
    proj_y, proj_core = after((proj_y, proj_core), marker)
    projs = [proj_low, proj_core, proj_y, swap_core(proj_y)]
    normed_part = low(
        (contract_cols(projs[0], qkv_weights[0]) + contract_cols(projs[1], qkv_weights[1]))
        + (contract_cols(projs[2], qkv_weights[2]) + contract_cols(projs[3], qkv_weights[3]))
    )
    small = jnp.concatenate([inner_attn[:, 0], q_gain_part[0], k_gain_part[0]])
    small = width_total(after(small, normed_part))
    small = jnp.concatenate([small, mlp_gain_part])
    normed_x, small_x = after((swap_x(normed_part), swap_x(small)), line.send(small))
    small = small + small_x
    inner_attn, gains = small[:rows], small[rows:]
    normed_grad = normed_part.astype(f32) + normed_x.astype(f32)
    token_grad = low(
        flip(res_rel).astype(f32)
        + attn_rstd[:, None]
        * (normed_grad * attn_gain[None, :] - attn_hat * (inner_attn / full_width)[:, None])
    )

    for part in projs:
        line.add("qkv", low(contract_rows(after(normed, normed_part), part)), 1)
    marker = line.send((token_grad, line.waiting()))
    for _ in range(4):
        marker = line.send(marker)
    pairs, own_ffn = after((pairs, own_ffn), marker)
    for k in (2, 3):
        block = lax.dynamic_index_in_dim(pairs, around[k], 0, keepdims=False)
        line.add("ffn", low(contract_rows(mlp_in, block)), 1)
    for _ in range(5):
        marker = line.send(marker)

    hiddens = after(hiddens, marker)
    for k in (2, 3):
        kept["down"][k - 2] = low(contract_rows(cols_of(hiddens, k, units), cot_rel))
    line.add("down", jnp.concatenate(kept["down"], axis=0), 0)
    mlp_away = low(dot(hiddens[half:], w_down))
    mlp_x_out = after(swap_x(mlp_away), line.send(mlp_away))
    mixed_half = low(residual + dot(hiddens[:half], w_down) + mlp_x_out.astype(f32))
    mixed_x = after(swap_x(mixed_half), line.send(mixed_half))
    mixed = flip(jnp.concatenate([mixed_half, mixed_x], axis=0))
    marker = mixed_x
    while line.queue:
        marker = line.send(marker)
    sums_of = line.finish()

    words = jnp.stack([*around, line.middle.astype(jnp.int32)]).astype(jnp.int32)
    everything = slice(None)

    def spread(start, size, extent):
        while size:
            piece, at = divmod(start, extent)
            taken = min(size, extent - at)
            yield (piece, slice(at, at + taken), taken)
            start, size = start + taken, size - taken

    def runs(first, start, size, extent, out, axis, to=0):
        plan = []
        for piece, at, taken in spread(start, size, extent):
            block = slice(to, to + taken)
            pair_of = lambda part: (part, everything) if axis == 0 else (everything, part)
            plan.append((first + piece, pair_of(at), out, pair_of(block)))
            to += taken
        return plan

    ffn_sums = [(own_ffn,), *sums_of("ffn")]
    ffn_plan = [[(0, (everything, slice(0, units)), 0, (everything, everything)),
                 (0, (everything, slice(units, 2 * units)), 1, (everything, everything))]]
    for k in range(3):
        ffn_plan.append(
            runs(1, 2 * k * units, units, width, 0, 1) + runs(1, (2 * k + 1) * units, units, width, 1, 1)
        )
    w_gate_grad, w_up_grad = place_sums(words, ffn_sums, [(w_gate.shape, 1), (w_up.shape, 1)], ffn_plan)
    [w_down_grad] = place_sums(
        words,
        sums_of("down"),
        [(w_down.shape, 0)],
        [runs(0, k * units, units, width, 0, 0) for k in range(4)],
    )
    [w_out_grad] = place_sums(
        words,
        sums_of("out"),
        [(w_out.shape, 0)],
        [runs(0, k * q_width, q_width, width, 0, 0) for k in range(4)],
    )
    block_width = q_width + 2 * k_width
    qkv_plan = [
        runs(0, k * block_width, q_width, width, 0, 1)
        + runs(0, k * block_width + q_width, k_width, width, 1, 1)
        + runs(0, k * block_width + q_width + k_width, k_width, width, 2, 1)
        for k in range(4)
    ]
    qkv_sums = sums_of("qkv")
    w_query_grad, w_key_grad, w_value_grad = place_sums(
        words, qkv_sums, [(w_query.shape, 1), (w_key.shape, 1), (w_value.shape, 1)], qkv_plan
    )
    attn_gain_part = sum(
        jnp.sum(w.astype(f32) * g, axis=1)
        for w, g in ((w_query, w_query_grad), (w_key, w_key_grad), (w_value, w_value_grad))
    )
    attn_gain_grad = (attn_gain_part + swap_x(attn_gain_part)) / attn_gain
    gains = lax.psum(gains, "dp")
    q_gain_grad = gains[:head_size]
    k_gain_grad = gains[head_size : 2 * head_size]
    mlp_gain_grad = gains[2 * head_size :]
    return (
        mixed,
        token_grad,
        attn_gain_grad,
        q_gain_grad,
        k_gain_grad,
        mlp_gain_grad,
        w_query_grad,
        w_key_grad,
        w_value_grad,
        w_out_grad,
        w_gate_grad,
        w_up_grad,
        w_down_grad,
    )


def solution(mesh):
    in_specs = (
        P("dp", "tc"),
        P("dp", "tc"),
        P("dp"),
        P("tc"),
        P(),
        P(),
        P("tc"),
        P("tc", "tr"),
        P("tc", "tr"),
        P("tc", "tr"),
        P("tr", "tc"),
        P("tc", "tr"),
        P("tc", "tr"),
        P("tr", "tc"),
    )
    out_specs = (
        P("dp", "tc"),
        P("dp", "tc"),
        P("tc"),
        P(),
        P(),
        P("tc"),
        P("tc", "tr"),
        P("tc", "tr"),
        P("tc", "tr"),
        P("tr", "tc"),
        P("tc", "tr"),
        P("tc", "tr"),
        P("tr", "tc"),
    )
    return jax.shard_map(
        on_device, mesh=mesh, in_specs=in_specs, out_specs=out_specs, check_vma=False
    )
```

```python
import jax
import jax.numpy as jnp
from jax import lax
from jax.experimental import pallas as pl
from jax.experimental.pallas import tpu as pltpu
from jax.sharding import PartitionSpec as P

norm_eps = 1e-06
rope_base = 1000000.0
neg_big = -1e30
f32 = jnp.float32
bf16 = jnp.bfloat16


def dot(left_side, right_side):
    return jnp.dot(left_side, right_side, preferred_element_type=f32)


def contract_rows(left_side, right_side):
    return lax.dot_general(
        left_side, right_side, (((0,), (0,)), ((), ())), preferred_element_type=f32
    )


def contract_cols(left_side, right_side):
    return lax.dot_general(
        left_side, right_side, (((1,), (1,)), ((), ())), preferred_element_type=f32
    )


def swap_core(block):
    return lax.ppermute(block, "tc", [(i, i ^ 1) for i in range(4)])


def swap_y(block):
    return lax.ppermute(block, "tc", [(i, i ^ 2) for i in range(4)])


def swap_diag(block):
    return lax.ppermute(block, "tc", [(i, i ^ 3) for i in range(4)])


def swap_x(block):
    return lax.ppermute(block, "tr", [(0, 1), (1, 0)])


def width_total(rows):
    rows = rows + swap_core(rows)
    return rows + swap_y(rows)


class LineSums:
    def __init__(self, lag=4):
        self.lag = lag
        self.last = ()
        self.short = lax.axis_size("dp") == 4
        place = lax.axis_index("dp")
        self.middle = (place == 1) | (place == 2)
        self.queue, self.names, self.pieces = [], [], []
        self.outer, self.total = [], []

    def add(self, name, grad, axis):
        size = min(grad.shape)
        for k in range(0, grad.shape[axis], size):
            self.queue.append((name, lax.slice_in_dim(grad, k, k + size, axis=axis)))

    def waiting(self):
        return [piece for _, piece in self.queue]

    def _consume(self, which, marker):
        got, piece = after((self.outer[which], self.pieces[which]), marker)
        inward = low(piece.astype(f32) + got.astype(f32))
        across = lax.ppermute(inward, "dp", [(1, 2), (2, 1)])
        self.total.append(low(inward.astype(f32) + across.astype(f32)))
        return inward

    def _swap_outer(self, piece):
        self.outer.append(lax.ppermute(piece, "dp", [(0, 1), (1, 0), (2, 3), (3, 2)]))

    def send(self, marker=()):
        which = len(self.pieces)
        name, piece = self.queue.pop(0)
        self.names.append(name)
        self.pieces.append(piece)
        if not self.short:
            return piece
        if which >= 2:
            marker = self._consume(which - 2, marker)
        out = after(piece, marker)
        if which >= self.lag:
            out = jnp.where(self.middle, self.total[which - self.lag], out)
        self._swap_outer(out)
        return marker

    def finish(self):
        count = len(self.pieces)
        if self.short:
            for which in (count - 2, count - 1):
                self.last = self._consume(which, ())
            for which in range(count - self.lag, count):
                self._swap_outer(self.total[which])
            sums = [(self.total[k], self.outer[k + self.lag]) for k in range(count)]
        else:
            sums = [(lax.psum(piece, "dp"),) for piece in self.pieces]
        return lambda name: [s for n, s in zip(self.names, sums) if n == name]


def after(value, *others):
    return lax.optimization_barrier((value, others))[0]


def low(array):
    return array.astype(bf16)


def scatter_width(product, near=lambda ready: ready):
    from_far = swap_core(low(product(3)))
    from_core = swap_core(low(product(1)))
    from_far = after(from_far, near(from_far))
    for_y = low(product(2) + from_far.astype(f32))
    from_y = swap_y(for_y)
    return (product(0) + from_core.astype(f32), from_y, for_y)


def scatter_all(product, started, turned):
    far_y, far_own = swap_core(low(product(3))), swap_core(low(product(1)))
    for_y = low(product(2) + far_y.astype(f32))
    own = low(product(0) + far_own.astype(f32))
    half = own.shape[0] // 2
    quarter = half // 2
    width = own.shape[1]
    y_first = swap_y(jnp.concatenate([for_y[quarter:half], for_y[half + quarter :]], axis=0))
    x_first = swap_x(
        jnp.concatenate([own[half : half + quarter], for_y[half : half + quarter]], axis=1)
    )
    x_first, y_first = after((x_first, y_first), started((own, for_y)))
    top_in = low(for_y[:quarter].astype(f32) + x_first[:, width:].astype(f32))
    low_in = low(own[half + quarter :].astype(f32) + y_first[quarter:].astype(f32))
    top_y, low_x = after((swap_y(top_in), swap_x(low_in)), turned((top_in, low_in)))
    top = own[:quarter].astype(f32) + x_first[:, :width].astype(f32) + top_y.astype(f32)
    bottom = own[quarter:half].astype(f32) + y_first[:quarter].astype(f32) + low_x.astype(f32)
    return jnp.concatenate([top, bottom], axis=0)


def positions_of(segment):
    slot_ids = jnp.arange(5, dtype=jnp.int32)
    before = jnp.sum((segment[None, :] < slot_ids[:, None]).astype(jnp.int32), axis=1)
    starts = jnp.sum(jnp.where(segment[:, None] == slot_ids[None, :], before[None, :], 0), axis=1)
    return jnp.arange(segment.shape[0], dtype=jnp.int32) - starts


def rope_tables(positions, head_size):
    half_size = head_size // 2
    frequency = rope_base ** (-jnp.arange(half_size, dtype=f32) * 2.0 / head_size)
    angles = positions.astype(f32)[:, None] * frequency[None, :]
    cosine, sine = jnp.cos(angles), jnp.sin(angles)
    return (
        jnp.concatenate([cosine, cosine], axis=1),
        jnp.concatenate([-sine, sine], axis=1),
    )


def turn(vectors):
    return pltpu.roll(vectors, vectors.shape[-1] // 2, axis=1)


def inverse_norm(vectors):
    return lax.rsqrt(jnp.mean(vectors * vectors, axis=-1, keepdims=True) + norm_eps)


def allowed_keys(seg_col, seg_row, start, size, extent):
    row = lax.broadcasted_iota(jnp.int32, (size, extent), 0) + start
    col = lax.broadcasted_iota(jnp.int32, (size, extent), 1)
    return (seg_col[start : start + size, :] == seg_row[:, :extent]) & (col <= row)


def attend_kernel(
    side, own, from_y, rstd, cos, sin, seg_col, seg_row, q_gain, k_gain,
    proj, q_out, k_out, v_out, lse, att,
):
    rows = own.shape[0]
    size = cos.shape[1]
    heads = q_out.shape[1] // size
    block = rows // 4
    scale = size**-0.5
    k_at = heads * size
    v_at = k_at + size

    def ready(i, carry):
        at = pl.ds(pl.multiple_of(i * block, block), block)
        raw = (own[at, :] + from_y[at, :].astype(f32)) * rstd[at, :]
        proj[at, :] = raw

        def rope(part, gain):
            n = part * inverse_norm(part) * gain[...]
            return (n * cos[at, :] + turn(n) * sin[at, :]).astype(bf16)

        for h in range(heads):
            q_out[at, h * size : (h + 1) * size] = rope(raw[:, h * size : (h + 1) * size], q_gain)
        k_out[at, :] = rope(raw[:, k_at:v_at], k_gain)
        v_out[at, :] = raw[:, v_at:].astype(bf16)
        return carry

    lax.fori_loop(0, 4, ready, 0)
    for i in range(4):
        start = i * block
        extent = start + block
        allowed = allowed_keys(seg_col, seg_row, start, block, extent)
        to = pl.ds(pl.multiple_of(lax.rem(start + side[0] * (rows // 2), rows), block), block)
        for h in range(heads):
            of_head = slice(h * size, (h + 1) * size)
            scores = contract_cols(q_out[start:extent, of_head], k_out[:extent, :]) * scale
            scores = jnp.where(allowed, scores, neg_big)
            top = jnp.max(scores, axis=-1, keepdims=True)
            expd = jnp.exp(scores - top)
            total = jnp.sum(expd, axis=-1, keepdims=True)
            weights = (expd * (1.0 / total)).astype(bf16)
            att[to, of_head] = dot(weights, v_out[:extent, :]).astype(bf16)
            lse[start:extent, h : h + 1] = top + jnp.log(total)


def attend_back_kernel(
    side, own, from_y, proj, q_in, k_in, v_in, lse, cos, sin, seg_col, seg_row, q_gain, k_gain,
    grads, q_gain_part, k_gain_part, inner, k_acc, v_acc,
):
    rows = own.shape[0]
    size = cos.shape[1]
    heads = q_in.shape[1] // size
    block = rows // 4
    scale = size**-0.5
    k_at = heads * size
    v_at = k_at + size

    def unrope(grad, part, gain, start):
        rows_at = slice(start, start + block)
        m = grad * cos[rows_at, :] - turn(grad) * sin[rows_at, :]
        r = inverse_norm(part)
        hat = part * r
        mg = m * gain[...]
        back = (r * (mg - hat * jnp.mean(mg * hat, axis=-1, keepdims=True))).astype(bf16)
        gain_part = jnp.sum(m * hat, axis=0, keepdims=True)
        return (back, gain_part, jnp.sum(back.astype(f32) * part, axis=-1, keepdims=True))

    k_acc[...] = jnp.zeros_like(k_acc)
    v_acc[...] = jnp.zeros_like(v_acc)
    q_total = jnp.zeros(q_gain_part.shape, f32)
    for i in range(4):
        start = i * block
        extent = start + block
        allowed = allowed_keys(seg_col, seg_row, start, block, extent)
        at = pl.ds(pl.multiple_of(lax.rem(start + side[0] * (rows // 2), rows), block), block)
        inner_sum = jnp.zeros((block, 1), f32)
        for h in range(heads):
            of_head = slice(h * size, (h + 1) * size)
            query = q_in[start:extent, of_head]
            grad = (own[at, of_head] + from_y[at, of_head].astype(f32)).astype(bf16)
            scores = contract_cols(query, k_in[:extent, :]) * scale
            scores = jnp.where(allowed, scores, neg_big)
            probs = jnp.exp(scores - lse[start:extent, h : h + 1])
            prob_grad = contract_cols(grad, v_in[:extent, :])
            delta = jnp.sum(probs * prob_grad, axis=-1, keepdims=True)
            score_grad = (probs * (prob_grad - delta)).astype(bf16)
            query_grad = dot(score_grad, k_in[:extent, :]) * scale
            k_acc[:extent, :] += contract_rows(score_grad, query) * scale
            v_acc[:extent, :] += contract_rows(probs.astype(bf16), grad)
            back, gain_part, part_inner = unrope(
                query_grad, proj[start:extent, of_head], q_gain, start
            )
            grads[start:extent, of_head] = back
            q_total = q_total + gain_part
            inner_sum = inner_sum + part_inner
        inner[start:extent, :] = inner_sum
    q_gain_part[...] = q_total
    k_total = jnp.zeros(k_gain_part.shape, f32)
    for i in range(4):
        start = i * block
        extent = start + block
        back, gain_part, part_inner = unrope(
            k_acc[start:extent, :], proj[start:extent, k_at:v_at], k_gain, start
        )
        grads[start:extent, k_at:v_at] = back
        k_total = k_total + gain_part
        v_back = v_acc[start:extent, :].astype(bf16)
        grads[start:extent, v_at:] = v_back
        inner[start:extent, :] += part_inner + jnp.sum(
            v_back.astype(f32) * proj[start:extent, v_at:], axis=-1, keepdims=True
        )
    k_gain_part[...] = k_total


vmem = pl.BlockSpec(memory_space=pltpu.VMEM)
smem = pl.BlockSpec(memory_space=pltpu.SMEM)
def whole_kernel(body, outs, scratch=(), grant=50):
    def call(*operands):
        return pl.pallas_call(
            body,
            out_shape=outs,
            in_specs=[smem if o.ndim == 1 else vmem for o in operands],
            out_specs=[vmem] * len(outs),
            scratch_shapes=scratch,
            compiler_params=pltpu.CompilerParams(vmem_limit_bytes=grant * 2**20),
            cost_estimate=pl.CostEstimate(flops=0, bytes_accessed=2**10, transcendentals=0),
        )(*operands)

    return call


def units_kernel(*refs):
    ins, weights, cots, downs = refs[:4], refs[4:8], refs[8:12], refs[12:16]
    rstd_ref = refs[16]
    hidden, pair, scaled, inner = refs[-4:]
    units = hidden.shape[1]
    chunk = min(256, units)
    rstd = rstd_ref[...]

    def product(at):
        total = dot(ins[0][...], weights[0][:, at])
        for k in range(1, 4):
            total = total + dot(ins[k][...], weights[k][:, at])
        return total * rstd

    inner_sum = jnp.zeros(inner.shape, f32)
    for start in range(0, units, chunk):
        of_gate = slice(start, start + chunk)
        of_up = slice(units + start, units + start + chunk)
        gate, up = product(of_gate), product(of_up)
        grad = contract_cols(cots[0][...], downs[0][of_gate, :])
        for k in range(1, 4):
            grad = grad + contract_cols(cots[k][...], downs[k][of_gate, :])
        sig = jax.nn.sigmoid(gate)
        silu = gate * sig
        hidden[:, of_gate] = low(silu * up)
        gate_grad = low(grad * up * sig * (1.0 + gate * (1.0 - sig)))
        up_grad = low(grad * silu)
        pair[:, of_gate] = gate_grad
        pair[:, of_up] = up_grad
        gate_grad, up_grad = gate_grad.astype(f32), up_grad.astype(f32)
        scaled[:, of_gate] = low(gate_grad * rstd)
        scaled[:, of_up] = low(up_grad * rstd)
        inner_sum = inner_sum + jnp.sum(gate_grad * gate + up_grad * up, axis=-1, keepdims=True)
    inner[...] = inner_sum


def units_of_half(ins, weights, cots, downs, rstd, which, earlier):
    half, depth = ins[0].shape
    units = downs[0].shape[0]
    block = half // 2
    first = which * (half // block)
    outs = [
        jax.ShapeDtypeStruct((2 * half, units), bf16),
        jax.ShapeDtypeStruct((2 * half, 2 * units), bf16),
        jax.ShapeDtypeStruct((2 * half, 2 * units), bf16),
        jax.ShapeDtypeStruct((2 * half, 1), f32),
    ]

    def whole(array):
        return pl.BlockSpec(array.shape, lambda i: (0, 0))

    def of_two(array, k):
        return pl.BlockSpec((None, *array.shape[1:]), lambda i: (k, 0, 0))

    near_by, core, both = downs
    downs = [near_by, core, both, both]
    down_specs = [whole(near_by), whole(core), of_two(both, 0), of_two(both, 1)]
    here = pl.BlockSpec((block, depth), lambda i: (i, 0))
    at = lambda i: (first + i, 0)
    of_all = pl.BlockSpec((block, depth), at)
    earlier = list(earlier or [])
    return pl.pallas_call(
        units_kernel,
        grid=(half // block,),
        out_shape=outs,
        in_specs=[here] * 4
        + [whole(w) for w in weights]
        + [of_all, of_all, here, here]
        + down_specs
        + [pl.BlockSpec((block, 1), at)]
        + [pl.BlockSpec(memory_space=pl.ANY)] * len(earlier),
        out_specs=[pl.BlockSpec((block, o.shape[1]), at) for o in outs],
        input_output_aliases={17 + k: k for k in range(len(earlier))},
        compiler_params=pltpu.CompilerParams(vmem_limit_bytes=50 * 2**20),
        cost_estimate=pl.CostEstimate(flops=0, bytes_accessed=2**10, transcendentals=0),
    )(*ins, *weights, *cots, *downs, rstd, *earlier)


def place_sums(scalars, pieces, outs, plan):
    flat = [a for piece in pieces for a in piece]

    def kernel(words, *refs):
        ins, results = list(refs[: len(flat)]), refs[len(flat) :]
        groups = [[ins.pop(0) for _ in piece] for piece in pieces]
        for k in range(4):

            @pl.when(pl.program_id(0) == k)
            def _(k=k):
                for piece, at, out, to in plan[k]:
                    value = groups[piece][0][at]
                    if len(groups[piece]) == 2:
                        value = jnp.where(words[4] == 1, value, groups[piece][1][at])
                    results[out][to] = value.astype(f32)

    def quarter(shape, axis):
        block = tuple(n // 4 if i == axis else n for i, n in enumerate(shape))
        if axis == 0:
            return pl.BlockSpec(block, lambda k, words: (words[k], 0))
        return pl.BlockSpec(block, lambda k, words: (0, words[k]))

    return pl.pallas_call(
        kernel,
        grid_spec=pltpu.PrefetchScalarGridSpec(
            num_scalar_prefetch=1,
            grid=(4,),
            in_specs=[pl.BlockSpec(a.shape, lambda k, words: (0, 0)) for a in flat],
            out_specs=[quarter(*out) for out in outs],
        ),
        out_shape=[jax.ShapeDtypeStruct(shape, f32) for shape, _ in outs],
        compiler_params=pltpu.CompilerParams(vmem_limit_bytes=50 * 2**20),
        cost_estimate=pl.CostEstimate(flops=0, bytes_accessed=2**10, transcendentals=0),
    )(scalars, *flat)


def on_device(
    tokens,
    cotangent,
    segment_ids,
    attn_gain,
    q_gain,
    k_gain,
    mlp_gain,
    w_query,
    w_key,
    w_value,
    w_out,
    w_gate,
    w_up,
    w_down,
):
    assert lax.axis_size("tc") == 4 and lax.axis_size("tr") == 2
    col = lax.axis_index("tc")
    side = lax.axis_index("tr")
    rows, width = tokens.shape
    half = rows // 2
    full_width = width * 4
    head_size = q_gain.shape[0]
    q_width = w_query.shape[1] // 4
    k_width = w_key.shape[1] // 4
    units = w_gate.shape[1] // 4
    around = [col, col ^ 1, col ^ 2, col ^ 3]

    def cols_of(array, which, size):
        return lax.dynamic_slice_in_dim(array, around[which] * size, size, 1)

    def rows_of(array, which, size):
        return lax.dynamic_slice_in_dim(array, around[which] * size, size, 0)

    def flip(array):
        return jnp.concatenate(
            [
                lax.dynamic_slice_in_dim(array, side * half, half, 0),
                lax.dynamic_slice_in_dim(array, (1 - side) * half, half, 0),
            ],
            axis=0,
        )

    shares = lax.axis_size("dp")
    place = lax.axis_index("dp")

    def share_of(block):
        size = block.shape[0] // shares
        return lax.dynamic_slice_in_dim(block, place * size, size, 0)

    def gather_shares(from_y, from_diag):
        return lax.all_gather(jnp.stack([from_y, from_diag]), "dp", axis=1, tiled=True)

    def ffn_columns(which, rows_at):
        return jnp.concatenate(
            [rows_at(cols_of(w, which, units)) for w in (w_gate, w_up)], axis=1
        )

    down_y, down_diag = (share_of(rows_of(w_down, k, units)) for k in (2, 3))
    share_y, share_diag = ffn_columns(2, share_of), ffn_columns(3, share_of)

    qkv_weights = [
        jnp.concatenate(
            [cols_of(w_query, k, q_width), cols_of(w_key, k, k_width), cols_of(w_value, k, k_width)],
            axis=1,
        )
        for k in range(4)
    ]
    inputs = tokens.astype(f32)
    down_y, down_diag = swap_y(down_y), swap_diag(down_diag)
    share_y, share_diag, inputs = after((share_y, share_diag, inputs), down_y, down_diag)
    scaled_in = low(inputs * attn_gain[None, :])
    raw_own, raw_y, for_y = scatter_width(lambda k: dot(scaled_in, qkv_weights[k]))
    down_gathered = gather_shares(down_y, down_diag)
    w_gate, w_up, w_down, w_out, segment_ids, cotangent, inputs = after(
        (w_gate, w_up, w_down, w_out, segment_ids, cotangent, inputs), for_y
    )
    square_sum = width_total(jnp.sum(inputs * inputs, axis=1))
    cos_table, sin_table = rope_tables(positions_of(segment_ids), head_size)
    side_word = side.astype(jnp.int32).reshape(1)
    tables = (
        cos_table,
        sin_table,
        segment_ids.reshape(rows, 1),
        segment_ids.reshape(1, rows),
        q_gain.reshape(1, head_size),
        k_gain.reshape(1, head_size),
    )
    whole = lambda block: block
    blocks_core = (ffn_columns(1, whole), rows_of(w_down, 1, units))
    raw_y, share_y, share_diag, square_sum = after(
        (raw_y, swap_y(share_y), swap_diag(share_diag), square_sum), raw_own, tables, blocks_core
    )
    ffn_y, ffn_diag = (lax.all_gather(w, "dp", axis=0, tiled=True) for w in (share_y, share_diag))
    attn_rstd = lax.rsqrt(square_sum / full_width + norm_eps)
    attn_hat = inputs * attn_rstd[:, None]
    normed = low(attn_hat * attn_gain[None, :])

    heads = q_width // head_size
    projected, q_low, k_low, v_low, log_totals, att_rel = whole_kernel(
        attend_kernel,
        [
            jax.ShapeDtypeStruct((rows, q_width + 2 * k_width), f32),
            jax.ShapeDtypeStruct((rows, q_width), bf16),
            jax.ShapeDtypeStruct((rows, k_width), bf16),
            jax.ShapeDtypeStruct((rows, k_width), bf16),
            jax.ShapeDtypeStruct((rows, heads), f32),
            jax.ShapeDtypeStruct((rows, q_width), bf16),
        ],
    )(side_word, raw_own, raw_y, attn_rstd.reshape(rows, 1), *tables)
    cot_rel = flip(cotangent)
    cot_y = swap_y(after(cot_rel[:half], raw_y))
    att_y, cot_x, down_gathered = after((swap_y(att_rel), swap_x(cot_y), down_gathered), att_rel)
    atts = [att_rel, swap_core(att_rel), att_y, swap_core(att_y)]
    outs = [rows_of(w_out, k, q_width) for k in range(4)]

    def out_rows(at):
        return (dot(atts[0][at], outs[0]) + dot(atts[1][at], outs[1])) + (
            dot(atts[2][at], outs[2]) + dot(atts[3][at], outs[3])
        )

    from_x = swap_x(low(out_rows(slice(half, rows))))
    home = out_rows(slice(0, half))

    prefetched = (
        swap_core(cot_rel),
        *map(swap_core, blocks_core),
    )
    from_x, (cot_core, ffn_core, down_core), ffn_y = after((from_x, prefetched, ffn_y), home)
    cot_y_core, cot_x_core = swap_core(cot_y), swap_core(cot_x)
    downs = (rows_of(w_down, 0, units), down_core, down_gathered)
    tokens_half = lax.dynamic_slice_in_dim(tokens, side * half, half, 0).astype(f32)
    residual = tokens_half + home + from_x.astype(f32)

    mlp_square = jnp.sum(residual * residual, axis=1)
    mlp_square = width_total(jnp.concatenate([mlp_square, swap_x(mlp_square)]))
    mlp_own = low(residual * mlp_gain[None, :])
    mlp_rstd = lax.rsqrt(mlp_square / full_width + norm_eps)
    quarter = half // 2
    mlp_x, mlp_y, mlp_rstd = after(
        (swap_x(mlp_own), swap_y(mlp_own), mlp_rstd), cot_y_core, cot_x_core
    )
    mlp_xy = (swap_y(mlp_x[:quarter]), swap_x(mlp_y[quarter:]))
    mlp_x_core = swap_core(mlp_x)
    ffns = [ffn_columns(0, whole), ffn_core, ffn_y, ffn_diag]
    downs = [rows_of(w_down, 0, units), down_core, down_gathered]
    ins_own = [mlp_own, swap_core(mlp_own), mlp_y, swap_core(mlp_y)]
    cots_own = [cot_rel, cot_core, cot_y, cot_y_core]
    cots_other = [cot_rel, cot_core, cot_x, cot_x_core]
    rstd_rel = mlp_rstd.reshape(rows, 1)
    first = units_of_half(ins_own, ffns, cots_own, downs, rstd_rel, 0, None)
    mlp_xy, mlp_x_core = after((mlp_xy, mlp_x_core), first)
    mlp_xy = jnp.concatenate(mlp_xy, axis=0)
    ins_other = [mlp_x, mlp_x_core, mlp_xy, swap_core(mlp_xy)]
    hidden, pair, pair_scaled, inner = units_of_half(
        ins_other, ffns, cots_other, downs, rstd_rel, 1, first
    )

    mlp_in, mlp_core = (jnp.concatenate([ins_own[k], ins_other[k]], axis=0) for k in (0, 1))
    own_ffn = low(contract_rows(mlp_in, pair_scaled))
    pair = after(pair, own_ffn)
    own_ffn = lax.psum(own_ffn, "dp")

    kept = {}

    def started(marker):
        sums = width_total(after(inner[:, 0], marker))
        kept["inner"] = sums
        block = low(contract_rows(mlp_core, after(pair_scaled, marker)))
        kept["core"] = swap_core(block)
        down_core = low(contract_rows(after(hidden, block), cot_core))
        down_own = low(contract_rows(after(hidden, block), cot_rel))
        kept["down"] = [down_own, swap_core(down_core)]
        return (down_own, sums)

    def turned(marker):
        sums = after(kept["inner"], marker)
        kept["inner"] = sums[:half] + swap_x(sums[half:])
        return kept["inner"]

    mlp_in_grad = scatter_all(lambda k: contract_cols(pair, ffns[k]), started, turned)
    inner_total = kept["inner"]
    mlp_hat = residual * mlp_rstd[:half, None]
    mlp_gain_part = jnp.sum(mlp_in_grad * mlp_hat, axis=0)
    residual_grad = cot_rel[:half].astype(f32) + mlp_rstd[:half, None] * (
        mlp_in_grad * mlp_gain[None, :] - mlp_hat * (inner_total / full_width)[:, None]
    )
    residual_low = low(residual_grad)
    res_x = swap_x(residual_low)
    res_rel = jnp.concatenate([residual_low, res_x], axis=0)
    head_own, head_y, head_sent = scatter_width(lambda k: contract_cols(res_rel, outs[k]))

    line = LineSums()
    line.add("down", jnp.concatenate(kept["down"], axis=0), 0)
    line.add("ffn", kept["core"], 1)
    marker = line.send(line.send((head_sent, line.waiting())))
    out_grads = [low(contract_rows(after(part, marker), res_rel)) for part in atts]
    line.add("out", jnp.concatenate(out_grads, axis=0), 0)
    head_own, head_y = after((head_own, head_y), line.waiting())

    proj_low, q_gain_part, k_gain_part, inner_attn = whole_kernel(
        attend_back_kernel,
        [
            jax.ShapeDtypeStruct((rows, q_width + 2 * k_width), bf16),
            jax.ShapeDtypeStruct((1, head_size), f32),
            jax.ShapeDtypeStruct((1, head_size), f32),
            jax.ShapeDtypeStruct((rows, 1), f32),
        ],
        scratch=[pltpu.VMEM((rows, k_width), f32), pltpu.VMEM((rows, k_width), f32)],
    )(side_word, head_own, head_y, projected, q_low, k_low, v_low, log_totals, *tables)
    proj_y, proj_core = swap_y(proj_low), swap_core(proj_low)

    marker = proj_low
    for _ in range(4):
        marker = line.send(marker)
    proj_y, proj_core = after((proj_y, proj_core), marker)
    pairs = lax.all_gather(after(pair_scaled, proj_y), "tc")
    projs = [proj_low, proj_core, proj_y, swap_core(proj_y)]
    normed_part = low(
        (contract_cols(projs[0], qkv_weights[0]) + contract_cols(projs[1], qkv_weights[1]))
        + (contract_cols(projs[2], qkv_weights[2]) + contract_cols(projs[3], qkv_weights[3]))
    )
    small = jnp.concatenate([inner_attn[:, 0], q_gain_part[0], k_gain_part[0]])
    small = width_total(after(small, normed_part))
    small = jnp.concatenate([small, mlp_gain_part])
    normed_x, small_x = after((swap_x(normed_part), swap_x(small)), line.send(small))
    small = small + small_x
    inner_attn, gains = small[:rows], small[rows:]
    hiddens = lax.all_gather(after(hidden, inner_attn), "tc", axis=1, tiled=True)
    gains = jnp.pad(gains, (0, 64 * width - gains.shape[0])).reshape(64, width)
    gains = lax.psum(gains, "dp").reshape(-1)
    normed_grad = normed_part.astype(f32) + normed_x.astype(f32)
    token_grad = low(
        flip(res_rel).astype(f32)
        + attn_rstd[:, None]
        * (normed_grad * attn_gain[None, :] - attn_hat * (inner_attn / full_width)[:, None])
    )

    for part in projs:
        line.add("qkv", low(contract_rows(after(normed, normed_part), part)), 1)
    marker = line.send((token_grad, line.waiting()))
    for _ in range(4):
        marker = line.send(marker)
    pairs, own_ffn = after((pairs, own_ffn), marker)
    for k in (2, 3):
        block = lax.dynamic_index_in_dim(pairs, around[k], 0, keepdims=False)
        line.add("ffn", low(contract_rows(mlp_in, block)), 1)
    for _ in range(5):
        marker = line.send(marker)

    hiddens = after(hiddens, marker)
    for k in (2, 3):
        kept["down"][k - 2] = low(contract_rows(cols_of(hiddens, k, units), cot_rel))
    line.add("down", jnp.concatenate(kept["down"], axis=0), 0)
    mlp_away = low(dot(hiddens[half:], w_down))
    mlp_x_out = after(swap_x(mlp_away), line.send(mlp_away))
    mixed_half = low(residual + dot(hiddens[:half], w_down) + mlp_x_out.astype(f32))
    mixed_x = after(swap_x(mixed_half), line.send(mixed_half))
    mixed = flip(jnp.concatenate([mixed_half, mixed_x], axis=0))
    marker = mixed_x
    while line.queue:
        marker = line.send(marker)
    sums_of = line.finish()

    words = jnp.stack([*around, line.middle.astype(jnp.int32)]).astype(jnp.int32)
    everything = slice(None)

    def spread(start, size, extent):
        while size:
            piece, at = divmod(start, extent)
            taken = min(size, extent - at)
            yield (piece, slice(at, at + taken), taken)
            start, size = start + taken, size - taken

    def runs(first, start, size, extent, out, axis, to=0):
        plan = []
        for piece, at, taken in spread(start, size, extent):
            block = slice(to, to + taken)
            pair_of = lambda part: (part, everything) if axis == 0 else (everything, part)
            plan.append((first + piece, pair_of(at), out, pair_of(block)))
            to += taken
        return plan

    out_sums, qkv_sums, ffn_sums = after(
        (sums_of("out"), sums_of("qkv"), [(own_ffn,), *sums_of("ffn")]), line.last
    )
    ffn_plan = [[(0, (everything, slice(0, units)), 0, (everything, everything)),
                 (0, (everything, slice(units, 2 * units)), 1, (everything, everything))]]
    for k in range(3):
        ffn_plan.append(
            runs(1, 2 * k * units, units, width, 0, 1) + runs(1, (2 * k + 1) * units, units, width, 1, 1)
        )
    w_gate_grad, w_up_grad = place_sums(words, ffn_sums, [(w_gate.shape, 1), (w_up.shape, 1)], ffn_plan)
    [w_down_grad] = place_sums(
        words,
        sums_of("down"),
        [(w_down.shape, 0)],
        [runs(0, k * units, units, width, 0, 0) for k in range(4)],
    )
    [w_out_grad] = place_sums(
        words,
        out_sums,
        [(w_out.shape, 0)],
        [runs(0, k * q_width, q_width, width, 0, 0) for k in range(4)],
    )
    block_width = q_width + 2 * k_width
    qkv_plan = [
        runs(0, k * block_width, q_width, width, 0, 1)
        + runs(0, k * block_width + q_width, k_width, width, 1, 1)
        + runs(0, k * block_width + q_width + k_width, k_width, width, 2, 1)
        for k in range(4)
    ]
    w_query_grad, w_key_grad, w_value_grad = place_sums(
        words, qkv_sums, [(w_query.shape, 1), (w_key.shape, 1), (w_value.shape, 1)], qkv_plan
    )
    attn_gain_part = sum(
        jnp.sum(w.astype(f32) * g, axis=1)
        for w, g in ((w_query, w_query_grad), (w_key, w_key_grad), (w_value, w_value_grad))
    )
    attn_gain_grad = (attn_gain_part + swap_x(attn_gain_part)) / attn_gain
    q_gain_grad = gains[:head_size]
    k_gain_grad = gains[head_size : 2 * head_size]
    mlp_gain_grad = gains[2 * head_size : 2 * head_size + width]
    return (
        mixed,
        token_grad,
        attn_gain_grad,
        q_gain_grad,
        k_gain_grad,
        mlp_gain_grad,
        w_query_grad,
        w_key_grad,
        w_value_grad,
        w_out_grad,
        w_gate_grad,
        w_up_grad,
        w_down_grad,
    )


def solution(mesh):
    in_specs = (
        P("dp", "tc"),
        P("dp", "tc"),
        P("dp"),
        P("tc"),
        P(),
        P(),
        P("tc"),
        P("tc", "tr"),
        P("tc", "tr"),
        P("tc", "tr"),
        P("tr", "tc"),
        P("tc", "tr"),
        P("tc", "tr"),
        P("tr", "tc"),
    )
    out_specs = (
        P("dp", "tc"),
        P("dp", "tc"),
        P("tc"),
        P(),
        P(),
        P("tc"),
        P("tc", "tr"),
        P("tc", "tr"),
        P("tc", "tr"),
        P("tr", "tc"),
        P("tc", "tr"),
        P("tc", "tr"),
        P("tr", "tc"),
    )
    return jax.shard_map(
        on_device, mesh=mesh, in_specs=in_specs, out_specs=out_specs, check_vma=False
    )
```

```python
import jax
import jax.numpy as jnp
from jax import lax
from jax.experimental import pallas as pl
from jax.experimental.pallas import tpu as pltpu
from jax.sharding import PartitionSpec as P

norm_eps = 1e-06
rope_base = 1000000.0
neg_big = -1e30
f32 = jnp.float32
bf16 = jnp.bfloat16


def dot(left_side, right_side):
    return jnp.dot(left_side, right_side, preferred_element_type=f32)


def contract_rows(left_side, right_side):
    return lax.dot_general(
        left_side, right_side, (((0,), (0,)), ((), ())), preferred_element_type=f32
    )


def contract_cols(left_side, right_side):
    return lax.dot_general(
        left_side, right_side, (((1,), (1,)), ((), ())), preferred_element_type=f32
    )


def swap_core(block):
    return lax.ppermute(block, "tc", [(i, i ^ 1) for i in range(4)])


def swap_y(block):
    return lax.ppermute(block, "tc", [(i, i ^ 2) for i in range(4)])


def swap_diag(block):
    return lax.ppermute(block, "tc", [(i, i ^ 3) for i in range(4)])


def swap_x(block):
    return lax.ppermute(block, "tr", [(0, 1), (1, 0)])


def width_total(rows):
    rows = rows + swap_core(rows)
    return rows + swap_y(rows)


class LineSums:
    def __init__(self, lag=4):
        self.lag = lag
        self.last = ()
        self.short = lax.axis_size("dp") == 4
        place = lax.axis_index("dp")
        self.middle = (place == 1) | (place == 2)
        self.queue, self.names, self.pieces = [], [], []
        self.outer, self.total = [], []

    def add(self, name, grad, axis):
        size = min(grad.shape)
        for k in range(0, grad.shape[axis], size):
            self.queue.append((name, lax.slice_in_dim(grad, k, k + size, axis=axis)))

    def waiting(self):
        return [piece for _, piece in self.queue]

    def _consume(self, which, marker):
        got, piece = after((self.outer[which], self.pieces[which]), marker)
        inward = low(piece.astype(f32) + got.astype(f32))
        across = lax.ppermute(inward, "dp", [(1, 2), (2, 1)])
        self.total.append(low(inward.astype(f32) + across.astype(f32)))
        return inward

    def _swap_outer(self, piece):
        self.outer.append(lax.ppermute(piece, "dp", [(0, 1), (1, 0), (2, 3), (3, 2)]))

    def send(self, marker=()):
        which = len(self.pieces)
        name, piece = self.queue.pop(0)
        self.names.append(name)
        self.pieces.append(piece)
        if not self.short:
            return piece
        if which >= 2:
            marker = self._consume(which - 2, marker)
        out = after(piece, marker)
        if which >= self.lag:
            out = jnp.where(self.middle, self.total[which - self.lag], out)
        self._swap_outer(out)
        return marker

    def finish(self):
        count = len(self.pieces)
        if self.short:
            for which in (count - 2, count - 1):
                self.last = self._consume(which, ())
            for which in range(count - self.lag, count):
                self._swap_outer(self.total[which])
            sums = [(self.total[k], self.outer[k + self.lag]) for k in range(count)]
        else:
            sums = [(lax.psum(piece, "dp"),) for piece in self.pieces]
        return lambda name: [s for n, s in zip(self.names, sums) if n == name]


def after(value, *others):
    return lax.optimization_barrier((value, others))[0]


def low(array):
    return array.astype(bf16)


def scatter_width(product, near=lambda ready: ready):
    from_far = swap_core(low(product(3)))
    from_core = swap_core(low(product(1)))
    from_far = after(from_far, near(from_far))
    for_y = low(product(2) + from_far.astype(f32))
    from_y = swap_y(for_y)
    return (product(0) + from_core.astype(f32), from_y, for_y)


def scatter_all(product, started, turned):
    far_y, far_own = swap_core(low(product(3))), swap_core(low(product(1)))
    for_y = low(product(2) + far_y.astype(f32))
    own = low(product(0) + far_own.astype(f32))
    half = own.shape[0] // 2
    quarter = half // 2
    width = own.shape[1]
    y_first = swap_y(jnp.concatenate([for_y[quarter:half], for_y[half + quarter :]], axis=0))
    x_first = swap_x(
        jnp.concatenate([own[half : half + quarter], for_y[half : half + quarter]], axis=1)
    )
    x_first, y_first = after((x_first, y_first), started((own, for_y)))
    top_in = low(for_y[:quarter].astype(f32) + x_first[:, width:].astype(f32))
    low_in = low(own[half + quarter :].astype(f32) + y_first[quarter:].astype(f32))
    top_y, low_x = after((swap_y(top_in), swap_x(low_in)), turned((top_in, low_in)))
    top = own[:quarter].astype(f32) + x_first[:, :width].astype(f32) + top_y.astype(f32)
    bottom = own[quarter:half].astype(f32) + y_first[:quarter].astype(f32) + low_x.astype(f32)
    return jnp.concatenate([top, bottom], axis=0)


def positions_of(segment):
    slot_ids = jnp.arange(5, dtype=jnp.int32)
    before = jnp.sum((segment[None, :] < slot_ids[:, None]).astype(jnp.int32), axis=1)
    starts = jnp.sum(jnp.where(segment[:, None] == slot_ids[None, :], before[None, :], 0), axis=1)
    return jnp.arange(segment.shape[0], dtype=jnp.int32) - starts


def rope_tables(positions, head_size):
    half_size = head_size // 2
    frequency = rope_base ** (-jnp.arange(half_size, dtype=f32) * 2.0 / head_size)
    angles = positions.astype(f32)[:, None] * frequency[None, :]
    cosine, sine = jnp.cos(angles), jnp.sin(angles)
    return (
        jnp.concatenate([cosine, cosine], axis=1),
        jnp.concatenate([-sine, sine], axis=1),
    )


def turn(vectors):
    return pltpu.roll(vectors, vectors.shape[-1] // 2, axis=1)


def inverse_norm(vectors):
    return lax.rsqrt(jnp.mean(vectors * vectors, axis=-1, keepdims=True) + norm_eps)


def allowed_keys(seg_col, seg_row, start, size, extent):
    row = lax.broadcasted_iota(jnp.int32, (size, extent), 0) + start
    col = lax.broadcasted_iota(jnp.int32, (size, extent), 1)
    return (seg_col[start : start + size, :] == seg_row[:, :extent]) & (col <= row)


def attend_kernel(
    side, own, from_y, rstd, cos, sin, seg_col, seg_row, q_gain, k_gain,
    proj, q_out, k_out, v_out, lse, att,
):
    rows = own.shape[0]
    size = cos.shape[1]
    heads = q_out.shape[1] // size
    block = rows // 4
    scale = size**-0.5
    k_at = heads * size
    v_at = k_at + size

    def ready(i, carry):
        at = pl.ds(pl.multiple_of(i * block, block), block)
        raw = (own[at, :] + from_y[at, :].astype(f32)) * rstd[at, :]
        proj[at, :] = raw

        def rope(part, gain):
            n = part * inverse_norm(part) * gain[...]
            return (n * cos[at, :] + turn(n) * sin[at, :]).astype(bf16)

        for h in range(heads):
            q_out[at, h * size : (h + 1) * size] = rope(raw[:, h * size : (h + 1) * size], q_gain)
        k_out[at, :] = rope(raw[:, k_at:v_at], k_gain)
        v_out[at, :] = raw[:, v_at:].astype(bf16)
        return carry

    lax.fori_loop(0, 4, ready, 0)
    for i in range(4):
        start = i * block
        extent = start + block
        allowed = allowed_keys(seg_col, seg_row, start, block, extent)
        to = pl.ds(pl.multiple_of(lax.rem(start + side[0] * (rows // 2), rows), block), block)
        for h in range(heads):
            of_head = slice(h * size, (h + 1) * size)
            scores = contract_cols(q_out[start:extent, of_head], k_out[:extent, :]) * scale
            scores = jnp.where(allowed, scores, neg_big)
            top = jnp.max(scores, axis=-1, keepdims=True)
            expd = jnp.exp(scores - top)
            total = jnp.sum(expd, axis=-1, keepdims=True)
            weights = (expd * (1.0 / total)).astype(bf16)
            att[to, of_head] = dot(weights, v_out[:extent, :]).astype(bf16)
            lse[start:extent, h : h + 1] = top + jnp.log(total)


def attend_back_kernel(
    side, own, from_y, proj, q_in, k_in, v_in, lse, cos, sin, seg_col, seg_row, q_gain, k_gain,
    grads, q_gain_part, k_gain_part, inner, k_acc, v_acc,
):
    rows = own.shape[0]
    size = cos.shape[1]
    heads = q_in.shape[1] // size
    block = rows // 4
    scale = size**-0.5
    k_at = heads * size
    v_at = k_at + size

    def unrope(grad, part, gain, start):
        rows_at = slice(start, start + block)
        m = grad * cos[rows_at, :] - turn(grad) * sin[rows_at, :]
        r = inverse_norm(part)
        hat = part * r
        mg = m * gain[...]
        back = (r * (mg - hat * jnp.mean(mg * hat, axis=-1, keepdims=True))).astype(bf16)
        gain_part = jnp.sum(m * hat, axis=0, keepdims=True)
        return (back, gain_part, jnp.sum(back.astype(f32) * part, axis=-1, keepdims=True))

    k_acc[...] = jnp.zeros_like(k_acc)
    v_acc[...] = jnp.zeros_like(v_acc)
    q_total = jnp.zeros(q_gain_part.shape, f32)
    for i in range(4):
        start = i * block
        extent = start + block
        allowed = allowed_keys(seg_col, seg_row, start, block, extent)
        at = pl.ds(pl.multiple_of(lax.rem(start + side[0] * (rows // 2), rows), block), block)
        inner_sum = jnp.zeros((block, 1), f32)
        for h in range(heads):
            of_head = slice(h * size, (h + 1) * size)
            query = q_in[start:extent, of_head]
            grad = (own[at, of_head] + from_y[at, of_head].astype(f32)).astype(bf16)
            scores = contract_cols(query, k_in[:extent, :]) * scale
            scores = jnp.where(allowed, scores, neg_big)
            probs = jnp.exp(scores - lse[start:extent, h : h + 1])
            prob_grad = contract_cols(grad, v_in[:extent, :])
            delta = jnp.sum(probs * prob_grad, axis=-1, keepdims=True)
            score_grad = (probs * (prob_grad - delta)).astype(bf16)
            query_grad = dot(score_grad, k_in[:extent, :]) * scale
            k_acc[:extent, :] += contract_rows(score_grad, query) * scale
            v_acc[:extent, :] += contract_rows(probs.astype(bf16), grad)
            back, gain_part, part_inner = unrope(
                query_grad, proj[start:extent, of_head], q_gain, start
            )
            grads[start:extent, of_head] = back
            q_total = q_total + gain_part
            inner_sum = inner_sum + part_inner
        inner[start:extent, :] = inner_sum
    q_gain_part[...] = q_total
    k_total = jnp.zeros(k_gain_part.shape, f32)
    for i in range(4):
        start = i * block
        extent = start + block
        back, gain_part, part_inner = unrope(
            k_acc[start:extent, :], proj[start:extent, k_at:v_at], k_gain, start
        )
        grads[start:extent, k_at:v_at] = back
        k_total = k_total + gain_part
        v_back = v_acc[start:extent, :].astype(bf16)
        grads[start:extent, v_at:] = v_back
        inner[start:extent, :] += part_inner + jnp.sum(
            v_back.astype(f32) * proj[start:extent, v_at:], axis=-1, keepdims=True
        )
    k_gain_part[...] = k_total


vmem = pl.BlockSpec(memory_space=pltpu.VMEM)
smem = pl.BlockSpec(memory_space=pltpu.SMEM)
def whole_kernel(body, outs, scratch=(), grant=50):
    def call(*operands):
        return pl.pallas_call(
            body,
            out_shape=outs,
            in_specs=[smem if o.ndim == 1 else vmem for o in operands],
            out_specs=[vmem] * len(outs),
            scratch_shapes=scratch,
            compiler_params=pltpu.CompilerParams(vmem_limit_bytes=grant * 2**20),
            cost_estimate=pl.CostEstimate(flops=0, bytes_accessed=2**10, transcendentals=0),
        )(*operands)

    return call


def units_kernel(*refs):
    ins, weights, cots, downs = refs[:4], refs[4:8], refs[8:12], refs[12:16]
    rstd_ref = refs[16]
    hidden, pair, scaled, inner = refs[-4:]
    units = hidden.shape[1]
    chunk = min(256, units)
    rstd = rstd_ref[...]

    def product(at):
        total = dot(ins[0][...], weights[0][:, at])
        for k in range(1, 4):
            total = total + dot(ins[k][...], weights[k][:, at])
        return total * rstd

    inner_sum = jnp.zeros(inner.shape, f32)
    for start in range(0, units, chunk):
        of_gate = slice(start, start + chunk)
        of_up = slice(units + start, units + start + chunk)
        gate, up = product(of_gate), product(of_up)
        grad = contract_cols(cots[0][...], downs[0][of_gate, :])
        for k in range(1, 4):
            grad = grad + contract_cols(cots[k][...], downs[k][of_gate, :])
        sig = jax.nn.sigmoid(gate)
        silu = gate * sig
        hidden[:, of_gate] = low(silu * up)
        gate_grad = low(grad * up * sig * (1.0 + gate * (1.0 - sig)))
        up_grad = low(grad * silu)
        pair[:, of_gate] = gate_grad
        pair[:, of_up] = up_grad
        gate_grad, up_grad = gate_grad.astype(f32), up_grad.astype(f32)
        scaled[:, of_gate] = low(gate_grad * rstd)
        scaled[:, of_up] = low(up_grad * rstd)
        inner_sum = inner_sum + jnp.sum(gate_grad * gate + up_grad * up, axis=-1, keepdims=True)
    inner[...] = inner_sum


def units_of_half(ins, weights, cots, downs, rstd, which, earlier):
    half, depth = ins[0].shape
    units = downs[0].shape[0]
    block = half // 2
    first = which * (half // block)
    outs = [
        jax.ShapeDtypeStruct((2 * half, units), bf16),
        jax.ShapeDtypeStruct((2 * half, 2 * units), bf16),
        jax.ShapeDtypeStruct((2 * half, 2 * units), bf16),
        jax.ShapeDtypeStruct((2 * half, 1), f32),
    ]

    def whole(array):
        return pl.BlockSpec(array.shape, lambda i: (0, 0))

    def of_two(array, k):
        return pl.BlockSpec((None, *array.shape[1:]), lambda i: (k, 0, 0))

    near_by, core, both = downs
    downs = [near_by, core, both, both]
    down_specs = [whole(near_by), whole(core), of_two(both, 0), of_two(both, 1)]
    here = pl.BlockSpec((block, depth), lambda i: (i, 0))
    at = lambda i: (first + i, 0)
    of_all = pl.BlockSpec((block, depth), at)
    earlier = list(earlier or [])
    return pl.pallas_call(
        units_kernel,
        grid=(half // block,),
        out_shape=outs,
        in_specs=[here] * 4
        + [whole(w) for w in weights]
        + [of_all, of_all, here, here]
        + down_specs
        + [pl.BlockSpec((block, 1), at)]
        + [pl.BlockSpec(memory_space=pl.ANY)] * len(earlier),
        out_specs=[pl.BlockSpec((block, o.shape[1]), at) for o in outs],
        input_output_aliases={17 + k: k for k in range(len(earlier))},
        compiler_params=pltpu.CompilerParams(vmem_limit_bytes=50 * 2**20),
        cost_estimate=pl.CostEstimate(flops=0, bytes_accessed=2**10, transcendentals=0),
    )(*ins, *weights, *cots, *downs, rstd, *earlier)


def place_sums(scalars, pieces, outs, plan):
    flat = [a for piece in pieces for a in piece]

    def kernel(words, *refs):
        ins, results = list(refs[: len(flat)]), refs[len(flat) :]
        groups = [[ins.pop(0) for _ in piece] for piece in pieces]
        for k in range(4):

            @pl.when(pl.program_id(0) == k)
            def _(k=k):
                for piece, at, out, to in plan[k]:
                    value = groups[piece][0][at]
                    if len(groups[piece]) == 2:
                        value = jnp.where(words[4] == 1, value, groups[piece][1][at])
                    results[out][to] = value.astype(f32)

    def quarter(shape, axis):
        block = tuple(n // 4 if i == axis else n for i, n in enumerate(shape))
        if axis == 0:
            return pl.BlockSpec(block, lambda k, words: (words[k], 0))
        return pl.BlockSpec(block, lambda k, words: (0, words[k]))

    return pl.pallas_call(
        kernel,
        grid_spec=pltpu.PrefetchScalarGridSpec(
            num_scalar_prefetch=1,
            grid=(4,),
            in_specs=[pl.BlockSpec(a.shape, lambda k, words: (0, 0)) for a in flat],
            out_specs=[quarter(*out) for out in outs],
        ),
        out_shape=[jax.ShapeDtypeStruct(shape, f32) for shape, _ in outs],
        compiler_params=pltpu.CompilerParams(vmem_limit_bytes=50 * 2**20),
        cost_estimate=pl.CostEstimate(flops=0, bytes_accessed=2**10, transcendentals=0),
    )(scalars, *flat)


def on_device(
    tokens,
    cotangent,
    segment_ids,
    attn_gain,
    q_gain,
    k_gain,
    mlp_gain,
    w_query,
    w_key,
    w_value,
    w_out,
    w_gate,
    w_up,
    w_down,
):
    assert lax.axis_size("tc") == 4 and lax.axis_size("tr") == 2
    col = lax.axis_index("tc")
    side = lax.axis_index("tr")
    rows, width = tokens.shape
    half = rows // 2
    full_width = width * 4
    head_size = q_gain.shape[0]
    q_width = w_query.shape[1] // 4
    k_width = w_key.shape[1] // 4
    units = w_gate.shape[1] // 4
    around = [col, col ^ 1, col ^ 2, col ^ 3]

    def cols_of(array, which, size):
        return lax.dynamic_slice_in_dim(array, around[which] * size, size, 1)

    def rows_of(array, which, size):
        return lax.dynamic_slice_in_dim(array, around[which] * size, size, 0)

    def flip(array):
        return jnp.concatenate(
            [
                lax.dynamic_slice_in_dim(array, side * half, half, 0),
                lax.dynamic_slice_in_dim(array, (1 - side) * half, half, 0),
            ],
            axis=0,
        )

    shares = lax.axis_size("dp")
    place = lax.axis_index("dp")

    def share_of(block):
        size = block.shape[0] // shares
        return lax.dynamic_slice_in_dim(block, place * size, size, 0)

    def gather_shares(from_y, from_diag):
        return lax.all_gather(jnp.stack([from_y, from_diag]), "dp", axis=1, tiled=True)

    def ffn_columns(which, rows_at):
        return jnp.concatenate(
            [rows_at(cols_of(w, which, units)) for w in (w_gate, w_up)], axis=1
        )

    down_y, down_diag = (share_of(rows_of(w_down, k, units)) for k in (2, 3))
    share_y, share_diag = ffn_columns(2, share_of), ffn_columns(3, share_of)

    qkv_weights = [
        jnp.concatenate(
            [cols_of(w_query, k, q_width), cols_of(w_key, k, k_width), cols_of(w_value, k, k_width)],
            axis=1,
        )
        for k in range(4)
    ]
    inputs = tokens.astype(f32)
    down_y, down_diag = swap_y(down_y), swap_diag(down_diag)
    share_y, share_diag, inputs = after((share_y, share_diag, inputs), down_y, down_diag)
    scaled_in = low(inputs * attn_gain[None, :])
    raw_own, raw_y, for_y = scatter_width(lambda k: dot(scaled_in, qkv_weights[k]))
    down_gathered = gather_shares(down_y, down_diag)
    w_gate, w_up, w_down, w_out, segment_ids, cotangent, inputs = after(
        (w_gate, w_up, w_down, w_out, segment_ids, cotangent, inputs), for_y
    )
    square_sum = width_total(jnp.sum(inputs * inputs, axis=1))
    cos_table, sin_table = rope_tables(positions_of(segment_ids), head_size)
    side_word = side.astype(jnp.int32).reshape(1)
    tables = (
        cos_table,
        sin_table,
        segment_ids.reshape(rows, 1),
        segment_ids.reshape(1, rows),
        q_gain.reshape(1, head_size),
        k_gain.reshape(1, head_size),
    )
    whole = lambda block: block
    blocks_core = (ffn_columns(1, whole), rows_of(w_down, 1, units))
    raw_y, share_y, share_diag, square_sum = after(
        (raw_y, swap_y(share_y), swap_diag(share_diag), square_sum), raw_own, tables, blocks_core
    )
    ffn_y, ffn_diag = (lax.all_gather(w, "dp", axis=0, tiled=True) for w in (share_y, share_diag))
    attn_rstd = lax.rsqrt(square_sum / full_width + norm_eps)
    attn_hat = inputs * attn_rstd[:, None]
    normed = low(attn_hat * attn_gain[None, :])

    heads = q_width // head_size
    projected, q_low, k_low, v_low, log_totals, att_rel = whole_kernel(
        attend_kernel,
        [
            jax.ShapeDtypeStruct((rows, q_width + 2 * k_width), f32),
            jax.ShapeDtypeStruct((rows, q_width), bf16),
            jax.ShapeDtypeStruct((rows, k_width), bf16),
            jax.ShapeDtypeStruct((rows, k_width), bf16),
            jax.ShapeDtypeStruct((rows, heads), f32),
            jax.ShapeDtypeStruct((rows, q_width), bf16),
        ],
    )(side_word, raw_own, raw_y, attn_rstd.reshape(rows, 1), *tables)
    cot_rel = flip(cotangent)
    cot_y = swap_y(after(cot_rel[:half], raw_y))
    att_y, cot_x, down_gathered = after((swap_y(att_rel), swap_x(cot_y), down_gathered), att_rel)
    atts = [att_rel, swap_core(att_rel), att_y, swap_core(att_y)]
    outs = [rows_of(w_out, k, q_width) for k in range(4)]

    def out_rows(at):
        return (dot(atts[0][at], outs[0]) + dot(atts[1][at], outs[1])) + (
            dot(atts[2][at], outs[2]) + dot(atts[3][at], outs[3])
        )

    from_x = swap_x(low(out_rows(slice(half, rows))))
    home = out_rows(slice(0, half))

    prefetched = (
        swap_core(cot_rel),
        *map(swap_core, blocks_core),
    )
    from_x, (cot_core, ffn_core, down_core), ffn_y = after((from_x, prefetched, ffn_y), home)
    cot_y_core, cot_x_core = swap_core(cot_y), swap_core(cot_x)
    downs = (rows_of(w_down, 0, units), down_core, down_gathered)
    tokens_half = lax.dynamic_slice_in_dim(tokens, side * half, half, 0).astype(f32)
    residual = tokens_half + home + from_x.astype(f32)

    mlp_square = jnp.sum(residual * residual, axis=1)
    mlp_square = width_total(jnp.concatenate([mlp_square, swap_x(mlp_square)]))
    mlp_own = low(residual * mlp_gain[None, :])
    mlp_rstd = lax.rsqrt(mlp_square / full_width + norm_eps)
    quarter = half // 2
    mlp_x, mlp_y, mlp_rstd = after(
        (swap_x(mlp_own), swap_y(mlp_own), mlp_rstd), cot_y_core, cot_x_core
    )
    mlp_xy = (swap_y(mlp_x[:quarter]), swap_x(mlp_y[quarter:]))
    mlp_x_core = swap_core(mlp_x)
    ffns = [ffn_columns(0, whole), ffn_core, ffn_y, ffn_diag]
    downs = [rows_of(w_down, 0, units), down_core, down_gathered]
    ins_own = [mlp_own, swap_core(mlp_own), mlp_y, swap_core(mlp_y)]
    cots_own = [cot_rel, cot_core, cot_y, cot_y_core]
    cots_other = [cot_rel, cot_core, cot_x, cot_x_core]
    rstd_rel = mlp_rstd.reshape(rows, 1)
    first = units_of_half(ins_own, ffns, cots_own, downs, rstd_rel, 0, None)
    mlp_xy, mlp_x_core = after((mlp_xy, mlp_x_core), first)
    mlp_xy = jnp.concatenate(mlp_xy, axis=0)
    ins_other = [mlp_x, mlp_x_core, mlp_xy, swap_core(mlp_xy)]
    hidden, pair, pair_scaled, inner = units_of_half(
        ins_other, ffns, cots_other, downs, rstd_rel, 1, first
    )

    line = LineSums()
    mlp_in, mlp_core = (jnp.concatenate([ins_own[k], ins_other[k]], axis=0) for k in (0, 1))
    line.add("ffn", low(contract_rows(mlp_in, pair_scaled)), 1)
    line.send(line.send())
    pair = after(pair, line.pieces, line.waiting())

    kept = {}

    def started(marker):
        sums = width_total(after(inner[:, 0], marker))
        kept["inner"] = sums
        block = low(contract_rows(mlp_core, after(pair_scaled, marker)))
        kept["core"] = swap_core(block)
        down_core = low(contract_rows(after(hidden, block), cot_core))
        down_own = low(contract_rows(after(hidden, block), cot_rel))
        line.add("down", jnp.concatenate([down_own, swap_core(down_core)], axis=0), 0)
        return (down_own, sums)

    def turned(marker):
        sums = after(kept["inner"], marker)
        kept["inner"] = sums[:half] + swap_x(sums[half:])
        return (kept["inner"], line.send(line.send(marker)))

    mlp_in_grad = scatter_all(lambda k: contract_cols(pair, ffns[k]), started, turned)
    inner_total = kept["inner"]
    mlp_hat = residual * mlp_rstd[:half, None]
    mlp_gain_part = jnp.sum(mlp_in_grad * mlp_hat, axis=0)
    residual_grad = cot_rel[:half].astype(f32) + mlp_rstd[:half, None] * (
        mlp_in_grad * mlp_gain[None, :] - mlp_hat * (inner_total / full_width)[:, None]
    )
    residual_low = low(residual_grad)
    res_x = swap_x(residual_low)
    res_rel = jnp.concatenate([residual_low, res_x], axis=0)
    head_own, head_y, head_sent = scatter_width(lambda k: contract_cols(res_rel, outs[k]))

    line.add("ffn", kept["core"], 1)
    marker = line.send(line.send((head_sent, line.waiting())))
    out_grads = [low(contract_rows(after(part, marker), res_rel)) for part in atts]
    line.add("out", jnp.concatenate(out_grads, axis=0), 0)
    head_own, head_y = after((head_own, head_y), line.waiting())

    proj_low, q_gain_part, k_gain_part, inner_attn = whole_kernel(
        attend_back_kernel,
        [
            jax.ShapeDtypeStruct((rows, q_width + 2 * k_width), bf16),
            jax.ShapeDtypeStruct((1, head_size), f32),
            jax.ShapeDtypeStruct((1, head_size), f32),
            jax.ShapeDtypeStruct((rows, 1), f32),
        ],
        scratch=[pltpu.VMEM((rows, k_width), f32), pltpu.VMEM((rows, k_width), f32)],
    )(side_word, head_own, head_y, projected, q_low, k_low, v_low, log_totals, *tables)
    proj_y, proj_core = swap_y(proj_low), swap_core(proj_low)

    marker = proj_low
    for _ in range(4):
        marker = line.send(marker)
    proj_y, proj_core = after((proj_y, proj_core), marker)
    pairs = lax.all_gather(after(pair_scaled, proj_y), "tc")
    projs = [proj_low, proj_core, proj_y, swap_core(proj_y)]
    normed_part = low(
        (contract_cols(projs[0], qkv_weights[0]) + contract_cols(projs[1], qkv_weights[1]))
        + (contract_cols(projs[2], qkv_weights[2]) + contract_cols(projs[3], qkv_weights[3]))
    )
    small = jnp.concatenate([inner_attn[:, 0], q_gain_part[0], k_gain_part[0]])
    small = width_total(after(small, normed_part))
    small = jnp.concatenate([small, mlp_gain_part])
    normed_x, small_x = after((swap_x(normed_part), swap_x(small)), line.send(small))
    small = small + small_x
    inner_attn, gains = small[:rows], small[rows:]
    hiddens = lax.all_gather(after(hidden, inner_attn), "tc", axis=1, tiled=True)
    gains = jnp.pad(gains, (0, 64 * width - gains.shape[0])).reshape(64, width)
    gains = lax.psum(gains, "dp")
    normed_grad = normed_part.astype(f32) + normed_x.astype(f32)
    token_grad = low(
        flip(res_rel).astype(f32)
        + attn_rstd[:, None]
        * (normed_grad * attn_gain[None, :] - attn_hat * (inner_attn / full_width)[:, None])
    )

    for part in projs:
        line.add("qkv", low(contract_rows(after(normed, normed_part), part)), 1)
    marker = line.send((token_grad, line.waiting()))
    for _ in range(3):
        marker = line.send(marker)
    pairs = after(pairs, marker)
    for k in (2, 3):
        block = lax.dynamic_index_in_dim(pairs, around[k], 0, keepdims=False)
        line.add("ffn", low(contract_rows(mlp_in, block)), 1)
    for _ in range(5):
        marker = line.send(marker)

    hiddens = after(hiddens, marker)
    far_down = [low(contract_rows(cols_of(hiddens, k, units), cot_rel)) for k in (2, 3)]
    line.add("down", jnp.concatenate(far_down, axis=0), 0)
    mlp_away = low(dot(hiddens[half:], w_down))
    mlp_x_out = after(swap_x(mlp_away), line.send(mlp_away))
    mixed_half = low(residual + dot(hiddens[:half], w_down) + mlp_x_out.astype(f32))
    mixed_x = after(swap_x(mixed_half), line.send(mixed_half))
    mixed = flip(jnp.concatenate([mixed_half, mixed_x], axis=0))
    marker = mixed_x
    while line.queue:
        marker = line.send(marker)
    sums_of = line.finish()

    words = jnp.stack([*around, line.middle.astype(jnp.int32)]).astype(jnp.int32)
    everything = slice(None)

    def spread(start, size, extent):
        while size:
            piece, at = divmod(start, extent)
            taken = min(size, extent - at)
            yield (piece, slice(at, at + taken), taken)
            start, size = start + taken, size - taken

    def runs(first, start, size, extent, out, axis, to=0):
        plan = []
        for piece, at, taken in spread(start, size, extent):
            block = slice(to, to + taken)
            pair_of = lambda part: (part, everything) if axis == 0 else (everything, part)
            plan.append((first + piece, pair_of(at), out, pair_of(block)))
            to += taken
        return plan

    out_sums, qkv_sums, ffn_sums = after(
        (sums_of("out"), sums_of("qkv"), sums_of("ffn")), line.last
    )
    ffn_plan = [
        runs(0, 2 * k * units, units, width, 0, 1) + runs(0, (2 * k + 1) * units, units, width, 1, 1)
        for k in range(4)
    ]
    w_gate_grad, w_up_grad = place_sums(words, ffn_sums, [(w_gate.shape, 1), (w_up.shape, 1)], ffn_plan)
    [w_down_grad] = place_sums(
        words,
        sums_of("down"),
        [(w_down.shape, 0)],
        [runs(0, k * units, units, width, 0, 0) for k in range(4)],
    )
    [w_out_grad] = place_sums(
        words,
        out_sums,
        [(w_out.shape, 0)],
        [runs(0, k * q_width, q_width, width, 0, 0) for k in range(4)],
    )
    block_width = q_width + 2 * k_width
    qkv_plan = [
        runs(0, k * block_width, q_width, width, 0, 1)
        + runs(0, k * block_width + q_width, k_width, width, 1, 1)
        + runs(0, k * block_width + q_width + k_width, k_width, width, 2, 1)
        for k in range(4)
    ]
    w_query_grad, w_key_grad, w_value_grad = place_sums(
        words, qkv_sums, [(w_query.shape, 1), (w_key.shape, 1), (w_value.shape, 1)], qkv_plan
    )
    attn_gain_part = sum(
        jnp.sum(w.astype(f32) * g, axis=1)
        for w, g in ((w_query, w_query_grad), (w_key, w_key_grad), (w_value, w_value_grad))
    )
    attn_gain_grad = (attn_gain_part + swap_x(attn_gain_part)) / attn_gain
    gains = after(gains, line.last).reshape(-1)
    q_gain_grad = gains[:head_size]
    k_gain_grad = gains[head_size : 2 * head_size]
    mlp_gain_grad = gains[2 * head_size : 2 * head_size + width]
    return (
        mixed,
        token_grad,
        attn_gain_grad,
        q_gain_grad,
        k_gain_grad,
        mlp_gain_grad,
        w_query_grad,
        w_key_grad,
        w_value_grad,
        w_out_grad,
        w_gate_grad,
        w_up_grad,
        w_down_grad,
    )


def solution(mesh):
    in_specs = (
        P("dp", "tc"),
        P("dp", "tc"),
        P("dp"),
        P("tc"),
        P(),
        P(),
        P("tc"),
        P("tc", "tr"),
        P("tc", "tr"),
        P("tc", "tr"),
        P("tr", "tc"),
        P("tc", "tr"),
        P("tc", "tr"),
        P("tr", "tc"),
    )
    out_specs = (
        P("dp", "tc"),
        P("dp", "tc"),
        P("tc"),
        P(),
        P(),
        P("tc"),
        P("tc", "tr"),
        P("tc", "tr"),
        P("tc", "tr"),
        P("tr", "tc"),
        P("tc", "tr"),
        P("tc", "tr"),
        P("tr", "tc"),
    )
    return jax.shard_map(
        on_device, mesh=mesh, in_specs=in_specs, out_specs=out_specs, check_vma=False
    )
```

```python
import jax
import jax.numpy as jnp
from jax import lax
from jax.experimental import pallas as pl
from jax.experimental.pallas import tpu as pltpu
from jax.sharding import PartitionSpec as P

norm_eps = 1e-06
rope_base = 1000000.0
neg_big = -1e30
f32 = jnp.float32
bf16 = jnp.bfloat16


def dot(left_side, right_side):
    return jnp.dot(left_side, right_side, preferred_element_type=f32)


def contract_rows(left_side, right_side):
    return lax.dot_general(
        left_side, right_side, (((0,), (0,)), ((), ())), preferred_element_type=f32
    )


def contract_cols(left_side, right_side):
    return lax.dot_general(
        left_side, right_side, (((1,), (1,)), ((), ())), preferred_element_type=f32
    )


def swap_core(block):
    return lax.ppermute(block, "tc", [(i, i ^ 1) for i in range(4)])


def swap_y(block):
    return lax.ppermute(block, "tc", [(i, i ^ 2) for i in range(4)])


def swap_diag(block):
    return lax.ppermute(block, "tc", [(i, i ^ 3) for i in range(4)])


def swap_x(block):
    return lax.ppermute(block, "tr", [(0, 1), (1, 0)])


def width_total(rows):
    rows = rows + swap_core(rows)
    return rows + swap_y(rows)


class LineSums:
    def __init__(self, lag=4):
        self.lag = lag
        self.last = ()
        self.short = lax.axis_size("dp") == 4
        place = lax.axis_index("dp")
        self.middle = (place == 1) | (place == 2)
        self.queue, self.names, self.pieces = [], [], []
        self.outer, self.total = [], []

    def add(self, name, grad, axis):
        size = min(grad.shape)
        for k in range(0, grad.shape[axis], size):
            self.queue.append((name, lax.slice_in_dim(grad, k, k + size, axis=axis)))

    def waiting(self):
        return [piece for _, piece in self.queue]

    def _consume(self, which, marker):
        got, piece = after((self.outer[which], self.pieces[which]), marker)
        inward = low(piece.astype(f32) + got.astype(f32))
        across = lax.ppermute(inward, "dp", [(1, 2), (2, 1)])
        self.total.append(low(inward.astype(f32) + across.astype(f32)))
        return inward

    def _swap_outer(self, piece):
        self.outer.append(lax.ppermute(piece, "dp", [(0, 1), (1, 0), (2, 3), (3, 2)]))

    def send(self, marker=()):
        which = len(self.pieces)
        name, piece = self.queue.pop(0)
        self.names.append(name)
        self.pieces.append(piece)
        if not self.short:
            return piece
        if which >= self.lag:
            marker = (marker, self.total[which - self.lag])
        if which >= 2:
            marker = self._consume(which - 2, marker)
        out = after(piece, marker)
        if which >= self.lag:
            out = jnp.where(self.middle, self.total[which - self.lag], out)
        self._swap_outer(out)
        return marker

    def finish(self):
        count = len(self.pieces)
        if self.short:
            for which in (count - 2, count - 1):
                self.last = self._consume(which, ())
            for which in range(count - self.lag, count):
                self._swap_outer(self.total[which])
            sums = [(self.total[k], self.outer[k + self.lag]) for k in range(count)]
        else:
            sums = [(lax.psum(piece, "dp"),) for piece in self.pieces]
        return lambda name: [s for n, s in zip(self.names, sums) if n == name]


def after(value, *others):
    return lax.optimization_barrier((value, others))[0]


def low(array):
    return array.astype(bf16)


def scatter_width(product, near=lambda ready: ready):
    from_far = swap_core(low(product(3)))
    from_core = swap_core(low(product(1)))
    from_far = after(from_far, near(from_far))
    for_y = low(product(2) + from_far.astype(f32))
    from_y = swap_y(for_y)
    return (product(0) + from_core.astype(f32), from_y, for_y)


def scatter_all(product, started, turned):
    far_y, far_own = swap_core(low(product(3))), swap_core(low(product(1)))
    for_y = low(product(2) + far_y.astype(f32))
    own = low(product(0) + far_own.astype(f32))
    half = own.shape[0] // 2
    quarter = half // 2
    width = own.shape[1]
    y_first = swap_y(jnp.concatenate([for_y[quarter:half], for_y[half + quarter :]], axis=0))
    x_first = swap_x(
        jnp.concatenate([own[half : half + quarter], for_y[half : half + quarter]], axis=1)
    )
    x_first, y_first = after((x_first, y_first), started((own, for_y)))
    top_in = low(for_y[:quarter].astype(f32) + x_first[:, width:].astype(f32))
    low_in = low(own[half + quarter :].astype(f32) + y_first[quarter:].astype(f32))
    top_y, low_x = after((swap_y(top_in), swap_x(low_in)), turned((top_in, low_in)))
    top = own[:quarter].astype(f32) + x_first[:, :width].astype(f32) + top_y.astype(f32)
    bottom = own[quarter:half].astype(f32) + y_first[:quarter].astype(f32) + low_x.astype(f32)
    return jnp.concatenate([top, bottom], axis=0)


def positions_of(segment):
    slot_ids = jnp.arange(5, dtype=jnp.int32)
    before = jnp.sum((segment[None, :] < slot_ids[:, None]).astype(jnp.int32), axis=1)
    starts = jnp.sum(jnp.where(segment[:, None] == slot_ids[None, :], before[None, :], 0), axis=1)
    return jnp.arange(segment.shape[0], dtype=jnp.int32) - starts


def rope_tables(positions, head_size):
    half_size = head_size // 2
    frequency = rope_base ** (-jnp.arange(half_size, dtype=f32) * 2.0 / head_size)
    angles = positions.astype(f32)[:, None] * frequency[None, :]
    cosine, sine = jnp.cos(angles), jnp.sin(angles)
    return (
        jnp.concatenate([cosine, cosine], axis=1),
        jnp.concatenate([-sine, sine], axis=1),
    )


def turn(vectors):
    return pltpu.roll(vectors, vectors.shape[-1] // 2, axis=1)


def inverse_norm(vectors):
    return lax.rsqrt(jnp.mean(vectors * vectors, axis=-1, keepdims=True) + norm_eps)


def allowed_keys(seg_col, seg_row, start, size, extent):
    row = lax.broadcasted_iota(jnp.int32, (size, extent), 0) + start
    col = lax.broadcasted_iota(jnp.int32, (size, extent), 1)
    return (seg_col[start : start + size, :] == seg_row[:, :extent]) & (col <= row)


def attend_kernel(
    side, own, from_y, rstd, cos, sin, seg_col, seg_row, q_gain, k_gain,
    proj, q_out, k_out, v_out, lse, att,
):
    rows = own.shape[0]
    size = cos.shape[1]
    heads = q_out.shape[1] // size
    block = rows // 4
    scale = size**-0.5
    k_at = heads * size
    v_at = k_at + size

    def ready(i, carry):
        at = pl.ds(pl.multiple_of(i * block, block), block)
        raw = (own[at, :] + from_y[at, :].astype(f32)) * rstd[at, :]
        proj[at, :] = raw

        def rope(part, gain):
            n = part * inverse_norm(part) * gain[...]
            return (n * cos[at, :] + turn(n) * sin[at, :]).astype(bf16)

        for h in range(heads):
            q_out[at, h * size : (h + 1) * size] = rope(raw[:, h * size : (h + 1) * size], q_gain)
        k_out[at, :] = rope(raw[:, k_at:v_at], k_gain)
        v_out[at, :] = raw[:, v_at:].astype(bf16)
        return carry

    lax.fori_loop(0, 4, ready, 0)
    for i in range(4):
        start = i * block
        extent = start + block
        allowed = allowed_keys(seg_col, seg_row, start, block, extent)
        to = pl.ds(pl.multiple_of(lax.rem(start + side[0] * (rows // 2), rows), block), block)
        for h in range(heads):
            of_head = slice(h * size, (h + 1) * size)
            scores = contract_cols(q_out[start:extent, of_head], k_out[:extent, :]) * scale
            scores = jnp.where(allowed, scores, neg_big)
            top = jnp.max(scores, axis=-1, keepdims=True)
            expd = jnp.exp(scores - top)
            total = jnp.sum(expd, axis=-1, keepdims=True)
            weights = (expd * (1.0 / total)).astype(bf16)
            att[to, of_head] = dot(weights, v_out[:extent, :]).astype(bf16)
            lse[start:extent, h : h + 1] = top + jnp.log(total)


def attend_back_kernel(
    side, own, from_y, proj, q_in, k_in, v_in, lse, cos, sin, seg_col, seg_row, q_gain, k_gain,
    grads, q_gain_part, k_gain_part, inner, k_acc, v_acc,
):
    rows = own.shape[0]
    size = cos.shape[1]
    heads = q_in.shape[1] // size
    block = rows // 4
    scale = size**-0.5
    k_at = heads * size
    v_at = k_at + size

    def unrope(grad, part, gain, start):
        rows_at = slice(start, start + block)
        m = grad * cos[rows_at, :] - turn(grad) * sin[rows_at, :]
        r = inverse_norm(part)
        hat = part * r
        mg = m * gain[...]
        back = (r * (mg - hat * jnp.mean(mg * hat, axis=-1, keepdims=True))).astype(bf16)
        gain_part = jnp.sum(m * hat, axis=0, keepdims=True)
        return (back, gain_part, jnp.sum(back.astype(f32) * part, axis=-1, keepdims=True))

    k_acc[...] = jnp.zeros_like(k_acc)
    v_acc[...] = jnp.zeros_like(v_acc)
    q_total = jnp.zeros(q_gain_part.shape, f32)
    for i in range(4):
        start = i * block
        extent = start + block
        allowed = allowed_keys(seg_col, seg_row, start, block, extent)
        at = pl.ds(pl.multiple_of(lax.rem(start + side[0] * (rows // 2), rows), block), block)
        inner_sum = jnp.zeros((block, 1), f32)
        for h in range(heads):
            of_head = slice(h * size, (h + 1) * size)
            query = q_in[start:extent, of_head]
            grad = (own[at, of_head] + from_y[at, of_head].astype(f32)).astype(bf16)
            scores = contract_cols(query, k_in[:extent, :]) * scale
            scores = jnp.where(allowed, scores, neg_big)
            probs = jnp.exp(scores - lse[start:extent, h : h + 1])
            prob_grad = contract_cols(grad, v_in[:extent, :])
            delta = jnp.sum(probs * prob_grad, axis=-1, keepdims=True)
            score_grad = (probs * (prob_grad - delta)).astype(bf16)
            query_grad = dot(score_grad, k_in[:extent, :]) * scale
            k_acc[:extent, :] += contract_rows(score_grad, query) * scale
            v_acc[:extent, :] += contract_rows(probs.astype(bf16), grad)
            back, gain_part, part_inner = unrope(
                query_grad, proj[start:extent, of_head], q_gain, start
            )
            grads[start:extent, of_head] = back
            q_total = q_total + gain_part
            inner_sum = inner_sum + part_inner
        inner[start:extent, :] = inner_sum
    q_gain_part[...] = q_total
    k_total = jnp.zeros(k_gain_part.shape, f32)
    for i in range(4):
        start = i * block
        extent = start + block
        back, gain_part, part_inner = unrope(
            k_acc[start:extent, :], proj[start:extent, k_at:v_at], k_gain, start
        )
        grads[start:extent, k_at:v_at] = back
        k_total = k_total + gain_part
        v_back = v_acc[start:extent, :].astype(bf16)
        grads[start:extent, v_at:] = v_back
        inner[start:extent, :] += part_inner + jnp.sum(
            v_back.astype(f32) * proj[start:extent, v_at:], axis=-1, keepdims=True
        )
    k_gain_part[...] = k_total


vmem = pl.BlockSpec(memory_space=pltpu.VMEM)
smem = pl.BlockSpec(memory_space=pltpu.SMEM)
def whole_kernel(body, outs, scratch=(), grant=50):
    def call(*operands):
        return pl.pallas_call(
            body,
            out_shape=outs,
            in_specs=[smem if o.ndim == 1 else vmem for o in operands],
            out_specs=[vmem] * len(outs),
            scratch_shapes=scratch,
            compiler_params=pltpu.CompilerParams(vmem_limit_bytes=grant * 2**20),
            cost_estimate=pl.CostEstimate(flops=0, bytes_accessed=2**10, transcendentals=0),
        )(*operands)

    return call


def units_kernel(*refs):
    ins, weights, cots, downs = refs[:4], refs[4:8], refs[8:12], refs[12:16]
    rstd_ref = refs[16]
    hidden, pair, scaled, inner = refs[-4:]
    units = hidden.shape[1]
    chunk = min(256, units)
    rstd = rstd_ref[...]

    def product(at):
        total = dot(ins[0][...], weights[0][:, at])
        for k in range(1, 4):
            total = total + dot(ins[k][...], weights[k][:, at])
        return total * rstd

    inner_sum = jnp.zeros(inner.shape, f32)
    for start in range(0, units, chunk):
        of_gate = slice(start, start + chunk)
        of_up = slice(units + start, units + start + chunk)
        gate, up = product(of_gate), product(of_up)
        grad = contract_cols(cots[0][...], downs[0][of_gate, :])
        for k in range(1, 4):
            grad = grad + contract_cols(cots[k][...], downs[k][of_gate, :])
        sig = jax.nn.sigmoid(gate)
        silu = gate * sig
        hidden[:, of_gate] = low(silu * up)
        gate_grad = low(grad * up * sig * (1.0 + gate * (1.0 - sig)))
        up_grad = low(grad * silu)
        pair[:, of_gate] = gate_grad
        pair[:, of_up] = up_grad
        gate_grad, up_grad = gate_grad.astype(f32), up_grad.astype(f32)
        scaled[:, of_gate] = low(gate_grad * rstd)
        scaled[:, of_up] = low(up_grad * rstd)
        inner_sum = inner_sum + jnp.sum(gate_grad * gate + up_grad * up, axis=-1, keepdims=True)
    inner[...] = inner_sum


def units_of_half(ins, weights, cots, downs, rstd, which, earlier):
    half, depth = ins[0].shape
    units = downs[0].shape[0]
    block = half // 2
    first = which * (half // block)
    outs = [
        jax.ShapeDtypeStruct((2 * half, units), bf16),
        jax.ShapeDtypeStruct((2 * half, 2 * units), bf16),
        jax.ShapeDtypeStruct((2 * half, 2 * units), bf16),
        jax.ShapeDtypeStruct((2 * half, 1), f32),
    ]

    def whole(array):
        return pl.BlockSpec(array.shape, lambda i: (0, 0))

    def of_two(array, k):
        return pl.BlockSpec((None, *array.shape[1:]), lambda i: (k, 0, 0))

    near_by, core, both = downs
    downs = [near_by, core, both, both]
    down_specs = [whole(near_by), whole(core), of_two(both, 0), of_two(both, 1)]
    here = pl.BlockSpec((block, depth), lambda i: (i, 0))
    at = lambda i: (first + i, 0)
    of_all = pl.BlockSpec((block, depth), at)
    earlier = list(earlier or [])
    return pl.pallas_call(
        units_kernel,
        grid=(half // block,),
        out_shape=outs,
        in_specs=[here] * 4
        + [whole(w) for w in weights]
        + [of_all, of_all, here, here]
        + down_specs
        + [pl.BlockSpec((block, 1), at)]
        + [pl.BlockSpec(memory_space=pl.ANY)] * len(earlier),
        out_specs=[pl.BlockSpec((block, o.shape[1]), at) for o in outs],
        input_output_aliases={17 + k: k for k in range(len(earlier))},
        compiler_params=pltpu.CompilerParams(vmem_limit_bytes=50 * 2**20),
        cost_estimate=pl.CostEstimate(flops=0, bytes_accessed=2**10, transcendentals=0),
    )(*ins, *weights, *cots, *downs, rstd, *earlier)


def place_sums(scalars, pieces, outs, plan):
    flat = [a for piece in pieces for a in piece]

    def kernel(words, *refs):
        ins, results = list(refs[: len(flat)]), refs[len(flat) :]
        groups = [[ins.pop(0) for _ in piece] for piece in pieces]
        for k in range(4):

            @pl.when(pl.program_id(0) == k)
            def _(k=k):
                for piece, at, out, to in plan[k]:
                    value = groups[piece][0][at]
                    if len(groups[piece]) == 2:
                        value = jnp.where(words[4] == 1, value, groups[piece][1][at])
                    results[out][to] = value.astype(f32)

    def quarter(shape, axis):
        block = tuple(n // 4 if i == axis else n for i, n in enumerate(shape))
        if axis == 0:
            return pl.BlockSpec(block, lambda k, words: (words[k], 0))
        return pl.BlockSpec(block, lambda k, words: (0, words[k]))

    return pl.pallas_call(
        kernel,
        grid_spec=pltpu.PrefetchScalarGridSpec(
            num_scalar_prefetch=1,
            grid=(4,),
            in_specs=[pl.BlockSpec(a.shape, lambda k, words: (0, 0)) for a in flat],
            out_specs=[quarter(*out) for out in outs],
        ),
        out_shape=[jax.ShapeDtypeStruct(shape, f32) for shape, _ in outs],
        compiler_params=pltpu.CompilerParams(vmem_limit_bytes=50 * 2**20),
        cost_estimate=pl.CostEstimate(flops=0, bytes_accessed=2**10, transcendentals=0),
    )(scalars, *flat)


def on_device(
    tokens,
    cotangent,
    segment_ids,
    attn_gain,
    q_gain,
    k_gain,
    mlp_gain,
    w_query,
    w_key,
    w_value,
    w_out,
    w_gate,
    w_up,
    w_down,
):
    assert lax.axis_size("tc") == 4 and lax.axis_size("tr") == 2
    col = lax.axis_index("tc")
    side = lax.axis_index("tr")
    rows, width = tokens.shape
    half = rows // 2
    full_width = width * 4
    head_size = q_gain.shape[0]
    q_width = w_query.shape[1] // 4
    k_width = w_key.shape[1] // 4
    units = w_gate.shape[1] // 4
    around = [col, col ^ 1, col ^ 2, col ^ 3]

    def cols_of(array, which, size):
        return lax.dynamic_slice_in_dim(array, around[which] * size, size, 1)

    def rows_of(array, which, size):
        return lax.dynamic_slice_in_dim(array, around[which] * size, size, 0)

    def flip(array):
        return jnp.concatenate(
            [
                lax.dynamic_slice_in_dim(array, side * half, half, 0),
                lax.dynamic_slice_in_dim(array, (1 - side) * half, half, 0),
            ],
            axis=0,
        )

    shares = lax.axis_size("dp")
    place = lax.axis_index("dp")

    def share_of(block):
        size = block.shape[0] // shares
        return lax.dynamic_slice_in_dim(block, place * size, size, 0)

    def gather_shares(from_y, from_diag):
        return lax.all_gather(jnp.stack([from_y, from_diag]), "dp", axis=1, tiled=True)

    def ffn_columns(which, rows_at):
        return jnp.concatenate(
            [rows_at(cols_of(w, which, units)) for w in (w_gate, w_up)], axis=1
        )

    down_y, down_diag = (share_of(rows_of(w_down, k, units)) for k in (2, 3))
    share_y, share_diag = ffn_columns(2, share_of), ffn_columns(3, share_of)

    qkv_weights = [
        jnp.concatenate(
            [cols_of(w_query, k, q_width), cols_of(w_key, k, k_width), cols_of(w_value, k, k_width)],
            axis=1,
        )
        for k in range(4)
    ]
    inputs = tokens.astype(f32)
    down_y, down_diag = swap_y(down_y), swap_diag(down_diag)
    share_y, share_diag, inputs = after((share_y, share_diag, inputs), down_y, down_diag)
    scaled_in = low(inputs * attn_gain[None, :])
    raw_own, raw_y, for_y = scatter_width(lambda k: dot(scaled_in, qkv_weights[k]))
    down_gathered = gather_shares(down_y, down_diag)
    w_gate, w_up, w_down, w_out, segment_ids, cotangent, inputs = after(
        (w_gate, w_up, w_down, w_out, segment_ids, cotangent, inputs), for_y
    )
    square_sum = width_total(jnp.sum(inputs * inputs, axis=1))
    cos_table, sin_table = rope_tables(positions_of(segment_ids), head_size)
    side_word = side.astype(jnp.int32).reshape(1)
    tables = (
        cos_table,
        sin_table,
        segment_ids.reshape(rows, 1),
        segment_ids.reshape(1, rows),
        q_gain.reshape(1, head_size),
        k_gain.reshape(1, head_size),
    )
    whole = lambda block: block
    blocks_core = (ffn_columns(1, whole), rows_of(w_down, 1, units))
    raw_y, share_y, share_diag, square_sum = after(
        (raw_y, swap_y(share_y), swap_diag(share_diag), square_sum), raw_own, tables, blocks_core
    )
    ffn_y, ffn_diag = (lax.all_gather(w, "dp", axis=0, tiled=True) for w in (share_y, share_diag))
    attn_rstd = lax.rsqrt(square_sum / full_width + norm_eps)
    attn_hat = inputs * attn_rstd[:, None]
    normed = low(attn_hat * attn_gain[None, :])

    heads = q_width // head_size
    projected, q_low, k_low, v_low, log_totals, att_rel = whole_kernel(
        attend_kernel,
        [
            jax.ShapeDtypeStruct((rows, q_width + 2 * k_width), f32),
            jax.ShapeDtypeStruct((rows, q_width), bf16),
            jax.ShapeDtypeStruct((rows, k_width), bf16),
            jax.ShapeDtypeStruct((rows, k_width), bf16),
            jax.ShapeDtypeStruct((rows, heads), f32),
            jax.ShapeDtypeStruct((rows, q_width), bf16),
        ],
    )(side_word, raw_own, raw_y, attn_rstd.reshape(rows, 1), *tables)
    cot_rel = flip(cotangent)
    cot_y = swap_y(after(cot_rel[:half], raw_y))
    att_y, cot_x, down_gathered = after((swap_y(att_rel), swap_x(cot_y), down_gathered), att_rel)
    atts = [att_rel, swap_core(att_rel), att_y, swap_core(att_y)]
    outs = [rows_of(w_out, k, q_width) for k in range(4)]

    def out_rows(at):
        return (dot(atts[0][at], outs[0]) + dot(atts[1][at], outs[1])) + (
            dot(atts[2][at], outs[2]) + dot(atts[3][at], outs[3])
        )

    from_x = swap_x(low(out_rows(slice(half, rows))))
    home = out_rows(slice(0, half))

    prefetched = (
        swap_core(cot_rel),
        *map(swap_core, blocks_core),
    )
    from_x, (cot_core, ffn_core, down_core), ffn_y = after((from_x, prefetched, ffn_y), home)
    cot_y_core, cot_x_core = swap_core(cot_y), swap_core(cot_x)
    downs = (rows_of(w_down, 0, units), down_core, down_gathered)
    tokens_half = lax.dynamic_slice_in_dim(tokens, side * half, half, 0).astype(f32)
    residual = tokens_half + home + from_x.astype(f32)

    mlp_square = jnp.sum(residual * residual, axis=1)
    mlp_square = width_total(jnp.concatenate([mlp_square, swap_x(mlp_square)]))
    mlp_own = low(residual * mlp_gain[None, :])
    mlp_rstd = lax.rsqrt(mlp_square / full_width + norm_eps)
    quarter = half // 2
    mlp_x, mlp_y, mlp_rstd = after(
        (swap_x(mlp_own), swap_y(mlp_own), mlp_rstd), cot_y_core, cot_x_core
    )
    mlp_xy = (swap_y(mlp_x[:quarter]), swap_x(mlp_y[quarter:]))
    mlp_x_core = swap_core(mlp_x)
    ffns = [ffn_columns(0, whole), ffn_core, ffn_y, ffn_diag]
    downs = [rows_of(w_down, 0, units), down_core, down_gathered]
    ins_own = [mlp_own, swap_core(mlp_own), mlp_y, swap_core(mlp_y)]
    cots_own = [cot_rel, cot_core, cot_y, cot_y_core]
    cots_other = [cot_rel, cot_core, cot_x, cot_x_core]
    rstd_rel = mlp_rstd.reshape(rows, 1)
    first = units_of_half(ins_own, ffns, cots_own, downs, rstd_rel, 0, None)
    mlp_xy, mlp_x_core = after((mlp_xy, mlp_x_core), first)
    mlp_xy = jnp.concatenate(mlp_xy, axis=0)
    ins_other = [mlp_x, mlp_x_core, mlp_xy, swap_core(mlp_xy)]
    hidden, pair, pair_scaled, inner = units_of_half(
        ins_other, ffns, cots_other, downs, rstd_rel, 1, first
    )

    line = LineSums()
    mlp_in, mlp_core = (jnp.concatenate([ins_own[k], ins_other[k]], axis=0) for k in (0, 1))
    line.add("ffn", low(contract_rows(mlp_in, pair_scaled)), 1)
    line.send(line.send())
    pair = after(pair, line.pieces, line.waiting())

    kept = {}

    def started(marker):
        sums = width_total(after(inner[:, 0], marker))
        kept["inner"] = sums
        block = low(contract_rows(mlp_core, after(pair_scaled, marker)))
        kept["core"] = swap_core(block)
        down_core = low(contract_rows(after(hidden, block), cot_core))
        down_own = low(contract_rows(after(hidden, block), cot_rel))
        line.add("down", jnp.concatenate([down_own, swap_core(down_core)], axis=0), 0)
        return (down_own, sums)

    def turned(marker):
        sums = after(kept["inner"], marker)
        kept["inner"] = sums[:half] + swap_x(sums[half:])
        return (kept["inner"], line.send(line.send(marker)))

    mlp_in_grad = scatter_all(lambda k: contract_cols(pair, ffns[k]), started, turned)
    inner_total = kept["inner"]
    mlp_hat = residual * mlp_rstd[:half, None]
    mlp_gain_part = jnp.sum(mlp_in_grad * mlp_hat, axis=0)
    residual_grad = cot_rel[:half].astype(f32) + mlp_rstd[:half, None] * (
        mlp_in_grad * mlp_gain[None, :] - mlp_hat * (inner_total / full_width)[:, None]
    )
    residual_low = low(residual_grad)
    res_x = swap_x(residual_low)
    res_rel = jnp.concatenate([residual_low, res_x], axis=0)
    head_own, head_y, head_sent = scatter_width(lambda k: contract_cols(res_rel, outs[k]))

    line.add("ffn", kept["core"], 1)
    marker = line.send(line.send((head_sent, line.waiting())))
    out_grads = [low(contract_rows(after(part, marker), res_rel)) for part in atts]
    line.add("out", jnp.concatenate(out_grads, axis=0), 0)
    head_own, head_y = after((head_own, head_y), line.waiting())

    proj_low, q_gain_part, k_gain_part, inner_attn = whole_kernel(
        attend_back_kernel,
        [
            jax.ShapeDtypeStruct((rows, q_width + 2 * k_width), bf16),
            jax.ShapeDtypeStruct((1, head_size), f32),
            jax.ShapeDtypeStruct((1, head_size), f32),
            jax.ShapeDtypeStruct((rows, 1), f32),
        ],
        scratch=[pltpu.VMEM((rows, k_width), f32), pltpu.VMEM((rows, k_width), f32)],
    )(side_word, head_own, head_y, projected, q_low, k_low, v_low, log_totals, *tables)
    proj_y, proj_core = swap_y(proj_low), swap_core(proj_low)

    marker = proj_low
    for _ in range(4):
        marker = line.send(marker)
    proj_y, proj_core = after((proj_y, proj_core), marker)
    pairs = lax.all_gather(after(pair_scaled, proj_y), "tc")
    projs = [proj_low, proj_core, proj_y, swap_core(proj_y)]
    normed_part = low(
        (contract_cols(projs[0], qkv_weights[0]) + contract_cols(projs[1], qkv_weights[1]))
        + (contract_cols(projs[2], qkv_weights[2]) + contract_cols(projs[3], qkv_weights[3]))
    )
    small = jnp.concatenate([inner_attn[:, 0], q_gain_part[0], k_gain_part[0]])
    small = width_total(after(small, normed_part))
    small = jnp.concatenate([small, mlp_gain_part])
    normed_x, small_x = after((swap_x(normed_part), swap_x(small)), line.send(small))
    small = small + small_x
    inner_attn, gains = small[:rows], small[rows:]
    hiddens = lax.all_gather(after(hidden, inner_attn), "tc", axis=1, tiled=True)
    gains = jnp.pad(gains, (0, 64 * width - gains.shape[0])).reshape(64, width)
    gains = lax.psum(gains, "dp")
    normed_grad = normed_part.astype(f32) + normed_x.astype(f32)
    token_grad = low(
        flip(res_rel).astype(f32)
        + attn_rstd[:, None]
        * (normed_grad * attn_gain[None, :] - attn_hat * (inner_attn / full_width)[:, None])
    )

    for part in projs:
        line.add("qkv", low(contract_rows(after(normed, normed_part), part)), 1)
    marker = line.send((token_grad, line.waiting()))
    for _ in range(3):
        marker = line.send(marker)
    pairs = after(pairs, marker)
    for k in (2, 3):
        block = lax.dynamic_index_in_dim(pairs, around[k], 0, keepdims=False)
        line.add("ffn", low(contract_rows(mlp_in, block)), 1)
    marker = (marker, line.waiting())
    for _ in range(5):
        marker = line.send(marker)

    hiddens = after(hiddens, marker)
    far_down = [low(contract_rows(cols_of(hiddens, k, units), cot_rel)) for k in (2, 3)]
    line.add("down", jnp.concatenate(far_down, axis=0), 0)
    mlp_away = low(dot(hiddens[half:], w_down))
    mlp_x_out = after(swap_x(mlp_away), line.send((mlp_away, line.waiting())))
    mixed_half = low(residual + dot(hiddens[:half], w_down) + mlp_x_out.astype(f32))
    mixed_x = after(swap_x(mixed_half), line.send(mixed_half))
    mixed = flip(jnp.concatenate([mixed_half, mixed_x], axis=0))
    marker = mixed_x
    while line.queue:
        marker = line.send(marker)
    sums_of = line.finish()

    words = jnp.stack([*around, line.middle.astype(jnp.int32)]).astype(jnp.int32)
    everything = slice(None)

    def spread(start, size, extent):
        while size:
            piece, at = divmod(start, extent)
            taken = min(size, extent - at)
            yield (piece, slice(at, at + taken), taken)
            start, size = start + taken, size - taken

    def runs(first, start, size, extent, out, axis, to=0):
        plan = []
        for piece, at, taken in spread(start, size, extent):
            block = slice(to, to + taken)
            pair_of = lambda part: (part, everything) if axis == 0 else (everything, part)
            plan.append((first + piece, pair_of(at), out, pair_of(block)))
            to += taken
        return plan

    out_sums, qkv_sums, ffn_sums = after(
        (sums_of("out"), sums_of("qkv"), sums_of("ffn")), line.last
    )
    ffn_plan = [
        runs(0, 2 * k * units, units, width, 0, 1) + runs(0, (2 * k + 1) * units, units, width, 1, 1)
        for k in range(4)
    ]
    w_gate_grad, w_up_grad = place_sums(words, ffn_sums, [(w_gate.shape, 1), (w_up.shape, 1)], ffn_plan)
    [w_down_grad] = place_sums(
        words,
        sums_of("down"),
        [(w_down.shape, 0)],
        [runs(0, k * units, units, width, 0, 0) for k in range(4)],
    )
    [w_out_grad] = place_sums(
        words,
        out_sums,
        [(w_out.shape, 0)],
        [runs(0, k * q_width, q_width, width, 0, 0) for k in range(4)],
    )
    block_width = q_width + 2 * k_width
    qkv_plan = [
        runs(0, k * block_width, q_width, width, 0, 1)
        + runs(0, k * block_width + q_width, k_width, width, 1, 1)
        + runs(0, k * block_width + q_width + k_width, k_width, width, 2, 1)
        for k in range(4)
    ]
    w_query_grad, w_key_grad, w_value_grad = place_sums(
        words, qkv_sums, [(w_query.shape, 1), (w_key.shape, 1), (w_value.shape, 1)], qkv_plan
    )
    attn_gain_part = sum(
        jnp.sum(w.astype(f32) * g, axis=1)
        for w, g in ((w_query, w_query_grad), (w_key, w_key_grad), (w_value, w_value_grad))
    )
    attn_gain_grad = (attn_gain_part + swap_x(attn_gain_part)) / attn_gain
    gains = after(gains, line.last).reshape(-1)
    q_gain_grad = gains[:head_size]
    k_gain_grad = gains[head_size : 2 * head_size]
    mlp_gain_grad = gains[2 * head_size : 2 * head_size + width]
    return (
        mixed,
        token_grad,
        attn_gain_grad,
        q_gain_grad,
        k_gain_grad,
        mlp_gain_grad,
        w_query_grad,
        w_key_grad,
        w_value_grad,
        w_out_grad,
        w_gate_grad,
        w_up_grad,
        w_down_grad,
    )


def solution(mesh):
    in_specs = (
        P("dp", "tc"),
        P("dp", "tc"),
        P("dp"),
        P("tc"),
        P(),
        P(),
        P("tc"),
        P("tc", "tr"),
        P("tc", "tr"),
        P("tc", "tr"),
        P("tr", "tc"),
        P("tc", "tr"),
        P("tc", "tr"),
        P("tr", "tc"),
    )
    out_specs = (
        P("dp", "tc"),
        P("dp", "tc"),
        P("tc"),
        P(),
        P(),
        P("tc"),
        P("tc", "tr"),
        P("tc", "tr"),
        P("tc", "tr"),
        P("tr", "tc"),
        P("tc", "tr"),
        P("tc", "tr"),
        P("tr", "tc"),
    )
    return jax.shard_map(
        on_device, mesh=mesh, in_specs=in_specs, out_specs=out_specs, check_vma=False
    )
```

```python
import jax
import jax.numpy as jnp
from jax import lax
from jax.experimental import pallas as pl
from jax.experimental.pallas import tpu as pltpu
from jax.sharding import PartitionSpec as P

norm_eps = 1e-06
rope_base = 1000000.0
neg_big = -1e30
f32 = jnp.float32
bf16 = jnp.bfloat16


def dot(left_side, right_side):
    return jnp.dot(left_side, right_side, preferred_element_type=f32)


def contract_rows(left_side, right_side):
    return lax.dot_general(
        left_side, right_side, (((0,), (0,)), ((), ())), preferred_element_type=f32
    )


def contract_cols(left_side, right_side):
    return lax.dot_general(
        left_side, right_side, (((1,), (1,)), ((), ())), preferred_element_type=f32
    )


def swap_core(block):
    return lax.ppermute(block, "tc", [(i, i ^ 1) for i in range(4)])


def swap_y(block):
    return lax.ppermute(block, "tc", [(i, i ^ 2) for i in range(4)])


def swap_diag(block):
    return lax.ppermute(block, "tc", [(i, i ^ 3) for i in range(4)])


def swap_x(block):
    return lax.ppermute(block, "tr", [(0, 1), (1, 0)])


def width_total(rows):
    rows = rows + swap_core(rows)
    return rows + swap_y(rows)


class LineSums:
    def __init__(self, lag=4):
        self.lag = lag
        self.last = ()
        self.short = lax.axis_size("dp") == 4
        place = lax.axis_index("dp")
        self.middle = (place == 1) | (place == 2)
        self.queue, self.names, self.pieces = [], [], []
        self.outer, self.total = [], []

    def add(self, name, grad, axis):
        size = min(grad.shape)
        for k in range(0, grad.shape[axis], size):
            self.queue.append((name, lax.slice_in_dim(grad, k, k + size, axis=axis)))

    def waiting(self):
        return [piece for _, piece in self.queue]

    def _consume(self, which, marker):
        got, piece = after((self.outer[which], self.pieces[which]), marker)
        inward = low(piece.astype(f32) + got.astype(f32))
        across = lax.ppermute(inward, "dp", [(1, 2), (2, 1)])
        self.total.append(low(inward.astype(f32) + across.astype(f32)))
        return inward

    def _swap_outer(self, piece):
        self.outer.append(lax.ppermute(piece, "dp", [(0, 1), (1, 0), (2, 3), (3, 2)]))

    def send(self, marker=(), strict=True):
        which = len(self.pieces)
        name, piece = self.queue.pop(0)
        self.names.append(name)
        self.pieces.append(piece)
        if not self.short:
            return piece
        if which >= 2:
            marker = self._consume(which - 2, marker)
        out = after(piece, marker)
        if which >= self.lag:
            out = jnp.where(self.middle, self.total[which - self.lag], out)
        self._swap_outer(out)
        return (marker, out) if strict else marker

    def finish(self):
        count = len(self.pieces)
        if self.short:
            for which in (count - 2, count - 1):
                self.last = self._consume(which, ())
            for which in range(count - self.lag, count):
                self._swap_outer(self.total[which])
            sums = [(self.total[k], self.outer[k + self.lag]) for k in range(count)]
        else:
            sums = [(lax.psum(piece, "dp"),) for piece in self.pieces]
        return lambda name: [s for n, s in zip(self.names, sums) if n == name]


def after(value, *others):
    return lax.optimization_barrier((value, others))[0]


def low(array):
    return array.astype(bf16)


def scatter_width(product, near=lambda ready: ready):
    from_far = swap_core(low(product(3)))
    from_core = swap_core(low(product(1)))
    from_far = after(from_far, near(from_far))
    for_y = low(product(2) + from_far.astype(f32))
    from_y = swap_y(for_y)
    return (product(0) + from_core.astype(f32), from_y, for_y)


def scatter_all(product, started, turned):
    far_y, far_own = swap_core(low(product(3))), swap_core(low(product(1)))
    for_y = low(product(2) + far_y.astype(f32))
    own = low(product(0) + far_own.astype(f32))
    half = own.shape[0] // 2
    quarter = half // 2
    width = own.shape[1]
    y_first = swap_y(jnp.concatenate([for_y[quarter:half], for_y[half + quarter :]], axis=0))
    x_first = swap_x(
        jnp.concatenate([own[half : half + quarter], for_y[half : half + quarter]], axis=1)
    )
    x_first, y_first = after((x_first, y_first), started((own, for_y)))
    top_in = low(for_y[:quarter].astype(f32) + x_first[:, width:].astype(f32))
    low_in = low(own[half + quarter :].astype(f32) + y_first[quarter:].astype(f32))
    top_y, low_x = after((swap_y(top_in), swap_x(low_in)), turned((top_in, low_in)))
    top = own[:quarter].astype(f32) + x_first[:, :width].astype(f32) + top_y.astype(f32)
    bottom = own[quarter:half].astype(f32) + y_first[:quarter].astype(f32) + low_x.astype(f32)
    return jnp.concatenate([top, bottom], axis=0)


def positions_of(segment):
    slot_ids = jnp.arange(5, dtype=jnp.int32)
    before = jnp.sum((segment[None, :] < slot_ids[:, None]).astype(jnp.int32), axis=1)
    starts = jnp.sum(jnp.where(segment[:, None] == slot_ids[None, :], before[None, :], 0), axis=1)
    return jnp.arange(segment.shape[0], dtype=jnp.int32) - starts


def rope_tables(positions, head_size):
    half_size = head_size // 2
    frequency = rope_base ** (-jnp.arange(half_size, dtype=f32) * 2.0 / head_size)
    angles = positions.astype(f32)[:, None] * frequency[None, :]
    cosine, sine = jnp.cos(angles), jnp.sin(angles)
    return (
        jnp.concatenate([cosine, cosine], axis=1),
        jnp.concatenate([-sine, sine], axis=1),
    )


def turn(vectors):
    return pltpu.roll(vectors, vectors.shape[-1] // 2, axis=1)


def inverse_norm(vectors):
    return lax.rsqrt(jnp.mean(vectors * vectors, axis=-1, keepdims=True) + norm_eps)


def allowed_keys(seg_col, seg_row, start, size, extent):
    row = lax.broadcasted_iota(jnp.int32, (size, extent), 0) + start
    col = lax.broadcasted_iota(jnp.int32, (size, extent), 1)
    return (seg_col[start : start + size, :] == seg_row[:, :extent]) & (col <= row)


def attend_kernel(
    side, own, from_y, rstd, cos, sin, seg_col, seg_row, q_gain, k_gain,
    proj, q_out, k_out, v_out, lse, att,
):
    rows = own.shape[0]
    size = cos.shape[1]
    heads = q_out.shape[1] // size
    block = rows // 4
    scale = size**-0.5
    k_at = heads * size
    v_at = k_at + size

    def ready(i, carry):
        at = pl.ds(pl.multiple_of(i * block, block), block)
        raw = (own[at, :] + from_y[at, :].astype(f32)) * rstd[at, :]
        proj[at, :] = raw

        def rope(part, gain):
            n = part * inverse_norm(part) * gain[...]
            return (n * cos[at, :] + turn(n) * sin[at, :]).astype(bf16)

        for h in range(heads):
            q_out[at, h * size : (h + 1) * size] = rope(raw[:, h * size : (h + 1) * size], q_gain)
        k_out[at, :] = rope(raw[:, k_at:v_at], k_gain)
        v_out[at, :] = raw[:, v_at:].astype(bf16)
        return carry

    lax.fori_loop(0, 4, ready, 0)
    for i in range(4):
        start = i * block
        extent = start + block
        allowed = allowed_keys(seg_col, seg_row, start, block, extent)
        to = pl.ds(pl.multiple_of(lax.rem(start + side[0] * (rows // 2), rows), block), block)
        for h in range(heads):
            of_head = slice(h * size, (h + 1) * size)
            scores = contract_cols(q_out[start:extent, of_head], k_out[:extent, :]) * scale
            scores = jnp.where(allowed, scores, neg_big)
            top = jnp.max(scores, axis=-1, keepdims=True)
            expd = jnp.exp(scores - top)
            total = jnp.sum(expd, axis=-1, keepdims=True)
            weights = (expd * (1.0 / total)).astype(bf16)
            att[to, of_head] = dot(weights, v_out[:extent, :]).astype(bf16)
            lse[start:extent, h : h + 1] = top + jnp.log(total)


def attend_back_kernel(
    side, own, from_y, proj, q_in, k_in, v_in, lse, cos, sin, seg_col, seg_row, q_gain, k_gain,
    grads, q_gain_part, k_gain_part, inner, k_acc, v_acc,
):
    rows = own.shape[0]
    size = cos.shape[1]
    heads = q_in.shape[1] // size
    block = rows // 4
    scale = size**-0.5
    k_at = heads * size
    v_at = k_at + size

    def unrope(grad, part, gain, start):
        rows_at = slice(start, start + block)
        m = grad * cos[rows_at, :] - turn(grad) * sin[rows_at, :]
        r = inverse_norm(part)
        hat = part * r
        mg = m * gain[...]
        back = (r * (mg - hat * jnp.mean(mg * hat, axis=-1, keepdims=True))).astype(bf16)
        gain_part = jnp.sum(m * hat, axis=0, keepdims=True)
        return (back, gain_part, jnp.sum(back.astype(f32) * part, axis=-1, keepdims=True))

    k_acc[...] = jnp.zeros_like(k_acc)
    v_acc[...] = jnp.zeros_like(v_acc)
    q_total = jnp.zeros(q_gain_part.shape, f32)
    for i in range(4):
        start = i * block
        extent = start + block
        allowed = allowed_keys(seg_col, seg_row, start, block, extent)
        at = pl.ds(pl.multiple_of(lax.rem(start + side[0] * (rows // 2), rows), block), block)
        inner_sum = jnp.zeros((block, 1), f32)
        for h in range(heads):
            of_head = slice(h * size, (h + 1) * size)
            query = q_in[start:extent, of_head]
            grad = (own[at, of_head] + from_y[at, of_head].astype(f32)).astype(bf16)
            scores = contract_cols(query, k_in[:extent, :]) * scale
            scores = jnp.where(allowed, scores, neg_big)
            probs = jnp.exp(scores - lse[start:extent, h : h + 1])
            prob_grad = contract_cols(grad, v_in[:extent, :])
            delta = jnp.sum(probs * prob_grad, axis=-1, keepdims=True)
            score_grad = (probs * (prob_grad - delta)).astype(bf16)
            query_grad = dot(score_grad, k_in[:extent, :]) * scale
            k_acc[:extent, :] += contract_rows(score_grad, query) * scale
            v_acc[:extent, :] += contract_rows(probs.astype(bf16), grad)
            back, gain_part, part_inner = unrope(
                query_grad, proj[start:extent, of_head], q_gain, start
            )
            grads[start:extent, of_head] = back
            q_total = q_total + gain_part
            inner_sum = inner_sum + part_inner
        inner[start:extent, :] = inner_sum
    q_gain_part[...] = q_total
    k_total = jnp.zeros(k_gain_part.shape, f32)
    for i in range(4):
        start = i * block
        extent = start + block
        back, gain_part, part_inner = unrope(
            k_acc[start:extent, :], proj[start:extent, k_at:v_at], k_gain, start
        )
        grads[start:extent, k_at:v_at] = back
        k_total = k_total + gain_part
        v_back = v_acc[start:extent, :].astype(bf16)
        grads[start:extent, v_at:] = v_back
        inner[start:extent, :] += part_inner + jnp.sum(
            v_back.astype(f32) * proj[start:extent, v_at:], axis=-1, keepdims=True
        )
    k_gain_part[...] = k_total


vmem = pl.BlockSpec(memory_space=pltpu.VMEM)
smem = pl.BlockSpec(memory_space=pltpu.SMEM)
def whole_kernel(body, outs, scratch=(), grant=50):
    def call(*operands):
        return pl.pallas_call(
            body,
            out_shape=outs,
            in_specs=[smem if o.ndim == 1 else vmem for o in operands],
            out_specs=[vmem] * len(outs),
            scratch_shapes=scratch,
            compiler_params=pltpu.CompilerParams(vmem_limit_bytes=grant * 2**20),
            cost_estimate=pl.CostEstimate(flops=0, bytes_accessed=2**10, transcendentals=0),
        )(*operands)

    return call


def units_kernel(*refs):
    ins, weights, cots, downs = refs[:4], refs[4:8], refs[8:12], refs[12:16]
    rstd_ref = refs[16]
    hidden, pair, scaled, inner = refs[-4:]
    units = hidden.shape[1]
    chunk = min(256, units)
    rstd = rstd_ref[...]

    def product(at):
        total = dot(ins[0][...], weights[0][:, at])
        for k in range(1, 4):
            total = total + dot(ins[k][...], weights[k][:, at])
        return total * rstd

    inner_sum = jnp.zeros(inner.shape, f32)
    for start in range(0, units, chunk):
        of_gate = slice(start, start + chunk)
        of_up = slice(units + start, units + start + chunk)
        gate, up = product(of_gate), product(of_up)
        grad = contract_cols(cots[0][...], downs[0][of_gate, :])
        for k in range(1, 4):
            grad = grad + contract_cols(cots[k][...], downs[k][of_gate, :])
        sig = jax.nn.sigmoid(gate)
        silu = gate * sig
        hidden[:, of_gate] = low(silu * up)
        gate_grad = low(grad * up * sig * (1.0 + gate * (1.0 - sig)))
        up_grad = low(grad * silu)
        pair[:, of_gate] = gate_grad
        pair[:, of_up] = up_grad
        gate_grad, up_grad = gate_grad.astype(f32), up_grad.astype(f32)
        scaled[:, of_gate] = low(gate_grad * rstd)
        scaled[:, of_up] = low(up_grad * rstd)
        inner_sum = inner_sum + jnp.sum(gate_grad * gate + up_grad * up, axis=-1, keepdims=True)
    inner[...] = inner_sum


def units_of_half(ins, weights, cots, downs, rstd, which, earlier):
    half, depth = ins[0].shape
    units = downs[0].shape[0]
    block = half // 2
    first = which * (half // block)
    outs = [
        jax.ShapeDtypeStruct((2 * half, units), bf16),
        jax.ShapeDtypeStruct((2 * half, 2 * units), bf16),
        jax.ShapeDtypeStruct((2 * half, 2 * units), bf16),
        jax.ShapeDtypeStruct((2 * half, 1), f32),
    ]

    def whole(array):
        return pl.BlockSpec(array.shape, lambda i: (0, 0))

    def of_two(array, k):
        return pl.BlockSpec((None, *array.shape[1:]), lambda i: (k, 0, 0))

    near_by, core, both = downs
    downs = [near_by, core, both, both]
    down_specs = [whole(near_by), whole(core), of_two(both, 0), of_two(both, 1)]
    here = pl.BlockSpec((block, depth), lambda i: (i, 0))
    at = lambda i: (first + i, 0)
    of_all = pl.BlockSpec((block, depth), at)
    earlier = list(earlier or [])
    return pl.pallas_call(
        units_kernel,
        grid=(half // block,),
        out_shape=outs,
        in_specs=[here] * 4
        + [whole(w) for w in weights]
        + [of_all, of_all, here, here]
        + down_specs
        + [pl.BlockSpec((block, 1), at)]
        + [pl.BlockSpec(memory_space=pl.ANY)] * len(earlier),
        out_specs=[pl.BlockSpec((block, o.shape[1]), at) for o in outs],
        input_output_aliases={17 + k: k for k in range(len(earlier))},
        compiler_params=pltpu.CompilerParams(vmem_limit_bytes=50 * 2**20),
        cost_estimate=pl.CostEstimate(flops=0, bytes_accessed=2**10, transcendentals=0),
    )(*ins, *weights, *cots, *downs, rstd, *earlier)


def place_sums(scalars, pieces, outs, plan):
    flat = [a for piece in pieces for a in piece]

    def kernel(words, *refs):
        ins, results = list(refs[: len(flat)]), refs[len(flat) :]
        groups = [[ins.pop(0) for _ in piece] for piece in pieces]
        for k in range(4):

            @pl.when(pl.program_id(0) == k)
            def _(k=k):
                for piece, at, out, to in plan[k]:
                    value = groups[piece][0][at]
                    if len(groups[piece]) == 2:
                        value = jnp.where(words[4] == 1, value, groups[piece][1][at])
                    results[out][to] = value.astype(f32)

    def quarter(shape, axis):
        block = tuple(n // 4 if i == axis else n for i, n in enumerate(shape))
        if axis == 0:
            return pl.BlockSpec(block, lambda k, words: (words[k], 0))
        return pl.BlockSpec(block, lambda k, words: (0, words[k]))

    return pl.pallas_call(
        kernel,
        grid_spec=pltpu.PrefetchScalarGridSpec(
            num_scalar_prefetch=1,
            grid=(4,),
            in_specs=[pl.BlockSpec(a.shape, lambda k, words: (0, 0)) for a in flat],
            out_specs=[quarter(*out) for out in outs],
        ),
        out_shape=[jax.ShapeDtypeStruct(shape, f32) for shape, _ in outs],
        compiler_params=pltpu.CompilerParams(vmem_limit_bytes=50 * 2**20),
        cost_estimate=pl.CostEstimate(flops=0, bytes_accessed=2**10, transcendentals=0),
    )(scalars, *flat)


def on_device(
    tokens,
    cotangent,
    segment_ids,
    attn_gain,
    q_gain,
    k_gain,
    mlp_gain,
    w_query,
    w_key,
    w_value,
    w_out,
    w_gate,
    w_up,
    w_down,
):
    assert lax.axis_size("tc") == 4 and lax.axis_size("tr") == 2
    col = lax.axis_index("tc")
    side = lax.axis_index("tr")
    rows, width = tokens.shape
    half = rows // 2
    full_width = width * 4
    head_size = q_gain.shape[0]
    q_width = w_query.shape[1] // 4
    k_width = w_key.shape[1] // 4
    units = w_gate.shape[1] // 4
    around = [col, col ^ 1, col ^ 2, col ^ 3]

    def cols_of(array, which, size):
        return lax.dynamic_slice_in_dim(array, around[which] * size, size, 1)

    def rows_of(array, which, size):
        return lax.dynamic_slice_in_dim(array, around[which] * size, size, 0)

    def flip(array):
        return jnp.concatenate(
            [
                lax.dynamic_slice_in_dim(array, side * half, half, 0),
                lax.dynamic_slice_in_dim(array, (1 - side) * half, half, 0),
            ],
            axis=0,
        )

    shares = lax.axis_size("dp")
    place = lax.axis_index("dp")

    def share_of(block):
        size = block.shape[0] // shares
        return lax.dynamic_slice_in_dim(block, place * size, size, 0)

    def gather_shares(from_y, from_diag):
        return lax.all_gather(jnp.stack([from_y, from_diag]), "dp", axis=1, tiled=True)

    def ffn_columns(which, rows_at):
        return jnp.concatenate(
            [rows_at(cols_of(w, which, units)) for w in (w_gate, w_up)], axis=1
        )

    down_y, down_diag = (share_of(rows_of(w_down, k, units)) for k in (2, 3))
    share_y, share_diag = ffn_columns(2, share_of), ffn_columns(3, share_of)

    qkv_weights = [
        jnp.concatenate(
            [cols_of(w_query, k, q_width), cols_of(w_key, k, k_width), cols_of(w_value, k, k_width)],
            axis=1,
        )
        for k in range(4)
    ]
    inputs = tokens.astype(f32)
    down_y, down_diag = swap_y(down_y), swap_diag(down_diag)
    share_y, share_diag, inputs = after((share_y, share_diag, inputs), down_y, down_diag)
    scaled_in = low(inputs * attn_gain[None, :])
    raw_own, raw_y, for_y = scatter_width(lambda k: dot(scaled_in, qkv_weights[k]))
    down_gathered = gather_shares(down_y, down_diag)
    w_gate, w_up, w_down, w_out, segment_ids, cotangent, inputs = after(
        (w_gate, w_up, w_down, w_out, segment_ids, cotangent, inputs), for_y
    )
    square_sum = width_total(jnp.sum(inputs * inputs, axis=1))
    cos_table, sin_table = rope_tables(positions_of(segment_ids), head_size)
    side_word = side.astype(jnp.int32).reshape(1)
    tables = (
        cos_table,
        sin_table,
        segment_ids.reshape(rows, 1),
        segment_ids.reshape(1, rows),
        q_gain.reshape(1, head_size),
        k_gain.reshape(1, head_size),
    )
    whole = lambda block: block
    blocks_core = (ffn_columns(1, whole), rows_of(w_down, 1, units))
    raw_y, share_y, share_diag, square_sum = after(
        (raw_y, swap_y(share_y), swap_diag(share_diag), square_sum), raw_own, tables, blocks_core
    )
    ffn_y, ffn_diag = (lax.all_gather(w, "dp", axis=0, tiled=True) for w in (share_y, share_diag))
    attn_rstd = lax.rsqrt(square_sum / full_width + norm_eps)
    attn_hat = inputs * attn_rstd[:, None]
    normed = low(attn_hat * attn_gain[None, :])

    heads = q_width // head_size
    projected, q_low, k_low, v_low, log_totals, att_rel = whole_kernel(
        attend_kernel,
        [
            jax.ShapeDtypeStruct((rows, q_width + 2 * k_width), f32),
            jax.ShapeDtypeStruct((rows, q_width), bf16),
            jax.ShapeDtypeStruct((rows, k_width), bf16),
            jax.ShapeDtypeStruct((rows, k_width), bf16),
            jax.ShapeDtypeStruct((rows, heads), f32),
            jax.ShapeDtypeStruct((rows, q_width), bf16),
        ],
    )(side_word, raw_own, raw_y, attn_rstd.reshape(rows, 1), *tables)
    cot_rel = flip(cotangent)
    cot_y = swap_y(after(cot_rel[:half], raw_y))
    att_y, cot_x, down_gathered = after((swap_y(att_rel), swap_x(cot_y), down_gathered), att_rel)
    atts = [att_rel, swap_core(att_rel), att_y, swap_core(att_y)]
    outs = [rows_of(w_out, k, q_width) for k in range(4)]

    def out_rows(at):
        return (dot(atts[0][at], outs[0]) + dot(atts[1][at], outs[1])) + (
            dot(atts[2][at], outs[2]) + dot(atts[3][at], outs[3])
        )

    from_x = swap_x(low(out_rows(slice(half, rows))))
    home = out_rows(slice(0, half))

    prefetched = (
        swap_core(cot_rel),
        *map(swap_core, blocks_core),
    )
    from_x, (cot_core, ffn_core, down_core), ffn_y = after((from_x, prefetched, ffn_y), home)
    cot_y_core, cot_x_core = swap_core(cot_y), swap_core(cot_x)
    downs = (rows_of(w_down, 0, units), down_core, down_gathered)
    tokens_half = lax.dynamic_slice_in_dim(tokens, side * half, half, 0).astype(f32)
    residual = tokens_half + home + from_x.astype(f32)

    mlp_square = jnp.sum(residual * residual, axis=1)
    mlp_square = width_total(jnp.concatenate([mlp_square, swap_x(mlp_square)]))
    mlp_own = low(residual * mlp_gain[None, :])
    mlp_rstd = lax.rsqrt(mlp_square / full_width + norm_eps)
    quarter = half // 2
    mlp_x, mlp_y, mlp_rstd = after(
        (swap_x(mlp_own), swap_y(mlp_own), mlp_rstd), cot_y_core, cot_x_core
    )
    mlp_xy = (swap_y(mlp_x[:quarter]), swap_x(mlp_y[quarter:]))
    mlp_x_core = swap_core(mlp_x)
    ffns = [ffn_columns(0, whole), ffn_core, ffn_y, ffn_diag]
    downs = [rows_of(w_down, 0, units), down_core, down_gathered]
    ins_own = [mlp_own, swap_core(mlp_own), mlp_y, swap_core(mlp_y)]
    cots_own = [cot_rel, cot_core, cot_y, cot_y_core]
    cots_other = [cot_rel, cot_core, cot_x, cot_x_core]
    rstd_rel = mlp_rstd.reshape(rows, 1)
    first = units_of_half(ins_own, ffns, cots_own, downs, rstd_rel, 0, None)
    mlp_xy, mlp_x_core = after((mlp_xy, mlp_x_core), first)
    mlp_xy = jnp.concatenate(mlp_xy, axis=0)
    ins_other = [mlp_x, mlp_x_core, mlp_xy, swap_core(mlp_xy)]
    hidden, pair, pair_scaled, inner = units_of_half(
        ins_other, ffns, cots_other, downs, rstd_rel, 1, first
    )

    line = LineSums()
    mlp_in, mlp_core = (jnp.concatenate([ins_own[k], ins_other[k]], axis=0) for k in (0, 1))
    line.add("ffn", low(contract_rows(mlp_in, pair_scaled)), 1)
    line.send(line.send())
    pair = after(pair, line.pieces, line.waiting())

    kept = {}

    def started(marker):
        sums = width_total(after(inner[:, 0], marker))
        kept["inner"] = sums
        block = low(contract_rows(mlp_core, after(pair_scaled, marker)))
        kept["core"] = swap_core(block)
        down_core = low(contract_rows(after(hidden, block), cot_core))
        down_own = low(contract_rows(after(hidden, block), cot_rel))
        line.add("down", jnp.concatenate([down_own, swap_core(down_core)], axis=0), 0)
        return (line.send(down_own), sums)

    def turned(marker):
        sums = after(kept["inner"], marker)
        kept["inner"] = sums[:half] + swap_x(sums[half:])
        return (kept["inner"], line.send(marker))

    mlp_in_grad = scatter_all(lambda k: contract_cols(pair, ffns[k]), started, turned)
    inner_total = kept["inner"]
    mlp_hat = residual * mlp_rstd[:half, None]
    mlp_gain_part = jnp.sum(mlp_in_grad * mlp_hat, axis=0)
    residual_grad = cot_rel[:half].astype(f32) + mlp_rstd[:half, None] * (
        mlp_in_grad * mlp_gain[None, :] - mlp_hat * (inner_total / full_width)[:, None]
    )
    residual_low = low(residual_grad)
    res_x = after(swap_x(residual_low), line.send(residual_low))
    res_rel = jnp.concatenate([residual_low, res_x], axis=0)
    head_own, head_y, head_sent = scatter_width(
        lambda k: contract_cols(res_rel, outs[k]), line.send
    )

    line.add("ffn", kept["core"], 1)
    marker = line.send(head_sent)
    out_grads = [low(contract_rows(after(part, marker), res_rel)) for part in atts]
    line.add("out", jnp.concatenate(out_grads, axis=0), 0)
    head_own, head_y = after((head_own, head_y), line.waiting())

    proj_low, q_gain_part, k_gain_part, inner_attn = whole_kernel(
        attend_back_kernel,
        [
            jax.ShapeDtypeStruct((rows, q_width + 2 * k_width), bf16),
            jax.ShapeDtypeStruct((1, head_size), f32),
            jax.ShapeDtypeStruct((1, head_size), f32),
            jax.ShapeDtypeStruct((rows, 1), f32),
        ],
        scratch=[pltpu.VMEM((rows, k_width), f32), pltpu.VMEM((rows, k_width), f32)],
    )(side_word, head_own, head_y, projected, q_low, k_low, v_low, log_totals, *tables)
    proj_y, proj_core = swap_y(proj_low), swap_core(proj_low)

    marker = proj_low
    for _ in range(4):
        marker = line.send(marker)
    proj_y, proj_core = after((proj_y, proj_core), marker)
    pairs = lax.all_gather(after(pair_scaled, proj_y), "tc")
    projs = [proj_low, proj_core, proj_y, swap_core(proj_y)]
    normed_part = low(
        (contract_cols(projs[0], qkv_weights[0]) + contract_cols(projs[1], qkv_weights[1]))
        + (contract_cols(projs[2], qkv_weights[2]) + contract_cols(projs[3], qkv_weights[3]))
    )
    small = jnp.concatenate([inner_attn[:, 0], q_gain_part[0], k_gain_part[0]])
    small = width_total(after(small, normed_part))
    small = jnp.concatenate([small, mlp_gain_part])
    for part in projs:
        line.add("qkv", low(contract_rows(after(normed, normed_part), part)), 1)
    normed_x, small_x = after(
        (swap_x(normed_part), swap_x(small)), line.send((small, line.waiting()))
    )
    small = small + small_x
    inner_attn, gains = small[:rows], small[rows:]
    hiddens = lax.all_gather(after(hidden, inner_attn), "tc", axis=1, tiled=True)
    spare = jnp.pad(low(gains), (0, width * width - gains.shape[0]))
    line.add("gains", spare.reshape(width, width), 0)
    normed_grad = normed_part.astype(f32) + normed_x.astype(f32)
    token_grad = low(
        flip(res_rel).astype(f32)
        + attn_rstd[:, None]
        * (normed_grad * attn_gain[None, :] - attn_hat * (inner_attn / full_width)[:, None])
    )

    marker = line.send((token_grad, line.waiting()), False)
    for _ in range(3):
        marker = line.send(marker, False)
    pairs = after(pairs, marker)
    for k in (2, 3):
        block = lax.dynamic_index_in_dim(pairs, around[k], 0, keepdims=False)
        line.add("ffn", low(contract_rows(mlp_in, block)), 1)
    for _ in range(5):
        marker = line.send(marker, False)

    hiddens = after(hiddens, marker)
    far_down = [low(contract_rows(cols_of(hiddens, k, units), cot_rel)) for k in (2, 3)]
    line.add("down", jnp.concatenate(far_down, axis=0), 0)
    mlp_away = low(dot(hiddens[half:], w_down))
    mlp_x_out = after(swap_x(mlp_away), line.send(mlp_away, False))
    mixed_half = low(residual + dot(hiddens[:half], w_down) + mlp_x_out.astype(f32))
    mixed_x = after(swap_x(mixed_half), line.send(mixed_half, False))
    mixed = flip(jnp.concatenate([mixed_half, mixed_x], axis=0))
    marker = mixed_x
    while line.queue:
        marker = line.send(marker, False)
    sums_of = line.finish()

    words = jnp.stack([*around, line.middle.astype(jnp.int32)]).astype(jnp.int32)
    everything = slice(None)

    def spread(start, size, extent):
        while size:
            piece, at = divmod(start, extent)
            taken = min(size, extent - at)
            yield (piece, slice(at, at + taken), taken)
            start, size = start + taken, size - taken

    def runs(first, start, size, extent, out, axis, to=0):
        plan = []
        for piece, at, taken in spread(start, size, extent):
            block = slice(to, to + taken)
            pair_of = lambda part: (part, everything) if axis == 0 else (everything, part)
            plan.append((first + piece, pair_of(at), out, pair_of(block)))
            to += taken
        return plan

    out_sums, qkv_sums, ffn_sums = after(
        (sums_of("out"), sums_of("qkv"), sums_of("ffn")), line.last
    )
    ffn_plan = [
        runs(0, 2 * k * units, units, width, 0, 1) + runs(0, (2 * k + 1) * units, units, width, 1, 1)
        for k in range(4)
    ]
    w_gate_grad, w_up_grad = place_sums(words, ffn_sums, [(w_gate.shape, 1), (w_up.shape, 1)], ffn_plan)
    [w_down_grad] = place_sums(
        words,
        sums_of("down"),
        [(w_down.shape, 0)],
        [runs(0, k * units, units, width, 0, 0) for k in range(4)],
    )
    [w_out_grad] = place_sums(
        words,
        out_sums,
        [(w_out.shape, 0)],
        [runs(0, k * q_width, q_width, width, 0, 0) for k in range(4)],
    )
    block_width = q_width + 2 * k_width
    qkv_plan = [
        runs(0, k * block_width, q_width, width, 0, 1)
        + runs(0, k * block_width + q_width, k_width, width, 1, 1)
        + runs(0, k * block_width + q_width + k_width, k_width, width, 2, 1)
        for k in range(4)
    ]
    w_query_grad, w_key_grad, w_value_grad = place_sums(
        words, qkv_sums, [(w_query.shape, 1), (w_key.shape, 1), (w_value.shape, 1)], qkv_plan
    )
    attn_gain_part = sum(
        jnp.sum(w.astype(f32) * g, axis=1)
        for w, g in ((w_query, w_query_grad), (w_key, w_key_grad), (w_value, w_value_grad))
    )
    attn_gain_grad = (attn_gain_part + swap_x(attn_gain_part)) / attn_gain
    [gain_sums] = sums_of("gains")
    gains = jnp.where(line.middle, gain_sums[0], gain_sums[-1]).reshape(-1).astype(f32)
    q_gain_grad = gains[:head_size]
    k_gain_grad = gains[head_size : 2 * head_size]
    mlp_gain_grad = gains[2 * head_size : 2 * head_size + width]
    return (
        mixed,
        token_grad,
        attn_gain_grad,
        q_gain_grad,
        k_gain_grad,
        mlp_gain_grad,
        w_query_grad,
        w_key_grad,
        w_value_grad,
        w_out_grad,
        w_gate_grad,
        w_up_grad,
        w_down_grad,
    )


def solution(mesh):
    in_specs = (
        P("dp", "tc"),
        P("dp", "tc"),
        P("dp"),
        P("tc"),
        P(),
        P(),
        P("tc"),
        P("tc", "tr"),
        P("tc", "tr"),
        P("tc", "tr"),
        P("tr", "tc"),
        P("tc", "tr"),
        P("tc", "tr"),
        P("tr", "tc"),
    )
    out_specs = (
        P("dp", "tc"),
        P("dp", "tc"),
        P("tc"),
        P(),
        P(),
        P("tc"),
        P("tc", "tr"),
        P("tc", "tr"),
        P("tc", "tr"),
        P("tr", "tc"),
        P("tc", "tr"),
        P("tc", "tr"),
        P("tr", "tc"),
    )
    return jax.shard_map(
        on_device, mesh=mesh, in_specs=in_specs, out_specs=out_specs, check_vma=False
    )
```

```python
import jax
import jax.numpy as jnp
from jax import lax
from jax.experimental import pallas as pl
from jax.experimental.pallas import tpu as pltpu
from jax.sharding import PartitionSpec as P

norm_eps = 1e-06
rope_base = 1000000.0
neg_big = -1e30
f32 = jnp.float32
bf16 = jnp.bfloat16


def dot(left_side, right_side):
    return jnp.dot(left_side, right_side, preferred_element_type=f32)


def contract_rows(left_side, right_side):
    return lax.dot_general(
        left_side, right_side, (((0,), (0,)), ((), ())), preferred_element_type=f32
    )


def contract_cols(left_side, right_side):
    return lax.dot_general(
        left_side, right_side, (((1,), (1,)), ((), ())), preferred_element_type=f32
    )


def swap_core(block):
    return lax.ppermute(block, "tc", [(i, i ^ 1) for i in range(4)])


def swap_y(block):
    return lax.ppermute(block, "tc", [(i, i ^ 2) for i in range(4)])


def swap_diag(block):
    return lax.ppermute(block, "tc", [(i, i ^ 3) for i in range(4)])


def swap_x(block):
    return lax.ppermute(block, "tr", [(0, 1), (1, 0)])


def width_total(rows):
    rows = rows + swap_core(rows)
    return rows + swap_y(rows)


class LineSums:
    def __init__(self, lag=4):
        self.lag = lag
        self.last = ()
        self.short = lax.axis_size("dp") == 4
        place = lax.axis_index("dp")
        self.middle = (place == 1) | (place == 2)
        self.queue, self.names, self.pieces = [], [], []
        self.outer, self.total = [], []

    def add(self, name, grad, axis):
        size = min(grad.shape)
        for k in range(0, grad.shape[axis], size):
            self.queue.append((name, lax.slice_in_dim(grad, k, k + size, axis=axis)))

    def waiting(self):
        return [piece for _, piece in self.queue]

    def _consume(self, which, marker):
        got, piece = after((self.outer[which], self.pieces[which]), marker)
        inward = low(piece.astype(f32) + got.astype(f32))
        across = lax.ppermute(inward, "dp", [(1, 2), (2, 1)])
        self.total.append(low(inward.astype(f32) + across.astype(f32)))
        return inward

    def _swap_outer(self, piece):
        self.outer.append(lax.ppermute(piece, "dp", [(0, 1), (1, 0), (2, 3), (3, 2)]))

    def send(self, marker=(), strict=True):
        which = len(self.pieces)
        name, piece = self.queue.pop(0)
        self.names.append(name)
        self.pieces.append(piece)
        if not self.short:
            return piece
        if which >= 2:
            marker = self._consume(which - 2, marker)
        out = after(piece, marker)
        if which >= self.lag:
            out = jnp.where(self.middle, self.total[which - self.lag], out)
        self._swap_outer(out)
        return (marker, out) if strict else marker

    def finish(self):
        count = len(self.pieces)
        if self.short:
            self.last = self._consume(count - 2, ())
            self._consume(count - 1, ())
            for which in range(count - self.lag, count):
                self._swap_outer(self.total[which])
            sums = [(self.total[k], self.outer[k + self.lag]) for k in range(count)]
        else:
            sums = [(lax.psum(piece, "dp"),) for piece in self.pieces]
        return lambda name: [s for n, s in zip(self.names, sums) if n == name]


def after(value, *others):
    return lax.optimization_barrier((value, others))[0]


def low(array):
    return array.astype(bf16)


def scatter_width(product, near=lambda ready: ready):
    from_far = swap_core(low(product(3)))
    from_core = swap_core(low(product(1)))
    from_far = after(from_far, near(from_far))
    for_y = low(product(2) + from_far.astype(f32))
    from_y = swap_y(for_y)
    return (product(0) + from_core.astype(f32), from_y, for_y)


def scatter_all(product, started, turned):
    far_y, far_own = swap_core(low(product(3))), swap_core(low(product(1)))
    for_y = low(product(2) + far_y.astype(f32))
    own = low(product(0) + far_own.astype(f32))
    half = own.shape[0] // 2
    quarter = half // 2
    width = own.shape[1]
    y_first = swap_y(jnp.concatenate([for_y[quarter:half], for_y[half + quarter :]], axis=0))
    x_first = swap_x(
        jnp.concatenate([own[half : half + quarter], for_y[half : half + quarter]], axis=1)
    )
    x_first, y_first = after((x_first, y_first), started((own, for_y)))
    top_in = low(for_y[:quarter].astype(f32) + x_first[:, width:].astype(f32))
    low_in = low(own[half + quarter :].astype(f32) + y_first[quarter:].astype(f32))
    top_y, low_x = after((swap_y(top_in), swap_x(low_in)), turned((top_in, low_in)))
    top = own[:quarter].astype(f32) + x_first[:, :width].astype(f32) + top_y.astype(f32)
    bottom = own[quarter:half].astype(f32) + y_first[:quarter].astype(f32) + low_x.astype(f32)
    return jnp.concatenate([top, bottom], axis=0)


def positions_of(segment):
    slot_ids = jnp.arange(5, dtype=jnp.int32)
    before = jnp.sum((segment[None, :] < slot_ids[:, None]).astype(jnp.int32), axis=1)
    starts = jnp.sum(jnp.where(segment[:, None] == slot_ids[None, :], before[None, :], 0), axis=1)
    return jnp.arange(segment.shape[0], dtype=jnp.int32) - starts


def rope_tables(positions, head_size):
    half_size = head_size // 2
    frequency = rope_base ** (-jnp.arange(half_size, dtype=f32) * 2.0 / head_size)
    angles = positions.astype(f32)[:, None] * frequency[None, :]
    cosine, sine = jnp.cos(angles), jnp.sin(angles)
    return (
        jnp.concatenate([cosine, cosine], axis=1),
        jnp.concatenate([-sine, sine], axis=1),
    )


def turn(vectors):
    return pltpu.roll(vectors, vectors.shape[-1] // 2, axis=1)


def inverse_norm(vectors):
    return lax.rsqrt(jnp.mean(vectors * vectors, axis=-1, keepdims=True) + norm_eps)


def allowed_keys(seg_col, seg_row, start, size, extent):
    row = lax.broadcasted_iota(jnp.int32, (size, extent), 0) + start
    col = lax.broadcasted_iota(jnp.int32, (size, extent), 1)
    return (seg_col[start : start + size, :] == seg_row[:, :extent]) & (col <= row)


def attend_kernel(
    side, own, from_y, rstd, cos, sin, seg_col, seg_row, q_gain, k_gain,
    proj, q_out, k_out, v_out, lse, att,
):
    rows = own.shape[0]
    size = cos.shape[1]
    heads = q_out.shape[1] // size
    block = rows // 4
    scale = size**-0.5
    k_at = heads * size
    v_at = k_at + size

    def ready(i, carry):
        at = pl.ds(pl.multiple_of(i * block, block), block)
        raw = (own[at, :] + from_y[at, :].astype(f32)) * rstd[at, :]
        proj[at, :] = raw

        def rope(part, gain):
            n = part * inverse_norm(part) * gain[...]
            return (n * cos[at, :] + turn(n) * sin[at, :]).astype(bf16)

        for h in range(heads):
            q_out[at, h * size : (h + 1) * size] = rope(raw[:, h * size : (h + 1) * size], q_gain)
        k_out[at, :] = rope(raw[:, k_at:v_at], k_gain)
        v_out[at, :] = raw[:, v_at:].astype(bf16)
        return carry

    lax.fori_loop(0, 4, ready, 0)
    for i in range(4):
        start = i * block
        extent = start + block
        allowed = allowed_keys(seg_col, seg_row, start, block, extent)
        to = pl.ds(pl.multiple_of(lax.rem(start + side[0] * (rows // 2), rows), block), block)
        for h in range(heads):
            of_head = slice(h * size, (h + 1) * size)
            scores = contract_cols(q_out[start:extent, of_head], k_out[:extent, :]) * scale
            scores = jnp.where(allowed, scores, neg_big)
            top = jnp.max(scores, axis=-1, keepdims=True)
            expd = jnp.exp(scores - top)
            total = jnp.sum(expd, axis=-1, keepdims=True)
            weights = (expd * (1.0 / total)).astype(bf16)
            att[to, of_head] = dot(weights, v_out[:extent, :]).astype(bf16)
            lse[start:extent, h : h + 1] = top + jnp.log(total)


def attend_back_kernel(
    side, own, from_y, proj, q_in, k_in, v_in, lse, cos, sin, seg_col, seg_row, q_gain, k_gain,
    grads, q_gain_part, k_gain_part, inner, k_acc, v_acc,
):
    rows = own.shape[0]
    size = cos.shape[1]
    heads = q_in.shape[1] // size
    block = rows // 4
    scale = size**-0.5
    k_at = heads * size
    v_at = k_at + size

    def unrope(grad, part, gain, start):
        rows_at = slice(start, start + block)
        m = grad * cos[rows_at, :] - turn(grad) * sin[rows_at, :]
        r = inverse_norm(part)
        hat = part * r
        mg = m * gain[...]
        back = (r * (mg - hat * jnp.mean(mg * hat, axis=-1, keepdims=True))).astype(bf16)
        gain_part = jnp.sum(m * hat, axis=0, keepdims=True)
        return (back, gain_part, jnp.sum(back.astype(f32) * part, axis=-1, keepdims=True))

    k_acc[...] = jnp.zeros_like(k_acc)
    v_acc[...] = jnp.zeros_like(v_acc)
    q_total = jnp.zeros(q_gain_part.shape, f32)
    for i in range(4):
        start = i * block
        extent = start + block
        allowed = allowed_keys(seg_col, seg_row, start, block, extent)
        at = pl.ds(pl.multiple_of(lax.rem(start + side[0] * (rows // 2), rows), block), block)
        inner_sum = jnp.zeros((block, 1), f32)
        for h in range(heads):
            of_head = slice(h * size, (h + 1) * size)
            query = q_in[start:extent, of_head]
            grad = (own[at, of_head] + from_y[at, of_head].astype(f32)).astype(bf16)
            scores = contract_cols(query, k_in[:extent, :]) * scale
            scores = jnp.where(allowed, scores, neg_big)
            probs = jnp.exp(scores - lse[start:extent, h : h + 1])
            prob_grad = contract_cols(grad, v_in[:extent, :])
            delta = jnp.sum(probs * prob_grad, axis=-1, keepdims=True)
            score_grad = (probs * (prob_grad - delta)).astype(bf16)
            query_grad = dot(score_grad, k_in[:extent, :]) * scale
            k_acc[:extent, :] += contract_rows(score_grad, query) * scale
            v_acc[:extent, :] += contract_rows(probs.astype(bf16), grad)
            back, gain_part, part_inner = unrope(
                query_grad, proj[start:extent, of_head], q_gain, start
            )
            grads[start:extent, of_head] = back
            q_total = q_total + gain_part
            inner_sum = inner_sum + part_inner
        inner[start:extent, :] = inner_sum
    q_gain_part[...] = q_total
    k_total = jnp.zeros(k_gain_part.shape, f32)
    for i in range(4):
        start = i * block
        extent = start + block
        back, gain_part, part_inner = unrope(
            k_acc[start:extent, :], proj[start:extent, k_at:v_at], k_gain, start
        )
        grads[start:extent, k_at:v_at] = back
        k_total = k_total + gain_part
        v_back = v_acc[start:extent, :].astype(bf16)
        grads[start:extent, v_at:] = v_back
        inner[start:extent, :] += part_inner + jnp.sum(
            v_back.astype(f32) * proj[start:extent, v_at:], axis=-1, keepdims=True
        )
    k_gain_part[...] = k_total


vmem = pl.BlockSpec(memory_space=pltpu.VMEM)
smem = pl.BlockSpec(memory_space=pltpu.SMEM)
def whole_kernel(body, outs, scratch=(), grant=50):
    def call(*operands):
        return pl.pallas_call(
            body,
            out_shape=outs,
            in_specs=[smem if o.ndim == 1 else vmem for o in operands],
            out_specs=[vmem] * len(outs),
            scratch_shapes=scratch,
            compiler_params=pltpu.CompilerParams(vmem_limit_bytes=grant * 2**20),
            cost_estimate=pl.CostEstimate(flops=0, bytes_accessed=2**10, transcendentals=0),
        )(*operands)

    return call


def units_kernel(*refs):
    ins, weights, cots, downs = refs[:4], refs[4:8], refs[8:12], refs[12:16]
    rstd_ref = refs[16]
    hidden, pair, scaled, inner = refs[-4:]
    units = hidden.shape[1]
    chunk = min(256, units)
    rstd = rstd_ref[...]

    def product(at):
        total = dot(ins[0][...], weights[0][:, at])
        for k in range(1, 4):
            total = total + dot(ins[k][...], weights[k][:, at])
        return total * rstd

    inner_sum = jnp.zeros(inner.shape, f32)
    for start in range(0, units, chunk):
        of_gate = slice(start, start + chunk)
        of_up = slice(units + start, units + start + chunk)
        gate, up = product(of_gate), product(of_up)
        grad = contract_cols(cots[0][...], downs[0][of_gate, :])
        for k in range(1, 4):
            grad = grad + contract_cols(cots[k][...], downs[k][of_gate, :])
        sig = jax.nn.sigmoid(gate)
        silu = gate * sig
        hidden[:, of_gate] = low(silu * up)
        gate_grad = low(grad * up * sig * (1.0 + gate * (1.0 - sig)))
        up_grad = low(grad * silu)
        pair[:, of_gate] = gate_grad
        pair[:, of_up] = up_grad
        gate_grad, up_grad = gate_grad.astype(f32), up_grad.astype(f32)
        scaled[:, of_gate] = low(gate_grad * rstd)
        scaled[:, of_up] = low(up_grad * rstd)
        inner_sum = inner_sum + jnp.sum(gate_grad * gate + up_grad * up, axis=-1, keepdims=True)
    inner[...] = inner_sum


def units_of_half(ins, weights, cots, downs, rstd, which, earlier):
    half, depth = ins[0].shape
    units = downs[0].shape[0]
    block = half // 2
    first = which * (half // block)
    outs = [
        jax.ShapeDtypeStruct((2 * half, units), bf16),
        jax.ShapeDtypeStruct((2 * half, 2 * units), bf16),
        jax.ShapeDtypeStruct((2 * half, 2 * units), bf16),
        jax.ShapeDtypeStruct((2 * half, 1), f32),
    ]

    def whole(array):
        return pl.BlockSpec(array.shape, lambda i: (0, 0))

    def of_two(array, k):
        return pl.BlockSpec((None, *array.shape[1:]), lambda i: (k, 0, 0))

    near_by, core, both = downs
    downs = [near_by, core, both, both]
    down_specs = [whole(near_by), whole(core), of_two(both, 0), of_two(both, 1)]
    here = pl.BlockSpec((block, depth), lambda i: (i, 0))
    at = lambda i: (first + i, 0)
    of_all = pl.BlockSpec((block, depth), at)
    earlier = list(earlier or [])
    return pl.pallas_call(
        units_kernel,
        grid=(half // block,),
        out_shape=outs,
        in_specs=[here] * 4
        + [whole(w) for w in weights]
        + [of_all, of_all, here, here]
        + down_specs
        + [pl.BlockSpec((block, 1), at)]
        + [pl.BlockSpec(memory_space=pl.ANY)] * len(earlier),
        out_specs=[pl.BlockSpec((block, o.shape[1]), at) for o in outs],
        input_output_aliases={17 + k: k for k in range(len(earlier))},
        compiler_params=pltpu.CompilerParams(vmem_limit_bytes=50 * 2**20),
        cost_estimate=pl.CostEstimate(flops=0, bytes_accessed=2**10, transcendentals=0),
    )(*ins, *weights, *cots, *downs, rstd, *earlier)


def place_sums(scalars, pieces, outs, plan):
    flat = [a for piece in pieces for a in piece]

    def kernel(words, *refs):
        ins, results = list(refs[: len(flat)]), refs[len(flat) :]
        groups = [[ins.pop(0) for _ in piece] for piece in pieces]
        for k in range(4):

            @pl.when(pl.program_id(0) == k)
            def _(k=k):
                for piece, at, out, to in plan[k]:
                    value = groups[piece][0][at]
                    if len(groups[piece]) == 2:
                        value = jnp.where(words[4] == 1, value, groups[piece][1][at])
                    results[out][to] = value.astype(f32)

    def quarter(shape, axis):
        block = tuple(n // 4 if i == axis else n for i, n in enumerate(shape))
        if axis == 0:
            return pl.BlockSpec(block, lambda k, words: (words[k], 0))
        return pl.BlockSpec(block, lambda k, words: (0, words[k]))

    return pl.pallas_call(
        kernel,
        grid_spec=pltpu.PrefetchScalarGridSpec(
            num_scalar_prefetch=1,
            grid=(4,),
            in_specs=[pl.BlockSpec(a.shape, lambda k, words: (0, 0)) for a in flat],
            out_specs=[quarter(*out) for out in outs],
        ),
        out_shape=[jax.ShapeDtypeStruct(shape, f32) for shape, _ in outs],
        compiler_params=pltpu.CompilerParams(vmem_limit_bytes=50 * 2**20),
        cost_estimate=pl.CostEstimate(flops=0, bytes_accessed=2**10, transcendentals=0),
    )(scalars, *flat)


def on_device(
    tokens,
    cotangent,
    segment_ids,
    attn_gain,
    q_gain,
    k_gain,
    mlp_gain,
    w_query,
    w_key,
    w_value,
    w_out,
    w_gate,
    w_up,
    w_down,
):
    assert lax.axis_size("tc") == 4 and lax.axis_size("tr") == 2
    col = lax.axis_index("tc")
    side = lax.axis_index("tr")
    rows, width = tokens.shape
    half = rows // 2
    full_width = width * 4
    head_size = q_gain.shape[0]
    q_width = w_query.shape[1] // 4
    k_width = w_key.shape[1] // 4
    units = w_gate.shape[1] // 4
    around = [col, col ^ 1, col ^ 2, col ^ 3]

    def cols_of(array, which, size):
        return lax.dynamic_slice_in_dim(array, around[which] * size, size, 1)

    def rows_of(array, which, size):
        return lax.dynamic_slice_in_dim(array, around[which] * size, size, 0)

    def flip(array):
        return jnp.concatenate(
            [
                lax.dynamic_slice_in_dim(array, side * half, half, 0),
                lax.dynamic_slice_in_dim(array, (1 - side) * half, half, 0),
            ],
            axis=0,
        )

    shares = lax.axis_size("dp")
    place = lax.axis_index("dp")

    def share_of(block):
        size = block.shape[0] // shares
        return lax.dynamic_slice_in_dim(block, place * size, size, 0)

    def gather_shares(from_y, from_diag):
        return lax.all_gather(jnp.stack([from_y, from_diag]), "dp", axis=1, tiled=True)

    def ffn_columns(which, rows_at):
        return jnp.concatenate(
            [rows_at(cols_of(w, which, units)) for w in (w_gate, w_up)], axis=1
        )

    down_y, down_diag = (share_of(rows_of(w_down, k, units)) for k in (2, 3))
    share_y, share_diag = ffn_columns(2, share_of), ffn_columns(3, share_of)

    qkv_weights = [
        jnp.concatenate(
            [cols_of(w_query, k, q_width), cols_of(w_key, k, k_width), cols_of(w_value, k, k_width)],
            axis=1,
        )
        for k in range(4)
    ]
    inputs = tokens.astype(f32)
    down_y, down_diag = swap_y(down_y), swap_diag(down_diag)
    share_y, share_diag, inputs = after((share_y, share_diag, inputs), down_y, down_diag)
    scaled_in = low(inputs * attn_gain[None, :])
    raw_own, raw_y, for_y = scatter_width(lambda k: dot(scaled_in, qkv_weights[k]))
    down_gathered = gather_shares(down_y, down_diag)
    w_gate, w_up, w_down, w_out, segment_ids, cotangent, inputs = after(
        (w_gate, w_up, w_down, w_out, segment_ids, cotangent, inputs), for_y
    )
    square_sum = width_total(jnp.sum(inputs * inputs, axis=1))
    cos_table, sin_table = rope_tables(positions_of(segment_ids), head_size)
    side_word = side.astype(jnp.int32).reshape(1)
    tables = (
        cos_table,
        sin_table,
        segment_ids.reshape(rows, 1),
        segment_ids.reshape(1, rows),
        q_gain.reshape(1, head_size),
        k_gain.reshape(1, head_size),
    )
    whole = lambda block: block
    blocks_core = (ffn_columns(1, whole), rows_of(w_down, 1, units))
    raw_y, share_y, share_diag, square_sum = after(
        (raw_y, swap_y(share_y), swap_diag(share_diag), square_sum), raw_own, tables, blocks_core
    )
    ffn_y, ffn_diag = (lax.all_gather(w, "dp", axis=0, tiled=True) for w in (share_y, share_diag))
    attn_rstd = lax.rsqrt(square_sum / full_width + norm_eps)
    attn_hat = inputs * attn_rstd[:, None]
    normed = low(attn_hat * attn_gain[None, :])

    heads = q_width // head_size
    projected, q_low, k_low, v_low, log_totals, att_rel = whole_kernel(
        attend_kernel,
        [
            jax.ShapeDtypeStruct((rows, q_width + 2 * k_width), f32),
            jax.ShapeDtypeStruct((rows, q_width), bf16),
            jax.ShapeDtypeStruct((rows, k_width), bf16),
            jax.ShapeDtypeStruct((rows, k_width), bf16),
            jax.ShapeDtypeStruct((rows, heads), f32),
            jax.ShapeDtypeStruct((rows, q_width), bf16),
        ],
    )(side_word, raw_own, raw_y, attn_rstd.reshape(rows, 1), *tables)
    cot_rel = flip(cotangent)
    cot_y = swap_y(after(cot_rel[:half], raw_y))
    att_y, cot_x, down_gathered = after((swap_y(att_rel), swap_x(cot_y), down_gathered), att_rel)
    atts = [att_rel, swap_core(att_rel), att_y, swap_core(att_y)]
    outs = [rows_of(w_out, k, q_width) for k in range(4)]

    def out_rows(at):
        return (dot(atts[0][at], outs[0]) + dot(atts[1][at], outs[1])) + (
            dot(atts[2][at], outs[2]) + dot(atts[3][at], outs[3])
        )

    from_x = swap_x(low(out_rows(slice(half, rows))))
    home = out_rows(slice(0, half))

    prefetched = (
        swap_core(cot_rel),
        *map(swap_core, blocks_core),
    )
    from_x, (cot_core, ffn_core, down_core), ffn_y = after((from_x, prefetched, ffn_y), home)
    cot_y_core, cot_x_core = swap_core(cot_y), swap_core(cot_x)
    downs = (rows_of(w_down, 0, units), down_core, down_gathered)
    tokens_half = lax.dynamic_slice_in_dim(tokens, side * half, half, 0).astype(f32)
    residual = tokens_half + home + from_x.astype(f32)

    mlp_square = jnp.sum(residual * residual, axis=1)
    mlp_square = width_total(jnp.concatenate([mlp_square, swap_x(mlp_square)]))
    mlp_own = low(residual * mlp_gain[None, :])
    mlp_rstd = lax.rsqrt(mlp_square / full_width + norm_eps)
    quarter = half // 2
    mlp_x, mlp_y, mlp_rstd = after(
        (swap_x(mlp_own), swap_y(mlp_own), mlp_rstd), cot_y_core, cot_x_core
    )
    mlp_xy = (swap_y(mlp_x[:quarter]), swap_x(mlp_y[quarter:]))
    mlp_x_core = swap_core(mlp_x)
    ffns = [ffn_columns(0, whole), ffn_core, ffn_y, ffn_diag]
    downs = [rows_of(w_down, 0, units), down_core, down_gathered]
    ins_own = [mlp_own, swap_core(mlp_own), mlp_y, swap_core(mlp_y)]
    cots_own = [cot_rel, cot_core, cot_y, cot_y_core]
    cots_other = [cot_rel, cot_core, cot_x, cot_x_core]
    rstd_rel = mlp_rstd.reshape(rows, 1)
    first = units_of_half(ins_own, ffns, cots_own, downs, rstd_rel, 0, None)
    mlp_xy, mlp_x_core = after((mlp_xy, mlp_x_core), first)
    mlp_xy = jnp.concatenate(mlp_xy, axis=0)
    ins_other = [mlp_x, mlp_x_core, mlp_xy, swap_core(mlp_xy)]
    hidden, pair, pair_scaled, inner = units_of_half(
        ins_other, ffns, cots_other, downs, rstd_rel, 1, first
    )

    line = LineSums()
    mlp_in, mlp_core = (jnp.concatenate([ins_own[k], ins_other[k]], axis=0) for k in (0, 1))
    line.add("ffn", low(contract_rows(mlp_in, pair_scaled)), 1)
    line.send(line.send())
    pair = after(pair, line.pieces, line.waiting())

    kept = {}

    def started(marker):
        sums = width_total(after(inner[:, 0], marker))
        kept["inner"] = sums
        block = low(contract_rows(mlp_core, after(pair_scaled, marker)))
        kept["core"] = swap_core(block)
        down_core = low(contract_rows(after(hidden, block), cot_core))
        down_own = low(contract_rows(after(hidden, block), cot_rel))
        line.add("down", jnp.concatenate([down_own, swap_core(down_core)], axis=0), 0)
        return (line.send(down_own), sums)

    def turned(marker):
        sums = after(kept["inner"], marker)
        kept["inner"] = sums[:half] + swap_x(sums[half:])
        return (kept["inner"], line.send(marker))

    mlp_in_grad = scatter_all(lambda k: contract_cols(pair, ffns[k]), started, turned)
    inner_total = kept["inner"]
    mlp_hat = residual * mlp_rstd[:half, None]
    mlp_gain_part = jnp.sum(mlp_in_grad * mlp_hat, axis=0)
    residual_grad = cot_rel[:half].astype(f32) + mlp_rstd[:half, None] * (
        mlp_in_grad * mlp_gain[None, :] - mlp_hat * (inner_total / full_width)[:, None]
    )
    residual_low = low(residual_grad)
    res_x = after(swap_x(residual_low), line.send(residual_low))
    res_rel = jnp.concatenate([residual_low, res_x], axis=0)
    head_own, head_y, head_sent = scatter_width(
        lambda k: contract_cols(res_rel, outs[k]), line.send
    )

    line.add("ffn", kept["core"], 1)
    marker = line.send(head_sent)
    out_grads = [low(contract_rows(after(part, marker), res_rel)) for part in atts]
    line.add("out", jnp.concatenate(out_grads, axis=0), 0)
    head_own, head_y = after((head_own, head_y), line.waiting())

    proj_low, q_gain_part, k_gain_part, inner_attn = whole_kernel(
        attend_back_kernel,
        [
            jax.ShapeDtypeStruct((rows, q_width + 2 * k_width), bf16),
            jax.ShapeDtypeStruct((1, head_size), f32),
            jax.ShapeDtypeStruct((1, head_size), f32),
            jax.ShapeDtypeStruct((rows, 1), f32),
        ],
        scratch=[pltpu.VMEM((rows, k_width), f32), pltpu.VMEM((rows, k_width), f32)],
    )(side_word, head_own, head_y, projected, q_low, k_low, v_low, log_totals, *tables)
    proj_y, proj_core = swap_y(proj_low), swap_core(proj_low)

    marker = proj_low
    for _ in range(4):
        marker = line.send(marker)
    proj_y, proj_core = after((proj_y, proj_core), marker)
    pairs = lax.all_gather(after(pair_scaled, proj_y), "tc")
    projs = [proj_low, proj_core, proj_y, swap_core(proj_y)]
    normed_part = low(
        (contract_cols(projs[0], qkv_weights[0]) + contract_cols(projs[1], qkv_weights[1]))
        + (contract_cols(projs[2], qkv_weights[2]) + contract_cols(projs[3], qkv_weights[3]))
    )
    small = jnp.concatenate([inner_attn[:, 0], q_gain_part[0], k_gain_part[0]])
    small = width_total(after(small, normed_part))
    small = jnp.concatenate([small, mlp_gain_part])
    for part in projs:
        line.add("qkv", low(contract_rows(after(normed, normed_part), part)), 1)
    normed_x, small_x = after(
        (swap_x(normed_part), swap_x(small)), line.send((small, line.waiting()))
    )
    small = small + small_x
    inner_attn, gains = small[:rows], small[rows:]
    hiddens = lax.all_gather(after(hidden, inner_attn), "tc", axis=1, tiled=True)
    spare = jnp.pad(low(gains), (0, width * width - gains.shape[0])).reshape(width, width)
    normed_grad = normed_part.astype(f32) + normed_x.astype(f32)
    token_grad = low(
        flip(res_rel).astype(f32)
        + attn_rstd[:, None]
        * (normed_grad * attn_gain[None, :] - attn_hat * (inner_attn / full_width)[:, None])
    )

    marker = line.send((token_grad, line.waiting()), False)
    for _ in range(2):
        marker = line.send(marker, False)
    pairs = after(pairs, marker)
    for k in (2, 3):
        block = lax.dynamic_index_in_dim(pairs, around[k], 0, keepdims=False)
        line.add("ffn", low(contract_rows(mlp_in, block)), 1)
    marker = (marker, line.waiting())
    for _ in range(5):
        marker = line.send(marker, False)

    hiddens = after(hiddens, marker)
    far_down = [low(contract_rows(cols_of(hiddens, k, units), cot_rel)) for k in (2, 3)]
    line.add("down", jnp.concatenate(far_down, axis=0), 0)
    line.add("gains", spare, 0)
    mlp_away = low(dot(hiddens[half:], w_down))
    mlp_x_out = after(swap_x(mlp_away), line.send((mlp_away, line.waiting()), False))
    mixed_half = low(residual + dot(hiddens[:half], w_down) + mlp_x_out.astype(f32))
    mixed_x = after(swap_x(mixed_half), line.send(mixed_half, False))
    mixed = flip(jnp.concatenate([mixed_half, mixed_x], axis=0))
    marker = mixed_x
    while line.queue:
        marker = line.send(marker, False)
    sums_of = line.finish()

    words = jnp.stack([*around, line.middle.astype(jnp.int32)]).astype(jnp.int32)
    everything = slice(None)

    def spread(start, size, extent):
        while size:
            piece, at = divmod(start, extent)
            taken = min(size, extent - at)
            yield (piece, slice(at, at + taken), taken)
            start, size = start + taken, size - taken

    def runs(first, start, size, extent, out, axis, to=0):
        plan = []
        for piece, at, taken in spread(start, size, extent):
            block = slice(to, to + taken)
            pair_of = lambda part: (part, everything) if axis == 0 else (everything, part)
            plan.append((first + piece, pair_of(at), out, pair_of(block)))
            to += taken
        return plan

    out_sums, qkv_sums, ffn_sums = after(
        (sums_of("out"), sums_of("qkv"), sums_of("ffn")), line.last
    )
    ffn_plan = [
        runs(0, 2 * k * units, units, width, 0, 1) + runs(0, (2 * k + 1) * units, units, width, 1, 1)
        for k in range(4)
    ]
    w_gate_grad, w_up_grad = place_sums(words, ffn_sums, [(w_gate.shape, 1), (w_up.shape, 1)], ffn_plan)
    [w_down_grad] = place_sums(
        words,
        sums_of("down"),
        [(w_down.shape, 0)],
        [runs(0, k * units, units, width, 0, 0) for k in range(4)],
    )
    [w_out_grad] = place_sums(
        words,
        out_sums,
        [(w_out.shape, 0)],
        [runs(0, k * q_width, q_width, width, 0, 0) for k in range(4)],
    )
    block_width = q_width + 2 * k_width
    qkv_plan = [
        runs(0, k * block_width, q_width, width, 0, 1)
        + runs(0, k * block_width + q_width, k_width, width, 1, 1)
        + runs(0, k * block_width + q_width + k_width, k_width, width, 2, 1)
        for k in range(4)
    ]
    w_query_grad, w_key_grad, w_value_grad = place_sums(
        words, qkv_sums, [(w_query.shape, 1), (w_key.shape, 1), (w_value.shape, 1)], qkv_plan
    )
    attn_gain_part = sum(
        jnp.sum(w.astype(f32) * g, axis=1)
        for w, g in ((w_query, w_query_grad), (w_key, w_key_grad), (w_value, w_value_grad))
    )
    attn_gain_grad = (attn_gain_part + swap_x(attn_gain_part)) / attn_gain
    [gain_sums] = sums_of("gains")
    gains = jnp.where(line.middle, gain_sums[0], gain_sums[-1]).reshape(-1).astype(f32)
    q_gain_grad = gains[:head_size]
    k_gain_grad = gains[head_size : 2 * head_size]
    mlp_gain_grad = gains[2 * head_size : 2 * head_size + width]
    return (
        mixed,
        token_grad,
        attn_gain_grad,
        q_gain_grad,
        k_gain_grad,
        mlp_gain_grad,
        w_query_grad,
        w_key_grad,
        w_value_grad,
        w_out_grad,
        w_gate_grad,
        w_up_grad,
        w_down_grad,
    )


def solution(mesh):
    in_specs = (
        P("dp", "tc"),
        P("dp", "tc"),
        P("dp"),
        P("tc"),
        P(),
        P(),
        P("tc"),
        P("tc", "tr"),
        P("tc", "tr"),
        P("tc", "tr"),
        P("tr", "tc"),
        P("tc", "tr"),
        P("tc", "tr"),
        P("tr", "tc"),
    )
    out_specs = (
        P("dp", "tc"),
        P("dp", "tc"),
        P("tc"),
        P(),
        P(),
        P("tc"),
        P("tc", "tr"),
        P("tc", "tr"),
        P("tc", "tr"),
        P("tr", "tc"),
        P("tc", "tr"),
        P("tc", "tr"),
        P("tr", "tc"),
    )
    return jax.shard_map(
        on_device, mesh=mesh, in_specs=in_specs, out_specs=out_specs, check_vma=False
    )
```

```python
import jax
import jax.numpy as jnp
from jax import lax
from jax.experimental import pallas as pl
from jax.experimental.pallas import tpu as pltpu
from jax.sharding import PartitionSpec as P

norm_eps = 1e-06
rope_base = 1000000.0
neg_big = -1e30
f32 = jnp.float32
bf16 = jnp.bfloat16


def dot(left_side, right_side):
    return jnp.dot(left_side, right_side, preferred_element_type=f32)


def contract_rows(left_side, right_side):
    return lax.dot_general(
        left_side, right_side, (((0,), (0,)), ((), ())), preferred_element_type=f32
    )


def contract_cols(left_side, right_side):
    return lax.dot_general(
        left_side, right_side, (((1,), (1,)), ((), ())), preferred_element_type=f32
    )


def swap_core(block):
    return lax.ppermute(block, "tc", [(i, i ^ 1) for i in range(4)])


def swap_y(block):
    return lax.ppermute(block, "tc", [(i, i ^ 2) for i in range(4)])


def swap_diag(block):
    return lax.ppermute(block, "tc", [(i, i ^ 3) for i in range(4)])


def swap_x(block):
    return lax.ppermute(block, "tr", [(0, 1), (1, 0)])


def width_total(rows):
    rows = rows + swap_core(rows)
    return rows + swap_y(rows)


class LineSums:
    def __init__(self, lag=4):
        self.lag = lag
        self.short = lax.axis_size("dp") == 4
        place = lax.axis_index("dp")
        self.middle = (place == 1) | (place == 2)
        self.queue, self.names, self.pieces = [], [], []
        self.outer, self.total = [], []

    def add(self, name, grad, axis):
        size = min(grad.shape)
        for k in range(0, grad.shape[axis], size):
            self.queue.append((name, lax.slice_in_dim(grad, k, k + size, axis=axis)))

    def waiting(self):
        return [piece for _, piece in self.queue]

    def _consume(self, which, marker):
        got, piece = after((self.outer[which], self.pieces[which]), marker)
        inward = low(piece.astype(f32) + got.astype(f32))
        across = lax.ppermute(inward, "dp", [(1, 2), (2, 1)])
        self.total.append(low(inward.astype(f32) + across.astype(f32)))
        return inward

    def _swap_outer(self, piece):
        self.outer.append(lax.ppermute(piece, "dp", [(0, 1), (1, 0), (2, 3), (3, 2)]))

    def send(self, marker=(), strict=True):
        which = len(self.pieces)
        name, piece = self.queue.pop(0)
        self.names.append(name)
        self.pieces.append(piece)
        if not self.short:
            return piece
        if which >= 2:
            marker = self._consume(which - 2, marker)
        out = after(piece, marker)
        if which >= self.lag:
            out = jnp.where(self.middle, self.total[which - self.lag], out)
        self._swap_outer(out)
        return (marker, out) if strict else marker

    def _named(self, sums):
        return lambda name: [s for n, s in zip(self.names, sums) if n == name]

    def _ready(self):
        return [(total, outer) for total, outer in zip(self.total, self.outer[self.lag :])]

    def finish(self, filler):
        count = len(self.pieces)
        if not self.short:
            named = self._named([(lax.psum(piece, "dp"),) for piece in self.pieces])
            filler(named)
            return named
        self._consume(count - 2, ())
        self._consume(count - 1, ())
        for which in range(count - self.lag, count):
            piece = self.total[which]
            if which == count - 2:
                piece = after(piece, filler(self._named(self._ready())))
            self._swap_outer(piece)
        return self._named(self._ready())


def after(value, *others):
    return lax.optimization_barrier((value, others))[0]


def low(array):
    return array.astype(bf16)


def scatter_width(product, near=lambda ready: ready):
    from_far = swap_core(low(product(3)))
    from_core = swap_core(low(product(1)))
    from_far = after(from_far, near(from_far))
    for_y = low(product(2) + from_far.astype(f32))
    from_y = swap_y(for_y)
    return (product(0) + from_core.astype(f32), from_y, for_y)


def scatter_all(product, started, turned):
    far_y, far_own = swap_core(low(product(3))), swap_core(low(product(1)))
    for_y = low(product(2) + far_y.astype(f32))
    own = low(product(0) + far_own.astype(f32))
    half = own.shape[0] // 2
    quarter = half // 2
    width = own.shape[1]
    y_first = swap_y(jnp.concatenate([for_y[quarter:half], for_y[half + quarter :]], axis=0))
    x_first = swap_x(
        jnp.concatenate([own[half : half + quarter], for_y[half : half + quarter]], axis=1)
    )
    x_first, y_first = after((x_first, y_first), started((own, for_y)))
    top_in = low(for_y[:quarter].astype(f32) + x_first[:, width:].astype(f32))
    low_in = low(own[half + quarter :].astype(f32) + y_first[quarter:].astype(f32))
    top_y, low_x = after((swap_y(top_in), swap_x(low_in)), turned((top_in, low_in)))
    top = own[:quarter].astype(f32) + x_first[:, :width].astype(f32) + top_y.astype(f32)
    bottom = own[quarter:half].astype(f32) + y_first[:quarter].astype(f32) + low_x.astype(f32)
    return jnp.concatenate([top, bottom], axis=0)


def positions_of(segment):
    slot_ids = jnp.arange(5, dtype=jnp.int32)
    before = jnp.sum((segment[None, :] < slot_ids[:, None]).astype(jnp.int32), axis=1)
    starts = jnp.sum(jnp.where(segment[:, None] == slot_ids[None, :], before[None, :], 0), axis=1)
    return jnp.arange(segment.shape[0], dtype=jnp.int32) - starts


def rope_tables(positions, head_size):
    half_size = head_size // 2
    frequency = rope_base ** (-jnp.arange(half_size, dtype=f32) * 2.0 / head_size)
    angles = positions.astype(f32)[:, None] * frequency[None, :]
    cosine, sine = jnp.cos(angles), jnp.sin(angles)
    return (
        jnp.concatenate([cosine, cosine], axis=1),
        jnp.concatenate([-sine, sine], axis=1),
    )


def turn(vectors):
    return pltpu.roll(vectors, vectors.shape[-1] // 2, axis=1)


def inverse_norm(vectors):
    return lax.rsqrt(jnp.mean(vectors * vectors, axis=-1, keepdims=True) + norm_eps)


def allowed_keys(seg_col, seg_row, start, size, extent):
    row = lax.broadcasted_iota(jnp.int32, (size, extent), 0) + start
    col = lax.broadcasted_iota(jnp.int32, (size, extent), 1)
    return (seg_col[start : start + size, :] == seg_row[:, :extent]) & (col <= row)


def attend_kernel(
    side, own, from_y, rstd, cos, sin, seg_col, seg_row, q_gain, k_gain,
    proj, q_out, k_out, v_out, lse, att,
):
    rows = own.shape[0]
    size = cos.shape[1]
    heads = q_out.shape[1] // size
    block = rows // 4
    scale = size**-0.5
    k_at = heads * size
    v_at = k_at + size

    def ready(i, carry):
        at = pl.ds(pl.multiple_of(i * block, block), block)
        raw = (own[at, :] + from_y[at, :].astype(f32)) * rstd[at, :]
        proj[at, :] = raw

        def rope(part, gain):
            n = part * inverse_norm(part) * gain[...]
            return (n * cos[at, :] + turn(n) * sin[at, :]).astype(bf16)

        for h in range(heads):
            q_out[at, h * size : (h + 1) * size] = rope(raw[:, h * size : (h + 1) * size], q_gain)
        k_out[at, :] = rope(raw[:, k_at:v_at], k_gain)
        v_out[at, :] = raw[:, v_at:].astype(bf16)
        return carry

    lax.fori_loop(0, 4, ready, 0)
    for i in range(4):
        start = i * block
        extent = start + block
        allowed = allowed_keys(seg_col, seg_row, start, block, extent)
        to = pl.ds(pl.multiple_of(lax.rem(start + side[0] * (rows // 2), rows), block), block)
        for h in range(heads):
            of_head = slice(h * size, (h + 1) * size)
            scores = contract_cols(q_out[start:extent, of_head], k_out[:extent, :]) * scale
            scores = jnp.where(allowed, scores, neg_big)
            top = jnp.max(scores, axis=-1, keepdims=True)
            expd = jnp.exp(scores - top)
            total = jnp.sum(expd, axis=-1, keepdims=True)
            weights = (expd * (1.0 / total)).astype(bf16)
            att[to, of_head] = dot(weights, v_out[:extent, :]).astype(bf16)
            lse[start:extent, h : h + 1] = top + jnp.log(total)


def attend_back_kernel(
    side, own, from_y, proj, q_in, k_in, v_in, lse, cos, sin, seg_col, seg_row, q_gain, k_gain,
    grads, q_gain_part, k_gain_part, inner, k_acc, v_acc,
):
    rows = own.shape[0]
    size = cos.shape[1]
    heads = q_in.shape[1] // size
    block = rows // 4
    scale = size**-0.5
    k_at = heads * size
    v_at = k_at + size

    def unrope(grad, part, gain, start):
        rows_at = slice(start, start + block)
        m = grad * cos[rows_at, :] - turn(grad) * sin[rows_at, :]
        r = inverse_norm(part)
        hat = part * r
        mg = m * gain[...]
        back = (r * (mg - hat * jnp.mean(mg * hat, axis=-1, keepdims=True))).astype(bf16)
        gain_part = jnp.sum(m * hat, axis=0, keepdims=True)
        return (back, gain_part, jnp.sum(back.astype(f32) * part, axis=-1, keepdims=True))

    k_acc[...] = jnp.zeros_like(k_acc)
    v_acc[...] = jnp.zeros_like(v_acc)
    q_total = jnp.zeros(q_gain_part.shape, f32)
    for i in range(4):
        start = i * block
        extent = start + block
        allowed = allowed_keys(seg_col, seg_row, start, block, extent)
        at = pl.ds(pl.multiple_of(lax.rem(start + side[0] * (rows // 2), rows), block), block)
        inner_sum = jnp.zeros((block, 1), f32)
        for h in range(heads):
            of_head = slice(h * size, (h + 1) * size)
            query = q_in[start:extent, of_head]
            grad = (own[at, of_head] + from_y[at, of_head].astype(f32)).astype(bf16)
            scores = contract_cols(query, k_in[:extent, :]) * scale
            scores = jnp.where(allowed, scores, neg_big)
            probs = jnp.exp(scores - lse[start:extent, h : h + 1])
            prob_grad = contract_cols(grad, v_in[:extent, :])
            delta = jnp.sum(probs * prob_grad, axis=-1, keepdims=True)
            score_grad = (probs * (prob_grad - delta)).astype(bf16)
            query_grad = dot(score_grad, k_in[:extent, :]) * scale
            k_acc[:extent, :] += contract_rows(score_grad, query) * scale
            v_acc[:extent, :] += contract_rows(probs.astype(bf16), grad)
            back, gain_part, part_inner = unrope(
                query_grad, proj[start:extent, of_head], q_gain, start
            )
            grads[start:extent, of_head] = back
            q_total = q_total + gain_part
            inner_sum = inner_sum + part_inner
        inner[start:extent, :] = inner_sum
    q_gain_part[...] = q_total
    k_total = jnp.zeros(k_gain_part.shape, f32)
    for i in range(4):
        start = i * block
        extent = start + block
        back, gain_part, part_inner = unrope(
            k_acc[start:extent, :], proj[start:extent, k_at:v_at], k_gain, start
        )
        grads[start:extent, k_at:v_at] = back
        k_total = k_total + gain_part
        v_back = v_acc[start:extent, :].astype(bf16)
        grads[start:extent, v_at:] = v_back
        inner[start:extent, :] += part_inner + jnp.sum(
            v_back.astype(f32) * proj[start:extent, v_at:], axis=-1, keepdims=True
        )
    k_gain_part[...] = k_total


vmem = pl.BlockSpec(memory_space=pltpu.VMEM)
smem = pl.BlockSpec(memory_space=pltpu.SMEM)
def whole_kernel(body, outs, scratch=(), grant=50):
    def call(*operands):
        return pl.pallas_call(
            body,
            out_shape=outs,
            in_specs=[smem if o.ndim == 1 else vmem for o in operands],
            out_specs=[vmem] * len(outs),
            scratch_shapes=scratch,
            compiler_params=pltpu.CompilerParams(vmem_limit_bytes=grant * 2**20),
            cost_estimate=pl.CostEstimate(flops=0, bytes_accessed=2**10, transcendentals=0),
        )(*operands)

    return call


def units_kernel(*refs):
    ins, weights, cots, downs = refs[:4], refs[4:8], refs[8:12], refs[12:16]
    rstd_ref = refs[16]
    hidden, pair, scaled, inner = refs[-4:]
    units = hidden.shape[1]
    chunk = min(256, units)
    rstd = rstd_ref[...]

    def product(at):
        total = dot(ins[0][...], weights[0][:, at])
        for k in range(1, 4):
            total = total + dot(ins[k][...], weights[k][:, at])
        return total * rstd

    inner_sum = jnp.zeros(inner.shape, f32)
    for start in range(0, units, chunk):
        of_gate = slice(start, start + chunk)
        of_up = slice(units + start, units + start + chunk)
        gate, up = product(of_gate), product(of_up)
        grad = contract_cols(cots[0][...], downs[0][of_gate, :])
        for k in range(1, 4):
            grad = grad + contract_cols(cots[k][...], downs[k][of_gate, :])
        sig = jax.nn.sigmoid(gate)
        silu = gate * sig
        hidden[:, of_gate] = low(silu * up)
        gate_grad = low(grad * up * sig * (1.0 + gate * (1.0 - sig)))
        up_grad = low(grad * silu)
        pair[:, of_gate] = gate_grad
        pair[:, of_up] = up_grad
        gate_grad, up_grad = gate_grad.astype(f32), up_grad.astype(f32)
        scaled[:, of_gate] = low(gate_grad * rstd)
        scaled[:, of_up] = low(up_grad * rstd)
        inner_sum = inner_sum + jnp.sum(gate_grad * gate + up_grad * up, axis=-1, keepdims=True)
    inner[...] = inner_sum


def units_of_half(ins, weights, cots, downs, rstd, which, earlier):
    half, depth = ins[0].shape
    units = downs[0].shape[0]
    block = half // 2
    first = which * (half // block)
    outs = [
        jax.ShapeDtypeStruct((2 * half, units), bf16),
        jax.ShapeDtypeStruct((2 * half, 2 * units), bf16),
        jax.ShapeDtypeStruct((2 * half, 2 * units), bf16),
        jax.ShapeDtypeStruct((2 * half, 1), f32),
    ]

    def whole(array):
        return pl.BlockSpec(array.shape, lambda i: (0, 0))

    def of_two(array, k):
        return pl.BlockSpec((None, *array.shape[1:]), lambda i: (k, 0, 0))

    near_by, core, both = downs
    downs = [near_by, core, both, both]
    down_specs = [whole(near_by), whole(core), of_two(both, 0), of_two(both, 1)]
    here = pl.BlockSpec((block, depth), lambda i: (i, 0))
    at = lambda i: (first + i, 0)
    of_all = pl.BlockSpec((block, depth), at)
    earlier = list(earlier or [])
    return pl.pallas_call(
        units_kernel,
        grid=(half // block,),
        out_shape=outs,
        in_specs=[here] * 4
        + [whole(w) for w in weights]
        + [of_all, of_all, here, here]
        + down_specs
        + [pl.BlockSpec((block, 1), at)]
        + [pl.BlockSpec(memory_space=pl.ANY)] * len(earlier),
        out_specs=[pl.BlockSpec((block, o.shape[1]), at) for o in outs],
        input_output_aliases={17 + k: k for k in range(len(earlier))},
        compiler_params=pltpu.CompilerParams(vmem_limit_bytes=50 * 2**20),
        cost_estimate=pl.CostEstimate(flops=0, bytes_accessed=2**10, transcendentals=0),
    )(*ins, *weights, *cots, *downs, rstd, *earlier)


def place_sums(scalars, pieces, outs, plan):
    flat = [a for piece in pieces for a in piece]

    def kernel(words, *refs):
        ins, results = list(refs[: len(flat)]), refs[len(flat) :]
        groups = [[ins.pop(0) for _ in piece] for piece in pieces]
        for k in range(4):

            @pl.when(pl.program_id(0) == k)
            def _(k=k):
                for piece, at, out, to in plan[k]:
                    value = groups[piece][0][at]
                    if len(groups[piece]) == 2:
                        value = jnp.where(words[4] == 1, value, groups[piece][1][at])
                    results[out][to] = value.astype(f32)

    def quarter(shape, axis):
        block = tuple(n // 4 if i == axis else n for i, n in enumerate(shape))
        if axis == 0:
            return pl.BlockSpec(block, lambda k, words: (words[k], 0))
        return pl.BlockSpec(block, lambda k, words: (0, words[k]))

    return pl.pallas_call(
        kernel,
        grid_spec=pltpu.PrefetchScalarGridSpec(
            num_scalar_prefetch=1,
            grid=(4,),
            in_specs=[pl.BlockSpec(a.shape, lambda k, words: (0, 0)) for a in flat],
            out_specs=[quarter(*out) for out in outs],
        ),
        out_shape=[jax.ShapeDtypeStruct(shape, f32) for shape, _ in outs],
        compiler_params=pltpu.CompilerParams(vmem_limit_bytes=50 * 2**20),
        cost_estimate=pl.CostEstimate(flops=0, bytes_accessed=2**10, transcendentals=0),
    )(scalars, *flat)


def on_device(
    tokens,
    cotangent,
    segment_ids,
    attn_gain,
    q_gain,
    k_gain,
    mlp_gain,
    w_query,
    w_key,
    w_value,
    w_out,
    w_gate,
    w_up,
    w_down,
):
    assert lax.axis_size("tc") == 4 and lax.axis_size("tr") == 2
    col = lax.axis_index("tc")
    side = lax.axis_index("tr")
    rows, width = tokens.shape
    half = rows // 2
    full_width = width * 4
    head_size = q_gain.shape[0]
    q_width = w_query.shape[1] // 4
    k_width = w_key.shape[1] // 4
    units = w_gate.shape[1] // 4
    around = [col, col ^ 1, col ^ 2, col ^ 3]

    def cols_of(array, which, size):
        return lax.dynamic_slice_in_dim(array, around[which] * size, size, 1)

    def rows_of(array, which, size):
        return lax.dynamic_slice_in_dim(array, around[which] * size, size, 0)

    def flip(array):
        return jnp.concatenate(
            [
                lax.dynamic_slice_in_dim(array, side * half, half, 0),
                lax.dynamic_slice_in_dim(array, (1 - side) * half, half, 0),
            ],
            axis=0,
        )

    shares = lax.axis_size("dp")
    place = lax.axis_index("dp")

    def share_of(block):
        size = block.shape[0] // shares
        return lax.dynamic_slice_in_dim(block, place * size, size, 0)

    def gather_shares(from_y, from_diag):
        return lax.all_gather(jnp.stack([from_y, from_diag]), "dp", axis=1, tiled=True)

    def ffn_columns(which, rows_at):
        return jnp.concatenate(
            [rows_at(cols_of(w, which, units)) for w in (w_gate, w_up)], axis=1
        )

    down_y, down_diag = (share_of(rows_of(w_down, k, units)) for k in (2, 3))
    share_y, share_diag = ffn_columns(2, share_of), ffn_columns(3, share_of)

    qkv_weights = [
        jnp.concatenate(
            [cols_of(w_query, k, q_width), cols_of(w_key, k, k_width), cols_of(w_value, k, k_width)],
            axis=1,
        )
        for k in range(4)
    ]
    inputs = tokens.astype(f32)
    down_y, down_diag = swap_y(down_y), swap_diag(down_diag)
    share_y, share_diag, inputs = after((share_y, share_diag, inputs), down_y, down_diag)
    scaled_in = low(inputs * attn_gain[None, :])
    raw_own, raw_y, for_y = scatter_width(lambda k: dot(scaled_in, qkv_weights[k]))
    down_gathered = gather_shares(down_y, down_diag)
    w_gate, w_up, w_down, w_out, segment_ids, cotangent, inputs = after(
        (w_gate, w_up, w_down, w_out, segment_ids, cotangent, inputs), for_y
    )
    square_sum = width_total(jnp.sum(inputs * inputs, axis=1))
    cos_table, sin_table = rope_tables(positions_of(segment_ids), head_size)
    side_word = side.astype(jnp.int32).reshape(1)
    tables = (
        cos_table,
        sin_table,
        segment_ids.reshape(rows, 1),
        segment_ids.reshape(1, rows),
        q_gain.reshape(1, head_size),
        k_gain.reshape(1, head_size),
    )
    whole = lambda block: block
    blocks_core = (ffn_columns(1, whole), rows_of(w_down, 1, units))
    raw_y, share_y, share_diag, square_sum = after(
        (raw_y, swap_y(share_y), swap_diag(share_diag), square_sum), raw_own, tables, blocks_core
    )
    ffn_y, ffn_diag = (lax.all_gather(w, "dp", axis=0, tiled=True) for w in (share_y, share_diag))
    attn_rstd = lax.rsqrt(square_sum / full_width + norm_eps)
    attn_hat = inputs * attn_rstd[:, None]
    normed = low(attn_hat * attn_gain[None, :])

    heads = q_width // head_size
    projected, q_low, k_low, v_low, log_totals, att_rel = whole_kernel(
        attend_kernel,
        [
            jax.ShapeDtypeStruct((rows, q_width + 2 * k_width), f32),
            jax.ShapeDtypeStruct((rows, q_width), bf16),
            jax.ShapeDtypeStruct((rows, k_width), bf16),
            jax.ShapeDtypeStruct((rows, k_width), bf16),
            jax.ShapeDtypeStruct((rows, heads), f32),
            jax.ShapeDtypeStruct((rows, q_width), bf16),
        ],
    )(side_word, raw_own, raw_y, attn_rstd.reshape(rows, 1), *tables)
    cot_rel = flip(cotangent)
    cot_y = swap_y(after(cot_rel[:half], raw_y))
    att_y, cot_x, down_gathered = after((swap_y(att_rel), swap_x(cot_y), down_gathered), att_rel)
    atts = [att_rel, swap_core(att_rel), att_y, swap_core(att_y)]
    outs = [rows_of(w_out, k, q_width) for k in range(4)]

    def out_rows(at):
        return (dot(atts[0][at], outs[0]) + dot(atts[1][at], outs[1])) + (
            dot(atts[2][at], outs[2]) + dot(atts[3][at], outs[3])
        )

    from_x = swap_x(low(out_rows(slice(half, rows))))
    home = out_rows(slice(0, half))

    prefetched = (
        swap_core(cot_rel),
        *map(swap_core, blocks_core),
    )
    from_x, (cot_core, ffn_core, down_core), ffn_y = after((from_x, prefetched, ffn_y), home)
    cot_y_core, cot_x_core = swap_core(cot_y), swap_core(cot_x)
    downs = (rows_of(w_down, 0, units), down_core, down_gathered)
    tokens_half = lax.dynamic_slice_in_dim(tokens, side * half, half, 0).astype(f32)
    residual = tokens_half + home + from_x.astype(f32)

    mlp_square = jnp.sum(residual * residual, axis=1)
    mlp_square = width_total(jnp.concatenate([mlp_square, swap_x(mlp_square)]))
    mlp_own = low(residual * mlp_gain[None, :])
    mlp_rstd = lax.rsqrt(mlp_square / full_width + norm_eps)
    quarter = half // 2
    mlp_x, mlp_y, mlp_rstd = after(
        (swap_x(mlp_own), swap_y(mlp_own), mlp_rstd), cot_y_core, cot_x_core
    )
    mlp_xy = (swap_y(mlp_x[:quarter]), swap_x(mlp_y[quarter:]))
    mlp_x_core = swap_core(mlp_x)
    ffns = [ffn_columns(0, whole), ffn_core, ffn_y, ffn_diag]
    downs = [rows_of(w_down, 0, units), down_core, down_gathered]
    ins_own = [mlp_own, swap_core(mlp_own), mlp_y, swap_core(mlp_y)]
    cots_own = [cot_rel, cot_core, cot_y, cot_y_core]
    cots_other = [cot_rel, cot_core, cot_x, cot_x_core]
    rstd_rel = mlp_rstd.reshape(rows, 1)
    first = units_of_half(ins_own, ffns, cots_own, downs, rstd_rel, 0, None)
    mlp_xy, mlp_x_core = after((mlp_xy, mlp_x_core), first)
    mlp_xy = jnp.concatenate(mlp_xy, axis=0)
    ins_other = [mlp_x, mlp_x_core, mlp_xy, swap_core(mlp_xy)]
    hidden, pair, pair_scaled, inner = units_of_half(
        ins_other, ffns, cots_other, downs, rstd_rel, 1, first
    )

    line = LineSums()
    mlp_in, mlp_core = (jnp.concatenate([ins_own[k], ins_other[k]], axis=0) for k in (0, 1))
    line.add("ffn", low(contract_rows(mlp_in, pair_scaled)), 1)
    line.send(line.send())
    pair = after(pair, line.pieces, line.waiting())

    kept = {}

    def started(marker):
        sums = width_total(after(inner[:, 0], marker))
        kept["inner"] = sums
        block = low(contract_rows(mlp_core, after(pair_scaled, marker)))
        kept["core"] = swap_core(block)
        down_core = low(contract_rows(after(hidden, block), cot_core))
        down_own = low(contract_rows(after(hidden, block), cot_rel))
        line.add("down", jnp.concatenate([down_own, swap_core(down_core)], axis=0), 0)
        return (line.send(down_own), sums)

    def turned(marker):
        sums = after(kept["inner"], marker)
        kept["inner"] = sums[:half] + swap_x(sums[half:])
        return (kept["inner"], line.send(marker))

    mlp_in_grad = scatter_all(lambda k: contract_cols(pair, ffns[k]), started, turned)
    inner_total = kept["inner"]
    mlp_hat = residual * mlp_rstd[:half, None]
    mlp_gain_part = jnp.sum(mlp_in_grad * mlp_hat, axis=0)
    residual_grad = cot_rel[:half].astype(f32) + mlp_rstd[:half, None] * (
        mlp_in_grad * mlp_gain[None, :] - mlp_hat * (inner_total / full_width)[:, None]
    )
    residual_low = low(residual_grad)
    res_x = after(swap_x(residual_low), line.send(residual_low))
    res_rel = jnp.concatenate([residual_low, res_x], axis=0)
    head_own, head_y, head_sent = scatter_width(
        lambda k: contract_cols(res_rel, outs[k]), line.send
    )

    line.add("ffn", kept["core"], 1)
    marker = line.send(head_sent)
    out_grads = [low(contract_rows(after(part, marker), res_rel)) for part in atts]
    line.add("out", jnp.concatenate(out_grads, axis=0), 0)
    head_own, head_y = after((head_own, head_y), line.waiting())

    proj_low, q_gain_part, k_gain_part, inner_attn = whole_kernel(
        attend_back_kernel,
        [
            jax.ShapeDtypeStruct((rows, q_width + 2 * k_width), bf16),
            jax.ShapeDtypeStruct((1, head_size), f32),
            jax.ShapeDtypeStruct((1, head_size), f32),
            jax.ShapeDtypeStruct((rows, 1), f32),
        ],
        scratch=[pltpu.VMEM((rows, k_width), f32), pltpu.VMEM((rows, k_width), f32)],
    )(side_word, head_own, head_y, projected, q_low, k_low, v_low, log_totals, *tables)
    proj_y, proj_core = swap_y(proj_low), swap_core(proj_low)

    marker = proj_low
    for _ in range(4):
        marker = line.send(marker)
    proj_y, proj_core = after((proj_y, proj_core), marker)
    pairs = lax.all_gather(after(pair_scaled, proj_y), "tc")
    projs = [proj_low, proj_core, proj_y, swap_core(proj_y)]
    normed_part = low(
        (contract_cols(projs[0], qkv_weights[0]) + contract_cols(projs[1], qkv_weights[1]))
        + (contract_cols(projs[2], qkv_weights[2]) + contract_cols(projs[3], qkv_weights[3]))
    )
    small = jnp.concatenate([inner_attn[:, 0], q_gain_part[0], k_gain_part[0]])
    small = width_total(after(small, normed_part))
    small = jnp.concatenate([small, mlp_gain_part])
    for part in projs:
        line.add("qkv", low(contract_rows(after(normed, normed_part), part)), 1)
    normed_x, small_x = after(
        (swap_x(normed_part), swap_x(small)), line.send((small, line.waiting()))
    )
    small = small + small_x
    inner_attn, gains = small[:rows], small[rows:]
    hiddens = lax.all_gather(after(hidden, inner_attn), "tc", axis=1, tiled=True)
    spare = jnp.pad(low(gains), (0, width * width - gains.shape[0])).reshape(width, width)
    normed_grad = normed_part.astype(f32) + normed_x.astype(f32)
    token_grad = low(
        flip(res_rel).astype(f32)
        + attn_rstd[:, None]
        * (normed_grad * attn_gain[None, :] - attn_hat * (inner_attn / full_width)[:, None])
    )

    marker = line.send((token_grad, line.waiting()), False)
    for _ in range(2):
        marker = line.send(marker, False)
    pairs = after(pairs, marker)
    for k in (2, 3):
        block = lax.dynamic_index_in_dim(pairs, around[k], 0, keepdims=False)
        line.add("ffn", low(contract_rows(mlp_in, block)), 1)
    marker = (marker, line.waiting())
    for _ in range(5):
        marker = line.send(marker, False)

    hiddens = after(hiddens, marker)
    far_down = [low(contract_rows(cols_of(hiddens, k, units), cot_rel)) for k in (2, 3)]
    line.add("down", jnp.concatenate(far_down, axis=0), 0)
    line.add("gains", spare, 0)
    mlp_away = low(dot(hiddens[half:], w_down))
    mlp_x_out = after(swap_x(mlp_away), line.send((mlp_away, line.waiting()), False))
    mixed_half = low(residual + dot(hiddens[:half], w_down) + mlp_x_out.astype(f32))
    mixed_x = after(swap_x(mixed_half), line.send(mixed_half, False))
    mixed = flip(jnp.concatenate([mixed_half, mixed_x], axis=0))
    marker = mixed_x
    while line.queue:
        marker = line.send(marker, False)
    words = jnp.stack([*around, line.middle.astype(jnp.int32)]).astype(jnp.int32)
    everything = slice(None)

    def spread(start, size, extent):
        while size:
            piece, at = divmod(start, extent)
            taken = min(size, extent - at)
            yield (piece, slice(at, at + taken), taken)
            start, size = start + taken, size - taken

    def runs(first, start, size, extent, out, axis, to=0):
        plan = []
        for piece, at, taken in spread(start, size, extent):
            block = slice(to, to + taken)
            pair_of = lambda part: (part, everything) if axis == 0 else (everything, part)
            plan.append((first + piece, pair_of(at), out, pair_of(block)))
            to += taken
        return plan

    block_width = q_width + 2 * k_width
    qkv_plan = [
        runs(0, k * block_width, q_width, width, 0, 1)
        + runs(0, k * block_width + q_width, k_width, width, 1, 1)
        + runs(0, k * block_width + q_width + k_width, k_width, width, 2, 1)
        for k in range(4)
    ]
    ffn_plan = [
        runs(0, 2 * k * units, units, width, 0, 1) + runs(0, (2 * k + 1) * units, units, width, 1, 1)
        for k in range(4)
    ]
    placed = {}

    def fill(sums_of):
        out_plan = [runs(0, k * q_width, q_width, width, 0, 0) for k in range(4)]
        placed["out"] = place_sums(words, sums_of("out"), [(w_out.shape, 0)], out_plan)
        placed["qkv"] = place_sums(
            words, sums_of("qkv"), [(w.shape, 1) for w in (w_query, w_key, w_value)], qkv_plan
        )
        placed["ffn"] = place_sums(
            words, sums_of("ffn"), [(w.shape, 1) for w in (w_gate, w_up)], ffn_plan
        )
        return placed

    sums_of = line.finish(fill)
    [w_out_grad] = placed["out"]
    w_query_grad, w_key_grad, w_value_grad = placed["qkv"]
    w_gate_grad, w_up_grad = placed["ffn"]
    [w_down_grad] = place_sums(
        words,
        sums_of("down"),
        [(w_down.shape, 0)],
        [runs(0, k * units, units, width, 0, 0) for k in range(4)],
    )
    attn_gain_part = sum(
        jnp.sum(w.astype(f32) * g, axis=1)
        for w, g in ((w_query, w_query_grad), (w_key, w_key_grad), (w_value, w_value_grad))
    )
    attn_gain_grad = (attn_gain_part + swap_x(attn_gain_part)) / attn_gain
    [gain_sums] = sums_of("gains")
    gains = jnp.where(line.middle, gain_sums[0], gain_sums[-1]).reshape(-1).astype(f32)
    q_gain_grad = gains[:head_size]
    k_gain_grad = gains[head_size : 2 * head_size]
    mlp_gain_grad = gains[2 * head_size : 2 * head_size + width]
    return (
        mixed,
        token_grad,
        attn_gain_grad,
        q_gain_grad,
        k_gain_grad,
        mlp_gain_grad,
        w_query_grad,
        w_key_grad,
        w_value_grad,
        w_out_grad,
        w_gate_grad,
        w_up_grad,
        w_down_grad,
    )


def solution(mesh):
    in_specs = (
        P("dp", "tc"),
        P("dp", "tc"),
        P("dp"),
        P("tc"),
        P(),
        P(),
        P("tc"),
        P("tc", "tr"),
        P("tc", "tr"),
        P("tc", "tr"),
        P("tr", "tc"),
        P("tc", "tr"),
        P("tc", "tr"),
        P("tr", "tc"),
    )
    out_specs = (
        P("dp", "tc"),
        P("dp", "tc"),
        P("tc"),
        P(),
        P(),
        P("tc"),
        P("tc", "tr"),
        P("tc", "tr"),
        P("tc", "tr"),
        P("tr", "tc"),
        P("tc", "tr"),
        P("tc", "tr"),
        P("tr", "tc"),
    )
    return jax.shard_map(
        on_device, mesh=mesh, in_specs=in_specs, out_specs=out_specs, check_vma=False
    )
```

```python
import jax
import jax.numpy as jnp
from jax import lax
from jax.experimental import pallas as pl
from jax.experimental.pallas import tpu as pltpu
from jax.sharding import PartitionSpec as P

norm_eps = 1e-06
rope_base = 1000000.0
neg_big = -1e30
f32 = jnp.float32
bf16 = jnp.bfloat16


def dot(left_side, right_side):
    return jnp.dot(left_side, right_side, preferred_element_type=f32)


def contract_rows(left_side, right_side):
    return lax.dot_general(
        left_side, right_side, (((0,), (0,)), ((), ())), preferred_element_type=f32
    )


def contract_cols(left_side, right_side):
    return lax.dot_general(
        left_side, right_side, (((1,), (1,)), ((), ())), preferred_element_type=f32
    )


def swap_core(block):
    return lax.ppermute(block, "tc", [(i, i ^ 1) for i in range(4)])


def swap_y(block):
    return lax.ppermute(block, "tc", [(i, i ^ 2) for i in range(4)])


def swap_diag(block):
    return lax.ppermute(block, "tc", [(i, i ^ 3) for i in range(4)])


def swap_x(block):
    return lax.ppermute(block, "tr", [(0, 1), (1, 0)])


def width_total(rows):
    rows = rows + swap_core(rows)
    return rows + swap_y(rows)


class LineSums:
    def __init__(self, lag=4):
        self.lag = lag
        self.short = lax.axis_size("dp") == 4
        place = lax.axis_index("dp")
        self.middle = (place == 1) | (place == 2)
        self.queue, self.names, self.pieces = [], [], []
        self.outer, self.total = [], []

    def add(self, name, grad, axis):
        size = min(grad.shape)
        for k in range(0, grad.shape[axis], size):
            self.queue.append((name, lax.slice_in_dim(grad, k, k + size, axis=axis)))

    def waiting(self):
        return [piece for _, piece in self.queue]

    def _consume(self, which, marker):
        got, piece = after((self.outer[which], self.pieces[which]), marker)
        inward = low(piece.astype(f32) + got.astype(f32))
        across = lax.ppermute(inward, "dp", [(1, 2), (2, 1)])
        self.total.append(low(inward.astype(f32) + across.astype(f32)))
        return inward

    def _swap_outer(self, piece):
        self.outer.append(lax.ppermute(piece, "dp", [(0, 1), (1, 0), (2, 3), (3, 2)]))

    def send(self, marker=(), strict=True):
        which = len(self.pieces)
        name, piece = self.queue.pop(0)
        self.names.append(name)
        self.pieces.append(piece)
        if not self.short:
            return piece
        if which >= 2:
            marker = self._consume(which - 2, marker)
        out = after(piece, marker)
        if which >= self.lag:
            out = jnp.where(self.middle, self.total[which - self.lag], out)
        self._swap_outer(out)
        return (marker, out) if strict else marker

    def _named(self, sums):
        return lambda name: [s for n, s in zip(self.names, sums) if n == name]

    def _ready(self):
        return [(total, outer) for total, outer in zip(self.total, self.outer[self.lag :])]

    def finish(self, filler):
        count = len(self.pieces)
        if not self.short:
            named = self._named([(lax.psum(piece, "dp"),) for piece in self.pieces])
            filler(named)
            return named
        self._consume(count - 2, ())
        self._consume(count - 1, ())
        for which in range(count - self.lag, count):
            piece = self.total[which]
            if which == count - 2:
                piece = after(piece, filler(self._named(self._ready())))
            self._swap_outer(piece)
        return self._named(self._ready())


def after(value, *others):
    return lax.optimization_barrier((value, others))[0]


def low(array):
    return array.astype(bf16)


def scatter_width(product, near=lambda ready: ready):
    from_far = swap_core(low(product(3)))
    from_core = swap_core(low(product(1)))
    from_far = after(from_far, near(from_far))
    for_y = low(product(2) + from_far.astype(f32))
    from_y = swap_y(for_y)
    return (product(0) + from_core.astype(f32), from_y, for_y)


def scatter_all(product, started, turned):
    far_y, far_own = swap_core(low(product(3))), swap_core(low(product(1)))
    for_y = low(product(2) + far_y.astype(f32))
    own = low(product(0) + far_own.astype(f32))
    half = own.shape[0] // 2
    quarter = half // 2
    width = own.shape[1]
    y_first = swap_y(jnp.concatenate([for_y[quarter:half], for_y[half + quarter :]], axis=0))
    x_first = swap_x(
        jnp.concatenate([own[half : half + quarter], for_y[half : half + quarter]], axis=1)
    )
    x_first, y_first = after((x_first, y_first), started((own, for_y)))
    top_in = low(for_y[:quarter].astype(f32) + x_first[:, width:].astype(f32))
    low_in = low(own[half + quarter :].astype(f32) + y_first[quarter:].astype(f32))
    top_y, low_x = after((swap_y(top_in), swap_x(low_in)), turned((top_in, low_in)))
    top = own[:quarter].astype(f32) + x_first[:, :width].astype(f32) + top_y.astype(f32)
    bottom = own[quarter:half].astype(f32) + y_first[:quarter].astype(f32) + low_x.astype(f32)
    return jnp.concatenate([top, bottom], axis=0)


def positions_of(segment):
    slot_ids = jnp.arange(5, dtype=jnp.int32)
    before = jnp.sum((segment[None, :] < slot_ids[:, None]).astype(jnp.int32), axis=1)
    starts = jnp.sum(jnp.where(segment[:, None] == slot_ids[None, :], before[None, :], 0), axis=1)
    return jnp.arange(segment.shape[0], dtype=jnp.int32) - starts


def rope_tables(positions, head_size):
    half_size = head_size // 2
    frequency = rope_base ** (-jnp.arange(half_size, dtype=f32) * 2.0 / head_size)
    angles = positions.astype(f32)[:, None] * frequency[None, :]
    cosine, sine = jnp.cos(angles), jnp.sin(angles)
    return (
        jnp.concatenate([cosine, cosine], axis=1),
        jnp.concatenate([-sine, sine], axis=1),
    )


def turn(vectors):
    return pltpu.roll(vectors, vectors.shape[-1] // 2, axis=1)


def inverse_norm(vectors):
    return lax.rsqrt(jnp.mean(vectors * vectors, axis=-1, keepdims=True) + norm_eps)


def allowed_keys(seg_col, seg_row, start, size, extent):
    row = lax.broadcasted_iota(jnp.int32, (size, extent), 0) + start
    col = lax.broadcasted_iota(jnp.int32, (size, extent), 1)
    return (seg_col[start : start + size, :] == seg_row[:, :extent]) & (col <= row)


def attend_kernel(
    side, own, from_y, rstd, cos, sin, seg_col, seg_row, q_gain, k_gain,
    proj, q_out, k_out, v_out, lse, att,
):
    rows = own.shape[0]
    size = cos.shape[1]
    heads = q_out.shape[1] // size
    block = rows // 4
    scale = size**-0.5
    k_at = heads * size
    v_at = k_at + size

    def ready(i, carry):
        at = pl.ds(pl.multiple_of(i * block, block), block)
        raw = (own[at, :] + from_y[at, :].astype(f32)) * rstd[at, :]
        proj[at, :] = raw

        def rope(part, gain):
            n = part * inverse_norm(part) * gain[...]
            return (n * cos[at, :] + turn(n) * sin[at, :]).astype(bf16)

        for h in range(heads):
            q_out[at, h * size : (h + 1) * size] = rope(raw[:, h * size : (h + 1) * size], q_gain)
        k_out[at, :] = rope(raw[:, k_at:v_at], k_gain)
        v_out[at, :] = raw[:, v_at:].astype(bf16)
        return carry

    lax.fori_loop(0, 4, ready, 0)
    for i in range(4):
        start = i * block
        extent = start + block
        allowed = allowed_keys(seg_col, seg_row, start, block, extent)
        to = pl.ds(pl.multiple_of(lax.rem(start + side[0] * (rows // 2), rows), block), block)
        for h in range(heads):
            of_head = slice(h * size, (h + 1) * size)
            scores = contract_cols(q_out[start:extent, of_head], k_out[:extent, :]) * scale
            scores = jnp.where(allowed, scores, neg_big)
            top = jnp.max(scores, axis=-1, keepdims=True)
            expd = jnp.exp(scores - top)
            total = jnp.sum(expd, axis=-1, keepdims=True)
            weights = (expd * (1.0 / total)).astype(bf16)
            att[to, of_head] = dot(weights, v_out[:extent, :]).astype(bf16)
            lse[start:extent, h : h + 1] = top + jnp.log(total)


def attend_back_kernel(
    side, own, from_y, proj, q_in, k_in, v_in, lse, cos, sin, seg_col, seg_row, q_gain, k_gain,
    grads, q_gain_part, k_gain_part, inner, k_acc, v_acc,
):
    rows = own.shape[0]
    size = cos.shape[1]
    heads = q_in.shape[1] // size
    block = rows // 4
    scale = size**-0.5
    k_at = heads * size
    v_at = k_at + size

    def unrope(grad, part, gain, start):
        rows_at = slice(start, start + block)
        m = grad * cos[rows_at, :] - turn(grad) * sin[rows_at, :]
        r = inverse_norm(part)
        hat = part * r
        mg = m * gain[...]
        back = (r * (mg - hat * jnp.mean(mg * hat, axis=-1, keepdims=True))).astype(bf16)
        gain_part = jnp.sum(m * hat, axis=0, keepdims=True)
        return (back, gain_part, jnp.sum(back.astype(f32) * part, axis=-1, keepdims=True))

    k_acc[...] = jnp.zeros_like(k_acc)
    v_acc[...] = jnp.zeros_like(v_acc)
    q_total = jnp.zeros(q_gain_part.shape, f32)
    for i in range(4):
        start = i * block
        extent = start + block
        allowed = allowed_keys(seg_col, seg_row, start, block, extent)
        at = pl.ds(pl.multiple_of(lax.rem(start + side[0] * (rows // 2), rows), block), block)
        inner_sum = jnp.zeros((block, 1), f32)
        for h in range(heads):
            of_head = slice(h * size, (h + 1) * size)
            query = q_in[start:extent, of_head]
            grad = (own[at, of_head] + from_y[at, of_head].astype(f32)).astype(bf16)
            scores = contract_cols(query, k_in[:extent, :]) * scale
            scores = jnp.where(allowed, scores, neg_big)
            probs = jnp.exp(scores - lse[start:extent, h : h + 1])
            prob_grad = contract_cols(grad, v_in[:extent, :])
            delta = jnp.sum(probs * prob_grad, axis=-1, keepdims=True)
            score_grad = (probs * (prob_grad - delta)).astype(bf16)
            query_grad = dot(score_grad, k_in[:extent, :]) * scale
            k_acc[:extent, :] += contract_rows(score_grad, query) * scale
            v_acc[:extent, :] += contract_rows(probs.astype(bf16), grad)
            back, gain_part, part_inner = unrope(
                query_grad, proj[start:extent, of_head], q_gain, start
            )
            grads[start:extent, of_head] = back
            q_total = q_total + gain_part
            inner_sum = inner_sum + part_inner
        inner[start:extent, :] = inner_sum
    q_gain_part[...] = q_total
    k_total = jnp.zeros(k_gain_part.shape, f32)
    for i in range(4):
        start = i * block
        extent = start + block
        back, gain_part, part_inner = unrope(
            k_acc[start:extent, :], proj[start:extent, k_at:v_at], k_gain, start
        )
        grads[start:extent, k_at:v_at] = back
        k_total = k_total + gain_part
        v_back = v_acc[start:extent, :].astype(bf16)
        grads[start:extent, v_at:] = v_back
        inner[start:extent, :] += part_inner + jnp.sum(
            v_back.astype(f32) * proj[start:extent, v_at:], axis=-1, keepdims=True
        )
    k_gain_part[...] = k_total


vmem = pl.BlockSpec(memory_space=pltpu.VMEM)
smem = pl.BlockSpec(memory_space=pltpu.SMEM)
def whole_kernel(body, outs, scratch=(), grant=50):
    def call(*operands):
        return pl.pallas_call(
            body,
            out_shape=outs,
            in_specs=[smem if o.ndim == 1 else vmem for o in operands],
            out_specs=[vmem] * len(outs),
            scratch_shapes=scratch,
            compiler_params=pltpu.CompilerParams(vmem_limit_bytes=grant * 2**20),
            cost_estimate=pl.CostEstimate(flops=0, bytes_accessed=2**10, transcendentals=0),
        )(*operands)

    return call


def units_kernel(*refs):
    ins, weights, cots, downs = refs[:4], refs[4:8], refs[8:12], refs[12:16]
    rstd_ref = refs[16]
    hidden, pair, scaled, inner = refs[-4:]
    units = hidden.shape[1]
    chunk = min(256, units)
    rstd = rstd_ref[...]

    def product(at):
        total = dot(ins[0][...], weights[0][:, at])
        for k in range(1, 4):
            total = total + dot(ins[k][...], weights[k][:, at])
        return total * rstd

    inner_sum = jnp.zeros(inner.shape, f32)
    for start in range(0, units, chunk):
        of_gate = slice(start, start + chunk)
        of_up = slice(units + start, units + start + chunk)
        gate, up = product(of_gate), product(of_up)
        grad = contract_cols(cots[0][...], downs[0][of_gate, :])
        for k in range(1, 4):
            grad = grad + contract_cols(cots[k][...], downs[k][of_gate, :])
        sig = jax.nn.sigmoid(gate)
        silu = gate * sig
        hidden[:, of_gate] = low(silu * up)
        gate_grad = low(grad * up * sig * (1.0 + gate * (1.0 - sig)))
        up_grad = low(grad * silu)
        pair[:, of_gate] = gate_grad
        pair[:, of_up] = up_grad
        gate_grad, up_grad = gate_grad.astype(f32), up_grad.astype(f32)
        scaled[:, of_gate] = low(gate_grad * rstd)
        scaled[:, of_up] = low(up_grad * rstd)
        inner_sum = inner_sum + jnp.sum(gate_grad * gate + up_grad * up, axis=-1, keepdims=True)
    inner[...] = inner_sum


def units_of_half(ins, weights, cots, downs, rstd, which, earlier):
    half, depth = ins[0].shape
    units = downs[0].shape[0]
    block = half // 2
    first = which * (half // block)
    outs = [
        jax.ShapeDtypeStruct((2 * half, units), bf16),
        jax.ShapeDtypeStruct((2 * half, 2 * units), bf16),
        jax.ShapeDtypeStruct((2 * half, 2 * units), bf16),
        jax.ShapeDtypeStruct((2 * half, 1), f32),
    ]

    def whole(array):
        return pl.BlockSpec(array.shape, lambda i: (0, 0))

    def of_two(array, k):
        return pl.BlockSpec((None, *array.shape[1:]), lambda i: (k, 0, 0))

    near_by, core, both = downs
    downs = [near_by, core, both, both]
    down_specs = [whole(near_by), whole(core), of_two(both, 0), of_two(both, 1)]
    here = pl.BlockSpec((block, depth), lambda i: (i, 0))
    at = lambda i: (first + i, 0)
    of_all = pl.BlockSpec((block, depth), at)
    earlier = list(earlier or [])
    return pl.pallas_call(
        units_kernel,
        grid=(half // block,),
        out_shape=outs,
        in_specs=[here] * 4
        + [whole(w) for w in weights]
        + [of_all, of_all, here, here]
        + down_specs
        + [pl.BlockSpec((block, 1), at)]
        + [pl.BlockSpec(memory_space=pl.ANY)] * len(earlier),
        out_specs=[pl.BlockSpec((block, o.shape[1]), at) for o in outs],
        input_output_aliases={17 + k: k for k in range(len(earlier))},
        compiler_params=pltpu.CompilerParams(vmem_limit_bytes=50 * 2**20),
        cost_estimate=pl.CostEstimate(flops=0, bytes_accessed=2**10, transcendentals=0),
    )(*ins, *weights, *cots, *downs, rstd, *earlier)


def place_sums(scalars, pieces, outs, plan):
    flat = [a for piece in pieces for a in piece]

    def kernel(words, *refs):
        ins, results = list(refs[: len(flat)]), refs[len(flat) :]
        groups = [[ins.pop(0) for _ in piece] for piece in pieces]
        for k in range(4):

            @pl.when(pl.program_id(0) == k)
            def _(k=k):
                for piece, at, out, to in plan[k]:
                    value = groups[piece][0][at]
                    if len(groups[piece]) == 2:
                        value = jnp.where(words[4] == 1, value, groups[piece][1][at])
                    results[out][to] = value.astype(f32)

    def quarter(shape, axis):
        block = tuple(n // 4 if i == axis else n for i, n in enumerate(shape))
        if axis == 0:
            return pl.BlockSpec(block, lambda k, words: (words[k], 0))
        return pl.BlockSpec(block, lambda k, words: (0, words[k]))

    return pl.pallas_call(
        kernel,
        grid_spec=pltpu.PrefetchScalarGridSpec(
            num_scalar_prefetch=1,
            grid=(4,),
            in_specs=[pl.BlockSpec(a.shape, lambda k, words: (0, 0)) for a in flat],
            out_specs=[quarter(*out) for out in outs],
        ),
        out_shape=[jax.ShapeDtypeStruct(shape, f32) for shape, _ in outs],
        compiler_params=pltpu.CompilerParams(vmem_limit_bytes=50 * 2**20),
        cost_estimate=pl.CostEstimate(flops=0, bytes_accessed=2**10, transcendentals=0),
    )(scalars, *flat)


def on_device(
    tokens,
    cotangent,
    segment_ids,
    attn_gain,
    q_gain,
    k_gain,
    mlp_gain,
    w_query,
    w_key,
    w_value,
    w_out,
    w_gate,
    w_up,
    w_down,
):
    assert lax.axis_size("tc") == 4 and lax.axis_size("tr") == 2
    col = lax.axis_index("tc")
    side = lax.axis_index("tr")
    rows, width = tokens.shape
    half = rows // 2
    full_width = width * 4
    head_size = q_gain.shape[0]
    q_width = w_query.shape[1] // 4
    k_width = w_key.shape[1] // 4
    units = w_gate.shape[1] // 4
    around = [col, col ^ 1, col ^ 2, col ^ 3]

    def cols_of(array, which, size):
        return lax.dynamic_slice_in_dim(array, around[which] * size, size, 1)

    def rows_of(array, which, size):
        return lax.dynamic_slice_in_dim(array, around[which] * size, size, 0)

    def flip(array):
        return jnp.concatenate(
            [
                lax.dynamic_slice_in_dim(array, side * half, half, 0),
                lax.dynamic_slice_in_dim(array, (1 - side) * half, half, 0),
            ],
            axis=0,
        )

    shares = lax.axis_size("dp")
    place = lax.axis_index("dp")

    def share_of(block):
        size = block.shape[0] // shares
        return lax.dynamic_slice_in_dim(block, place * size, size, 0)

    def gather_shares(from_y, from_diag):
        return lax.all_gather(jnp.stack([from_y, from_diag]), "dp", axis=1, tiled=True)

    def ffn_columns(which, rows_at):
        return jnp.concatenate(
            [rows_at(cols_of(w, which, units)) for w in (w_gate, w_up)], axis=1
        )

    down_y, down_diag = (share_of(rows_of(w_down, k, units)) for k in (2, 3))
    share_y, share_diag = ffn_columns(2, share_of), ffn_columns(3, share_of)

    qkv_weights = [
        jnp.concatenate(
            [cols_of(w_query, k, q_width), cols_of(w_key, k, k_width), cols_of(w_value, k, k_width)],
            axis=1,
        )
        for k in range(4)
    ]
    inputs = tokens.astype(f32)
    down_y, down_diag = swap_y(down_y), swap_diag(down_diag)
    share_y, share_diag, inputs = after((share_y, share_diag, inputs), down_y, down_diag)
    scaled_in = low(inputs * attn_gain[None, :])
    raw_own, raw_y, for_y = scatter_width(lambda k: dot(scaled_in, qkv_weights[k]))
    down_gathered = gather_shares(down_y, down_diag)
    w_gate, w_up, w_down, w_out, segment_ids, cotangent, inputs = after(
        (w_gate, w_up, w_down, w_out, segment_ids, cotangent, inputs), for_y
    )
    square_sum = width_total(jnp.sum(inputs * inputs, axis=1))
    cos_table, sin_table = rope_tables(positions_of(segment_ids), head_size)
    side_word = side.astype(jnp.int32).reshape(1)
    tables = (
        cos_table,
        sin_table,
        segment_ids.reshape(rows, 1),
        segment_ids.reshape(1, rows),
        q_gain.reshape(1, head_size),
        k_gain.reshape(1, head_size),
    )
    whole = lambda block: block
    blocks_core = (ffn_columns(1, whole), rows_of(w_down, 1, units))
    raw_y, share_y, share_diag, square_sum = after(
        (raw_y, swap_y(share_y), swap_diag(share_diag), square_sum), raw_own, tables, blocks_core
    )
    ffn_y, ffn_diag = (lax.all_gather(w, "dp", axis=0, tiled=True) for w in (share_y, share_diag))
    attn_rstd = lax.rsqrt(square_sum / full_width + norm_eps)
    attn_hat = inputs * attn_rstd[:, None]
    normed = low(attn_hat * attn_gain[None, :])

    heads = q_width // head_size
    projected, q_low, k_low, v_low, log_totals, att_rel = whole_kernel(
        attend_kernel,
        [
            jax.ShapeDtypeStruct((rows, q_width + 2 * k_width), f32),
            jax.ShapeDtypeStruct((rows, q_width), bf16),
            jax.ShapeDtypeStruct((rows, k_width), bf16),
            jax.ShapeDtypeStruct((rows, k_width), bf16),
            jax.ShapeDtypeStruct((rows, heads), f32),
            jax.ShapeDtypeStruct((rows, q_width), bf16),
        ],
    )(side_word, raw_own, raw_y, attn_rstd.reshape(rows, 1), *tables)
    cot_rel = flip(cotangent)
    cot_y = swap_y(after(cot_rel[:half], raw_y))
    att_y, cot_x, down_gathered = after((swap_y(att_rel), swap_x(cot_y), down_gathered), att_rel)
    atts = [att_rel, swap_core(att_rel), att_y, swap_core(att_y)]
    outs = [rows_of(w_out, k, q_width) for k in range(4)]

    def out_rows(at):
        return (dot(atts[0][at], outs[0]) + dot(atts[1][at], outs[1])) + (
            dot(atts[2][at], outs[2]) + dot(atts[3][at], outs[3])
        )

    from_x = swap_x(low(out_rows(slice(half, rows))))
    home = out_rows(slice(0, half))

    prefetched = (
        swap_core(cot_rel),
        *map(swap_core, blocks_core),
    )
    from_x, (cot_core, ffn_core, down_core), ffn_y = after((from_x, prefetched, ffn_y), home)
    cot_y_core, cot_x_core = swap_core(cot_y), swap_core(cot_x)
    downs = (rows_of(w_down, 0, units), down_core, down_gathered)
    tokens_half = lax.dynamic_slice_in_dim(tokens, side * half, half, 0).astype(f32)
    residual = tokens_half + home + from_x.astype(f32)

    mlp_square = jnp.sum(residual * residual, axis=1)
    mlp_square = width_total(jnp.concatenate([mlp_square, swap_x(mlp_square)]))
    mlp_own = low(residual * mlp_gain[None, :])
    mlp_rstd = lax.rsqrt(mlp_square / full_width + norm_eps)
    quarter = half // 2
    mlp_x, mlp_y, mlp_rstd = after(
        (swap_x(mlp_own), swap_y(mlp_own), mlp_rstd), cot_y_core, cot_x_core
    )
    mlp_xy = (swap_y(mlp_x[:quarter]), swap_x(mlp_y[quarter:]))
    mlp_x_core = swap_core(mlp_x)
    ffns = [ffn_columns(0, whole), ffn_core, ffn_y, ffn_diag]
    downs = [rows_of(w_down, 0, units), down_core, down_gathered]
    ins_own = [mlp_own, swap_core(mlp_own), mlp_y, swap_core(mlp_y)]
    cots_own = [cot_rel, cot_core, cot_y, cot_y_core]
    cots_other = [cot_rel, cot_core, cot_x, cot_x_core]
    rstd_rel = mlp_rstd.reshape(rows, 1)
    first = units_of_half(ins_own, ffns, cots_own, downs, rstd_rel, 0, None)
    mlp_xy, mlp_x_core = after((mlp_xy, mlp_x_core), first)
    mlp_xy = jnp.concatenate(mlp_xy, axis=0)
    ins_other = [mlp_x, mlp_x_core, mlp_xy, swap_core(mlp_xy)]
    hidden, pair, pair_scaled, inner = units_of_half(
        ins_other, ffns, cots_other, downs, rstd_rel, 1, first
    )

    line = LineSums()
    mlp_in, mlp_core = (jnp.concatenate([ins_own[k], ins_other[k]], axis=0) for k in (0, 1))
    line.add("ffn", low(contract_rows(mlp_in, pair_scaled)), 1)
    line.send(line.send())
    pair = after(pair, line.pieces, line.waiting())

    kept = {}

    def started(marker):
        sums = width_total(after(inner[:, 0], marker))
        kept["inner"] = sums
        block = low(contract_rows(mlp_core, after(pair_scaled, marker)))
        kept["core"] = swap_core(block)
        down_core = low(contract_rows(after(hidden, block), cot_core))
        down_own = low(contract_rows(after(hidden, block), cot_rel))
        line.add("down", jnp.concatenate([down_own, swap_core(down_core)], axis=0), 0)
        return (line.send(down_own), sums)

    def turned(marker):
        sums = after(kept["inner"], marker)
        kept["inner"] = sums[:half] + swap_x(sums[half:])
        return (kept["inner"], line.send(marker))

    mlp_in_grad = scatter_all(lambda k: contract_cols(pair, ffns[k]), started, turned)
    inner_total = kept["inner"]
    mlp_hat = residual * mlp_rstd[:half, None]
    mlp_gain_part = jnp.sum(mlp_in_grad * mlp_hat, axis=0)
    residual_grad = cot_rel[:half].astype(f32) + mlp_rstd[:half, None] * (
        mlp_in_grad * mlp_gain[None, :] - mlp_hat * (inner_total / full_width)[:, None]
    )
    residual_low = low(residual_grad)
    res_x = after(swap_x(residual_low), line.send(residual_low))
    res_rel = jnp.concatenate([residual_low, res_x], axis=0)
    head_own, head_y, head_sent = scatter_width(
        lambda k: contract_cols(res_rel, outs[k]), line.send
    )

    line.add("ffn", kept["core"], 1)
    marker = line.send(head_sent)
    out_grads = [low(contract_rows(after(part, marker), res_rel)) for part in atts]
    line.add("out", jnp.concatenate(out_grads, axis=0), 0)
    head_own, head_y = after((head_own, head_y), line.waiting())

    proj_low, q_gain_part, k_gain_part, inner_attn = whole_kernel(
        attend_back_kernel,
        [
            jax.ShapeDtypeStruct((rows, q_width + 2 * k_width), bf16),
            jax.ShapeDtypeStruct((1, head_size), f32),
            jax.ShapeDtypeStruct((1, head_size), f32),
            jax.ShapeDtypeStruct((rows, 1), f32),
        ],
        scratch=[pltpu.VMEM((rows, k_width), f32), pltpu.VMEM((rows, k_width), f32)],
    )(side_word, head_own, head_y, projected, q_low, k_low, v_low, log_totals, *tables)
    proj_y, proj_core = swap_y(proj_low), swap_core(proj_low)

    line.add("qkv", low(contract_rows(after(normed, proj_low), proj_low)), 1)
    marker = proj_low
    for _ in range(5):
        marker = line.send(marker)
    proj_y, proj_core = after((proj_y, proj_core), marker)
    pairs = lax.all_gather(after(pair_scaled, proj_y), "tc")
    projs = [proj_low, proj_core, proj_y, swap_core(proj_y)]
    normed_part = low(
        (contract_cols(projs[0], qkv_weights[0]) + contract_cols(projs[1], qkv_weights[1]))
        + (contract_cols(projs[2], qkv_weights[2]) + contract_cols(projs[3], qkv_weights[3]))
    )
    small = jnp.concatenate([inner_attn[:, 0], q_gain_part[0], k_gain_part[0]])
    small = width_total(after(small, normed_part))
    small = jnp.concatenate([small, mlp_gain_part])
    for part in projs[1:]:
        line.add("qkv", low(contract_rows(after(normed, normed_part), part)), 1)
    normed_x, small_x = after(
        (swap_x(normed_part), swap_x(small)), line.send((small, line.waiting()))
    )
    small = small + small_x
    inner_attn, gains = small[:rows], small[rows:]
    hiddens = lax.all_gather(after(hidden, inner_attn), "tc", axis=1, tiled=True)
    spare = jnp.pad(low(gains), (0, width * width - gains.shape[0])).reshape(width, width)
    normed_grad = normed_part.astype(f32) + normed_x.astype(f32)
    token_grad = low(
        flip(res_rel).astype(f32)
        + attn_rstd[:, None]
        * (normed_grad * attn_gain[None, :] - attn_hat * (inner_attn / full_width)[:, None])
    )

    marker = line.send((token_grad, line.waiting()), False)
    marker = line.send(marker, False)
    pairs = after(pairs, marker)
    for k in (2, 3):
        block = lax.dynamic_index_in_dim(pairs, around[k], 0, keepdims=False)
        line.add("ffn", low(contract_rows(mlp_in, block)), 1)
    marker = (marker, line.waiting())
    for _ in range(5):
        marker = line.send(marker, False)

    hiddens = after(hiddens, marker)
    far_down = [low(contract_rows(cols_of(hiddens, k, units), cot_rel)) for k in (2, 3)]
    line.add("down", jnp.concatenate(far_down, axis=0), 0)
    line.add("gains", spare, 0)
    mlp_away = low(dot(hiddens[half:], w_down))
    mlp_x_out = after(swap_x(mlp_away), line.send((mlp_away, line.waiting()), False))
    mixed_half = low(residual + dot(hiddens[:half], w_down) + mlp_x_out.astype(f32))
    mixed_x = after(swap_x(mixed_half), line.send(mixed_half, False))
    mixed = flip(jnp.concatenate([mixed_half, mixed_x], axis=0))
    marker = mixed_x
    while line.queue:
        marker = line.send(marker, False)
    words = jnp.stack([*around, line.middle.astype(jnp.int32)]).astype(jnp.int32)
    everything = slice(None)

    def spread(start, size, extent):
        while size:
            piece, at = divmod(start, extent)
            taken = min(size, extent - at)
            yield (piece, slice(at, at + taken), taken)
            start, size = start + taken, size - taken

    def runs(first, start, size, extent, out, axis, to=0):
        plan = []
        for piece, at, taken in spread(start, size, extent):
            block = slice(to, to + taken)
            pair_of = lambda part: (part, everything) if axis == 0 else (everything, part)
            plan.append((first + piece, pair_of(at), out, pair_of(block)))
            to += taken
        return plan

    block_width = q_width + 2 * k_width
    qkv_plan = [
        runs(0, k * block_width, q_width, width, 0, 1)
        + runs(0, k * block_width + q_width, k_width, width, 1, 1)
        + runs(0, k * block_width + q_width + k_width, k_width, width, 2, 1)
        for k in range(4)
    ]
    ffn_plan = [
        runs(0, 2 * k * units, units, width, 0, 1) + runs(0, (2 * k + 1) * units, units, width, 1, 1)
        for k in range(4)
    ]
    placed = {}

    def fill(sums_of):
        out_plan = [runs(0, k * q_width, q_width, width, 0, 0) for k in range(4)]
        placed["out"] = place_sums(words, sums_of("out"), [(w_out.shape, 0)], out_plan)
        placed["qkv"] = place_sums(
            words, sums_of("qkv"), [(w.shape, 1) for w in (w_query, w_key, w_value)], qkv_plan
        )
        placed["ffn"] = place_sums(
            words, sums_of("ffn"), [(w.shape, 1) for w in (w_gate, w_up)], ffn_plan
        )
        return placed

    sums_of = line.finish(fill)
    [w_out_grad] = placed["out"]
    w_query_grad, w_key_grad, w_value_grad = placed["qkv"]
    w_gate_grad, w_up_grad = placed["ffn"]
    [w_down_grad] = place_sums(
        words,
        sums_of("down"),
        [(w_down.shape, 0)],
        [runs(0, k * units, units, width, 0, 0) for k in range(4)],
    )
    attn_gain_part = sum(
        jnp.sum(w.astype(f32) * g, axis=1)
        for w, g in ((w_query, w_query_grad), (w_key, w_key_grad), (w_value, w_value_grad))
    )
    attn_gain_grad = (attn_gain_part + swap_x(attn_gain_part)) / attn_gain
    [gain_sums] = sums_of("gains")
    gains = jnp.where(line.middle, gain_sums[0], gain_sums[-1]).reshape(-1).astype(f32)
    q_gain_grad = gains[:head_size]
    k_gain_grad = gains[head_size : 2 * head_size]
    mlp_gain_grad = gains[2 * head_size : 2 * head_size + width]
    return (
        mixed,
        token_grad,
        attn_gain_grad,
        q_gain_grad,
        k_gain_grad,
        mlp_gain_grad,
        w_query_grad,
        w_key_grad,
        w_value_grad,
        w_out_grad,
        w_gate_grad,
        w_up_grad,
        w_down_grad,
    )


def solution(mesh):
    in_specs = (
        P("dp", "tc"),
        P("dp", "tc"),
        P("dp"),
        P("tc"),
        P(),
        P(),
        P("tc"),
        P("tc", "tr"),
        P("tc", "tr"),
        P("tc", "tr"),
        P("tr", "tc"),
        P("tc", "tr"),
        P("tc", "tr"),
        P("tr", "tc"),
    )
    out_specs = (
        P("dp", "tc"),
        P("dp", "tc"),
        P("tc"),
        P(),
        P(),
        P("tc"),
        P("tc", "tr"),
        P("tc", "tr"),
        P("tc", "tr"),
        P("tr", "tc"),
        P("tc", "tr"),
        P("tc", "tr"),
        P("tr", "tc"),
    )
    return jax.shard_map(
        on_device, mesh=mesh, in_specs=in_specs, out_specs=out_specs, check_vma=False
    )
```

```python
import jax
import jax.numpy as jnp
from jax import lax
from jax.experimental import pallas as pl
from jax.experimental.pallas import tpu as pltpu
from jax.sharding import PartitionSpec as P

norm_eps = 1e-06
rope_base = 1000000.0
neg_big = -1e30
f32 = jnp.float32
bf16 = jnp.bfloat16


def dot(left_side, right_side):
    return jnp.dot(left_side, right_side, preferred_element_type=f32)


def contract_rows(left_side, right_side):
    return lax.dot_general(
        left_side, right_side, (((0,), (0,)), ((), ())), preferred_element_type=f32
    )


def contract_cols(left_side, right_side):
    return lax.dot_general(
        left_side, right_side, (((1,), (1,)), ((), ())), preferred_element_type=f32
    )


def swap_core(block):
    return lax.ppermute(block, "tc", [(i, i ^ 1) for i in range(4)])


def swap_y(block):
    return lax.ppermute(block, "tc", [(i, i ^ 2) for i in range(4)])


def swap_diag(block):
    return lax.ppermute(block, "tc", [(i, i ^ 3) for i in range(4)])


def swap_x(block):
    return lax.ppermute(block, "tr", [(0, 1), (1, 0)])


def width_total(rows):
    rows = rows + swap_core(rows)
    return rows + swap_y(rows)


class LineSums:
    def __init__(self, lag=3):
        self.lag = lag
        self.short = lax.axis_size("dp") == 4
        place = lax.axis_index("dp")
        self.middle = (place == 1) | (place == 2)
        self.queue, self.names, self.pieces = [], [], []
        self.outer, self.total = [], []

    def add(self, name, grad, axis):
        size = min(grad.shape)
        for k in range(0, grad.shape[axis], size):
            self.queue.append((name, lax.slice_in_dim(grad, k, k + size, axis=axis)))

    def waiting(self):
        return [piece for _, piece in self.queue]

    def _consume(self, which, marker):
        got, piece = after((self.outer[which], self.pieces[which]), marker)
        inward = low(piece.astype(f32) + got.astype(f32))
        across = lax.ppermute(inward, "dp", [(1, 2), (2, 1)])
        self.total.append(low(inward.astype(f32) + across.astype(f32)))
        return inward

    def _swap_outer(self, piece):
        self.outer.append(lax.ppermute(piece, "dp", [(0, 1), (1, 0), (2, 3), (3, 2)]))

    def send(self, marker=(), strict=True):
        which = len(self.pieces)
        name, piece = self.queue.pop(0)
        self.names.append(name)
        self.pieces.append(piece)
        if not self.short:
            return piece
        if which >= 2:
            marker = self._consume(which - 2, marker)
        out = after(piece, marker)
        if which >= self.lag:
            out = jnp.where(self.middle, self.total[which - self.lag], out)
        self._swap_outer(out)
        return (marker, out) if strict else marker

    def _named(self, sums):
        return lambda name: [s for n, s in zip(self.names, sums) if n == name]

    def _ready(self):
        return [(total, outer) for total, outer in zip(self.total, self.outer[self.lag :])]

    def finish(self, filler):
        count = len(self.pieces)
        if not self.short:
            named = self._named([(lax.psum(piece, "dp"),) for piece in self.pieces])
            filler(named)
            return named
        self._consume(count - 2, ())
        self._consume(count - 1, ())
        for which in range(count - self.lag, count):
            piece = self.total[which]
            if which == count - 2:
                piece = after(piece, filler(self._named(self._ready())))
            self._swap_outer(piece)
        return self._named(self._ready())


def after(value, *others):
    return lax.optimization_barrier((value, others))[0]


def low(array):
    return array.astype(bf16)


def scatter_width(product, near=lambda ready: ready):
    from_far = swap_core(low(product(3)))
    from_core = swap_core(low(product(1)))
    from_far = after(from_far, near(from_far))
    for_y = low(product(2) + from_far.astype(f32))
    from_y = swap_y(for_y)
    return (product(0) + from_core.astype(f32), from_y, for_y)


def scatter_all(product, started, turned):
    far_y, far_own = swap_core(low(product(3))), swap_core(low(product(1)))
    for_y = low(product(2) + far_y.astype(f32))
    own = low(product(0) + far_own.astype(f32))
    half = own.shape[0] // 2
    quarter = half // 2
    width = own.shape[1]
    y_first = swap_y(jnp.concatenate([for_y[quarter:half], for_y[half + quarter :]], axis=0))
    x_first = swap_x(
        jnp.concatenate([own[half : half + quarter], for_y[half : half + quarter]], axis=1)
    )
    x_first, y_first = after((x_first, y_first), started((own, for_y)))
    top_in = low(for_y[:quarter].astype(f32) + x_first[:, width:].astype(f32))
    low_in = low(own[half + quarter :].astype(f32) + y_first[quarter:].astype(f32))
    top_y, low_x = after((swap_y(top_in), swap_x(low_in)), turned((top_in, low_in)))
    top = own[:quarter].astype(f32) + x_first[:, :width].astype(f32) + top_y.astype(f32)
    bottom = own[quarter:half].astype(f32) + y_first[:quarter].astype(f32) + low_x.astype(f32)
    return jnp.concatenate([top, bottom], axis=0)


def positions_of(segment):
    slot_ids = jnp.arange(5, dtype=jnp.int32)
    before = jnp.sum((segment[None, :] < slot_ids[:, None]).astype(jnp.int32), axis=1)
    starts = jnp.sum(jnp.where(segment[:, None] == slot_ids[None, :], before[None, :], 0), axis=1)
    return jnp.arange(segment.shape[0], dtype=jnp.int32) - starts


def rope_tables(positions, head_size):
    half_size = head_size // 2
    frequency = rope_base ** (-jnp.arange(half_size, dtype=f32) * 2.0 / head_size)
    angles = positions.astype(f32)[:, None] * frequency[None, :]
    cosine, sine = jnp.cos(angles), jnp.sin(angles)
    return (
        jnp.concatenate([cosine, cosine], axis=1),
        jnp.concatenate([-sine, sine], axis=1),
    )


def turn(vectors):
    return pltpu.roll(vectors, vectors.shape[-1] // 2, axis=1)


def inverse_norm(vectors):
    return lax.rsqrt(jnp.mean(vectors * vectors, axis=-1, keepdims=True) + norm_eps)


def allowed_keys(seg_col, seg_row, start, size, extent):
    row = lax.broadcasted_iota(jnp.int32, (size, extent), 0) + start
    col = lax.broadcasted_iota(jnp.int32, (size, extent), 1)
    return (seg_col[start : start + size, :] == seg_row[:, :extent]) & (col <= row)


def attend_kernel(
    side, own, from_y, rstd, cos, sin, seg_col, seg_row, q_gain, k_gain,
    proj, q_out, k_out, v_out, lse, att,
):
    rows = own.shape[0]
    size = cos.shape[1]
    heads = q_out.shape[1] // size
    block = rows // 4
    scale = size**-0.5
    k_at = heads * size
    v_at = k_at + size

    def ready(i, carry):
        at = pl.ds(pl.multiple_of(i * block, block), block)
        raw = (own[at, :] + from_y[at, :].astype(f32)) * rstd[at, :]
        proj[at, :] = raw

        def rope(part, gain):
            n = part * inverse_norm(part) * gain[...]
            return (n * cos[at, :] + turn(n) * sin[at, :]).astype(bf16)

        for h in range(heads):
            q_out[at, h * size : (h + 1) * size] = rope(raw[:, h * size : (h + 1) * size], q_gain)
        k_out[at, :] = rope(raw[:, k_at:v_at], k_gain)
        v_out[at, :] = raw[:, v_at:].astype(bf16)
        return carry

    lax.fori_loop(0, 4, ready, 0)
    for i in range(4):
        start = i * block
        extent = start + block
        allowed = allowed_keys(seg_col, seg_row, start, block, extent)
        to = pl.ds(pl.multiple_of(lax.rem(start + side[0] * (rows // 2), rows), block), block)
        for h in range(heads):
            of_head = slice(h * size, (h + 1) * size)
            scores = contract_cols(q_out[start:extent, of_head], k_out[:extent, :]) * scale
            scores = jnp.where(allowed, scores, neg_big)
            top = jnp.max(scores, axis=-1, keepdims=True)
            expd = jnp.exp(scores - top)
            total = jnp.sum(expd, axis=-1, keepdims=True)
            weights = (expd * (1.0 / total)).astype(bf16)
            att[to, of_head] = dot(weights, v_out[:extent, :]).astype(bf16)
            lse[start:extent, h : h + 1] = top + jnp.log(total)


def attend_back_kernel(
    side, own, from_y, proj, q_in, k_in, v_in, lse, cos, sin, seg_col, seg_row, q_gain, k_gain,
    grads, q_gain_part, k_gain_part, inner, k_acc, v_acc,
):
    rows = own.shape[0]
    size = cos.shape[1]
    heads = q_in.shape[1] // size
    block = rows // 4
    scale = size**-0.5
    k_at = heads * size
    v_at = k_at + size

    def unrope(grad, part, gain, start):
        rows_at = slice(start, start + block)
        m = grad * cos[rows_at, :] - turn(grad) * sin[rows_at, :]
        r = inverse_norm(part)
        hat = part * r
        mg = m * gain[...]
        back = (r * (mg - hat * jnp.mean(mg * hat, axis=-1, keepdims=True))).astype(bf16)
        gain_part = jnp.sum(m * hat, axis=0, keepdims=True)
        return (back, gain_part, jnp.sum(back.astype(f32) * part, axis=-1, keepdims=True))

    k_acc[...] = jnp.zeros_like(k_acc)
    v_acc[...] = jnp.zeros_like(v_acc)
    q_total = jnp.zeros(q_gain_part.shape, f32)
    for i in range(4):
        start = i * block
        extent = start + block
        allowed = allowed_keys(seg_col, seg_row, start, block, extent)
        at = pl.ds(pl.multiple_of(lax.rem(start + side[0] * (rows // 2), rows), block), block)
        inner_sum = jnp.zeros((block, 1), f32)
        for h in range(heads):
            of_head = slice(h * size, (h + 1) * size)
            query = q_in[start:extent, of_head]
            grad = (own[at, of_head] + from_y[at, of_head].astype(f32)).astype(bf16)
            scores = contract_cols(query, k_in[:extent, :]) * scale
            scores = jnp.where(allowed, scores, neg_big)
            probs = jnp.exp(scores - lse[start:extent, h : h + 1])
            prob_grad = contract_cols(grad, v_in[:extent, :])
            delta = jnp.sum(probs * prob_grad, axis=-1, keepdims=True)
            score_grad = (probs * (prob_grad - delta)).astype(bf16)
            query_grad = dot(score_grad, k_in[:extent, :]) * scale
            k_acc[:extent, :] += contract_rows(score_grad, query) * scale
            v_acc[:extent, :] += contract_rows(probs.astype(bf16), grad)
            back, gain_part, part_inner = unrope(
                query_grad, proj[start:extent, of_head], q_gain, start
            )
            grads[start:extent, of_head] = back
            q_total = q_total + gain_part
            inner_sum = inner_sum + part_inner
        inner[start:extent, :] = inner_sum
    q_gain_part[...] = q_total
    k_total = jnp.zeros(k_gain_part.shape, f32)
    for i in range(4):
        start = i * block
        extent = start + block
        back, gain_part, part_inner = unrope(
            k_acc[start:extent, :], proj[start:extent, k_at:v_at], k_gain, start
        )
        grads[start:extent, k_at:v_at] = back
        k_total = k_total + gain_part
        v_back = v_acc[start:extent, :].astype(bf16)
        grads[start:extent, v_at:] = v_back
        inner[start:extent, :] += part_inner + jnp.sum(
            v_back.astype(f32) * proj[start:extent, v_at:], axis=-1, keepdims=True
        )
    k_gain_part[...] = k_total


vmem = pl.BlockSpec(memory_space=pltpu.VMEM)
smem = pl.BlockSpec(memory_space=pltpu.SMEM)
def whole_kernel(body, outs, scratch=(), grant=50):
    def call(*operands):
        return pl.pallas_call(
            body,
            out_shape=outs,
            in_specs=[smem if o.ndim == 1 else vmem for o in operands],
            out_specs=[vmem] * len(outs),
            scratch_shapes=scratch,
            compiler_params=pltpu.CompilerParams(vmem_limit_bytes=grant * 2**20),
            cost_estimate=pl.CostEstimate(flops=0, bytes_accessed=2**10, transcendentals=0),
        )(*operands)

    return call


def units_kernel(*refs):
    ins, weights, cots, downs = refs[:4], refs[4:8], refs[8:12], refs[12:16]
    rstd_ref = refs[16]
    hidden, pair, scaled, inner = refs[-4:]
    units = hidden.shape[1]
    chunk = min(256, units)
    rstd = rstd_ref[...]

    def product(at):
        total = dot(ins[0][...], weights[0][:, at])
        for k in range(1, 4):
            total = total + dot(ins[k][...], weights[k][:, at])
        return total * rstd

    inner_sum = jnp.zeros(inner.shape, f32)
    for start in range(0, units, chunk):
        of_gate = slice(start, start + chunk)
        of_up = slice(units + start, units + start + chunk)
        gate, up = product(of_gate), product(of_up)
        grad = contract_cols(cots[0][...], downs[0][of_gate, :])
        for k in range(1, 4):
            grad = grad + contract_cols(cots[k][...], downs[k][of_gate, :])
        sig = jax.nn.sigmoid(gate)
        silu = gate * sig
        hidden[:, of_gate] = low(silu * up)
        gate_grad = low(grad * up * sig * (1.0 + gate * (1.0 - sig)))
        up_grad = low(grad * silu)
        pair[:, of_gate] = gate_grad
        pair[:, of_up] = up_grad
        gate_grad, up_grad = gate_grad.astype(f32), up_grad.astype(f32)
        scaled[:, of_gate] = low(gate_grad * rstd)
        scaled[:, of_up] = low(up_grad * rstd)
        inner_sum = inner_sum + jnp.sum(gate_grad * gate + up_grad * up, axis=-1, keepdims=True)
    inner[...] = inner_sum


def units_of_half(ins, weights, cots, downs, rstd, which, earlier):
    half, depth = ins[0].shape
    units = downs[0].shape[0]
    block = half // 2
    first = which * (half // block)
    outs = [
        jax.ShapeDtypeStruct((2 * half, units), bf16),
        jax.ShapeDtypeStruct((2 * half, 2 * units), bf16),
        jax.ShapeDtypeStruct((2 * half, 2 * units), bf16),
        jax.ShapeDtypeStruct((2 * half, 1), f32),
    ]

    def whole(array):
        return pl.BlockSpec(array.shape, lambda i: (0, 0))

    def of_two(array, k):
        return pl.BlockSpec((None, *array.shape[1:]), lambda i: (k, 0, 0))

    near_by, core, both = downs
    downs = [near_by, core, both, both]
    down_specs = [whole(near_by), whole(core), of_two(both, 0), of_two(both, 1)]
    here = pl.BlockSpec((block, depth), lambda i: (i, 0))
    at = lambda i: (first + i, 0)
    of_all = pl.BlockSpec((block, depth), at)
    earlier = list(earlier or [])
    return pl.pallas_call(
        units_kernel,
        grid=(half // block,),
        out_shape=outs,
        in_specs=[here] * 4
        + [whole(w) for w in weights]
        + [of_all, of_all, here, here]
        + down_specs
        + [pl.BlockSpec((block, 1), at)]
        + [pl.BlockSpec(memory_space=pl.ANY)] * len(earlier),
        out_specs=[pl.BlockSpec((block, o.shape[1]), at) for o in outs],
        input_output_aliases={17 + k: k for k in range(len(earlier))},
        compiler_params=pltpu.CompilerParams(vmem_limit_bytes=50 * 2**20),
        cost_estimate=pl.CostEstimate(flops=0, bytes_accessed=2**10, transcendentals=0),
    )(*ins, *weights, *cots, *downs, rstd, *earlier)


def place_sums(scalars, pieces, outs, plan):
    flat = [a for piece in pieces for a in piece]

    def kernel(words, *refs):
        ins, results = list(refs[: len(flat)]), refs[len(flat) :]
        groups = [[ins.pop(0) for _ in piece] for piece in pieces]
        for k in range(4):

            @pl.when(pl.program_id(0) == k)
            def _(k=k):
                for piece, at, out, to in plan[k]:
                    value = groups[piece][0][at]
                    if len(groups[piece]) == 2:
                        value = jnp.where(words[4] == 1, value, groups[piece][1][at])
                    results[out][to] = value.astype(f32)

    def quarter(shape, axis):
        block = tuple(n // 4 if i == axis else n for i, n in enumerate(shape))
        if axis == 0:
            return pl.BlockSpec(block, lambda k, words: (words[k], 0))
        return pl.BlockSpec(block, lambda k, words: (0, words[k]))

    return pl.pallas_call(
        kernel,
        grid_spec=pltpu.PrefetchScalarGridSpec(
            num_scalar_prefetch=1,
            grid=(4,),
            in_specs=[pl.BlockSpec(a.shape, lambda k, words: (0, 0)) for a in flat],
            out_specs=[quarter(*out) for out in outs],
        ),
        out_shape=[jax.ShapeDtypeStruct(shape, f32) for shape, _ in outs],
        compiler_params=pltpu.CompilerParams(vmem_limit_bytes=50 * 2**20),
        cost_estimate=pl.CostEstimate(flops=0, bytes_accessed=2**10, transcendentals=0),
    )(scalars, *flat)


def on_device(
    tokens,
    cotangent,
    segment_ids,
    attn_gain,
    q_gain,
    k_gain,
    mlp_gain,
    w_query,
    w_key,
    w_value,
    w_out,
    w_gate,
    w_up,
    w_down,
):
    assert lax.axis_size("tc") == 4 and lax.axis_size("tr") == 2
    col = lax.axis_index("tc")
    side = lax.axis_index("tr")
    rows, width = tokens.shape
    half = rows // 2
    full_width = width * 4
    head_size = q_gain.shape[0]
    q_width = w_query.shape[1] // 4
    k_width = w_key.shape[1] // 4
    units = w_gate.shape[1] // 4
    around = [col, col ^ 1, col ^ 2, col ^ 3]

    def cols_of(array, which, size):
        return lax.dynamic_slice_in_dim(array, around[which] * size, size, 1)

    def rows_of(array, which, size):
        return lax.dynamic_slice_in_dim(array, around[which] * size, size, 0)

    def flip(array):
        return jnp.concatenate(
            [
                lax.dynamic_slice_in_dim(array, side * half, half, 0),
                lax.dynamic_slice_in_dim(array, (1 - side) * half, half, 0),
            ],
            axis=0,
        )

    shares = lax.axis_size("dp")
    place = lax.axis_index("dp")

    def share_of(block):
        size = block.shape[0] // shares
        return lax.dynamic_slice_in_dim(block, place * size, size, 0)

    def gather_shares(from_y, from_diag):
        return lax.all_gather(jnp.stack([from_y, from_diag]), "dp", axis=1, tiled=True)

    def ffn_columns(which, rows_at):
        return jnp.concatenate(
            [rows_at(cols_of(w, which, units)) for w in (w_gate, w_up)], axis=1
        )

    down_y, down_diag = (share_of(rows_of(w_down, k, units)) for k in (2, 3))
    share_y, share_diag = ffn_columns(2, share_of), ffn_columns(3, share_of)

    qkv_weights = [
        jnp.concatenate(
            [cols_of(w_query, k, q_width), cols_of(w_key, k, k_width), cols_of(w_value, k, k_width)],
            axis=1,
        )
        for k in range(4)
    ]
    inputs = tokens.astype(f32)
    down_y, down_diag = swap_y(down_y), swap_diag(down_diag)
    share_y, share_diag, inputs = after((share_y, share_diag, inputs), down_y, down_diag)
    scaled_in = low(inputs * attn_gain[None, :])
    raw_own, raw_y, for_y = scatter_width(lambda k: dot(scaled_in, qkv_weights[k]))
    down_gathered = gather_shares(down_y, down_diag)
    w_gate, w_up, w_down, w_out, segment_ids, cotangent, inputs = after(
        (w_gate, w_up, w_down, w_out, segment_ids, cotangent, inputs), for_y
    )
    square_sum = width_total(jnp.sum(inputs * inputs, axis=1))
    cos_table, sin_table = rope_tables(positions_of(segment_ids), head_size)
    side_word = side.astype(jnp.int32).reshape(1)
    tables = (
        cos_table,
        sin_table,
        segment_ids.reshape(rows, 1),
        segment_ids.reshape(1, rows),
        q_gain.reshape(1, head_size),
        k_gain.reshape(1, head_size),
    )
    whole = lambda block: block
    blocks_core = (ffn_columns(1, whole), rows_of(w_down, 1, units))
    raw_y, share_y, share_diag, square_sum = after(
        (raw_y, swap_y(share_y), swap_diag(share_diag), square_sum), raw_own, tables, blocks_core
    )
    ffn_y, ffn_diag = (lax.all_gather(w, "dp", axis=0, tiled=True) for w in (share_y, share_diag))
    attn_rstd = lax.rsqrt(square_sum / full_width + norm_eps)
    attn_hat = inputs * attn_rstd[:, None]
    normed = low(attn_hat * attn_gain[None, :])

    heads = q_width // head_size
    projected, q_low, k_low, v_low, log_totals, att_rel = whole_kernel(
        attend_kernel,
        [
            jax.ShapeDtypeStruct((rows, q_width + 2 * k_width), f32),
            jax.ShapeDtypeStruct((rows, q_width), bf16),
            jax.ShapeDtypeStruct((rows, k_width), bf16),
            jax.ShapeDtypeStruct((rows, k_width), bf16),
            jax.ShapeDtypeStruct((rows, heads), f32),
            jax.ShapeDtypeStruct((rows, q_width), bf16),
        ],
    )(side_word, raw_own, raw_y, attn_rstd.reshape(rows, 1), *tables)
    cot_rel = flip(cotangent)
    cot_y = swap_y(after(cot_rel[:half], raw_y))
    att_y, cot_x, down_gathered = after((swap_y(att_rel), swap_x(cot_y), down_gathered), att_rel)
    atts = [att_rel, swap_core(att_rel), att_y, swap_core(att_y)]
    outs = [rows_of(w_out, k, q_width) for k in range(4)]

    def out_rows(at):
        return (dot(atts[0][at], outs[0]) + dot(atts[1][at], outs[1])) + (
            dot(atts[2][at], outs[2]) + dot(atts[3][at], outs[3])
        )

    from_x = swap_x(low(out_rows(slice(half, rows))))
    home = out_rows(slice(0, half))

    prefetched = (
        swap_core(cot_rel),
        *map(swap_core, blocks_core),
    )
    from_x, (cot_core, ffn_core, down_core), ffn_y = after((from_x, prefetched, ffn_y), home)
    cot_y_core, cot_x_core = swap_core(cot_y), swap_core(cot_x)
    downs = (rows_of(w_down, 0, units), down_core, down_gathered)
    tokens_half = lax.dynamic_slice_in_dim(tokens, side * half, half, 0).astype(f32)
    residual = tokens_half + home + from_x.astype(f32)

    mlp_square = jnp.sum(residual * residual, axis=1)
    mlp_square = width_total(jnp.concatenate([mlp_square, swap_x(mlp_square)]))
    mlp_own = low(residual * mlp_gain[None, :])
    mlp_rstd = lax.rsqrt(mlp_square / full_width + norm_eps)
    quarter = half // 2
    mlp_x, mlp_y, mlp_rstd = after(
        (swap_x(mlp_own), swap_y(mlp_own), mlp_rstd), cot_y_core, cot_x_core
    )
    mlp_xy = (swap_y(mlp_x[:quarter]), swap_x(mlp_y[quarter:]))
    mlp_x_core = swap_core(mlp_x)
    ffns = [ffn_columns(0, whole), ffn_core, ffn_y, ffn_diag]
    downs = [rows_of(w_down, 0, units), down_core, down_gathered]
    ins_own = [mlp_own, swap_core(mlp_own), mlp_y, swap_core(mlp_y)]
    cots_own = [cot_rel, cot_core, cot_y, cot_y_core]
    cots_other = [cot_rel, cot_core, cot_x, cot_x_core]
    rstd_rel = mlp_rstd.reshape(rows, 1)
    first = units_of_half(ins_own, ffns, cots_own, downs, rstd_rel, 0, None)
    mlp_xy, mlp_x_core = after((mlp_xy, mlp_x_core), first)
    mlp_xy = jnp.concatenate(mlp_xy, axis=0)
    ins_other = [mlp_x, mlp_x_core, mlp_xy, swap_core(mlp_xy)]
    hidden, pair, pair_scaled, inner = units_of_half(
        ins_other, ffns, cots_other, downs, rstd_rel, 1, first
    )

    line = LineSums()
    mlp_in, mlp_core = (jnp.concatenate([ins_own[k], ins_other[k]], axis=0) for k in (0, 1))
    line.add("ffn", low(contract_rows(mlp_in, pair_scaled)), 1)
    line.send(line.send())
    pair = after(pair, line.pieces, line.waiting())

    kept = {}

    def started(marker):
        sums = width_total(after(inner[:, 0], marker))
        kept["inner"] = sums
        block = low(contract_rows(mlp_core, after(pair_scaled, marker)))
        kept["core"] = swap_core(block)
        down_core = low(contract_rows(after(hidden, block), cot_core))
        down_own = low(contract_rows(after(hidden, block), cot_rel))
        line.add("down", jnp.concatenate([down_own, swap_core(down_core)], axis=0), 0)
        return (line.send(down_own), sums)

    def turned(marker):
        sums = after(kept["inner"], marker)
        kept["inner"] = sums[:half] + swap_x(sums[half:])
        return (kept["inner"], line.send(marker))

    mlp_in_grad = scatter_all(lambda k: contract_cols(pair, ffns[k]), started, turned)
    inner_total = kept["inner"]
    mlp_hat = residual * mlp_rstd[:half, None]
    mlp_gain_part = jnp.sum(mlp_in_grad * mlp_hat, axis=0)
    residual_grad = cot_rel[:half].astype(f32) + mlp_rstd[:half, None] * (
        mlp_in_grad * mlp_gain[None, :] - mlp_hat * (inner_total / full_width)[:, None]
    )
    residual_low = low(residual_grad)
    res_x = after(swap_x(residual_low), line.send(residual_low))
    res_rel = jnp.concatenate([residual_low, res_x], axis=0)
    head_own, head_y, head_sent = scatter_width(
        lambda k: contract_cols(res_rel, outs[k]), line.send
    )

    line.add("ffn", kept["core"], 1)
    marker = line.send(head_sent)
    out_grads = [low(contract_rows(after(part, marker), res_rel)) for part in atts]
    line.add("out", jnp.concatenate(out_grads, axis=0), 0)
    head_own, head_y = after((head_own, head_y), line.waiting())

    proj_low, q_gain_part, k_gain_part, inner_attn = whole_kernel(
        attend_back_kernel,
        [
            jax.ShapeDtypeStruct((rows, q_width + 2 * k_width), bf16),
            jax.ShapeDtypeStruct((1, head_size), f32),
            jax.ShapeDtypeStruct((1, head_size), f32),
            jax.ShapeDtypeStruct((rows, 1), f32),
        ],
        scratch=[pltpu.VMEM((rows, k_width), f32), pltpu.VMEM((rows, k_width), f32)],
    )(side_word, head_own, head_y, projected, q_low, k_low, v_low, log_totals, *tables)
    proj_y, proj_core = swap_y(proj_low), swap_core(proj_low)

    marker = proj_low
    for _ in range(4):
        marker = line.send(marker)
    proj_y, proj_core = after((proj_y, proj_core), marker)
    pairs = lax.all_gather(after(pair_scaled, proj_y), "tc")
    projs = [proj_low, proj_core, proj_y, swap_core(proj_y)]
    normed_part = low(
        (contract_cols(projs[0], qkv_weights[0]) + contract_cols(projs[1], qkv_weights[1]))
        + (contract_cols(projs[2], qkv_weights[2]) + contract_cols(projs[3], qkv_weights[3]))
    )
    small = jnp.concatenate([inner_attn[:, 0], q_gain_part[0], k_gain_part[0]])
    small = width_total(after(small, normed_part))
    small = jnp.concatenate([small, mlp_gain_part])
    for part in projs:
        line.add("qkv", low(contract_rows(after(normed, normed_part), part)), 1)
    normed_x, small_x = after(
        (swap_x(normed_part), swap_x(small)), line.send((small, line.waiting()))
    )
    small = small + small_x
    inner_attn, gains = small[:rows], small[rows:]
    hiddens = lax.all_gather(after(hidden, inner_attn), "tc", axis=1, tiled=True)
    spare = jnp.pad(low(gains), (0, width * width - gains.shape[0])).reshape(width, width)
    normed_grad = normed_part.astype(f32) + normed_x.astype(f32)
    token_grad = low(
        flip(res_rel).astype(f32)
        + attn_rstd[:, None]
        * (normed_grad * attn_gain[None, :] - attn_hat * (inner_attn / full_width)[:, None])
    )

    marker = line.send((token_grad, line.waiting()), False)
    for _ in range(2):
        marker = line.send(marker, False)
    pairs = after(pairs, marker)
    for k in (2, 3):
        block = lax.dynamic_index_in_dim(pairs, around[k], 0, keepdims=False)
        line.add("ffn", low(contract_rows(mlp_in, block)), 1)
    marker = (marker, line.waiting())
    for _ in range(5):
        marker = line.send(marker, False)

    hiddens = after(hiddens, marker)
    far_down = [low(contract_rows(cols_of(hiddens, k, units), cot_rel)) for k in (2, 3)]
    line.add("down", jnp.concatenate(far_down, axis=0), 0)
    line.add("gains", spare, 0)
    mlp_away = low(dot(hiddens[half:], w_down))
    mlp_x_out = after(swap_x(mlp_away), line.send((mlp_away, line.waiting()), False))
    mixed_half = low(residual + dot(hiddens[:half], w_down) + mlp_x_out.astype(f32))
    mixed_x = after(swap_x(mixed_half), line.send(mixed_half, False))
    mixed = flip(jnp.concatenate([mixed_half, mixed_x], axis=0))
    marker = mixed_x
    while line.queue:
        marker = line.send(marker, False)
    words = jnp.stack([*around, line.middle.astype(jnp.int32)]).astype(jnp.int32)
    everything = slice(None)

    def spread(start, size, extent):
        while size:
            piece, at = divmod(start, extent)
            taken = min(size, extent - at)
            yield (piece, slice(at, at + taken), taken)
            start, size = start + taken, size - taken

    def runs(first, start, size, extent, out, axis, to=0):
        plan = []
        for piece, at, taken in spread(start, size, extent):
            block = slice(to, to + taken)
            pair_of = lambda part: (part, everything) if axis == 0 else (everything, part)
            plan.append((first + piece, pair_of(at), out, pair_of(block)))
            to += taken
        return plan

    block_width = q_width + 2 * k_width
    qkv_plan = [
        runs(0, k * block_width, q_width, width, 0, 1)
        + runs(0, k * block_width + q_width, k_width, width, 1, 1)
        + runs(0, k * block_width + q_width + k_width, k_width, width, 2, 1)
        for k in range(4)
    ]
    ffn_plan = [
        runs(0, 2 * k * units, units, width, 0, 1) + runs(0, (2 * k + 1) * units, units, width, 1, 1)
        for k in range(4)
    ]
    placed = {}

    def fill(sums_of):
        out_plan = [runs(0, k * q_width, q_width, width, 0, 0) for k in range(4)]
        placed["out"] = place_sums(words, sums_of("out"), [(w_out.shape, 0)], out_plan)
        placed["qkv"] = place_sums(
            words, sums_of("qkv"), [(w.shape, 1) for w in (w_query, w_key, w_value)], qkv_plan
        )
        placed["ffn"] = place_sums(
            words, sums_of("ffn"), [(w.shape, 1) for w in (w_gate, w_up)], ffn_plan
        )
        return placed

    sums_of = line.finish(fill)
    [w_out_grad] = placed["out"]
    w_query_grad, w_key_grad, w_value_grad = placed["qkv"]
    w_gate_grad, w_up_grad = placed["ffn"]
    [w_down_grad] = place_sums(
        words,
        sums_of("down"),
        [(w_down.shape, 0)],
        [runs(0, k * units, units, width, 0, 0) for k in range(4)],
    )
    attn_gain_part = sum(
        jnp.sum(w.astype(f32) * g, axis=1)
        for w, g in ((w_query, w_query_grad), (w_key, w_key_grad), (w_value, w_value_grad))
    )
    attn_gain_grad = (attn_gain_part + swap_x(attn_gain_part)) / attn_gain
    [gain_sums] = sums_of("gains")
    gains = jnp.where(line.middle, gain_sums[0], gain_sums[-1]).reshape(-1).astype(f32)
    q_gain_grad = gains[:head_size]
    k_gain_grad = gains[head_size : 2 * head_size]
    mlp_gain_grad = gains[2 * head_size : 2 * head_size + width]
    return (
        mixed,
        token_grad,
        attn_gain_grad,
        q_gain_grad,
        k_gain_grad,
        mlp_gain_grad,
        w_query_grad,
        w_key_grad,
        w_value_grad,
        w_out_grad,
        w_gate_grad,
        w_up_grad,
        w_down_grad,
    )


def solution(mesh):
    in_specs = (
        P("dp", "tc"),
        P("dp", "tc"),
        P("dp"),
        P("tc"),
        P(),
        P(),
        P("tc"),
        P("tc", "tr"),
        P("tc", "tr"),
        P("tc", "tr"),
        P("tr", "tc"),
        P("tc", "tr"),
        P("tc", "tr"),
        P("tr", "tc"),
    )
    out_specs = (
        P("dp", "tc"),
        P("dp", "tc"),
        P("tc"),
        P(),
        P(),
        P("tc"),
        P("tc", "tr"),
        P("tc", "tr"),
        P("tc", "tr"),
        P("tr", "tc"),
        P("tc", "tr"),
        P("tc", "tr"),
        P("tr", "tc"),
    )
    return jax.shard_map(
        on_device, mesh=mesh, in_specs=in_specs, out_specs=out_specs, check_vma=False
    )
```
